32 devices in a mesh: wide: 8 (over z, x), narrow: 4 (over y, core).
Axes of the slice: x: 2, y: 2, z: 4, core: 2. Of those that a mesh axis runs over, the one named last changes fastest.
Arguments:
- tokens: bfloat16 [64, 256, 1024], P('wide'), may hold values from -6 to 6
- frame_counts: int32 [4], replicated, may hold values from 4 to 16, as said below
- actions: int32 [64], P('wide'), may hold values from 0 to 7
- action_table: bfloat16 [8, 1024], replicated, may hold values from -3 to 3
- norm_gains: float32 [3, 1024], replicated, may hold values from 0.25 to 1.75
- spatial_project: bfloat16 [1024, 3, 1024], P(None, None, 'narrow'), may hold values from -0.1875 to 0.1875
- spatial_merge: bfloat16 [1024, 1024], P('narrow'), may hold values from -0.75 to 0.75
- temporal_project: bfloat16 [1024, 3, 1024], P(None, None, 'narrow'), may hold values from -0.1875 to 0.1875
- temporal_merge: bfloat16 [1024, 1024], P('narrow'), may hold values from -0.375 to 0.375
- expand_weight: bfloat16 [1024, 4096], P(None, 'narrow'), may hold values from -0.1875 to 0.1875
- reduce_weight: bfloat16 [4096, 1024], P('narrow'), may hold values from -0.09375 to 0.09375
- grad_out: bfloat16 [64, 256, 1024], P('wide'), may hold values from -6 to 6
Outputs:
- output: bfloat16 [64, 256, 1024], P('wide')
- grad_tokens: float32 [64, 256, 1024], P('wide')
- norm_gains_grad: float32 [3, 1024], P(None, 'wide')
- action_table_grad: float32 [8, 1024], P(None, 'wide')
- spatial_project_grad: float32 [1024, 3, 1024], P('wide', None, 'narrow')
- spatial_merge_grad: float32 [1024, 1024], P('narrow', 'wide')
- temporal_project_grad: float32 [1024, 3, 1024], P('wide', None, 'narrow')
- temporal_merge_grad: float32 [1024, 1024], P('narrow', 'wide')
- expand_weight_grad: float32 [1024, 4096], P('wide', 'narrow')
- reduce_weight_grad: float32 [4096, 1024], P('narrow', 'wide')
The draws below stay inside these ranges and needn't reach their ends.
Inputs may be any that keep to these rules, and one draw needn't show every extreme that they name: `frame_counts`: every clip has its real frames in its first slots; in every draw one clip has 16.
All inputs are finite; a program needn't handle non-finite values.
Results may differ from the reference program's by a relative error of at most 0.033.
Values may be sent and summed in bfloat16 or wider, within the bound.
A program may use at most 192 MiB of HBM per device.

```python
import jax
import jax.numpy as jnp
from jax import lax

D = 1024
HD = 64
FF = 4096
ACTIONS = 8
FRAMES = 16
S = 256
NF = 64
CLIPS = 4


def draw_frame_counts(key, part):
    key = jax.random.fold_in(key, 11)
    first_key, second_key, third_key = jax.random.split(key, 3)
    counted = jax.random.randint(first_key, (CLIPS,), 4, FRAMES + 1)
    longest = jax.random.randint(second_key, (), 0, CLIPS)
    shortest = (longest + 1 + jax.random.randint(third_key, (), 0, CLIPS - 1)) % CLIPS
    places = jnp.arange(CLIPS)
    counted = jnp.where((places == shortest) & (CLIPS > 2), 4, counted)
    counted = jnp.where(places == longest, FRAMES, counted)
    return counted.astype(jnp.int32)


def touch_ends(values, rng, smallest, largest):
    spot = [jax.random.randint(jax.random.fold_in(rng, axis), (), 0, length) for axis, length in enumerate(values.shape)]
    main_axis = values.shape.index(max(values.shape))
    beside = spot[:main_axis] + [(spot[main_axis] + 1) % values.shape[main_axis]] + spot[main_axis + 1:]
    return values.at[tuple(spot)].set(smallest).at[tuple(beside)].set(largest)


def spiked(entries, key, source, target, blocks, factor):
    owner, partner = [(jnp.arange(entries.shape[position]) // (entries.shape[position] // blocks)).reshape([-1 if axis == position else 1 for axis in range(entries.ndim)]) for position in (source, target)]
    chosen = jax.random.permutation(key, blocks)[partner]
    strong = (owner == chosen) | (owner == (partner + blocks // 2) % blocks)
    return jnp.where(strong, factor * entries, entries)


def level_of(own_key, dims, cuts, least, largest):
    loudness = 1.0
    for position, blocks in cuts:
        draws = jax.random.uniform(jax.random.fold_in(jax.random.fold_in(own_key, 6), position), (blocks,), jnp.float32, least / len(cuts), largest / len(cuts))
        loudness = loudness * jnp.repeat(jnp.exp(draws), dims[position] // blocks).reshape((-1,) + (1,) * (len(dims) - 1 - position))
    return loudness


def normal_values(stream_key, extent, deviation, reach, shards=(), kind=jnp.bfloat16):
    level = level_of(stream_key, extent, shards, -0.22, 0.18) if shards else 1.0
    drawn = jax.random.normal(stream_key, extent, jnp.float32) * deviation * level
    return jnp.minimum(jnp.maximum(drawn, -reach), reach).astype(kind)


def bell_draw_with(rng, extent, scale, limit, cuts, heavy, held_as=jnp.bfloat16):
    values = scale * jax.random.normal(rng, extent, jnp.float32)
    if cuts:
        values = values * level_of(rng, extent, cuts, -0.22, 0.18)
    return jnp.clip(spiked(values, jax.random.fold_in(rng, 3), *heavy), -limit, limit).astype(held_as)


def setup_inputs(seed: int = 0) -> dict:
    splits = jax.random.split(jax.random.key(seed), 13)
    return {
        "tokens": normal_values(splits[0], (NF, S, D), 1.0, 6.0, ((0, 8),)),
        "frame_counts": draw_frame_counts(jax.random.fold_in(splits[12], 71), 0),
        "actions": touch_ends(jax.random.randint(splits[2], (NF,), 0, ACTIONS), jax.random.fold_in(splits[2], 1), 0, ACTIONS - 1).astype(jnp.int32),
        "action_table": normal_values(splits[3], (ACTIONS, D), 0.5, 3.0),
        "norm_gains": jnp.clip(1.0 + 0.15 * jax.random.normal(splits[4], (3, D), jnp.float32), 0.25, 1.75),
        "spatial_project": normal_values(splits[5], (D, 3, D), D ** -0.5, 0.1875, ((2, 4),)),
        "spatial_merge": normal_values(splits[6], (D, D), (D // 16) ** -0.5, 0.75, ((0, 4),)),
        "temporal_project": normal_values(splits[7], (D, 3, D), D ** -0.5, 0.1875, ((2, 4),)),
        "temporal_merge": normal_values(splits[8], (D, D), (D // 4) ** -0.5, 0.375, ((0, 4),)),
        "expand_weight": normal_values(splits[9], (D, FF), D ** -0.5, 0.1875, ((1, 4),)),
        "reduce_weight": normal_values(splits[10], (FF, D), FF ** -0.5, 0.09375, ((0, 4),)),
        "grad_out": bell_draw_with(splits[11], (NF, S, D), 1.0, 6.0, ((0, 8),), (0, 2, 8, 2.0)),
    }


EPSILON = 1e-06
NEGATIVE = -1e+30
HIGHEST = lax.Precision.HIGHEST

@jax.custom_vjp
def low(v):
    return lax.optimization_barrier(v.astype(jnp.bfloat16)).astype(jnp.float32)

@jax.custom_vjp
def low_back(v):
    return v

def low_keep(v):
    return (low(v), None)

def low_pass(kept, grad):
    return (grad,)

def back_keep(v):
    return (v, None)

def back_low(kept, grad):
    return (low(grad),)
low.defvjp(low_keep, low_pass)
low_back.defvjp(back_keep, back_low)

def rounded(value):
    return low_back(low(value))

def normalize(value, gain):
    return value * lax.rsqrt(lax.optimization_barrier(jnp.mean(value * value, axis=-1, keepdims=True)) + EPSILON) * gain

def split_heads(packed):
    shaped = packed.reshape(packed.shape[:-1] + (packed.shape[-1] // HD, HD))
    return (shaped[..., 0, :, :], shaped[..., 1, :, :], shaped[..., 2, :, :])

def clip_block(weights, portion):
    norm_gains, spatial_project, spatial_merge, temporal_project, temporal_merge, expand_weight, reduce_weight = weights
    begin, keep_mask, extra = portion
    frames, width = (begin.shape[0], begin.shape[2])
    keep_mask = keep_mask[:, None, None]
    factor = HD ** (-0.5)
    start = begin + extra[:, None, :]
    normed1 = low(normalize(start, norm_gains[0]))
    project1 = rounded(jnp.einsum('fsd,dce->fsce', normed1, spatial_project, precision=HIGHEST))
    queries, key_rows, value_rows = split_heads(project1)
    scores = low_back(jnp.einsum('fqhd,fkhd->fhqk', queries, key_rows, precision=HIGHEST) * factor)
    shares = low(jax.nn.softmax(scores, axis=-1))
    mixed1 = rounded(jnp.einsum('fhqk,fkhd->fqhd', shares, value_rows, precision=HIGHEST)).reshape(frames, S, width)
    branch1 = low_back(jnp.einsum('fse,ed->fsd', mixed1, spatial_merge, precision=HIGHEST))
    hidden1 = start + keep_mask * branch1
    normed2 = low(normalize(hidden1, norm_gains[1]))
    project2 = rounded(jnp.einsum('fsd,dce->fsce', normed2, temporal_project, precision=HIGHEST))
    queries, key_rows, value_rows = split_heads(project2)
    steps_all = jnp.arange(frames, dtype=jnp.int32)
    allowed = steps_all[None, :] <= steps_all[:, None]
    scores = low_back(jnp.einsum('qshd,kshd->shqk', queries, key_rows, precision=HIGHEST) * factor)
    scores = jnp.where(allowed, scores, NEGATIVE)
    shares = low(jax.nn.softmax(scores, axis=-1))
    mixed2 = rounded(jnp.einsum('shqk,kshd->qshd', shares, value_rows, precision=HIGHEST)).reshape(frames, S, width)
    branch2 = low_back(jnp.einsum('fse,ed->fsd', mixed2, temporal_merge, precision=HIGHEST))
    hidden2 = hidden1 + keep_mask * branch2
    normed3 = low(normalize(hidden2, norm_gains[2]))
    inner = low_back(jnp.einsum('fsd,de->fse', normed3, expand_weight, precision=HIGHEST))
    active = low(jax.nn.gelu(inner))
    branch3 = low_back(jnp.einsum('fse,ed->fsd', active, reduce_weight, precision=HIGHEST))
    return hidden2 + keep_mask * branch3

def reference(tokens, frame_counts, actions, action_table, norm_gains, spatial_project, spatial_merge, temporal_project, temporal_merge, expand_weight, reduce_weight, grad_out):
    frame_ids = jnp.arange(NF, dtype=jnp.int32)
    clip_count = frame_counts[(frame_ids // FRAMES).astype(jnp.int32)]
    keep_mask = (frame_ids % FRAMES < clip_count).astype(jnp.float32)
    choose = (actions[:, None] == jnp.arange(ACTIONS, dtype=jnp.int32)[None, :]).astype(jnp.float32)
    parameters = (norm_gains.astype(jnp.float32), action_table.astype(jnp.float32), spatial_project.astype(jnp.float32), spatial_merge.astype(jnp.float32), temporal_project.astype(jnp.float32), temporal_merge.astype(jnp.float32), expand_weight.astype(jnp.float32), reduce_weight.astype(jnp.float32))

    def whole_block(parameters, begin):
        embedding = parameters[1]
        weights = (parameters[0],) + tuple(parameters[2:])
        extra = jnp.dot(choose, embedding, precision=HIGHEST)
        portions = (begin.reshape(CLIPS, FRAMES, S, D), keep_mask.reshape(CLIPS, FRAMES), extra.reshape(CLIPS, FRAMES, D))
        per_clip = jax.checkpoint(lambda portion: clip_block(weights, portion))
        return lax.map(per_clip, portions).reshape(NF, S, D)
    result, pullback = jax.vjp(whole_block, parameters, tokens.astype(jnp.float32))
    gradients, grad_tokens = pullback(grad_out.astype(jnp.float32))
    return (result.astype(jnp.bfloat16), grad_tokens, gradients[0], gradients[1], gradients[2], gradients[3], gradients[4], gradients[5], gradients[6], gradients[7])
```

```python
import jax
import jax.numpy as jnp
from jax import lax
from jax.sharding import PartitionSpec as P

HD = 64
FRAMES = 16
GROUP = 16

EPSILON = 1e-06
NEGATIVE = -1e30
HIGHEST = lax.Precision.HIGHEST
SCORE = "fqhd,fkhd->fhqk"
OUT = "fhqk,fkhd->fqhd"
KEY = "fhqk,fqhd->fkhd"
F32 = jnp.float32
BF16 = jnp.bfloat16


def dot(form, *terms):
    return jnp.einsum(form, *terms, preferred_element_type=F32)


def normalize(value, gain):
    return value * lax.rsqrt(jnp.mean(value * value, axis=-1, keepdims=True) + EPSILON) * gain


def norm_back(value, gain, incoming):
    _, pullback = jax.vjp(normalize, value, gain)
    return pullback(incoming)


def split_heads(packed):
    shaped = packed.reshape(packed.shape[:-1] + (packed.shape[-1] // HD, HD))
    return (shaped[..., 0, :, :], shaped[..., 1, :, :], shaped[..., 2, :, :])


def scored(queries, key_rows, allowed):
    scores = dot(SCORE, queries, key_rows) * HD ** (-0.5)
    return scores if allowed is None else jnp.where(allowed, scores, NEGATIVE)


def attend(queries, key_rows, value_rows, allowed):
    scores = scored(queries, key_rows, allowed)
    highest = jnp.max(scores, axis=-1, keepdims=True)
    log_total = jnp.log(jnp.sum(jnp.exp(scores - highest), axis=-1, keepdims=True)) + highest
    shares = jnp.exp(scores - log_total).astype(BF16)
    return dot(OUT, shares, value_rows).astype(BF16), log_total


def attend_back(queries, key_rows, value_rows, log_total, grad_mixed, allowed):
    factor = HD ** (-0.5)
    chances = jnp.exp(scored(queries, key_rows, allowed) - log_total)
    grad_values = dot(KEY, chances.astype(BF16), grad_mixed)
    grad_chances = dot(SCORE, grad_mixed, value_rows)
    grad_scores = (
        chances * (grad_chances - jnp.sum(grad_chances * chances, axis=-1, keepdims=True))
    ).astype(BF16)
    grad_queries = dot(OUT, grad_scores, key_rows) * factor
    grad_keys = dot(KEY, grad_scores, queries) * factor
    return jnp.stack([grad_queries, grad_keys, grad_values], axis=-3).astype(BF16)


def swap(value, axis, bit):
    size = lax.axis_size(axis)
    return lax.ppermute(value, axis, [(i, i ^ bit) for i in range(size)])


def pick(value, place, dim):
    return lax.dynamic_index_in_dim(value, place, dim, keepdims=False)


def added(left, right):
    return (left.astype(F32) + right.astype(F32)).astype(BF16)


def halve(value, dim, axis, bit, place):
    received = swap(pick(value, 1 - place, dim), axis, bit)
    return added(pick(value, place, dim), received)


def scatter_wide(value, dim):
    wide = lax.axis_size("wide")
    me = lax.axis_index("wide")
    block = value.shape[dim] // wide
    left, bit = wide, 1
    while left > 1:
        shape = value.shape[:dim] + (left // 2, 2, block) + value.shape[dim + 1 :]
        value = halve(value.reshape(shape), dim + 1, "wide", bit, (me // bit) % 2)
        left, bit = left // 2, bit * 2
        value = value.reshape(value.shape[:dim] + (left * block,) + value.shape[dim + 2 :])
    return value


def gather_narrow(value):
    other = swap(value, "narrow", 2)
    pair = jnp.stack([value, other])
    near = swap(pair, "narrow", 1)
    return jnp.stack([pair[0], near[0], pair[1], near[1]])


def scatter_narrow(value):
    pair = added(value[:2], swap(value[2:], "narrow", 2))
    return added(pair[0], swap(pair[1], "narrow", 1))


def body(
    tokens,
    frame_counts,
    actions,
    action_table,
    norm_gains,
    spatial_project,
    spatial_merge,
    temporal_project,
    temporal_merge,
    expand_weight,
    reduce_weight,
    grad_out,
):
    frames_dev, tokens_frame, width = tokens.shape
    local = spatial_merge.shape[0]
    wide_me, narrow_me = lax.axis_index("wide"), lax.axis_index("narrow")
    x_me, y_me, c_me = wide_me % 2, narrow_me // 2, narrow_me % 2
    span = tokens_frame // 8
    groups = span // GROUP
    rows = 2 * frames_dev * span

    def keep_of(wide_place):
        frame_ids = wide_place * frames_dev + jnp.arange(frames_dev, dtype=jnp.int32)
        clip_places = jnp.arange(frame_counts.shape[0], dtype=jnp.int32)
        clip_count = jnp.sum(
            jnp.where((frame_ids // FRAMES)[:, None] == clip_places[None, :], frame_counts[None, :], 0),
            axis=1,
        )
        return (frame_ids % FRAMES < clip_count).astype(F32)

    def by_place(near, far):
        both = jnp.concatenate([near, far], axis=0)
        both = both.reshape(2 * frames_dev, groups, GROUP, both.shape[-1])
        return both.transpose(1, 0, 2, 3)

    def by_frame(value):
        value = value.reshape(groups, 2 * frames_dev, GROUP, value.shape[-1]).transpose(1, 0, 2, 3)
        return value.reshape(2, frames_dev, span, value.shape[-1])

    def cut(value, x_place, y_place):
        start = (x_place * 4 + y_place * 2 + c_me) * span
        return lax.dynamic_slice_in_dim(value, start, span, axis=1)

    keep_own = keep_of(wide_me)
    keep_far = keep_of(wide_me + 1 - 2 * x_me)
    keep_place = jnp.broadcast_to(
        jnp.concatenate([keep_own, keep_far])[None, :, None], (groups, 2 * frames_dev, GROUP)
    ).reshape(rows, 1)
    choose = (
        actions[:, None] == jnp.arange(action_table.shape[0], dtype=jnp.int32)[None, :]
    ).astype(BF16)
    extra = dot("fa,ad->fd", choose, action_table)

    far_tokens = swap(cut(tokens, 1 - x_me, y_me), "wide", 1)
    far_extra = swap(extra.astype(BF16), "wide", 1).astype(F32)
    merge1_all = gather_narrow(spatial_merge)
    project_all = gather_narrow(temporal_project)
    merge2_all = gather_narrow(temporal_merge)
    expand_pair = jnp.stack([expand_weight, swap(expand_weight, "narrow", 1)])
    reduce_pair = jnp.stack([reduce_weight, swap(reduce_weight, "narrow", 1)])
    grad_far = swap(
        jnp.stack([cut(grad_out, 1 - x_me, y_me), cut(grad_out, 1 - x_me, 1 - y_me)]), "wide", 1
    )

    start = tokens.astype(F32) + extra[:, None, :]
    normed1 = normalize(start, norm_gains[0]).astype(BF16)
    project1 = dot("fsd,dce->fsce", normed1, spatial_project).astype(BF16)
    heads1 = split_heads(project1)
    mixed1, total1 = attend(heads1[0], heads1[1], heads1[2], None)
    mixed1 = mixed1.reshape(frames_dev, tokens_frame, local)

    shaped = mixed1.reshape(frames_dev, 2, tokens_frame // 2, local)
    moved = jnp.stack([pick(shaped, x_me, 1), swap(pick(shaped, 1 - x_me, 1), "wide", 1)])
    moved = moved.reshape(2, frames_dev, 2, tokens_frame // 4, local)
    moved = jnp.stack([pick(moved, y_me, 2), swap(pick(moved, 1 - y_me, 2), "narrow", 2)])
    moved = moved.reshape(2, 2, frames_dev, 2, span, local)
    moved = jnp.stack([pick(moved, c_me, 3), swap(pick(moved, 1 - c_me, 3), "narrow", 1)], axis=1)
    mixed1_all = moved.reshape(4, 2 * frames_dev, groups, GROUP, local).transpose(0, 2, 1, 3, 4)
    mixed1_all = mixed1_all.reshape(4, rows, local)

    start_place = by_place(
        cut(tokens, x_me, y_me).astype(F32) + extra[:, None, :],
        far_tokens.astype(F32) + far_extra[:, None, :],
    ).reshape(rows, width)
    branch1 = dot("nte,ned->td", mixed1_all, merge1_all)
    hidden1 = start_place + keep_place * branch1
    normed2 = normalize(hidden1, norm_gains[1]).astype(BF16)
    project2 = dot("td,ndce->ntce", normed2, project_all).astype(BF16)
    heads2 = split_heads(project2.reshape(4 * groups, 2 * frames_dev * GROUP, 3, local))
    row_ids = jnp.arange(2 * frames_dev * GROUP, dtype=jnp.int32)
    row_place = row_ids % GROUP
    row_frame = (row_ids // GROUP + x_me * frames_dev) % (2 * frames_dev)
    allowed = (row_place[:, None] == row_place[None, :]) & (row_frame[None, :] <= row_frame[:, None])
    mixed2, total2 = attend(heads2[0], heads2[1], heads2[2], allowed)
    mixed2 = mixed2.reshape(4, rows, local)
    branch2 = dot("nte,ned->td", mixed2, merge2_all)
    hidden2 = hidden1 + keep_place * branch2
    normed3 = normalize(hidden2, norm_gains[2]).astype(BF16)

    grad_result = by_place(cut(grad_out, x_me, y_me), grad_far[0]).reshape(rows, width)
    grad_result_far = by_place(cut(grad_out, x_me, 1 - y_me), grad_far[1]).reshape(rows, width)
    normed3_far = swap(normed3, "narrow", 2)

    def feed(normed, grad):
        grad_branch = (keep_place * grad.astype(F32)).astype(BF16)
        inner = dot("td,cde->cte", normed, expand_pair)
        active, gelu_pull = jax.vjp(jax.nn.gelu, inner)
        active = active.astype(BF16)
        branch = dot("cte,ced->td", active, reduce_pair).astype(BF16)
        grad_active = dot("td,ced->cte", grad_branch, reduce_pair)
        grad_inner = gelu_pull(grad_active)[0].astype(BF16)
        grad_normed = dot("cte,cde->td", grad_inner, expand_pair).astype(BF16)
        return grad_branch, active, branch, grad_inner, grad_normed

    grad_branch3, active, branch3, grad_inner, grad_normed3 = feed(normed3, grad_result)
    far = feed(normed3_far, grad_result_far)
    grad_normed3 = grad_normed3.astype(F32) + swap(far[4], "narrow", 2).astype(F32)
    branch3 = branch3.astype(F32) + swap(far[2], "narrow", 2).astype(F32)
    result = (hidden2 + keep_place * branch3).astype(BF16)
    reduce_grad = dot("cte,td->ced", active, grad_branch3) + dot("cte,td->ced", far[1], far[0])
    expand_grad = dot("td,cte->cde", normed3, grad_inner) + dot("td,cte->cde", normed3_far, far[3])
    reduce_grad = reduce_grad.astype(BF16)
    expand_grad = expand_grad.astype(BF16)
    reduce_grad = added(reduce_grad[0], swap(reduce_grad[1], "narrow", 1))
    expand_grad = added(expand_grad[0], swap(expand_grad[1], "narrow", 1))
    reduce_out = scatter_wide(reduce_grad, 1).astype(F32)
    expand_out = scatter_wide(expand_grad, 0).astype(F32)

    result = by_frame(result)
    result = jnp.stack([result[0], swap(result[1], "wide", 1)])
    result = jnp.stack([result, swap(result, "narrow", 2)])
    result = jnp.stack([result, swap(result, "narrow", 1)])

    def in_order(value):
        value = lax.cond(c_me == 0, lambda v: v, lambda v: v[::-1], value)
        value = lax.cond(y_me == 0, lambda v: v, lambda v: v[:, ::-1], value)
        value = lax.cond(x_me == 0, lambda v: v, lambda v: v[:, :, ::-1], value)
        return value.transpose(3, 2, 1, 0, 4, 5).reshape(frames_dev, tokens_frame, width)

    output = in_order(result)

    back_three, gain_three = norm_back(hidden2, norm_gains[2], grad_normed3)
    grad_hidden2 = grad_result.astype(F32) + back_three
    grad_branch2 = (keep_place * grad_hidden2).astype(BF16)
    merge2_grad = dot("nte,td->ned", mixed2, grad_branch2).astype(BF16)
    grad_mixed2 = dot("td,ned->nte", grad_branch2, merge2_all).astype(BF16)
    grad_mixed2 = grad_mixed2.reshape(heads2[0].shape)
    grad_project2 = attend_back(heads2[0], heads2[1], heads2[2], total2, grad_mixed2, allowed)
    grad_project2 = grad_project2.reshape(4, rows, 3, local)
    project2_grad = dot("td,ntce->ndce", normed2, grad_project2).astype(BF16)
    grad_normed2 = dot("ntce,ndce->td", grad_project2, project_all)
    back_two, gain_two = norm_back(hidden1, norm_gains[1], grad_normed2)
    grad_hidden1 = grad_hidden2 + back_two
    grad_branch1 = (keep_place * grad_hidden1).astype(BF16)
    merge1_grad = dot("nte,td->ned", mixed1_all, grad_branch1).astype(BF16)
    grad_mixed1 = dot("td,ned->nte", grad_branch1, merge1_all).astype(BF16)

    moved = grad_mixed1.reshape(2, 2, groups, 2, frames_dev, GROUP, local)
    moved = moved.transpose(0, 1, 3, 4, 2, 5, 6).reshape(2, 2, 2, frames_dev, span, local)
    near, other = moved[:, 0], swap(moved[:, 1], "narrow", 1)
    moved = jnp.stack(
        [jnp.where(c_me == 0, near, other), jnp.where(c_me == 0, other, near)], axis=3
    )
    near, other = moved[0], swap(moved[1], "narrow", 2)
    moved = jnp.stack(
        [jnp.where(y_me == 0, near, other), jnp.where(y_me == 0, other, near)], axis=2
    )
    near, other = moved[0], swap(moved[1], "wide", 1)
    moved = jnp.stack(
        [jnp.where(x_me == 0, near, other), jnp.where(x_me == 0, other, near)], axis=1
    )
    grad_mixed1 = moved.reshape(heads1[0].shape)

    hidden_parts = by_frame(grad_hidden1.astype(BF16))
    grad_hidden_own = jnp.stack([hidden_parts[0], swap(hidden_parts[1], "wide", 1)], axis=1)

    grad_project1 = attend_back(heads1[0], heads1[1], heads1[2], total1, grad_mixed1, None)
    grad_project1 = grad_project1.reshape(frames_dev, tokens_frame, 3, local)
    project1_grad = dot("fsd,fsce->dce", normed1, grad_project1).astype(BF16)
    partial = dot("fsce,dce->fsd", grad_project1, spatial_project).astype(BF16)
    partial = partial.reshape(frames_dev, 2, 2, 2, span, width)
    partial = halve(partial, 3, "narrow", 1, c_me)
    partial = halve(partial, 2, "narrow", 2, y_me)
    grad_normed1 = jnp.stack([pick(partial, x_me, 1), pick(partial, 1 - x_me, 1)], axis=1).astype(F32)
    start_own = (
        jnp.stack([cut(tokens, x_me, y_me), cut(tokens, 1 - x_me, y_me)], axis=1).astype(F32)
        + extra[:, None, None, :]
    )
    back_one, gain_one = norm_back(start_own, norm_gains[0], grad_normed1)
    grad_start = grad_hidden_own.astype(F32) + back_one
    frame_totals = jnp.sum(grad_start, axis=(1, 2))
    table_grad = jnp.dot(choose.astype(F32).T, frame_totals, precision=HIGHEST)
    grad_part = grad_start.astype(BF16).transpose(1, 0, 2, 3)
    grad_part = jnp.stack([grad_part, swap(grad_part, "narrow", 2)])
    grad_part = jnp.stack([grad_part, swap(grad_part, "narrow", 1)])
    grad_tokens = in_order(grad_part).astype(F32)

    small = jnp.concatenate([jnp.stack([gain_one, gain_two, gain_three]), table_grad])
    small = small + swap(small, "narrow", 1)
    small = small + swap(small, "narrow", 2)
    wide = lax.axis_size("wide")
    bit = 1
    while bit < wide:
        small = small + swap(small, "wide", bit)
        bit *= 2
    small = lax.dynamic_slice_in_dim(small, wide_me * (width // wide), width // wide, axis=1)

    project2_out = scatter_wide(scatter_narrow(project2_grad), 0).astype(F32)
    merge2_out = scatter_wide(scatter_narrow(merge2_grad), 1).astype(F32)
    merge1_out = scatter_wide(scatter_narrow(merge1_grad), 1).astype(F32)
    project1_out = scatter_wide(project1_grad, 0).astype(F32)
    return (
        output,
        grad_tokens,
        small[:3],
        small[3:],
        project1_out,
        merge1_out,
        project2_out,
        merge2_out,
        expand_out,
        reduce_out,
    )


def solution(mesh):
    return jax.shard_map(
        body,
        mesh=mesh,
        in_specs=(
            P("wide", None, None),
            P(),
            P("wide"),
            P(),
            P(),
            P(None, None, "narrow"),
            P("narrow", None),
            P(None, None, "narrow"),
            P("narrow", None),
            P(None, "narrow"),
            P("narrow", None),
            P("wide", None, None),
        ),
        out_specs=(
            P("wide", None, None),
            P("wide", None, None),
            P(None, "wide"),
            P(None, "wide"),
            P("wide", None, "narrow"),
            P("narrow", "wide"),
            P("wide", None, "narrow"),
            P("narrow", "wide"),
            P("wide", "narrow"),
            P("narrow", "wide"),
        ),
        check_vma=False,
    )
```

```python
import jax
import jax.numpy as jnp
from jax import lax
from jax.experimental import pallas as pl
from jax.experimental.pallas import tpu as pltpu
from jax.sharding import PartitionSpec as P

HD = 64
FRAMES = 16
GROUP = 16
PAIR = 2 * HD

EPSILON = 1e-06
NEGATIVE = -1e30
HIGHEST = lax.Precision.HIGHEST
F32 = jnp.float32
BF16 = jnp.bfloat16
VMEM_LIMIT = 56 * 1024 * 1024
NN = (((1,), (0,)), ((), ()))
NT = (((1,), (1,)), ((), ()))
TN = (((0,), (0,)), ((), ()))


def mm(left, right, form=NN):
    return lax.dot_general(left, right, form, preferred_element_type=F32)


def root(value):
    return lax.rsqrt(jnp.mean(value * value, axis=-1, keepdims=True) + EPSILON)


def norm_back(value, gain, incoming):
    scale = root(value)
    scaled = gain * incoming
    inner = jnp.mean(scaled * value, axis=-1, keepdims=True)
    back = scale * scaled - (scale * scale * scale) * inner * value
    return back, jnp.sum(incoming * value * scale, axis=0, keepdims=True)


def sides():
    lane = lax.broadcasted_iota(jnp.int32, (1, PAIR), 1)
    low = (lane < HD).astype(F32)
    return lane < HD, low.astype(BF16), (1.0 - low).astype(BF16)


def attend_pair(queries, key_rows, value_rows, allowed):
    is_low, low, high = sides()
    mixed = []
    for side in (low, high):
        scores = mm(queries * (side * HD ** (-0.5)), key_rows, NT)
        if allowed is not None:
            scores = jnp.where(allowed, scores, NEGATIVE)
        shares = jnp.exp(scores - jnp.max(scores, axis=-1, keepdims=True))
        shares = shares * (1.0 / jnp.sum(shares, axis=-1, keepdims=True))
        mixed.append(mm(shares.astype(BF16), value_rows))
    return jnp.where(is_low, mixed[0], mixed[1]).astype(BF16)


def attend_back_pair(queries, key_rows, value_rows, grad_mixed, allowed):
    factor = HD ** (-0.5)
    is_low, low, high = sides()
    parts = []
    for side in (low, high):
        scores = mm(key_rows, queries * (side * factor), NT)
        if allowed is not None:
            scores = jnp.where(allowed, scores, NEGATIVE)
        chances = jnp.exp(scores - jnp.max(scores, axis=0, keepdims=True))
        chances = chances * (1.0 / jnp.sum(chances, axis=0, keepdims=True))
        grad_chances = mm(value_rows, grad_mixed * side, NT)
        shift = jnp.sum(grad_chances * chances, axis=0, keepdims=True)
        grad_scores = (chances * (grad_chances - shift)).astype(BF16)
        parts.append(
            (
                mm(grad_scores, key_rows, TN) * factor,
                mm(grad_scores, queries) * factor,
                mm(chances.astype(BF16), grad_mixed),
            )
        )
    return [jnp.where(is_low, a, b).astype(BF16) for a, b in zip(parts[0], parts[1])]


def whole(shape):
    return pl.BlockSpec(shape, lambda *_: (0,) * len(shape))


def call(kernel, grid, in_specs, out_specs, out_shape, scratch=(), flops=0, moved=0):
    return pl.pallas_call(
        kernel,
        grid=grid,
        in_specs=in_specs,
        out_specs=out_specs,
        out_shape=out_shape,
        scratch_shapes=list(scratch),
        compiler_params=pltpu.CompilerParams(vmem_limit_bytes=VMEM_LIMIT),
        cost_estimate=pl.CostEstimate(flops=flops, bytes_accessed=moved, transcendentals=0),
    )


def shape_of(shape, kind=BF16):
    return jax.ShapeDtypeStruct(shape, kind)


def spatial_forward(tokens, extra, gain, project):
    frames, places, width = tokens.shape
    local = project.shape[-1]

    def kernel(tokens_ref, extra_ref, gain_ref, project_ref, normed_ref, heads_ref, mixed_ref):
        start = tokens_ref[0].astype(F32) + extra_ref[0]
        normed = (start * root(start) * gain_ref[...]).astype(BF16)
        normed_ref[0] = normed
        for c in range(3):
            heads_ref[c, 0] = mm(normed, project_ref[c]).astype(BF16)
        for at in range(0, local, PAIR):
            part = pl.ds(at, PAIR)
            mixed_ref[0, :, part] = attend_pair(
                heads_ref[0, 0, :, part], heads_ref[1, 0, :, part], heads_ref[2, 0, :, part], None
            )

    return call(
        kernel,
        (frames,),
        [
            pl.BlockSpec((1, places, width), lambda f: (f, 0, 0)),
            pl.BlockSpec((1, 1, width), lambda f: (f, 0, 0)),
            whole((1, width)),
            whole(project.shape),
        ],
        [
            pl.BlockSpec((1, places, width), lambda f: (f, 0, 0)),
            pl.BlockSpec((3, 1, places, local), lambda f: (0, f, 0, 0)),
            pl.BlockSpec((1, places, local), lambda f: (f, 0, 0)),
        ],
        [
            shape_of((frames, places, width)),
            shape_of((3, frames, places, local)),
            shape_of((frames, places, local)),
        ],
        flops=2 * frames * places * width * local * 4,
        moved=12 * 2**20,
    )(tokens, extra[:, None, :], gain, project)


def place_masks(x_me, frames_all, transposed):
    rows = frames_all * GROUP
    shape = (rows, rows)
    query = lax.broadcasted_iota(jnp.int32, shape, 1 if transposed else 0)
    key = lax.broadcasted_iota(jnp.int32, shape, 0 if transposed else 1)
    query_frame = (query // GROUP + x_me * (frames_all // 2)) % frames_all
    key_frame = (key // GROUP + x_me * (frames_all // 2)) % frames_all
    return (query % GROUP == key % GROUP) & (key_frame <= query_frame)


def temporal_forward(begin, keep, gains, mixed1, merge1, project, merge2):
    rows, width = begin.shape
    local = mixed1.shape[-1]
    group_rows = FRAMES * GROUP

    def kernel(
        begin_ref,
        keep_ref,
        gains_ref,
        mixed1_ref,
        merge1_ref,
        project_ref,
        merge2_ref,
        hidden1_ref,
        normed2_ref,
        heads_ref,
        mixed2_ref,
        hidden2_ref,
        normed3_ref,
    ):
        step = pl.program_id(0)
        keep_rows = keep_ref[...]

        @pl.when(step == 0)
        def _():
            branch = mm(mixed1_ref[0], merge1_ref[0])
            for n in range(1, 4):
                branch += mm(mixed1_ref[n], merge1_ref[n])
            hidden1 = begin_ref[...] + keep_rows * branch
            hidden1_ref[...] = hidden1
            hidden2_ref[...] = hidden1
            normed2_ref[...] = (hidden1 * root(hidden1) * gains_ref[1:2]).astype(BF16)

        for c in range(3):
            heads_ref[0, c] = mm(normed2_ref[...], project_ref[0, c]).astype(BF16)
        allowed = place_masks(lax.axis_index("wide") % 2, FRAMES, False)
        for g in range(rows // group_rows):
            band = pl.ds(g * group_rows, group_rows)
            for at in range(0, local, PAIR):
                part = pl.ds(at, PAIR)
                mixed2_ref[0, band, part] = attend_pair(
                    heads_ref[0, 0, band, part],
                    heads_ref[0, 1, band, part],
                    heads_ref[0, 2, band, part],
                    allowed,
                )
        hidden2_ref[...] += keep_rows * mm(mixed2_ref[0], merge2_ref[0])

        @pl.when(step == 3)
        def _():
            hidden2 = hidden2_ref[...]
            normed3_ref[...] = (hidden2 * root(hidden2) * gains_ref[2:3]).astype(BF16)

    return call(
        kernel,
        (4,),
        [
            whole((rows, width)),
            whole((rows, 1)),
            whole((3, width)),
            whole((4, rows, local)),
            whole((4, local, width)),
            pl.BlockSpec((1, 3, width, local), lambda n: (n, 0, 0, 0)),
            pl.BlockSpec((1, local, width), lambda n: (n, 0, 0)),
        ],
        [
            whole((rows, width)),
            whole((rows, width)),
            pl.BlockSpec((1, 3, rows, local), lambda n: (n, 0, 0, 0)),
            pl.BlockSpec((1, rows, local), lambda n: (n, 0, 0)),
            whole((rows, width)),
            whole((rows, width)),
        ],
        [
            shape_of((rows, width), F32),
            shape_of((rows, width)),
            shape_of((4, 3, rows, local)),
            shape_of((4, rows, local)),
            shape_of((rows, width), F32),
            shape_of((rows, width)),
        ],
        flops=2 * rows * width * width * 6,
        moved=24 * 2**20,
    )(begin, keep, gains, mixed1, merge1, project, merge2)


RATE = 0.7978845608028654
CUBIC = 0.044715


def feed_forward(normed, grad, keep, expand, reduce):
    rows, width = normed.shape
    cores, _, units = expand.shape
    block = 512
    per = units // block

    def kernel(
        normed_ref,
        grad_ref,
        keep_ref,
        expand_ref,
        reduce_ref,
        active_ref,
        inner_ref,
        grad_branch_ref,
        branch_ref,
        grad_normed_ref,
        branch_sum,
        grad_sum,
    ):
        step = pl.program_id(0)

        @pl.when(step == 0)
        def _():
            grad_branch_ref[...] = (keep_ref[...] * grad_ref[...].astype(F32)).astype(BF16)
            branch_sum[...] = jnp.zeros_like(branch_sum)
            grad_sum[...] = jnp.zeros_like(grad_sum)

        inner = mm(normed_ref[...], expand_ref[0])
        grad_active = mm(grad_branch_ref[...], reduce_ref[0], NT)
        square = inner * inner
        bend = jnp.tanh(RATE * inner * (1.0 + CUBIC * square))
        half = 0.5 * (1.0 + bend)
        active = (inner * half).astype(BF16)
        slope = half + (0.5 * RATE) * inner * (1.0 - bend * bend) * (1.0 + (3.0 * CUBIC) * square)
        grad_inner = (grad_active * slope).astype(BF16)
        active_ref[...] = active
        inner_ref[...] = grad_inner
        branch_sum[...] += mm(active, reduce_ref[0])
        grad_sum[...] += mm(grad_inner, expand_ref[0], NT)

        @pl.when(step == cores * per - 1)
        def _():
            branch_ref[...] = branch_sum[...].astype(BF16)
            grad_normed_ref[...] = grad_sum[...].astype(BF16)

    full = whole((rows, width))
    return call(
        kernel,
        (cores * per,),
        [
            full,
            full,
            whole((rows, 1)),
            pl.BlockSpec((1, width, block), lambda j: (j // per, 0, j % per)),
            pl.BlockSpec((1, block, width), lambda j: (j // per, j % per, 0)),
        ],
        [
            pl.BlockSpec((rows, block), lambda j: (0, j)),
            pl.BlockSpec((rows, block), lambda j: (0, j)),
            full,
            full,
            full,
        ],
        [
            shape_of((rows, cores * units)),
            shape_of((rows, cores * units)),
            shape_of((rows, width)),
            shape_of((rows, width)),
            shape_of((rows, width)),
        ],
        scratch=[pltpu.VMEM((rows, width), F32), pltpu.VMEM((rows, width), F32)],
        flops=8 * rows * width * cores * units,
        moved=18 * 2**20,
    )(normed, grad, keep, expand, reduce)


def outer(pairs, blocks, left_map, right_map, out_map, left_block, right_block, out_shape, flops):
    count = len(pairs)

    def kernel(*refs):
        total = mm(refs[0][...].reshape(refs[0].shape[-2:]), refs[1][...].reshape(refs[1].shape[-2:]), TN)
        for i in range(1, count):
            left, right = refs[2 * i], refs[2 * i + 1]
            total += mm(left[...].reshape(left.shape[-2:]), right[...].reshape(right.shape[-2:]), TN)
        out = refs[-1]
        out[...] = total.astype(BF16).reshape(out.shape)

    specs = []
    for left, right in pairs:
        specs += [pl.BlockSpec(left_block, left_map), pl.BlockSpec(right_block, right_map)]
    out_block = (1,) * (len(out_shape) - 2) + (left_block[-1], right_block[-1])
    return call(
        kernel,
        blocks,
        specs,
        pl.BlockSpec(out_block, out_map),
        shape_of(out_shape),
        flops=flops,
        moved=16 * 2**20,
    )(*[term for pair in pairs for term in pair])


def temporal_backward(
    grad_near, grad_far, hidden2, hidden1, grad_result, keep, gains, heads, merge2, project, merge1
):
    rows, width = hidden1.shape
    local = merge1.shape[1]
    group_rows = FRAMES * GROUP

    def kernel(
        near_ref,
        far_ref,
        hidden2_ref,
        hidden1_ref,
        result_ref,
        keep_ref,
        gains_ref,
        heads_ref,
        merge2_ref,
        project_ref,
        merge1_ref,
        branch2_ref,
        grad_heads_ref,
        branch1_ref,
        mixed1_ref,
        carried_ref,
        gain3_ref,
        gain2_ref,
        grad_hidden,
        grad_normed,
        grad_mixed,
    ):
        step = pl.program_id(0)

        @pl.when(step == 0)
        def _():
            incoming = near_ref[...].astype(F32) + far_ref[...].astype(F32)
            back, gain3_ref[...] = norm_back(hidden2_ref[...], gains_ref[2:3], incoming)
            total = result_ref[...].astype(F32) + back
            grad_hidden[...] = total
            branch2_ref[...] = (keep_ref[...] * total).astype(BF16)
            grad_normed[...] = jnp.zeros_like(grad_normed)

        grad_mixed[...] = mm(branch2_ref[...], merge2_ref[0], NT).astype(BF16)
        allowed = place_masks(lax.axis_index("wide") % 2, FRAMES, True)
        for g in range(rows // group_rows):
            band = pl.ds(g * group_rows, group_rows)
            for at in range(0, local, PAIR):
                part = pl.ds(at, PAIR)
                grads = attend_back_pair(
                    heads_ref[0, 0, band, part],
                    heads_ref[0, 1, band, part],
                    heads_ref[0, 2, band, part],
                    grad_mixed[band, part],
                    allowed,
                )
                for c in range(3):
                    grad_heads_ref[0, c, band, part] = grads[c]
        total = mm(grad_heads_ref[0, 0], project_ref[0, 0], NT)
        for c in range(1, 3):
            total += mm(grad_heads_ref[0, c], project_ref[0, c], NT)
        grad_normed[...] += total

        @pl.when(step == 3)
        def _():
            back, gain2_ref[...] = norm_back(hidden1_ref[...], gains_ref[1:2], grad_normed[...])
            total = grad_hidden[...] + back
            carried_ref[...] = total.astype(BF16)
            branch1_ref[...] = (keep_ref[...] * total).astype(BF16)
            for n in range(4):
                mixed1_ref[n] = mm(branch1_ref[...], merge1_ref[n], NT).astype(BF16)

    full = whole((rows, width))
    row = whole((1, width))
    return call(
        kernel,
        (4,),
        [
            full,
            full,
            full,
            full,
            full,
            whole((rows, 1)),
            whole((3, width)),
            pl.BlockSpec((1, 3, rows, local), lambda n: (n, 0, 0, 0)),
            pl.BlockSpec((1, local, width), lambda n: (n, 0, 0)),
            pl.BlockSpec((1, 3, width, local), lambda n: (n, 0, 0, 0)),
            whole((4, local, width)),
        ],
        [
            full,
            pl.BlockSpec((1, 3, rows, local), lambda n: (n, 0, 0, 0)),
            full,
            whole((4, rows, local)),
            full,
            row,
            row,
        ],
        [
            shape_of((rows, width)),
            shape_of((4, 3, rows, local)),
            shape_of((rows, width)),
            shape_of((4, rows, local)),
            shape_of((rows, width)),
            shape_of((1, width), F32),
            shape_of((1, width), F32),
        ],
        scratch=[
            pltpu.VMEM((rows, width), F32),
            pltpu.VMEM((rows, width), F32),
            pltpu.VMEM((rows, local), BF16),
        ],
        flops=2 * rows * width * width * 8,
        moved=30 * 2**20,
    )(grad_near, grad_far, hidden2, hidden1, grad_result, keep, gains, heads, merge2, project, merge1)


def spatial_backward(heads, grad_mixed, project):
    _, frames, places, local = heads.shape
    width = project.shape[1]

    def kernel(heads_ref, mixed_ref, project_ref, grad_heads_ref, partial_ref):
        for at in range(0, local, PAIR):
            part = pl.ds(at, PAIR)
            grads = attend_back_pair(
                heads_ref[0, 0, :, part],
                heads_ref[1, 0, :, part],
                heads_ref[2, 0, :, part],
                mixed_ref[0, :, part],
                None,
            )
            for c in range(3):
                grad_heads_ref[c, 0, :, part] = grads[c]
        total = mm(grad_heads_ref[0, 0], project_ref[0], NT)
        for c in range(1, 3):
            total += mm(grad_heads_ref[c, 0], project_ref[c], NT)
        partial_ref[0] = total.astype(BF16)

    return call(
        kernel,
        (frames,),
        [
            pl.BlockSpec((3, 1, places, local), lambda f: (0, f, 0, 0)),
            pl.BlockSpec((1, places, local), lambda f: (f, 0, 0)),
            whole(project.shape),
        ],
        [
            pl.BlockSpec((3, 1, places, local), lambda f: (0, f, 0, 0)),
            pl.BlockSpec((1, places, width), lambda f: (f, 0, 0)),
        ],
        [shape_of((3, frames, places, local)), shape_of((frames, places, width))],
        flops=2 * frames * places * width * local * 5,
        moved=14 * 2**20,
    )(heads, grad_mixed, project)


def in_order(value, kind):
    _, _, _, frames, span, width = value.shape
    wide_me, narrow_me = lax.axis_index("wide"), lax.axis_index("narrow")
    me = jnp.stack([narrow_me % 2, narrow_me // 2, wide_me % 2]).astype(jnp.int32)

    def kernel(me_ref, value_ref, out_ref):
        out_ref[...] = value_ref[0, 0, 0].astype(kind)

    return pl.pallas_call(
        kernel,
        grid_spec=pltpu.PrefetchScalarGridSpec(
            num_scalar_prefetch=1,
            grid=(2, 2, 2),
            in_specs=[
                pl.BlockSpec((1, 1, 1, frames, span, width), lambda c, y, x, me: (c, y, x, 0, 0, 0))
            ],
            out_specs=pl.BlockSpec(
                (frames, span, width),
                lambda c, y, x, me: (0, (x ^ me[2]) * 4 + (y ^ me[1]) * 2 + (c ^ me[0]), 0),
            ),
        ),
        out_shape=shape_of((frames, 8 * span, width), kind),
        compiler_params=pltpu.CompilerParams(vmem_limit_bytes=VMEM_LIMIT),
        cost_estimate=pl.CostEstimate(flops=0, bytes_accessed=12 * 2**20, transcendentals=0),
    )(me, value)


def swap(value, axis, bit):
    size = lax.axis_size(axis)
    return lax.ppermute(value, axis, [(i, i ^ bit) for i in range(size)])


def pick(value, place, dim):
    return lax.dynamic_index_in_dim(value, place, dim, keepdims=False)


def added(left, right):
    return (left.astype(F32) + right.astype(F32)).astype(BF16)


def after(value, *earlier):
    return lax.optimization_barrier((value,) + earlier)[0]


def halve(value, dim, axis, bit, place):
    received = swap(pick(value, 1 - place, dim), axis, bit)
    return added(pick(value, place, dim), received)


def scatter_wide(value, dim):
    wide = lax.axis_size("wide")
    me = lax.axis_index("wide")
    block = value.shape[dim] // wide
    left, bit = wide, 1
    while left > 1:
        shape = value.shape[:dim] + (left // 2, 2, block) + value.shape[dim + 1 :]
        value = halve(value.reshape(shape), dim + 1, "wide", bit, (me // bit) % 2)
        left, bit = left // 2, bit * 2
        value = value.reshape(value.shape[:dim] + (left * block,) + value.shape[dim + 2 :])
    return value


def gather_narrow(value):
    other = swap(value, "narrow", 2)
    pair = jnp.stack([value, other])
    near = swap(pair, "narrow", 1)
    return jnp.stack([pair[0], near[0], pair[1], near[1]])


def scatter_narrow(value):
    pair = added(value[:2], swap(value[2:], "narrow", 2))
    return added(pair[0], swap(pair[1], "narrow", 1))


def body(
    tokens,
    frame_counts,
    actions,
    action_table,
    norm_gains,
    spatial_project,
    spatial_merge,
    temporal_project,
    temporal_merge,
    expand_weight,
    reduce_weight,
    grad_out,
):
    frames_dev, tokens_frame, width = tokens.shape
    local = spatial_merge.shape[0]
    wide_me, narrow_me = lax.axis_index("wide"), lax.axis_index("narrow")
    x_me, y_me, c_me = wide_me % 2, narrow_me // 2, narrow_me % 2
    span = tokens_frame // 8
    groups = span // GROUP
    rows = 2 * frames_dev * span
    spatial_project = spatial_project.transpose(1, 0, 2)
    temporal_project = temporal_project.transpose(1, 0, 2)

    def keep_of(wide_place):
        frame_ids = wide_place * frames_dev + jnp.arange(frames_dev, dtype=jnp.int32)
        clip_places = jnp.arange(frame_counts.shape[0], dtype=jnp.int32)
        clip_count = jnp.sum(
            jnp.where((frame_ids // FRAMES)[:, None] == clip_places[None, :], frame_counts[None, :], 0),
            axis=1,
        )
        return (frame_ids % FRAMES < clip_count).astype(F32)

    def by_place(near, far):
        both = jnp.concatenate([near, far], axis=0)
        both = both.reshape(2 * frames_dev, groups, GROUP, both.shape[-1])
        return both.transpose(1, 0, 2, 3).reshape(rows, both.shape[-1])

    def by_frame(value):
        value = value.reshape(groups, 2 * frames_dev, GROUP, value.shape[-1]).transpose(1, 0, 2, 3)
        return value.reshape(2, frames_dev, span, value.shape[-1])

    def cut(value, x_place, y_place):
        start = (x_place * 4 + y_place * 2 + c_me) * span
        return lax.dynamic_slice_in_dim(value, start, span, axis=1)

    keep_own = keep_of(wide_me)
    keep_far = keep_of(wide_me + 1 - 2 * x_me)
    keep_place = jnp.broadcast_to(
        jnp.concatenate([keep_own, keep_far])[None, :, None], (groups, 2 * frames_dev, GROUP)
    ).reshape(rows, 1)
    choose = (
        actions[:, None] == jnp.arange(action_table.shape[0], dtype=jnp.int32)[None, :]
    ).astype(BF16)
    extra = jnp.dot(choose, action_table, preferred_element_type=F32)

    far_tokens = swap(cut(tokens, 1 - x_me, y_me), "wide", 1)
    far_extra = swap(extra.astype(BF16), "wide", 1).astype(F32)
    merge1_all = gather_narrow(spatial_merge)
    project_all = gather_narrow(temporal_project)
    merge2_all = gather_narrow(temporal_merge)

    normed1, heads1, mixed1 = spatial_forward(tokens, extra, norm_gains[0:1], spatial_project)

    shaped = mixed1.reshape(frames_dev, 2, tokens_frame // 2, local)
    moved = jnp.stack([pick(shaped, x_me, 1), swap(pick(shaped, 1 - x_me, 1), "wide", 1)])
    moved = moved.reshape(2, frames_dev, 2, tokens_frame // 4, local)
    moved = jnp.stack([pick(moved, y_me, 2), swap(pick(moved, 1 - y_me, 2), "narrow", 2)])
    moved = moved.reshape(2, 2, frames_dev, 2, span, local)
    moved = jnp.stack([pick(moved, c_me, 3), swap(pick(moved, 1 - c_me, 3), "narrow", 1)], axis=1)
    mixed1_all = moved.reshape(4, 2 * frames_dev, groups, GROUP, local).transpose(0, 2, 1, 3, 4)
    mixed1_all = mixed1_all.reshape(4, rows, local)

    expand_pair = jnp.stack([expand_weight, swap(after(expand_weight, mixed1), "narrow", 1)])
    reduce_pair = jnp.stack([reduce_weight, swap(after(reduce_weight, mixed1), "narrow", 1)])
    grad_far = swap(
        after(
            jnp.stack([cut(grad_out, 1 - x_me, y_me), cut(grad_out, 1 - x_me, 1 - y_me)]), mixed1_all
        ),
        "wide",
        1,
    )

    start_place = by_place(
        cut(tokens, x_me, y_me).astype(F32) + extra[:, None, :],
        far_tokens.astype(F32) + far_extra[:, None, :],
    )
    hidden1, normed2, heads2, mixed2, hidden2, normed3 = temporal_forward(
        start_place, keep_place, norm_gains, mixed1_all, merge1_all, project_all, merge2_all
    )

    grad_result = by_place(cut(grad_out, x_me, y_me), grad_far[0])
    grad_result_far = by_place(cut(grad_out, x_me, 1 - y_me), grad_far[1])
    normed3_far = swap(normed3, "narrow", 2)
    near = feed_forward(normed3, grad_result, keep_place, expand_pair, reduce_pair)
    far = feed_forward(normed3_far, grad_result_far, keep_place, expand_pair, reduce_pair)
    grad_normed3_far = swap(far[4], "narrow", 2)
    units = expand_weight.shape[1]
    per = units // 256
    reduce_grad = outer(
        [(near[0], near[2]), (far[0], far[2])],
        (2 * per,),
        lambda j: (0, j),
        lambda j: (0, 0),
        lambda j: (j // per, j % per, 0),
        (rows, 256),
        (rows, width),
        (2, units, width),
        2 * 2 * rows * 2 * units * width,
    )
    expand_grad = outer(
        [(normed3, near[1]), (normed3_far, far[1])],
        (2, width // 256),
        lambda c, j: (0, j),
        lambda c, j: (0, c),
        lambda c, j: (c, j, 0),
        (rows, 256),
        (rows, units),
        (2, width, units),
        2 * 2 * rows * 2 * units * width,
    )

    branch2_grad, grad_heads2, branch1_grad, grad_mixed1, carried, gain_three, gain_two = temporal_backward(
        near[4],
        grad_normed3_far,
        hidden2,
        hidden1,
        grad_result,
        keep_place,
        norm_gains,
        heads2,
        merge2_all,
        project_all,
        merge1_all,
    )

    moved = grad_mixed1.reshape(2, 2, groups, 2, frames_dev, GROUP, local)
    moved = moved.transpose(0, 1, 3, 4, 2, 5, 6).reshape(2, 2, 2, frames_dev, span, local)
    near_part, other = moved[:, 0], swap(moved[:, 1], "narrow", 1)
    moved = jnp.stack(
        [jnp.where(c_me == 0, near_part, other), jnp.where(c_me == 0, other, near_part)], axis=3
    )
    near_part, other = moved[0], swap(moved[1], "narrow", 2)
    moved = jnp.stack(
        [jnp.where(y_me == 0, near_part, other), jnp.where(y_me == 0, other, near_part)], axis=2
    )
    near_part, other = moved[0], swap(moved[1], "wide", 1)
    moved = jnp.stack(
        [jnp.where(x_me == 0, near_part, other), jnp.where(x_me == 0, other, near_part)], axis=1
    )
    grad_mixed1 = moved.reshape(frames_dev, tokens_frame, local)

    hidden_parts = by_frame(carried)
    grad_hidden_own = jnp.stack([hidden_parts[0], swap(hidden_parts[1], "wide", 1)], axis=1)

    branch3 = near[3].astype(F32) + swap(after(far[3], grad_normed3_far), "narrow", 2).astype(F32)
    result = (hidden2 + keep_place * branch3).astype(BF16)
    result = after(by_frame(result), grad_mixed1)
    result = jnp.stack([result[0], swap(result[1], "wide", 1)])
    result = jnp.stack([result, swap(result, "narrow", 2)])
    result = jnp.stack([result, swap(result, "narrow", 1)])
    output = in_order(result, BF16)

    grad_heads1, partial = spatial_backward(heads1, grad_mixed1, spatial_project)
    partial = partial.reshape(frames_dev, 2, 2, 2, span, width)
    partial = halve(partial, 3, "narrow", 1, c_me)
    partial = halve(partial, 2, "narrow", 2, y_me)
    grad_normed1 = jnp.stack([pick(partial, x_me, 1), pick(partial, 1 - x_me, 1)], axis=1).astype(F32)
    start_own = (
        jnp.stack([cut(tokens, x_me, y_me), cut(tokens, 1 - x_me, y_me)], axis=1).astype(F32)
        + extra[:, None, None, :]
    )
    flat = (2 * frames_dev * span, width)
    back_one, gain_one = norm_back(start_own.reshape(flat), norm_gains[0:1], grad_normed1.reshape(flat))
    grad_start = grad_hidden_own.astype(F32) + back_one.reshape(grad_hidden_own.shape)
    frame_totals = jnp.sum(grad_start, axis=(1, 2))
    table_grad = jnp.dot(choose.astype(F32).T, frame_totals, precision=HIGHEST)
    grad_part = grad_start.astype(BF16).transpose(1, 0, 2, 3)
    grad_part = jnp.stack([grad_part, swap(grad_part, "narrow", 2)])
    grad_part = jnp.stack([grad_part, swap(grad_part, "narrow", 1)])
    grad_tokens = in_order(grad_part, F32)

    small = jnp.concatenate([gain_one, gain_two, gain_three, table_grad])
    small = small + swap(small, "narrow", 1)
    small = small + swap(small, "narrow", 2)
    wide = lax.axis_size("wide")
    bit = 1
    while bit < wide:
        small = small + swap(small, "wide", bit)
        bit *= 2
    small = lax.dynamic_slice_in_dim(small, wide_me * (width // wide), width // wide, axis=1)

    reduce_grad = after(reduce_grad, grad_mixed1)
    expand_grad = after(expand_grad, grad_mixed1)
    reduce_grad = added(reduce_grad[0], swap(reduce_grad[1], "narrow", 1))
    expand_grad = added(expand_grad[0], swap(expand_grad[1], "narrow", 1))
    reduce_out = scatter_wide(reduce_grad, 1).astype(F32)
    expand_out = scatter_wide(expand_grad, 0).astype(F32)

    def merge_grad(mixed, grad):
        return outer(
            [(mixed, grad)],
            (4,),
            lambda n: (n, 0, 0),
            lambda n: (0, 0),
            lambda n: (n, 0, 0),
            (1, rows, local),
            (rows, width),
            (4, local, width),
            2 * rows * width * width,
        )

    merge2_grad = merge_grad(mixed2, branch2_grad)
    merge1_grad = merge_grad(mixed1_all, branch1_grad)
    project2_grad = outer(
        [(normed2, grad_heads2)],
        (4, 3),
        lambda n, c: (0, 0),
        lambda n, c: (n, c, 0, 0),
        lambda n, c: (n, c, 0, 0),
        (rows, width),
        (1, 1, rows, local),
        (4, 3, width, local),
        6 * rows * width * width,
    )
    all_rows = frames_dev * tokens_frame
    project1_grad = outer(
        [(normed1.reshape(all_rows, width), grad_heads1.reshape(3, all_rows, local))],
        (3, width // 256),
        lambda c, j: (0, j),
        lambda c, j: (c, 0, 0),
        lambda c, j: (c, j, 0),
        (all_rows, 256),
        (1, all_rows, local),
        (3, width, local),
        6 * all_rows * width * local,
    )
    project2_out = scatter_wide(scatter_narrow(project2_grad), 1).astype(F32).transpose(1, 0, 2)
    merge2_out = scatter_wide(scatter_narrow(merge2_grad), 1).astype(F32)
    merge1_out = scatter_wide(scatter_narrow(merge1_grad), 1).astype(F32)
    project1_out = scatter_wide(project1_grad, 1).astype(F32).transpose(1, 0, 2)
    return (
        output,
        grad_tokens,
        small[:3],
        small[3:],
        project1_out,
        merge1_out,
        project2_out,
        merge2_out,
        expand_out,
        reduce_out,
    )


def solution(mesh):
    return jax.shard_map(
        body,
        mesh=mesh,
        in_specs=(
            P("wide", None, None),
            P(),
            P("wide"),
            P(),
            P(),
            P(None, None, "narrow"),
            P("narrow", None),
            P(None, None, "narrow"),
            P("narrow", None),
            P(None, "narrow"),
            P("narrow", None),
            P("wide", None, None),
        ),
        out_specs=(
            P("wide", None, None),
            P("wide", None, None),
            P(None, "wide"),
            P(None, "wide"),
            P("wide", None, "narrow"),
            P("narrow", "wide"),
            P("wide", None, "narrow"),
            P("narrow", "wide"),
            P("wide", "narrow"),
            P("narrow", "wide"),
        ),
        check_vma=False,
    )
```

```python
import jax
import jax.numpy as jnp
from jax import lax
from jax.experimental import pallas as pl
from jax.experimental.pallas import tpu as pltpu
from jax.sharding import PartitionSpec as P

HD = 64
FRAMES = 16
GROUP = 16
PAIR = 2 * HD

EPSILON = 1e-06
NEGATIVE = -1e30
HIGHEST = lax.Precision.HIGHEST
F32 = jnp.float32
BF16 = jnp.bfloat16
VMEM_LIMIT = 56 * 1024 * 1024
NN = (((1,), (0,)), ((), ()))
NT = (((1,), (1,)), ((), ()))
TN = (((0,), (0,)), ((), ()))


def mm(left, right, form=NN):
    return lax.dot_general(left, right, form, preferred_element_type=F32)


def root(value):
    return lax.rsqrt(jnp.mean(value * value, axis=-1, keepdims=True) + EPSILON)


def norm_back(value, gain, incoming):
    scale = root(value)
    scaled = gain * incoming
    inner = jnp.mean(scaled * value, axis=-1, keepdims=True)
    back = scale * scaled - (scale * scale * scale) * inner * value
    return back, jnp.sum(incoming * value * scale, axis=0, keepdims=True)


def sides():
    lane = lax.broadcasted_iota(jnp.int32, (1, PAIR), 1)
    low = (lane < HD).astype(F32)
    return lane < HD, low.astype(BF16), (1.0 - low).astype(BF16)


def attend_pair(queries, key_rows, value_rows, allowed):
    is_low, low, high = sides()
    mixed = []
    for side in (low, high):
        scores = mm(queries * (side * HD ** (-0.5)), key_rows, NT)
        if allowed is not None:
            scores = jnp.where(allowed, scores, NEGATIVE)
        shares = jnp.exp(scores - jnp.max(scores, axis=-1, keepdims=True))
        shares = shares * (1.0 / jnp.sum(shares, axis=-1, keepdims=True))
        mixed.append(mm(shares.astype(BF16), value_rows))
    return jnp.where(is_low, mixed[0], mixed[1]).astype(BF16)


def attend_back_pair(queries, key_rows, value_rows, grad_mixed, allowed):
    factor = HD ** (-0.5)
    is_low, low, high = sides()
    parts = []
    for side in (low, high):
        scores = mm(key_rows, queries * (side * factor), NT)
        if allowed is not None:
            scores = jnp.where(allowed, scores, NEGATIVE)
        chances = jnp.exp(scores - jnp.max(scores, axis=0, keepdims=True))
        chances = chances * (1.0 / jnp.sum(chances, axis=0, keepdims=True))
        grad_chances = mm(value_rows, grad_mixed * side, NT)
        shift = jnp.sum(grad_chances * chances, axis=0, keepdims=True)
        grad_scores = (chances * (grad_chances - shift)).astype(BF16)
        parts.append(
            (
                mm(grad_scores, key_rows, TN) * factor,
                mm(grad_scores, queries) * factor,
                mm(chances.astype(BF16), grad_mixed),
            )
        )
    return [jnp.where(is_low, a, b).astype(BF16) for a, b in zip(parts[0], parts[1])]


def whole(shape):
    return pl.BlockSpec(shape, lambda *_: (0,) * len(shape))


def call(kernel, grid, in_specs, out_specs, out_shape, scratch=(), flops=0, moved=0):
    return pl.pallas_call(
        kernel,
        grid=grid,
        in_specs=in_specs,
        out_specs=out_specs,
        out_shape=out_shape,
        scratch_shapes=list(scratch),
        compiler_params=pltpu.CompilerParams(vmem_limit_bytes=VMEM_LIMIT),
        cost_estimate=pl.CostEstimate(flops=flops, bytes_accessed=moved, transcendentals=0),
    )


def shape_of(shape, kind=BF16):
    return jax.ShapeDtypeStruct(shape, kind)


def place_masks(x_me, frames_all, transposed):
    rows = frames_all * GROUP
    shape = (rows, rows)
    query = lax.broadcasted_iota(jnp.int32, shape, 1 if transposed else 0)
    key = lax.broadcasted_iota(jnp.int32, shape, 0 if transposed else 1)
    query_frame = (query // GROUP + x_me * (frames_all // 2)) % frames_all
    key_frame = (key // GROUP + x_me * (frames_all // 2)) % frames_all
    return (query % GROUP == key % GROUP) & (key_frame <= query_frame)


def temporal_forward(tokens, extra, keep, gains, mixed1, merge1, project, merge2):
    _, span, width = tokens.shape
    rows = FRAMES * span
    local = mixed1.shape[-1]
    group_rows = FRAMES * GROUP

    def kernel(
        tokens_ref,
        extra_ref,
        keep_ref,
        gains_ref,
        mixed1_ref,
        merge1_ref,
        project_ref,
        merge2_ref,
        hidden1_ref,
        normed2_ref,
        heads_ref,
        mixed2_ref,
        hidden2_ref,
        normed3_ref,
    ):
        step = pl.program_id(0)
        keep_rows = keep_ref[...]

        @pl.when(step == 0)
        def _():
            branch = mm(mixed1_ref[0], merge1_ref[0])
            for n in range(1, 4):
                branch += mm(mixed1_ref[n], merge1_ref[n])
            begin = tokens_ref[...].astype(F32) + extra_ref[...]
            hidden1 = begin.reshape(rows, width) + keep_rows * branch
            hidden1_ref[...] = hidden1
            hidden2_ref[...] = hidden1
            normed2_ref[...] = (hidden1 * root(hidden1) * gains_ref[1:2]).astype(BF16)

        for c in range(3):
            head = mm(normed2_ref[...], project_ref[0, c]).astype(BF16)
            heads_ref[0, c] = head.reshape(FRAMES, span, local)
        allowed = place_masks(lax.axis_index("wide") % 2, FRAMES, False)
        for g in range(span // GROUP):
            band = pl.ds(g * GROUP, GROUP)
            for at in range(0, local, PAIR):
                part = pl.ds(at, PAIR)
                terms = [heads_ref[0, c, :, band, part].reshape(group_rows, PAIR) for c in range(3)]
                mixed = attend_pair(*terms, allowed)
                mixed2_ref[0, :, band, part] = mixed.reshape(FRAMES, GROUP, PAIR)
        hidden2_ref[...] += keep_rows * mm(mixed2_ref[0].reshape(rows, local), merge2_ref[0])

        @pl.when(step == 3)
        def _():
            hidden2 = hidden2_ref[...]
            normed3_ref[...] = (hidden2 * root(hidden2) * gains_ref[2:3]).astype(BF16)

    return call(
        kernel,
        (4,),
        [
            whole((FRAMES, span, width)),
            whole((FRAMES, 1, width)),
            whole((rows, 1)),
            whole((3, width)),
            whole((4, rows, local)),
            whole((4, local, width)),
            pl.BlockSpec((1, 3, width, local), lambda n: (n, 0, 0, 0)),
            pl.BlockSpec((1, local, width), lambda n: (n, 0, 0)),
        ],
        [
            whole((rows, width)),
            whole((rows, width)),
            pl.BlockSpec((1, 3, FRAMES, span, local), lambda n: (n, 0, 0, 0, 0)),
            pl.BlockSpec((1, FRAMES, span, local), lambda n: (n, 0, 0, 0)),
            whole((rows, width)),
            whole((rows, width)),
        ],
        [
            shape_of((rows, width), F32),
            shape_of((rows, width)),
            shape_of((4, 3, FRAMES, span, local)),
            shape_of((4, FRAMES, span, local)),
            shape_of((rows, width), F32),
            shape_of((rows, width)),
        ],
        flops=2 * rows * width * width * 6,
        moved=24 * 2**20,
    )(tokens, extra, keep, gains, mixed1, merge1, project, merge2)


RATE = 0.7978845608028654
CUBIC = 0.044715


def feed_forward(normed, grad, keep, expand, reduce):
    rows, width = normed.shape
    cores, _, units = expand.shape
    block = 512
    per = units // block

    def kernel(
        normed_ref,
        grad_ref,
        keep_ref,
        expand_ref,
        reduce_ref,
        active_ref,
        inner_ref,
        grad_branch_ref,
        branch_ref,
        grad_normed_ref,
        branch_sum,
        grad_sum,
    ):
        step = pl.program_id(0)

        @pl.when(step == 0)
        def _():
            grad_branch_ref[...] = (keep_ref[...] * grad_ref[...].astype(F32)).astype(BF16)
            branch_sum[...] = jnp.zeros_like(branch_sum)
            grad_sum[...] = jnp.zeros_like(grad_sum)

        inner = mm(normed_ref[...], expand_ref[0])
        grad_active = mm(grad_branch_ref[...], reduce_ref[0], NT)
        square = inner * inner
        bend = jnp.tanh(RATE * inner * (1.0 + CUBIC * square))
        half = 0.5 * (1.0 + bend)
        active = (inner * half).astype(BF16)
        slope = half + (0.5 * RATE) * inner * (1.0 - bend * bend) * (1.0 + (3.0 * CUBIC) * square)
        grad_inner = (grad_active * slope).astype(BF16)
        active_ref[...] = active
        inner_ref[...] = grad_inner
        branch_sum[...] += mm(active, reduce_ref[0])
        grad_sum[...] += mm(grad_inner, expand_ref[0], NT)

        @pl.when(step == cores * per - 1)
        def _():
            branch_ref[...] = branch_sum[...].astype(BF16)
            grad_normed_ref[...] = grad_sum[...].astype(BF16)

    full = whole((rows, width))
    return call(
        kernel,
        (cores * per,),
        [
            full,
            full,
            whole((rows, 1)),
            pl.BlockSpec((1, width, block), lambda j: (j // per, 0, j % per)),
            pl.BlockSpec((1, block, width), lambda j: (j // per, j % per, 0)),
        ],
        [
            pl.BlockSpec((rows, block), lambda j: (0, j)),
            pl.BlockSpec((rows, block), lambda j: (0, j)),
            full,
            full,
            full,
        ],
        [
            shape_of((rows, cores * units)),
            shape_of((rows, cores * units)),
            shape_of((rows, width)),
            shape_of((rows, width)),
            shape_of((rows, width)),
        ],
        scratch=[pltpu.VMEM((rows, width), F32), pltpu.VMEM((rows, width), F32)],
        flops=8 * rows * width * cores * units,
        moved=18 * 2**20,
    )(normed, grad, keep, expand, reduce)


def temporal_backward(
    grad_near, grad_far, hidden2, hidden1, grad_result, keep, gains, heads, merge2, project, merge1
):
    rows, width = hidden1.shape
    local = merge1.shape[1]
    span = rows // FRAMES
    group_rows = FRAMES * GROUP

    def kernel(
        near_ref,
        far_ref,
        hidden2_ref,
        hidden1_ref,
        result_ref,
        keep_ref,
        gains_ref,
        heads_ref,
        merge2_ref,
        project_ref,
        merge1_ref,
        branch2_ref,
        grad_heads_ref,
        branch1_ref,
        mixed1_ref,
        carried_ref,
        gain3_ref,
        gain2_ref,
        grad_hidden,
        grad_normed,
        grad_mixed,
    ):
        step = pl.program_id(0)

        @pl.when(step == 0)
        def _():
            incoming = near_ref[...].astype(F32) + far_ref[...].astype(F32)
            back, gain3_ref[...] = norm_back(hidden2_ref[...], gains_ref[2:3], incoming)
            total = result_ref[...].astype(F32) + back
            grad_hidden[...] = total
            branch2_ref[...] = (keep_ref[...] * total).astype(BF16)
            grad_normed[...] = jnp.zeros_like(grad_normed)

        back_mixed = mm(branch2_ref[...], merge2_ref[0], NT).astype(BF16)
        grad_mixed[...] = back_mixed.reshape(FRAMES, span, local)
        allowed = place_masks(lax.axis_index("wide") % 2, FRAMES, True)
        for g in range(span // GROUP):
            band = pl.ds(g * GROUP, GROUP)
            for at in range(0, local, PAIR):
                part = pl.ds(at, PAIR)
                terms = [heads_ref[0, c, :, band, part].reshape(group_rows, PAIR) for c in range(3)]
                grad = grad_mixed[:, band, part].reshape(group_rows, PAIR)
                grads = attend_back_pair(*terms, grad, allowed)
                for c in range(3):
                    grad_heads_ref[0, c, :, band, part] = grads[c].reshape(FRAMES, GROUP, PAIR)
        total = mm(grad_heads_ref[0, 0].reshape(rows, local), project_ref[0, 0], NT)
        for c in range(1, 3):
            total += mm(grad_heads_ref[0, c].reshape(rows, local), project_ref[0, c], NT)
        grad_normed[...] += total

        @pl.when(step == 3)
        def _():
            back, gain2_ref[...] = norm_back(hidden1_ref[...], gains_ref[1:2], grad_normed[...])
            total = grad_hidden[...] + back
            carried_ref[...] = total.astype(BF16)
            branch1_ref[...] = (keep_ref[...] * total).astype(BF16)
            for n in range(4):
                mixed1_ref[n] = mm(branch1_ref[...], merge1_ref[n], NT).astype(BF16)

    full = whole((rows, width))
    row = whole((1, width))
    return call(
        kernel,
        (4,),
        [
            full,
            full,
            full,
            full,
            full,
            whole((rows, 1)),
            whole((3, width)),
            pl.BlockSpec((1, 3, FRAMES, span, local), lambda n: (n, 0, 0, 0, 0)),
            pl.BlockSpec((1, local, width), lambda n: (n, 0, 0)),
            pl.BlockSpec((1, 3, width, local), lambda n: (n, 0, 0, 0)),
            whole((4, local, width)),
        ],
        [
            full,
            pl.BlockSpec((1, 3, FRAMES, span, local), lambda n: (n, 0, 0, 0, 0)),
            full,
            whole((4, rows, local)),
            full,
            row,
            row,
        ],
        [
            shape_of((rows, width)),
            shape_of((4, 3, FRAMES, span, local)),
            shape_of((rows, width)),
            shape_of((4, rows, local)),
            shape_of((rows, width)),
            shape_of((1, width), F32),
            shape_of((1, width), F32),
        ],
        scratch=[
            pltpu.VMEM((rows, width), F32),
            pltpu.VMEM((rows, width), F32),
            pltpu.VMEM((FRAMES, span, local), BF16),
        ],
        flops=2 * rows * width * width * 8,
        moved=30 * 2**20,
    )(grad_near, grad_far, hidden2, hidden1, grad_result, keep, gains, heads, merge2, project, merge1)


def here():
    wide, narrow = lax.axis_index("wide"), lax.axis_index("narrow")
    return wide, narrow, wide % 2, narrow // 2, narrow % 2


def other(wide, narrow, x, y, core):
    if x:
        wide = wide + 1 - 2 * (wide % 2)
    if y:
        narrow = (narrow + 2) % 4
    if core:
        narrow = narrow + 1 - 2 * (narrow % 2)
    return wide, narrow


def beyond(wide, narrow):
    return wide + 2 - 4 * ((wide // 2) % 2), narrow


def place_of(wide, narrow, span):
    return pl.multiple_of(((wide % 2) * 4 + narrow) * span, span)


def remote(src, dst, sems, i, device):
    return pltpu.make_async_remote_copy(
        src_ref=src,
        dst_ref=dst,
        send_sem=sems.at[0, i],
        recv_sem=sems.at[1, i],
        device_id=device,
        device_id_type=pl.DeviceIdType.MESH,
    )


def greet(devices):
    barrier = pltpu.get_barrier_semaphore()
    for device in devices:
        pl.semaphore_signal(
            barrier, inc=1, device_id=device, device_id_type=pl.DeviceIdType.MESH
        )
    pl.semaphore_wait(barrier, len(devices))


OTHERS = [(x, y, c) for x in range(2) for y in range(2) for c in range(2) if x + y + c > 0]
ANY = pl.BlockSpec(memory_space=pl.ANY)


def comm_call(kernel, number, grid, in_specs, out_specs, out_shape, scratch, flops):
    return pl.pallas_call(
        kernel,
        grid=grid,
        in_specs=in_specs,
        out_specs=out_specs,
        out_shape=out_shape,
        scratch_shapes=scratch,
        compiler_params=pltpu.CompilerParams(
            vmem_limit_bytes=VMEM_LIMIT, collective_id=number, has_side_effects=True
        ),
        cost_estimate=pl.CostEstimate(flops=flops, bytes_accessed=30 * 2**20, transcendentals=0),
    )


def spatial_forward(
    tokens, extra, gain, project, merge1, project2, merge2, expand, reduce, grad_out
):
    frames, places, width = tokens.shape
    local = project.shape[-1]
    span = places // 8
    half = frames // 2
    shards = (merge1, project2.reshape(3 * width, local), merge2)
    count = len(shards)

    def kernel(
        tokens_ref,
        extra_ref,
        gain_ref,
        project_ref,
        all_tokens,
        all_extra,
        grad_ref,
        expand_ref,
        reduce_ref,
        shard0,
        shard1,
        shard2,
        normed_ref,
        heads_ref,
        mixed_all,
        tokens_place,
        extra_place,
        grad_place,
        expand_pair,
        reduce_pair,
        full0,
        full1,
        full2,
        mixed_ref,
        local_sems,
        move_sems,
        shard_sems,
        mixed_sems,
        *stage,
    ):
        step = pl.program_id(0)
        wide, narrow, x_me, _, _ = here()
        half_me = (wide // 2) % 2
        x_other = other(wide, narrow, 1, 0, 0)
        y_other = other(wide, narrow, 0, 1, 0)
        core_other = other(wide, narrow, 0, 0, 1)
        z_other = beyond(wide, narrow)
        mine = pl.ds(place_of(wide, narrow, span), span)
        near_y = pl.ds(place_of(*y_other, span), span)
        shard = (shard0, shard1, shard2)
        full = (full0, full1, full2)

        own = [
            (expand_ref, expand_pair.at[0]),
            (reduce_ref, reduce_pair.at[0]),
            (all_tokens.at[:, mine], tokens_place.at[0]),
            (all_extra, extra_place.at[0]),
            (grad_ref.at[:, mine], grad_place.at[0, 0]),
            (grad_ref.at[:, near_y], grad_place.at[1, 0]),
        ] + [(shard[k], full[k].at[0]) for k in range(count)]
        into = [pltpu.make_async_copy(a, v, local_sems.at[0, i]) for i, ((a, _), v) in enumerate(zip(own, stage))]
        back = [pltpu.make_async_copy(v, b, local_sems.at[1, i]) for i, ((_, b), v) in enumerate(zip(own, stage))]
        far = pl.ds(place_of(*x_other, span), span)
        far_y = pl.ds(place_of(*other(wide, narrow, 1, 1, 0), span), span)
        first = [
            remote(all_tokens.at[:, far], tokens_place.at[1], move_sems, 0, x_other),
            remote(all_extra, extra_place.at[1], move_sems, 1, x_other),
            remote(expand_ref, expand_pair.at[1], move_sems, 2, core_other),
            remote(reduce_ref, reduce_pair.at[1], move_sems, 3, core_other),
        ]
        last = [
            remote(grad_ref.at[:, far], grad_place.at[0, 1], move_sems, 4, x_other),
            remote(grad_ref.at[:, far_y], grad_place.at[1, 1], move_sems, 5, x_other),
        ]

        def part(k, which):
            rows = shards[k].shape[0] // 2
            return pl.ds(pl.multiple_of(which * rows, rows), rows)

        def over_core(k):
            return remote(shard[k], full[k].at[1], shard_sems, 5 * k, core_other)

        def over_y(k):
            rows = part(k, half_me)
            return remote(shard[k].at[rows], full[k].at[2, rows], shard_sems, 5 * k + 1, y_other)

        def onward(k, which, i, device, slot):
            rows = part(k, which)
            return remote(full[k].at[2, rows], full[k].at[slot, rows], shard_sems, 5 * k + i, device)

        def over_z(k):
            return onward(k, half_me, 2, z_other, 2)

        def near_half(k):
            return onward(k, half_me, 3, core_other, 3)

        def far_half(k):
            return onward(k, 1 - half_me, 4, core_other, 3)

        def mixed_copies(chunk):
            copies = []
            some = pl.ds(chunk * half, half)
            for i, (x, y, c) in enumerate(OTHERS):
                device = other(wide, narrow, x, y, c)
                copies.append(
                    remote(
                        mixed_ref.at[some, pl.ds(place_of(*device, span), span)],
                        mixed_all.at[2 * y + c, x, some],
                        mixed_sems,
                        7 * chunk + i,
                        device,
                    )
                )
            here_copy = pltpu.make_async_copy(
                mixed_ref.at[some, mine], mixed_all.at[0, 0, some], local_sems.at[chunk, len(own)]
            )
            return copies, here_copy

        @pl.when(step == 0)
        def _():
            greet([other(wide, narrow, *o) for o in OTHERS] + [z_other])
            for k in range(count):
                over_y(k).start()
            for copy in first:
                copy.start()
            for k in range(count):
                over_core(k).start()
            for copy in into:
                copy.start()

        @pl.when(step == 2)
        def _():
            for copy in into:
                copy.wait()
            for copy in back:
                copy.start()

        start = tokens_ref[0].astype(F32) + extra_ref[0]
        normed = (start * root(start) * gain_ref[...]).astype(BF16)
        normed_ref[0] = normed
        for c in range(3):
            heads_ref[c, 0] = mm(normed, project_ref[c]).astype(BF16)
        for at in range(0, local, PAIR):
            lanes = pl.ds(at, PAIR)
            mixed_ref[step, :, lanes] = attend_pair(
                heads_ref[0, 0, :, lanes], heads_ref[1, 0, :, lanes], heads_ref[2, 0, :, lanes], None
            )

        def forward(k):
            over_y(k).wait_recv()
            over_z(k).start()
            near_half(k).start()

        @pl.when(step == half - 1)
        def _():
            copies, here_copy = mixed_copies(0)
            for copy in copies:
                copy.start()
            here_copy.start()
            forward(0)

        @pl.when(step == frames - 1)
        def _():
            copies, here_copy = mixed_copies(1)
            for copy in copies:
                copy.start()
            here_copy.start()
            for copy in last:
                copy.start()
            forward(1)
            forward(2)
            for k in range(count):
                over_z(k).wait_recv()
                far_half(k).start()
            for chunk in range(2):
                copies, here_copy = mixed_copies(chunk)
                for copy in copies:
                    copy.wait()
                here_copy.wait()
            for copy in first + last:
                copy.wait()
            for copy in back:
                copy.wait()
            for k in range(count):
                over_core(k).wait()
                over_y(k).wait_send()
                over_z(k).wait_send()
                near_half(k).wait()
                far_half(k).wait()

    out = comm_call(
        kernel,
        0,
        (frames,),
        [
            pl.BlockSpec((1, places, width), lambda f: (f, 0, 0)),
            pl.BlockSpec((1, 1, width), lambda f: (f, 0, 0)),
            whole((1, width)),
            whole(project.shape),
        ]
        + [ANY] * 8,
        [
            pl.BlockSpec((1, places, width), lambda f: (f, 0, 0)),
            pl.BlockSpec((3, 1, places, local), lambda f: (0, f, 0, 0)),
        ]
        + [ANY] * 9,
        [
            shape_of((frames, places, width)),
            shape_of((3, frames, places, local)),
            shape_of((4, 2, frames, span, local)),
            shape_of((2, frames, span, width)),
            shape_of((2, frames, 1, width), F32),
            shape_of((2, 2, frames, span, width)),
            shape_of((2,) + expand.shape),
            shape_of((2,) + reduce.shape),
        ]
        + [shape_of((4,) + shard.shape) for shard in shards],
        [
            pltpu.VMEM((frames, places, local), BF16),
            pltpu.SemaphoreType.DMA((2, 7 + count)),
            pltpu.SemaphoreType.DMA((2, 6)),
            pltpu.SemaphoreType.DMA((2, 5 * count)),
            pltpu.SemaphoreType.DMA((2, 14)),
            pltpu.VMEM(expand.shape, BF16),
            pltpu.VMEM(reduce.shape, BF16),
            pltpu.VMEM((frames, span, width), BF16),
            pltpu.VMEM((frames, 1, width), F32),
            pltpu.VMEM((frames, span, width), BF16),
            pltpu.VMEM((frames, span, width), BF16),
        ]
        + [pltpu.VMEM(shard.shape, BF16) for shard in shards],
        2 * frames * places * width * local * 4,
    )(
        tokens,
        extra[:, None, :],
        gain,
        project,
        tokens,
        extra[:, None, :],
        grad_out,
        expand,
        reduce,
        *shards,
    )
    out = list(out)
    out[9] = out[9].reshape(4, 3, width, local)
    return out


def feed_outer(normed, grad_inner, grad_branch, active):
    rows, width = normed[0].shape
    units = active[0].shape[1] // 2
    block = 512
    per = units // block

    def kernel(
        normed0, normed1, branch0, branch1, inner0, inner1, active0, active1, out_ref, left, right
    ):
        @pl.when(pl.program_id(0) == 0)
        def _():
            left[:, :rows] = normed0[...].T
            left[:, rows:] = normed1[...].T
            right[:, :rows] = branch0[...].T
            right[:, rows:] = branch1[...].T

        total = mm(left[:, :rows], inner0[...]) + mm(left[:, rows:], inner1[...])
        out_ref[0, 0] = total.astype(BF16)
        total = mm(right[:, :rows], active0[...]) + mm(right[:, rows:], active1[...])
        out_ref[0, 1] = total.astype(BF16)

    full = whole((rows, width))
    part = pl.BlockSpec((rows, block), lambda j: (0, j))
    return call(
        kernel,
        (2 * per,),
        [full] * 4 + [part] * 4,
        pl.BlockSpec((1, 2, width, block), lambda j: (j // per, 0, 0, j % per)),
        shape_of((2, 2, width, units)),
        scratch=[pltpu.VMEM((width, 2 * rows), BF16)] * 2,
        flops=16 * rows * width * units,
        moved=16 * 2**20,
    )(*normed, *grad_branch, *grad_inner, *active)


def temporal_outer(
    grad_mixed1, carried, mixed1, branch1, mixed2, branch2, normed2, grad_heads
):
    rows, width = branch1.shape
    local = mixed1.shape[-1]
    span = rows // FRAMES
    frames = FRAMES // 2

    def kernel(
        grad_ref,
        carried_ref,
        mixed1_ref,
        branch1_ref,
        mixed2_ref,
        branch2_ref,
        normed2_ref,
        heads_ref,
        out_ref,
        grad_own,
        carried_own,
        left,
        grad_stage,
        carried_stage,
        local_sems,
        sems,
    ):
        step = pl.program_id(0)
        wide, narrow, x_me, _, _ = here()
        x_other = other(wide, narrow, 1, 0, 0)
        mine = pl.ds(place_of(wide, narrow, span), span)
        copies = [
            remote(
                grad_ref.at[2 * y + c, x],
                grad_own.at[:, mine],
                sems,
                i,
                other(wide, narrow, x, y, c),
            )
            for i, (x, y, c) in enumerate(OTHERS)
        ]
        copies.append(remote(carried_ref.at[1], carried_own.at[:, x_me], sems, 7, x_other))
        into = [
            pltpu.make_async_copy(grad_ref.at[0, 0], grad_stage, local_sems.at[0]),
            pltpu.make_async_copy(carried_ref.at[0], carried_stage, local_sems.at[1]),
        ]
        back = [
            pltpu.make_async_copy(grad_stage, grad_own.at[:, mine], local_sems.at[2]),
            pltpu.make_async_copy(carried_stage, carried_own.at[:, x_me], local_sems.at[3]),
        ]

        @pl.when(step == 0)
        def _():
            greet([other(wide, narrow, *o) for o in OTHERS])
            for copy in copies + into:
                copy.start()
            left[0] = branch1_ref[...].T
            left[1] = branch2_ref[...].T
            left[2] = normed2_ref[...].T

        out_ref[0, 0] = mm(left[0], mixed1_ref[0]).astype(BF16)
        out_ref[0, 1] = mm(left[1], mixed2_ref[0]).astype(BF16)
        for c in range(3):
            out_ref[0, 2 + c] = mm(left[2], heads_ref[0, c]).astype(BF16)

        @pl.when(step == 1)
        def _():
            for copy in into:
                copy.wait()
            for copy in back:
                copy.start()

        @pl.when(step == 3)
        def _():
            for copy in copies + back:
                copy.wait()

    full = whole((rows, width))
    part = pl.BlockSpec((1, rows, local), lambda n: (n, 0, 0))
    return comm_call(
        kernel,
        1,
        (4,),
        [ANY, ANY, part, full, part, full, full, pl.BlockSpec((1, 3, rows, local), lambda n: (n, 0, 0, 0))],
        [pl.BlockSpec((1, 5, width, local), lambda n: (n, 0, 0, 0)), ANY, ANY],
        [
            shape_of((4, 5, width, local)),
            shape_of((frames, 8 * span, local)),
            shape_of((frames, 2, span, width)),
        ],
        [
            pltpu.VMEM((3, width, rows), BF16),
            pltpu.VMEM((frames, span, local), BF16),
            pltpu.VMEM((frames, span, width), BF16),
            pltpu.SemaphoreType.DMA((4,)),
            pltpu.SemaphoreType.DMA((2, 8)),
        ],
        10 * rows * width * width,
    )(
        grad_mixed1.reshape(4, 2, frames, span, local),
        carried.reshape(2, frames, span, width),
        mixed1,
        branch1,
        mixed2.reshape(4, rows, local),
        branch2,
        normed2,
        grad_heads.reshape(4, 3, rows, local),
    )


SUM_LAG = 4
SEND_LAG = 6


def spatial_backward(heads, grad_mixed, project, normed, tokens, extra, gain, carried):
    _, frames, places, local = heads.shape
    width = project.shape[1]
    span = places // 8
    tile = width // 4

    def kernel(
        heads_ref,
        mixed_ref,
        project_ref,
        normed_ref,
        tokens_ref,
        extra_ref,
        gain_ref,
        carried_ref,
        project_grad_ref,
        gain_grad_ref,
        totals_ref,
        out_ref,
        grad_heads,
        partial,
        from_core,
        halved,
        from_y,
        done,
        local_sems,
        sems,
    ):
        step = pl.program_id(0)
        wide, narrow, x_me, y_me, c_me = here()
        y_other = other(wide, narrow, 0, 1, 0)
        core_other = other(wide, narrow, 0, 0, 1)

        def core_sum(f):
            return remote(partial.at[f, :, :, 1 - c_me], from_core.at[f], sems, f, core_other)

        def y_sum(f):
            return remote(halved.at[f, :, 1 - y_me], from_y.at[f], sems, frames + f, y_other)

        def y_back(f):
            return remote(done.at[f], out_ref.at[f, :, y_me, c_me], sems, 2 * frames + f, y_other)

        def core_back(f):
            return remote(done.at[f], out_ref.at[f, :, y_me, c_me], sems, 3 * frames + f, core_other)

        def core_onward(f):
            there = out_ref.at[f, :, 1 - y_me, c_me]
            return remote(there, there, sems, 4 * frames + f, core_other)

        def keep_own(f):
            return pltpu.make_async_copy(done.at[f], out_ref.at[f, :, y_me, c_me], local_sems.at[f])

        @pl.when(step == 0)
        def _():
            greet([y_other, core_other])
            gain_grad_ref[...] = jnp.zeros_like(gain_grad_ref)

        @pl.when(step < frames)
        def _():
            rows = pl.ds(pl.multiple_of(step * places, places), places)
            for at in range(0, local, PAIR):
                lanes = pl.ds(at, PAIR)
                grads = attend_back_pair(
                    heads_ref[0, 0, :, lanes],
                    heads_ref[1, 0, :, lanes],
                    heads_ref[2, 0, :, lanes],
                    mixed_ref[0, :, lanes],
                    None,
                )
                for c in range(3):
                    grad_heads[c, rows, lanes] = grads[c]
            total = mm(grad_heads[0, rows], project_ref[0], NT)
            for c in range(1, 3):
                total += mm(grad_heads[c, rows], project_ref[c], NT)
            partial[step] = total.astype(BF16).reshape(2, 2, 2, span, width)
            core_sum(step).start()

        @pl.when((step >= 1) & (step < frames + 1))
        def _():
            f = step - 1
            core_sum(f).wait_recv()
            own = partial[f, :, :, pl.ds(c_me, 1)].reshape(2, 2, span, width)
            halved[f] = (own.astype(F32) + from_core[f].astype(F32)).astype(BF16)
            y_sum(f).start()

        @pl.when(step >= frames)
        def _():
            for c in range(3):
                project_grad_ref[c] = mm(normed_ref[...], grad_heads[c], TN).astype(BF16)

        @pl.when((step >= SUM_LAG) & (step < frames + SUM_LAG))
        def _():
            f = step - SUM_LAG
            y_sum(f).wait_recv()
            own = halved[f, :, pl.ds(y_me, 1)].reshape(2 * span, width)
            incoming = own.astype(F32) + from_y[f].reshape(2 * span, width).astype(F32)
            at = pl.multiple_of(narrow * span, span)
            begin = jnp.concatenate(
                [tokens_ref[0, pl.ds(at, span)], tokens_ref[0, pl.ds(4 * span + at, span)]]
            )
            begin = begin.astype(F32) + extra_ref[0]
            back, gain_part = norm_back(begin, gain_ref[...], incoming)
            gain_grad_ref[...] += gain_part
            grad = carried_ref[0].reshape(2 * span, width).astype(F32) + back
            totals_ref[0] = jnp.sum(grad, axis=0, keepdims=True)
            done[f] = grad.astype(BF16).reshape(2, span, width)
            y_back(f).start()
            core_back(f).start()
            keep_own(f).start()

        def onward(f):
            y_back(f).wait_recv()
            core_onward(f).start()

        @pl.when((step >= SEND_LAG) & (step < frames + SUM_LAG))
        def _():
            onward(step - SEND_LAG)

        @pl.when(step == frames + SUM_LAG - 1)
        def _():
            for f in range(frames + SUM_LAG - SEND_LAG, frames):
                onward(f)
            for f in range(frames):
                core_sum(f).wait_send()
                y_sum(f).wait_send()
                y_back(f).wait_send()
                core_back(f).wait()
                core_onward(f).wait()
                keep_own(f).wait()

    def frame(step):
        return jnp.minimum(step, frames - 1)

    def late(step):
        return jnp.clip(step - SUM_LAG, 0, frames - 1)

    def piece(step):
        return jnp.maximum(step - frames, 0)

    return comm_call(
        kernel,
        2,
        (frames + SUM_LAG,),
        [
            pl.BlockSpec((3, 1, places, local), lambda s: (0, frame(s), 0, 0)),
            pl.BlockSpec((1, places, local), lambda s: (frame(s), 0, 0)),
            whole(project.shape),
            pl.BlockSpec((frames * places, tile), lambda s: (0, piece(s))),
            pl.BlockSpec((1, places, width), lambda s: (late(s), 0, 0)),
            pl.BlockSpec((1, 1, width), lambda s: (late(s), 0, 0)),
            whole((1, width)),
            pl.BlockSpec((1, 2, span, width), lambda s: (late(s), 0, 0, 0)),
        ],
        [
            pl.BlockSpec((3, tile, local), lambda s: (0, piece(s), 0)),
            whole((1, width)),
            pl.BlockSpec((1, 1, width), lambda s: (late(s), 0, 0)),
            ANY,
        ],
        [
            shape_of((3, width, local)),
            shape_of((1, width), F32),
            shape_of((frames, 1, width), F32),
            shape_of((frames, 2, 2, 2, span, width)),
        ],
        [
            pltpu.VMEM((3, frames * places, local), BF16),
            pltpu.VMEM((frames, 2, 2, 2, span, width), BF16),
            pltpu.VMEM((frames, 2, 2, span, width), BF16),
            pltpu.VMEM((frames, 2, 2, span, width), BF16),
            pltpu.VMEM((frames, 2, span, width), BF16),
            pltpu.VMEM((frames, 2, span, width), BF16),
            pltpu.SemaphoreType.DMA((frames,)),
            pltpu.SemaphoreType.DMA((2, 5 * frames)),
        ],
        2 * frames * places * width * local * 8,
    )(
        heads,
        grad_mixed,
        project,
        normed.reshape(frames * places, width),
        tokens,
        extra[:, None, :],
        gain,
        carried,
    )


def in_order(value, kind):
    _, _, _, frames, span, width = value.shape
    wide_me, narrow_me = lax.axis_index("wide"), lax.axis_index("narrow")
    me = jnp.stack([narrow_me % 2, narrow_me // 2, wide_me % 2]).astype(jnp.int32)

    def kernel(me_ref, value_ref, out_ref):
        out_ref[...] = value_ref[0, 0, 0].astype(kind)

    return pl.pallas_call(
        kernel,
        grid_spec=pltpu.PrefetchScalarGridSpec(
            num_scalar_prefetch=1,
            grid=(2, 2, 2),
            in_specs=[
                pl.BlockSpec((1, 1, 1, frames, span, width), lambda c, y, x, me: (c, y, x, 0, 0, 0))
            ],
            out_specs=pl.BlockSpec(
                (frames, span, width),
                lambda c, y, x, me: (0, (x ^ me[2]) * 4 + (y ^ me[1]) * 2 + (c ^ me[0]), 0),
            ),
        ),
        out_shape=shape_of((frames, 8 * span, width), kind),
        compiler_params=pltpu.CompilerParams(vmem_limit_bytes=VMEM_LIMIT),
        cost_estimate=pl.CostEstimate(flops=0, bytes_accessed=12 * 2**20, transcendentals=0),
    )(me, value)


def swap(value, axis, bit):
    size = lax.axis_size(axis)
    return lax.ppermute(value, axis, [(i, i ^ bit) for i in range(size)])


def pick(value, place, dim):
    return lax.dynamic_index_in_dim(value, place, dim, keepdims=False)


def added(left, right):
    return (left.astype(F32) + right.astype(F32)).astype(BF16)


def after(value, *earlier):
    return lax.optimization_barrier((value,) + earlier)[0]


def halve(value, dim, axis, bit, place):
    received = swap(pick(value, 1 - place, dim), axis, bit)
    return added(pick(value, place, dim), received)


def scatter_wide(value, dim):
    wide = lax.axis_size("wide")
    me = lax.axis_index("wide")
    block = value.shape[dim] // wide
    left, bit = wide, 1
    while left > 1:
        shape = value.shape[:dim] + (left // 2, 2, block) + value.shape[dim + 1 :]
        value = halve(value.reshape(shape), dim + 1, "wide", bit, (me // bit) % 2)
        left, bit = left // 2, bit * 2
        value = value.reshape(value.shape[:dim] + (left * block,) + value.shape[dim + 2 :])
    return value


def scatter_narrow(value):
    value = value.reshape((2, 2) + value.shape[1:])
    pair = added(value[:, 0], swap(value[:, 1], "narrow", 1))
    return added(pair[0], swap(pair[1], "narrow", 2))


def body(
    tokens,
    frame_counts,
    actions,
    action_table,
    norm_gains,
    spatial_project,
    spatial_merge,
    temporal_project,
    temporal_merge,
    expand_weight,
    reduce_weight,
    grad_out,
):
    frames_dev, tokens_frame, width = tokens.shape
    wide_me, narrow_me = lax.axis_index("wide"), lax.axis_index("narrow")
    x_me = wide_me % 2
    span = tokens_frame // 8
    rows = 2 * frames_dev * span
    spatial_project = spatial_project.transpose(1, 0, 2)
    temporal_project = temporal_project.transpose(1, 0, 2)

    def keep_of(wide_place):
        frame_ids = wide_place * frames_dev + jnp.arange(frames_dev, dtype=jnp.int32)
        clip_places = jnp.arange(frame_counts.shape[0], dtype=jnp.int32)
        clip_count = jnp.sum(
            jnp.where((frame_ids // FRAMES)[:, None] == clip_places[None, :], frame_counts[None, :], 0),
            axis=1,
        )
        return (frame_ids % FRAMES < clip_count).astype(F32)

    keep_place = jnp.concatenate([keep_of(wide_me), keep_of(wide_me + 1 - 2 * x_me)])
    keep_place = jnp.broadcast_to(keep_place[:, None], (2 * frames_dev, span)).reshape(rows, 1)
    choose = (
        actions[:, None] == jnp.arange(action_table.shape[0], dtype=jnp.int32)[None, :]
    ).astype(BF16)
    extra = jnp.dot(choose, action_table, preferred_element_type=F32)

    (
        normed1,
        heads1,
        mixed1,
        tokens_place,
        extra_place,
        grad_place,
        expand_pair,
        reduce_pair,
        merge1_all,
        project_all,
        merge2_all,
    ) = spatial_forward(
        tokens,
        extra,
        norm_gains[0:1],
        spatial_project,
        spatial_merge,
        temporal_project,
        temporal_merge,
        expand_weight,
        reduce_weight,
        grad_out,
    )
    mixed1 = mixed1.reshape(4, rows, mixed1.shape[-1])
    hidden1, normed2, heads2, mixed2, hidden2, normed3 = temporal_forward(
        tokens_place.reshape(2 * frames_dev, span, width),
        extra_place.reshape(2 * frames_dev, 1, width),
        keep_place,
        norm_gains,
        mixed1,
        merge1_all,
        project_all,
        merge2_all,
    )

    grad_result = grad_place[0].reshape(rows, width)
    grad_result_far = grad_place[1].reshape(rows, width)
    normed3_far = swap(normed3, "narrow", 2)
    near = feed_forward(normed3, grad_result, keep_place, expand_pair, reduce_pair)
    far = feed_forward(
        after(normed3_far, near[0]), grad_result_far, keep_place, expand_pair, reduce_pair
    )
    grad_normed3_far = swap(far[4], "narrow", 2)
    feed_grad = feed_outer(
        (normed3, normed3_far), (near[1], far[1]), (near[2], far[2]), (near[0], far[0])
    )

    branch2_grad, grad_heads2, branch1_grad, grad_mixed1, carried, gain_three, gain_two = temporal_backward(
        near[4],
        after(grad_normed3_far, feed_grad),
        hidden2,
        hidden1,
        grad_result,
        keep_place,
        norm_gains,
        heads2,
        merge2_all,
        project_all,
        merge1_all,
    )
    branch3_far = swap(after(far[3], grad_normed3_far), "narrow", 2)
    feed_grad = added(feed_grad[0], swap(after(feed_grad[1], grad_normed3_far), "narrow", 1))

    temporal_grad, grad_mixed1, carried = temporal_outer(
        grad_mixed1, carried, mixed1, branch1_grad, mixed2, branch2_grad, normed2, grad_heads2
    )

    branch3 = near[3].astype(F32) + branch3_far.astype(F32)
    result = (hidden2 + keep_place * branch3).astype(BF16)
    result = after(result, grad_mixed1).reshape(2, frames_dev, span, width)
    result = jnp.stack([result[0], swap(result[1], "wide", 1)])
    result = jnp.stack([result, swap(result, "narrow", 2)])
    result = jnp.stack([result, swap(result, "narrow", 1)])
    output = in_order(result, BF16)

    project1_grad, gain_one, totals, grad_tokens = spatial_backward(
        heads1, grad_mixed1, spatial_project, normed1, tokens, extra, norm_gains[0:1], carried
    )
    grad_tokens = grad_tokens.reshape(frames_dev, tokens_frame, width).astype(F32)
    table_grad = jnp.dot(choose.astype(F32).T, totals[:, 0], precision=HIGHEST)

    small = jnp.concatenate([gain_one, gain_two, gain_three, table_grad])
    small = small + swap(small, "narrow", 1)
    small = small + swap(small, "narrow", 2)
    wide = lax.axis_size("wide")
    bit = 1
    while bit < wide:
        small = small + swap(small, "wide", bit)
        bit *= 2
    small = lax.dynamic_slice_in_dim(small, wide_me * (width // wide), width // wide, axis=1)

    feed_grad = scatter_wide(after(feed_grad, grad_mixed1), 1).astype(F32)
    temporal_grad = scatter_wide(scatter_narrow(temporal_grad), 1).astype(F32)
    project1_grad = scatter_wide(project1_grad, 1).astype(F32)
    return (
        output,
        grad_tokens,
        small[:3],
        small[3:],
        project1_grad.transpose(1, 0, 2),
        temporal_grad[0].T,
        temporal_grad[2:].transpose(1, 0, 2),
        temporal_grad[1].T,
        feed_grad[0],
        feed_grad[1].T,
    )


def solution(mesh):
    return jax.shard_map(
        body,
        mesh=mesh,
        in_specs=(
            P("wide", None, None),
            P(),
            P("wide"),
            P(),
            P(),
            P(None, None, "narrow"),
            P("narrow", None),
            P(None, None, "narrow"),
            P("narrow", None),
            P(None, "narrow"),
            P("narrow", None),
            P("wide", None, None),
        ),
        out_specs=(
            P("wide", None, None),
            P("wide", None, None),
            P(None, "wide"),
            P(None, "wide"),
            P("wide", None, "narrow"),
            P("narrow", "wide"),
            P("wide", None, "narrow"),
            P("narrow", "wide"),
            P("wide", "narrow"),
            P("narrow", "wide"),
        ),
        check_vma=False,
    )
```

```python
import jax
import jax.numpy as jnp
from jax import lax
from jax.experimental import pallas as pl
from jax.experimental.pallas import tpu as pltpu
from jax.sharding import PartitionSpec as P

HD = 64
FRAMES = 16
GROUP = 16
PAIR = 2 * HD

EPSILON = 1e-06
NEGATIVE = -1e30
F32 = jnp.float32
BF16 = jnp.bfloat16
VMEM_LIMIT = 56 * 1024 * 1024
NN = (((1,), (0,)), ((), ()))
NT = (((1,), (1,)), ((), ()))
TN = (((0,), (0,)), ((), ()))


def mm(left, right, form=NN):
    return lax.dot_general(left, right, form, preferred_element_type=F32)


def root(value):
    return lax.rsqrt(jnp.mean(value * value, axis=-1, keepdims=True) + EPSILON)


def norm_back(value, gain, incoming):
    scale = root(value)
    scaled = gain * incoming
    inner = jnp.mean(scaled * value, axis=-1, keepdims=True)
    back = scale * scaled - (scale * scale * scale) * inner * value
    return back, jnp.sum(incoming * value * scale, axis=0, keepdims=True)


def sides():
    lane = lax.broadcasted_iota(jnp.int32, (1, PAIR), 1)
    low = (lane < HD).astype(F32)
    return lane < HD, low.astype(BF16), (1.0 - low).astype(BF16)


def attend_pair(queries, key_rows, value_rows, allowed):
    is_low, low, high = sides()
    mixed = []
    for side in (low, high):
        scores = mm(queries * (side * HD ** (-0.5)), key_rows, NT)
        if allowed is not None:
            scores = jnp.where(allowed, scores, NEGATIVE)
        shares = jnp.exp(scores - jnp.max(scores, axis=-1, keepdims=True))
        shares = shares * (1.0 / jnp.sum(shares, axis=-1, keepdims=True))
        mixed.append(mm(shares.astype(BF16), value_rows))
    return jnp.where(is_low, mixed[0], mixed[1]).astype(BF16)


def attend_back_pair(queries, key_rows, value_rows, grad_mixed, allowed):
    factor = HD ** (-0.5)
    is_low, low, high = sides()
    parts = []
    for side in (low, high):
        scores = mm(key_rows, queries * (side * factor), NT)
        if allowed is not None:
            scores = jnp.where(allowed, scores, NEGATIVE)
        chances = jnp.exp(scores - jnp.max(scores, axis=0, keepdims=True))
        chances = chances * (1.0 / jnp.sum(chances, axis=0, keepdims=True))
        grad_chances = mm(value_rows, grad_mixed * side, NT)
        shift = jnp.sum(grad_chances * chances, axis=0, keepdims=True)
        grad_scores = (chances * (grad_chances - shift)).astype(BF16)
        parts.append(
            (
                mm(grad_scores, key_rows, TN) * factor,
                mm(grad_scores, queries) * factor,
                mm(chances.astype(BF16), grad_mixed),
            )
        )
    return [jnp.where(is_low, a, b).astype(BF16) for a, b in zip(parts[0], parts[1])]


def whole(shape):
    return pl.BlockSpec(shape, lambda *_: (0,) * len(shape))


def call(kernel, grid, in_specs, out_specs, out_shape, scratch=(), flops=0, moved=0):
    return pl.pallas_call(
        kernel,
        grid=grid,
        in_specs=in_specs,
        out_specs=out_specs,
        out_shape=out_shape,
        scratch_shapes=list(scratch),
        compiler_params=pltpu.CompilerParams(vmem_limit_bytes=VMEM_LIMIT),
        cost_estimate=pl.CostEstimate(flops=flops, bytes_accessed=moved, transcendentals=0),
    )


def shape_of(shape, kind=BF16):
    return jax.ShapeDtypeStruct(shape, kind)


def place_masks(x_me, frames_all, transposed):
    rows = frames_all * GROUP
    shape = (rows, rows)
    query = lax.broadcasted_iota(jnp.int32, shape, 1 if transposed else 0)
    key = lax.broadcasted_iota(jnp.int32, shape, 0 if transposed else 1)
    query_frame = (query // GROUP + x_me * (frames_all // 2)) % frames_all
    key_frame = (key // GROUP + x_me * (frames_all // 2)) % frames_all
    return (query % GROUP == key % GROUP) & (key_frame <= query_frame)


def temporal_forward(tokens, extra, keep, gains, mixed1, merge1, project, merge2):
    _, span, width = tokens.shape
    rows = FRAMES * span
    local = mixed1.shape[-1]
    group_rows = FRAMES * GROUP

    def kernel(
        tokens_ref,
        extra_ref,
        keep_ref,
        gains_ref,
        mixed1_ref,
        merge1_ref,
        project_ref,
        merge2_ref,
        hidden1_ref,
        normed2_ref,
        heads_ref,
        mixed2_ref,
        hidden2_ref,
        normed3_ref,
    ):
        step = pl.program_id(0)
        keep_rows = keep_ref[...]

        @pl.when(step == 0)
        def _():
            branch = mm(mixed1_ref[0], merge1_ref[0])
            for n in range(1, 4):
                branch += mm(mixed1_ref[n], merge1_ref[n])
            begin = tokens_ref[...].astype(F32) + extra_ref[...]
            hidden1 = begin.reshape(rows, width) + keep_rows * branch
            hidden1_ref[...] = hidden1
            hidden2_ref[...] = hidden1
            normed2_ref[...] = (hidden1 * root(hidden1) * gains_ref[1:2]).astype(BF16)

        for c in range(3):
            head = mm(normed2_ref[...], project_ref[0, c]).astype(BF16)
            heads_ref[0, c] = head.reshape(FRAMES, span, local)
        allowed = place_masks(lax.axis_index("wide") % 2, FRAMES, False)
        for g in range(span // GROUP):
            band = pl.ds(g * GROUP, GROUP)
            for at in range(0, local, PAIR):
                part = pl.ds(at, PAIR)
                terms = [heads_ref[0, c, :, band, part].reshape(group_rows, PAIR) for c in range(3)]
                mixed = attend_pair(*terms, allowed)
                mixed2_ref[0, :, band, part] = mixed.reshape(FRAMES, GROUP, PAIR)
        hidden2_ref[...] += keep_rows * mm(mixed2_ref[0].reshape(rows, local), merge2_ref[0])

        @pl.when(step == 3)
        def _():
            hidden2 = hidden2_ref[...]
            normed3_ref[...] = (hidden2 * root(hidden2) * gains_ref[2:3]).astype(BF16)

    return call(
        kernel,
        (4,),
        [
            whole((FRAMES, span, width)),
            whole((FRAMES, 1, width)),
            whole((rows, 1)),
            whole((3, width)),
            whole((4, rows, local)),
            whole((4, local, width)),
            pl.BlockSpec((1, 3, width, local), lambda n: (n, 0, 0, 0)),
            pl.BlockSpec((1, local, width), lambda n: (n, 0, 0)),
        ],
        [
            whole((rows, width)),
            whole((rows, width)),
            pl.BlockSpec((1, 3, FRAMES, span, local), lambda n: (n, 0, 0, 0, 0)),
            pl.BlockSpec((1, FRAMES, span, local), lambda n: (n, 0, 0, 0)),
            whole((rows, width)),
            whole((rows, width)),
        ],
        [
            shape_of((rows, width), F32),
            shape_of((rows, width)),
            shape_of((4, 3, FRAMES, span, local)),
            shape_of((4, FRAMES, span, local)),
            shape_of((rows, width), F32),
            shape_of((rows, width)),
        ],
        flops=2 * rows * width * width * 6,
        moved=24 * 2**20,
    )(tokens, extra, keep, gains, mixed1, merge1, project, merge2)


RATE = 0.7978845608028654
CUBIC = 0.044715


def feed_forward(normed, grad, keep, expand, reduce):
    rows, width = normed.shape
    cores, _, units = expand.shape
    block = 512
    per = units // block

    def kernel(
        normed_ref,
        grad_ref,
        keep_ref,
        expand_ref,
        reduce_ref,
        active_ref,
        inner_ref,
        grad_branch_ref,
        branch_ref,
        grad_normed_ref,
        branch_sum,
        grad_sum,
    ):
        step = pl.program_id(0)

        @pl.when(step == 0)
        def _():
            grad_branch_ref[...] = (keep_ref[...] * grad_ref[...].astype(F32)).astype(BF16)
            branch_sum[...] = jnp.zeros_like(branch_sum)
            grad_sum[...] = jnp.zeros_like(grad_sum)

        inner = mm(normed_ref[...], expand_ref[0])
        grad_active = mm(grad_branch_ref[...], reduce_ref[0], NT)
        square = inner * inner
        bend = jnp.tanh(RATE * inner * (1.0 + CUBIC * square))
        half = 0.5 * (1.0 + bend)
        active = (inner * half).astype(BF16)
        slope = half + (0.5 * RATE) * inner * (1.0 - bend * bend) * (1.0 + (3.0 * CUBIC) * square)
        grad_inner = (grad_active * slope).astype(BF16)
        active_ref[...] = active
        inner_ref[...] = grad_inner
        branch_sum[...] += mm(active, reduce_ref[0])
        grad_sum[...] += mm(grad_inner, expand_ref[0], NT)

        @pl.when(step == cores * per - 1)
        def _():
            branch_ref[...] = branch_sum[...].astype(BF16)
            grad_normed_ref[...] = grad_sum[...].astype(BF16)

    full = whole((rows, width))
    return call(
        kernel,
        (cores * per,),
        [
            full,
            full,
            whole((rows, 1)),
            pl.BlockSpec((1, width, block), lambda j: (j // per, 0, j % per)),
            pl.BlockSpec((1, block, width), lambda j: (j // per, j % per, 0)),
        ],
        [
            pl.BlockSpec((rows, block), lambda j: (0, j)),
            pl.BlockSpec((rows, block), lambda j: (0, j)),
            full,
            full,
            full,
        ],
        [
            shape_of((rows, cores * units)),
            shape_of((rows, cores * units)),
            shape_of((rows, width)),
            shape_of((rows, width)),
            shape_of((rows, width)),
        ],
        scratch=[pltpu.VMEM((rows, width), F32), pltpu.VMEM((rows, width), F32)],
        flops=8 * rows * width * cores * units,
        moved=18 * 2**20,
    )(normed, grad, keep, expand, reduce)


def temporal_backward(
    grad_near, grad_far, hidden2, hidden1, grad_result, keep, gains, heads, merge2, project, merge1
):
    rows, width = hidden1.shape
    local = merge1.shape[1]
    span = rows // FRAMES
    group_rows = FRAMES * GROUP

    def kernel(
        near_ref,
        far_ref,
        hidden2_ref,
        hidden1_ref,
        result_ref,
        keep_ref,
        gains_ref,
        heads_ref,
        merge2_ref,
        project_ref,
        merge1_ref,
        branch2_ref,
        grad_heads_ref,
        branch1_ref,
        mixed1_ref,
        carried_ref,
        gain3_ref,
        gain2_ref,
        grad_hidden,
        grad_normed,
        grad_mixed,
    ):
        step = pl.program_id(0)

        @pl.when(step == 0)
        def _():
            incoming = near_ref[...].astype(F32) + far_ref[...].astype(F32)
            back, gain3_ref[...] = norm_back(hidden2_ref[...], gains_ref[2:3], incoming)
            total = result_ref[...].astype(F32) + back
            grad_hidden[...] = total
            branch2_ref[...] = (keep_ref[...] * total).astype(BF16)
            grad_normed[...] = jnp.zeros_like(grad_normed)

        back_mixed = mm(branch2_ref[...], merge2_ref[0], NT).astype(BF16)
        grad_mixed[...] = back_mixed.reshape(FRAMES, span, local)
        allowed = place_masks(lax.axis_index("wide") % 2, FRAMES, True)
        for g in range(span // GROUP):
            band = pl.ds(g * GROUP, GROUP)
            for at in range(0, local, PAIR):
                part = pl.ds(at, PAIR)
                terms = [heads_ref[0, c, :, band, part].reshape(group_rows, PAIR) for c in range(3)]
                grad = grad_mixed[:, band, part].reshape(group_rows, PAIR)
                grads = attend_back_pair(*terms, grad, allowed)
                for c in range(3):
                    grad_heads_ref[0, c, :, band, part] = grads[c].reshape(FRAMES, GROUP, PAIR)
        total = mm(grad_heads_ref[0, 0].reshape(rows, local), project_ref[0, 0], NT)
        for c in range(1, 3):
            total += mm(grad_heads_ref[0, c].reshape(rows, local), project_ref[0, c], NT)
        grad_normed[...] += total

        @pl.when(step == 3)
        def _():
            back, gain2_ref[...] = norm_back(hidden1_ref[...], gains_ref[1:2], grad_normed[...])
            total = grad_hidden[...] + back
            carried_ref[...] = total.astype(BF16)
            branch1_ref[...] = (keep_ref[...] * total).astype(BF16)
            for n in range(4):
                mixed1_ref[n] = mm(branch1_ref[...], merge1_ref[n], NT).astype(BF16)

    full = whole((rows, width))
    row = whole((1, width))
    return call(
        kernel,
        (4,),
        [
            full,
            full,
            full,
            full,
            full,
            whole((rows, 1)),
            whole((3, width)),
            pl.BlockSpec((1, 3, FRAMES, span, local), lambda n: (n, 0, 0, 0, 0)),
            pl.BlockSpec((1, local, width), lambda n: (n, 0, 0)),
            pl.BlockSpec((1, 3, width, local), lambda n: (n, 0, 0, 0)),
            whole((4, local, width)),
        ],
        [
            full,
            pl.BlockSpec((1, 3, FRAMES, span, local), lambda n: (n, 0, 0, 0, 0)),
            full,
            whole((4, rows, local)),
            full,
            row,
            row,
        ],
        [
            shape_of((rows, width)),
            shape_of((4, 3, FRAMES, span, local)),
            shape_of((rows, width)),
            shape_of((4, rows, local)),
            shape_of((rows, width)),
            shape_of((1, width), F32),
            shape_of((1, width), F32),
        ],
        scratch=[
            pltpu.VMEM((rows, width), F32),
            pltpu.VMEM((rows, width), F32),
            pltpu.VMEM((FRAMES, span, local), BF16),
        ],
        flops=2 * rows * width * width * 8,
        moved=30 * 2**20,
    )(grad_near, grad_far, hidden2, hidden1, grad_result, keep, gains, heads, merge2, project, merge1)


def here():
    wide, narrow = lax.axis_index("wide"), lax.axis_index("narrow")
    return wide, narrow, wide % 2, narrow // 2, narrow % 2


def other(wide, narrow, x, y, core):
    if x:
        wide = wide + 1 - 2 * (wide % 2)
    if y:
        narrow = (narrow + 2) % 4
    if core:
        narrow = narrow + 1 - 2 * (narrow % 2)
    return wide, narrow


def beyond(wide, narrow):
    return wide + 2 - 4 * ((wide // 2) % 2), narrow


def place_of(wide, narrow, span):
    return pl.multiple_of(((wide % 2) * 4 + narrow) * span, span)


def remote(src, dst, sems, i, device):
    return pltpu.make_async_remote_copy(
        src_ref=src,
        dst_ref=dst,
        send_sem=sems.at[0, i],
        recv_sem=sems.at[1, i],
        device_id=device,
        device_id_type=pl.DeviceIdType.MESH,
    )


def greet(devices):
    barrier = pltpu.get_barrier_semaphore()
    for device in devices:
        pl.semaphore_signal(
            barrier, inc=1, device_id=device, device_id_type=pl.DeviceIdType.MESH
        )
    pl.semaphore_wait(barrier, len(devices))


OTHERS = [(x, y, c) for x in range(2) for y in range(2) for c in range(2) if x + y + c > 0]
ANY = pl.BlockSpec(memory_space=pl.ANY)


def comm_call(kernel, number, grid, in_specs, out_specs, out_shape, scratch, flops):
    return pl.pallas_call(
        kernel,
        grid=grid,
        in_specs=in_specs,
        out_specs=out_specs,
        out_shape=out_shape,
        scratch_shapes=scratch,
        compiler_params=pltpu.CompilerParams(
            vmem_limit_bytes=VMEM_LIMIT, collective_id=number, has_side_effects=True
        ),
        cost_estimate=pl.CostEstimate(flops=flops, bytes_accessed=30 * 2**20, transcendentals=0),
    )


def spatial_forward(
    tokens, extra, gain, project, merge1, project2, merge2, expand, reduce, grad_out
):
    frames, places, width = tokens.shape
    local = project.shape[-1]
    span = places // 8
    half = frames // 2
    shards = (merge1, project2.reshape(3 * width, local), merge2)
    count = len(shards)

    def kernel(
        tokens_ref,
        extra_ref,
        gain_ref,
        project_ref,
        all_tokens,
        all_extra,
        grad_ref,
        expand_ref,
        reduce_ref,
        shard0,
        shard1,
        shard2,
        normed_ref,
        heads_ref,
        mixed_all,
        tokens_place,
        extra_place,
        grad_place,
        expand_pair,
        reduce_pair,
        full0,
        full1,
        full2,
        mixed_ref,
        local_sems,
        move_sems,
        shard_sems,
        mixed_sems,
        *stage,
    ):
        step = pl.program_id(0)
        wide, narrow, x_me, _, _ = here()
        half_me = (wide // 2) % 2
        x_other = other(wide, narrow, 1, 0, 0)
        y_other = other(wide, narrow, 0, 1, 0)
        core_other = other(wide, narrow, 0, 0, 1)
        z_other = beyond(wide, narrow)
        mine = pl.ds(place_of(wide, narrow, span), span)
        near_y = pl.ds(place_of(*y_other, span), span)
        shard = (shard0, shard1, shard2)
        full = (full0, full1, full2)

        own = [
            (expand_ref, expand_pair.at[0]),
            (reduce_ref, reduce_pair.at[0]),
            (all_tokens.at[:, mine], tokens_place.at[0]),
            (all_extra, extra_place.at[0]),
            (grad_ref.at[:, mine], grad_place.at[0, 0]),
            (grad_ref.at[:, near_y], grad_place.at[1, 0]),
        ] + [(shard[k], full[k].at[0]) for k in range(count)]
        into = [pltpu.make_async_copy(a, v, local_sems.at[0, i]) for i, ((a, _), v) in enumerate(zip(own, stage))]
        back = [pltpu.make_async_copy(v, b, local_sems.at[1, i]) for i, ((_, b), v) in enumerate(zip(own, stage))]
        far = pl.ds(place_of(*x_other, span), span)
        far_y = pl.ds(place_of(*other(wide, narrow, 1, 1, 0), span), span)
        first = [
            remote(all_tokens.at[:, far], tokens_place.at[1], move_sems, 0, x_other),
            remote(all_extra, extra_place.at[1], move_sems, 1, x_other),
            remote(expand_ref, expand_pair.at[1], move_sems, 2, core_other),
            remote(reduce_ref, reduce_pair.at[1], move_sems, 3, core_other),
        ]
        last = [
            remote(grad_ref.at[:, far], grad_place.at[0, 1], move_sems, 4, x_other),
            remote(grad_ref.at[:, far_y], grad_place.at[1, 1], move_sems, 5, x_other),
        ]

        def part(k, which):
            rows = shards[k].shape[0] // 2
            return pl.ds(pl.multiple_of(which * rows, rows), rows)

        def over_core(k):
            return remote(shard[k], full[k].at[1], shard_sems, 5 * k, core_other)

        def over_y(k):
            rows = part(k, half_me)
            return remote(shard[k].at[rows], full[k].at[2, rows], shard_sems, 5 * k + 1, y_other)

        def onward(k, which, i, device, slot):
            rows = part(k, which)
            return remote(full[k].at[2, rows], full[k].at[slot, rows], shard_sems, 5 * k + i, device)

        def over_z(k):
            return onward(k, half_me, 2, z_other, 2)

        def near_half(k):
            return onward(k, half_me, 3, core_other, 3)

        def far_half(k):
            return onward(k, 1 - half_me, 4, core_other, 3)

        def mixed_copies(chunk):
            copies = []
            some = pl.ds(chunk * half, half)
            for i, (x, y, c) in enumerate(OTHERS):
                device = other(wide, narrow, x, y, c)
                copies.append(
                    remote(
                        mixed_ref.at[some, pl.ds(place_of(*device, span), span)],
                        mixed_all.at[2 * y + c, x, some],
                        mixed_sems,
                        7 * chunk + i,
                        device,
                    )
                )
            here_copy = pltpu.make_async_copy(
                mixed_ref.at[some, mine], mixed_all.at[0, 0, some], local_sems.at[chunk, len(own)]
            )
            return copies, here_copy

        @pl.when(step == 0)
        def _():
            greet([other(wide, narrow, *o) for o in OTHERS] + [z_other])
            for k in range(count):
                over_y(k).start()
            for copy in first:
                copy.start()
            for k in range(count):
                over_core(k).start()
            for copy in into:
                copy.start()

        @pl.when(step == 2)
        def _():
            for copy in into:
                copy.wait()
            for copy in back:
                copy.start()

        start = tokens_ref[0].astype(F32) + extra_ref[0]
        normed = (start * root(start) * gain_ref[...]).astype(BF16)
        normed_ref[0] = normed
        for c in range(3):
            heads_ref[c, 0] = mm(normed, project_ref[c]).astype(BF16)
        for at in range(0, local, PAIR):
            lanes = pl.ds(at, PAIR)
            mixed_ref[step, :, lanes] = attend_pair(
                heads_ref[0, 0, :, lanes], heads_ref[1, 0, :, lanes], heads_ref[2, 0, :, lanes], None
            )

        def forward(k):
            over_y(k).wait_recv()
            over_z(k).start()
            near_half(k).start()

        @pl.when(step == half - 1)
        def _():
            copies, here_copy = mixed_copies(0)
            for copy in copies:
                copy.start()
            here_copy.start()
            forward(0)

        @pl.when(step == frames - 1)
        def _():
            copies, here_copy = mixed_copies(1)
            for copy in copies:
                copy.start()
            here_copy.start()
            for copy in last:
                copy.start()
            forward(1)
            forward(2)
            for k in range(count):
                over_z(k).wait_recv()
                far_half(k).start()
            for chunk in range(2):
                copies, here_copy = mixed_copies(chunk)
                for copy in copies:
                    copy.wait()
                here_copy.wait()
            for copy in first + last:
                copy.wait()
            for copy in back:
                copy.wait()
            for k in range(count):
                over_core(k).wait()
                over_y(k).wait_send()
                over_z(k).wait_send()
                near_half(k).wait()
                far_half(k).wait()

    out = comm_call(
        kernel,
        0,
        (frames,),
        [
            pl.BlockSpec((1, places, width), lambda f: (f, 0, 0)),
            pl.BlockSpec((1, 1, width), lambda f: (f, 0, 0)),
            whole((1, width)),
            whole(project.shape),
        ]
        + [ANY] * 8,
        [
            pl.BlockSpec((1, places, width), lambda f: (f, 0, 0)),
            pl.BlockSpec((3, 1, places, local), lambda f: (0, f, 0, 0)),
        ]
        + [ANY] * 9,
        [
            shape_of((frames, places, width)),
            shape_of((3, frames, places, local)),
            shape_of((4, 2, frames, span, local)),
            shape_of((2, frames, span, width)),
            shape_of((2, frames, 1, width), F32),
            shape_of((2, 2, frames, span, width)),
            shape_of((2,) + expand.shape),
            shape_of((2,) + reduce.shape),
        ]
        + [shape_of((4,) + shard.shape) for shard in shards],
        [
            pltpu.VMEM((frames, places, local), BF16),
            pltpu.SemaphoreType.DMA((2, 7 + count)),
            pltpu.SemaphoreType.DMA((2, 6)),
            pltpu.SemaphoreType.DMA((2, 5 * count)),
            pltpu.SemaphoreType.DMA((2, 14)),
            pltpu.VMEM(expand.shape, BF16),
            pltpu.VMEM(reduce.shape, BF16),
            pltpu.VMEM((frames, span, width), BF16),
            pltpu.VMEM((frames, 1, width), F32),
            pltpu.VMEM((frames, span, width), BF16),
            pltpu.VMEM((frames, span, width), BF16),
        ]
        + [pltpu.VMEM(shard.shape, BF16) for shard in shards],
        2 * frames * places * width * local * 4,
    )(
        tokens,
        extra[:, None, :],
        gain,
        project,
        tokens,
        extra[:, None, :],
        grad_out,
        expand,
        reduce,
        *shards,
    )
    out = list(out)
    out[9] = out[9].reshape(4, 3, width, local)
    return out


def feed_outer(normed, grad_inner, grad_branch, active):
    rows, width = normed[0].shape
    units = active[0].shape[1] // 2
    block = 512
    per = units // block
    wide = lax.axis_size("wide")
    split = (2, wide // 2, 2, width // wide, block)

    def kernel(
        normed0,
        normed1,
        branch0,
        branch1,
        inner0,
        inner1,
        active0,
        active1,
        keep_ref,
        send_ref,
        left,
        right,
        total,
        given,
        taken,
        sems,
    ):
        step = pl.program_id(0)
        wide, narrow, x_me, _, _ = here()
        core_other = other(wide, narrow, 0, 0, 1)

        def over(j):
            return remote(given.at[j], taken.at[j], sems, j, core_other)

        @pl.when(step == 0)
        def _():
            left[:, :rows] = normed0[...].T
            left[:, rows:] = normed1[...].T
            right[:, :rows] = branch0[...].T
            right[:, rows:] = branch1[...].T

        expand = mm(left[:, :rows], inner0[...]) + mm(left[:, rows:], inner1[...])
        reduce = mm(right[:, :rows], active0[...]) + mm(right[:, rows:], active1[...])

        @pl.when(step == 0)
        def _():
            greet([core_other])

        @pl.when(step < per)
        def _():
            given[step, 0] = expand.astype(BF16)
            given[step, 1] = reduce.astype(BF16)
            over(step).start()

        @pl.when(step >= per)
        def _():
            j = step - per
            over(j).wait_recv()
            half = split[1:]
            total[0] = (expand + taken[j, 0].astype(F32)).astype(BF16).reshape(half)
            total[1] = (reduce + taken[j, 1].astype(F32)).astype(BF16).reshape(half)
            out = keep_ref.shape
            keep_ref[...] = total[:, :, pl.ds(x_me, 1)].reshape(out)
            send_ref[...] = total[:, :, pl.ds(1 - x_me, 1)].reshape(out)

        @pl.when(step == 2 * per - 1)
        def _():
            for j in range(per):
                over(j).wait_send()

    full = whole((rows, width))
    part = pl.BlockSpec((rows, block), lambda j: (0, (j + per) % (2 * per)))
    out = pl.BlockSpec((2, width // 2, block), lambda j: (0, 0, jnp.maximum(j - per, 0)))
    return comm_call(
        kernel,
        3,
        (2 * per,),
        [full] * 4 + [part] * 4,
        [out, out],
        [shape_of((2, width // 2, units))] * 2,
        [
            pltpu.VMEM((width, 2 * rows), BF16),
            pltpu.VMEM((width, 2 * rows), BF16),
            pltpu.VMEM(split, BF16),
            pltpu.VMEM((per, 2, width, block), BF16),
            pltpu.VMEM((per, 2, width, block), BF16),
            pltpu.SemaphoreType.DMA((2, per)),
        ],
        16 * rows * width * units,
    )(*normed, *grad_branch, *grad_inner, *active)


def temporal_outer(
    grad_mixed1, carried, result, mixed1, branch1, mixed2, branch2, normed2, grad_heads
):
    rows, width = branch1.shape
    local = mixed1.shape[-1]
    span = rows // FRAMES
    frames = FRAMES // 2

    def kernel(
        grad_ref,
        carried_ref,
        result_ref,
        mixed1_ref,
        branch1_ref,
        mixed2_ref,
        branch2_ref,
        normed2_ref,
        heads_ref,
        out_ref,
        grad_own,
        carried_own,
        result_far,
        left,
        given,
        taken,
        grad_stage,
        carried_stage,
        local_sems,
        sems,
    ):
        step = pl.program_id(0)
        wide, narrow, x_me, _, _ = here()
        x_other = other(wide, narrow, 1, 0, 0)
        mine = pl.ds(place_of(wide, narrow, span), span)
        copies = [
            remote(
                grad_ref.at[2 * y + c, x],
                grad_own.at[:, mine],
                sems,
                i,
                other(wide, narrow, x, y, c),
            )
            for i, (x, y, c) in enumerate(OTHERS)
        ]
        copies.append(remote(carried_ref.at[1], carried_own.at[:, x_me], sems, 7, x_other))
        copies.append(remote(result_ref, result_far, sems, 8, other(wide, narrow, 0, 1, 0)))

        def over(y):
            return remote(given.at[y], taken.at[y], sems, 9 + y, other(wide, narrow, 0, 0, 1))

        into = [
            pltpu.make_async_copy(grad_ref.at[0, 0], grad_stage, local_sems.at[0]),
            pltpu.make_async_copy(carried_ref.at[0], carried_stage, local_sems.at[1]),
        ]
        back = [
            pltpu.make_async_copy(grad_stage, grad_own.at[:, mine], local_sems.at[2]),
            pltpu.make_async_copy(carried_stage, carried_own.at[:, x_me], local_sems.at[3]),
        ]

        @pl.when(step == 0)
        def _():
            greet([other(wide, narrow, *o) for o in OTHERS])
            for copy in copies + into:
                copy.start()
            left[0] = branch1_ref[...].T
            left[1] = branch2_ref[...].T
            left[2] = normed2_ref[...].T

        terms = [(0, mixed1_ref[0]), (1, mixed2_ref[0])] + [(2, heads_ref[0, c]) for c in range(3)]
        for k, (which, term) in enumerate(terms):
            total = mm(left[which], term)

            @pl.when(step < 2)
            def _():
                given[step, k] = total.astype(BF16)

            @pl.when(step >= 2)
            def _():
                out_ref[0, k] = total.astype(BF16)

        @pl.when(step < 2)
        def _():
            over(step).start()

        @pl.when(step >= 2)
        def _():
            over(step - 2).wait_recv()
            out_ref[0] = (out_ref[0].astype(F32) + taken[step - 2].astype(F32)).astype(BF16)

        @pl.when(step == 1)
        def _():
            for copy in into:
                copy.wait()
            for copy in back:
                copy.start()

        @pl.when(step == 3)
        def _():
            for copy in copies + back:
                copy.wait()
            for y in range(2):
                over(y).wait_send()

    full = whole((rows, width))

    def turn(j):
        return 2 * (j % 2) + 1 - j // 2

    part = pl.BlockSpec((1, rows, local), lambda j: (turn(j), 0, 0))
    return comm_call(
        kernel,
        1,
        (4,),
        [ANY] * 3
        + [part, full, part, full, full]
        + [pl.BlockSpec((1, 3, rows, local), lambda j: (turn(j), 0, 0, 0))],
        [pl.BlockSpec((1, 5, width, local), lambda j: (jnp.maximum(j - 2, 0), 0, 0, 0))] + [ANY] * 3,
        [
            shape_of((2, 5, width, local)),
            shape_of((frames, 8 * span, local)),
            shape_of((frames, 2, span, width)),
            shape_of(result.shape),
        ],
        [
            pltpu.VMEM((3, width, rows), BF16),
            pltpu.VMEM((2, 5, width, local), BF16),
            pltpu.VMEM((2, 5, width, local), BF16),
            pltpu.VMEM((frames, span, local), BF16),
            pltpu.VMEM((frames, span, width), BF16),
            pltpu.SemaphoreType.DMA((4,)),
            pltpu.SemaphoreType.DMA((2, 11)),
        ],
        10 * rows * width * width,
    )(
        grad_mixed1.reshape(4, 2, frames, span, local),
        carried.reshape(2, frames, span, width),
        result,
        mixed1,
        branch1,
        mixed2.reshape(4, rows, local),
        branch2,
        normed2,
        grad_heads.reshape(4, 3, rows, local),
    )


class Halving:
    def __init__(self, slots, rows, columns, blocks, first):
        self.slots, self.rows, self.columns, self.first = slots, rows, columns, first
        self.blocks = []
        while blocks > 1:
            blocks //= 2
            self.blocks.append(blocks)

    def scratch(self):
        out = []
        for blocks in self.blocks:
            out.append(pltpu.VMEM((self.slots, blocks, 2, self.rows, self.columns), BF16))
            out.append(pltpu.VMEM((self.slots, blocks, self.rows, self.columns), BF16))
        return out

    def bind(self, refs, sems, base, wide, narrow):
        self.held, self.taken = refs[0::2], refs[1::2]
        self.sems, self.base, self.wide, self.narrow = sems, base, wide, narrow

    def bit(self, level):
        step = 2 ** (self.first + level)
        return step, (self.wide // step) % 2

    def copy(self, level):
        step, bit = self.bit(level)
        device = (self.wide + step - 2 * step * bit, self.narrow)
        return remote(
            self.held[level].at[:, :, 1 - bit],
            self.taken[level],
            self.sems,
            self.base + level,
            device,
        )

    def fill(self, level, value, slot=0):
        count = value.shape[0]
        self.held[level][slot : slot + count] = value.astype(BF16).reshape(
            (count,) + self.held[level].shape[1:]
        )

    def result(self, level):
        _, bit = self.bit(level)
        shape = self.taken[level].shape
        own = self.held[level][:, :, pl.ds(bit, 1)].reshape(shape)
        return own.astype(F32) + self.taken[level][...].astype(F32)

    def advance(self, level):
        self.copy(level).wait_recv()
        total = self.result(level)
        if level + 1 < len(self.blocks):
            self.fill(level + 1, total)
            self.copy(level + 1).start()
            return None
        return total.reshape(self.slots, self.rows, self.columns)

    def close(self):
        for level in range(len(self.blocks)):
            self.copy(level).wait_send()


FIRST = 3


def spatial_backward(
    heads,
    grad_mixed,
    project,
    normed,
    tokens,
    extra,
    gain,
    carried,
    choose,
    gains_grad,
    result_near,
    result_far,
    temporal_grad,
    feed_keep,
    feed_taken,
):
    _, frames, places, local = heads.shape
    width = project.shape[1]
    span = places // 8
    tile = width // 4
    wide_size = lax.axis_size("wide")
    half = wide_size // 2
    block = width // wide_size
    bits = wide_size.bit_length() - 1
    slots = temporal_grad.shape[1]
    units = feed_keep.shape[-1]
    last = slots - FIRST
    feed = Halving(2, block, units, half, 1)
    own = Halving(3, block, local, wide_size, 0)
    timed = Halving(slots, block, local, half, 1)
    engines = (feed, own, timed)
    levels = [len(engine.blocks) for engine in engines]
    attend_end = frames
    outer_end = attend_end + 4
    part_end = outer_end + frames
    sum_end = part_end + frames

    def kernel(
        heads_ref,
        mixed_ref,
        project_ref,
        normed_ref,
        tokens_ref,
        extra_ref,
        gain_ref,
        carried_ref,
        choose_ref,
        gains_ref,
        feed_keep_ref,
        feed_taken_ref,
        near_ref,
        far_ref,
        temporal_ref,
        own_out,
        timed_out,
        feed_out,
        small_out,
        output_ref,
        out_ref,
        grad_heads,
        partial,
        from_core,
        halved,
        from_y,
        done,
        gain_grad,
        table,
        small,
        small_taken,
        first_own,
        first_taken,
        first_sum,
        first_y,
        last_own,
        last_taken,
        last_sum,
        last_x,
        result_stage,
        local_sems,
        sems,
        move_sems,
        small_sems,
        halving_sems,
        *held,
    ):
        step = pl.program_id(0)
        wide, narrow, x_me, y_me, c_me = here()
        x_other = other(wide, narrow, 1, 0, 0)
        y_other = other(wide, narrow, 0, 1, 0)
        core_other = other(wide, narrow, 0, 0, 1)
        beyond_x = [
            (wide + 2**k - 2 ** (k + 1) * ((wide // 2**k) % 2), narrow) for k in range(1, bits)
        ]
        partners = [core_other, y_other, x_other] + beyond_x
        at = base = 0
        for engine, count in zip(engines, levels):
            engine.bind(held[at : at + 2 * count], halving_sems, base, wide, narrow)
            at, base = at + 2 * count, base + count

        def core_sum(f):
            return remote(partial.at[f, :, :, 1 - c_me], from_core.at[f], sems, f, core_other)

        def y_sum(f):
            return remote(halved.at[f, :, 1 - y_me], from_y.at[f], sems, frames + f, y_other)

        def y_back(f):
            return remote(done.at[f], out_ref.at[f, :, y_me, c_me], sems, 2 * frames + f, y_other)

        def core_back(f):
            return remote(done.at[f], out_ref.at[f, :, y_me, c_me], sems, 3 * frames + f, core_other)

        def core_onward(f):
            there = out_ref.at[f, :, 1 - y_me, c_me]
            return remote(there, there, sems, 4 * frames + f, core_other)

        def keep_own(f):
            return pltpu.make_async_copy(done.at[f], out_ref.at[f, :, y_me, c_me], local_sems.at[f])

        result = (near_ref, far_ref)

        def place(y):
            return y_me if y == 0 else 1 - y_me

        def result_x(y):
            there = output_ref.at[:, x_me, place(y), c_me]
            return remote(result[y].at[1], there, move_sems, y, x_other)

        def result_core(y):
            there = output_ref.at[:, x_me, place(y), c_me]
            return remote(result[y].at[0], there, move_sems, 2 + y, core_other)

        def result_onward(y):
            there = output_ref.at[:, 1 - x_me, place(y), c_me]
            return remote(there, there, move_sems, 4 + y, core_other)

        def result_in(y):
            return pltpu.make_async_copy(
                result[y].at[0], result_stage.at[y], local_sems.at[frames + y]
            )

        def result_own(y):
            there = output_ref.at[:, x_me, place(y), c_me]
            return pltpu.make_async_copy(result_stage.at[y], there, local_sems.at[frames + 2 + y])

        early, late_slots = pl.ds(0, FIRST), pl.ds(FIRST, last)
        first_in = pltpu.make_async_copy(
            temporal_ref.at[:, early, :, x_me], first_own, local_sems.at[frames + 4]
        )
        last_in = pltpu.make_async_copy(
            temporal_ref.at[0, late_slots], last_own, local_sems.at[frames + 5]
        )
        first_over_x = remote(
            temporal_ref.at[:, early, :, 1 - x_me], first_taken, move_sems, 6, x_other
        )
        first_over_y = remote(first_sum.at[1], first_y, move_sems, 7, y_other)
        last_over_y = remote(temporal_ref.at[1, late_slots], last_taken, move_sems, 8, y_other)
        last_over_x = remote(last_sum.at[:, :, 1 - x_me], last_x, move_sems, 9, x_other)

        def small_copy(k):
            return remote(small.at[k], small_taken.at[k], small_sems, k, partners[k])

        @pl.when(step == 0)
        def _():
            greet(partners)
            last_over_y.start()
            first_over_x.start()
            feed.fill(0, feed_keep_ref[...].astype(F32) + feed_taken_ref[...].astype(F32))
            feed.copy(0).start()
            first_in.start()
            last_in.start()
            for y in range(2):
                result_core(y).start()
                result_in(y).start()
            gain_grad[...] = jnp.zeros_like(gain_grad)
            table[...] = jnp.zeros_like(table)

        @pl.when(step < attend_end)
        def _():
            rows = pl.ds(pl.multiple_of(step * places, places), places)
            for at in range(0, local, PAIR):
                lanes = pl.ds(at, PAIR)
                grads = attend_back_pair(
                    heads_ref[0, 0, :, lanes],
                    heads_ref[1, 0, :, lanes],
                    heads_ref[2, 0, :, lanes],
                    mixed_ref[0, :, lanes],
                    None,
                )
                for c in range(3):
                    grad_heads[c, rows, lanes] = grads[c]

        @pl.when(step == 1)
        def _():
            for y in range(2):
                result_in(y).wait()
                result_own(y).start()

        @pl.when((step >= attend_end) & (step < outer_end))
        def _():
            pairs = tile // (2 * block)
            j = (step - attend_end) * pairs
            for c in range(3):
                grad = mm(normed_ref[...], grad_heads[c], TN).astype(BF16)
                own.held[0][c, pl.ds(j, pairs)] = grad.reshape(pairs, 2, block, local)

        @pl.when(step == outer_end)
        def _():
            own.copy(0).start()
            last_in.wait()
            last_over_y.wait_recv()
            last_sum[...] = (last_own[...].astype(F32) + last_taken[...].astype(F32)).astype(BF16)
            last_over_x.start()
            feed.advance(0)

        @pl.when((step >= outer_end) & (step < part_end))
        def _():
            f = step - outer_end
            rows = pl.ds(pl.multiple_of(f * places, places), places)
            total = mm(grad_heads[0, rows], project_ref[0], NT)
            for c in range(1, 3):
                total += mm(grad_heads[c, rows], project_ref[c], NT)
            partial[f] = total.astype(BF16).reshape(2, 2, 2, span, width)
            core_sum(f).start()

        @pl.when((step >= outer_end + 1) & (step < part_end + 1))
        def _():
            f = step - outer_end - 1
            core_sum(f).wait_recv()
            mine = partial[f, :, :, pl.ds(c_me, 1)].reshape(2, 2, span, width)
            halved[f] = (mine.astype(F32) + from_core[f].astype(F32)).astype(BF16)
            y_sum(f).start()

        @pl.when(step == part_end)
        def _():
            for y in range(2):
                result_x(y).start()
            first_in.wait()
            first_over_x.wait_recv()
            first_sum[...] = (first_own[...].astype(F32) + first_taken[...].astype(F32)).astype(BF16)
            first_over_y.start()

        @pl.when((step >= part_end) & (step < sum_end))
        def _():
            f = step - part_end
            y_sum(f).wait_recv()
            mine = halved[f, :, pl.ds(y_me, 1)].reshape(2 * span, width)
            incoming = mine.astype(F32) + from_y[f].reshape(2 * span, width).astype(F32)
            start = pl.multiple_of(narrow * span, span)
            begin = jnp.concatenate(
                [tokens_ref[0, pl.ds(start, span)], tokens_ref[0, pl.ds(4 * span + start, span)]]
            )
            begin = begin.astype(F32) + extra_ref[0]
            back, gain_part = norm_back(begin, gain_ref[...], incoming)
            gain_grad[...] += gain_part
            grad = carried_ref[0].reshape(2 * span, width).astype(F32) + back
            table[...] += choose_ref[0] * jnp.sum(grad, axis=0, keepdims=True)
            done[f] = grad.astype(BF16).reshape(2, span, width)
            y_back(f).start()
            core_back(f).start()
            keep_own(f).start()

        @pl.when(step == part_end + frames // 2)
        def _():
            own.advance(0)
            if levels[0] > 1:
                total = feed.advance(1)
                if total is not None:
                    feed_out[...] = total

        @pl.when(step == sum_end - 1)
        def _():
            small[0, 0:1] = gain_grad[...]
            small[0, 1:3] = gains_ref[...]
            small[0, 3:11] = table[...]
            small[0, 11:] = jnp.zeros_like(small[0, 11:])
            small_copy(0).start()
            first_over_y.wait_recv()
            mine = first_sum[0].astype(F32) + first_y[...].astype(F32)
            timed.fill(0, mine)
            last_over_x.wait_recv()
            shape = last_x.shape
            mine = last_sum[:, :, pl.ds(x_me, 1)].reshape(shape)
            timed.fill(0, mine.astype(F32) + last_x[...].astype(F32), FIRST)
            timed.copy(0).start()
            own.advance(1)
            for k in range(len(partners)):
                small_copy(k).wait_recv()
                total = small[k] + small_taken[k]
                if k + 1 < len(partners):
                    small[k + 1] = total
                    small_copy(k + 1).start()
                else:
                    small[k + 1] = total
            small_out[...] = small[len(partners)]
            for y in range(2):
                result_x(y).wait_recv()
                result_onward(y).start()
            for f in range(frames):
                y_back(f).wait_recv()
                core_onward(f).start()
            timed.advance(0)
            for level in range(2, max(levels[0], levels[1], levels[2] + 1)):
                for engine, out in ((feed, feed_out), (own, own_out)):
                    if level < len(engine.blocks):
                        total = engine.advance(level)
                        if total is not None:
                            out[...] = total
                if level - 1 < len(timed.blocks):
                    total = timed.advance(level - 1)
                    if total is not None:
                        timed_out[...] = total
            for engine in engines:
                engine.close()
            for k in range(len(partners)):
                small_copy(k).wait_send()
            for f in range(frames):
                core_sum(f).wait_send()
                y_sum(f).wait_send()
                y_back(f).wait_send()
                core_back(f).wait()
                core_onward(f).wait()
                keep_own(f).wait()
            for y in range(2):
                result_x(y).wait_send()
                result_core(y).wait()
                result_onward(y).wait()
                result_own(y).wait()
            for copy in (first_over_x, first_over_y, last_over_y, last_over_x):
                copy.wait_send()

    def frame(step):
        return jnp.minimum(step, frames - 1)

    def late(step):
        return jnp.clip(step - part_end, 0, frames - 1)

    def piece(step):
        return jnp.clip(step - attend_end, 0, 3)

    block_shape = (half, 2, block, local)
    small_rows = 16
    scratch = [
        pltpu.VMEM((3, frames * places, local), BF16),
        pltpu.VMEM((frames, 2, 2, 2, span, width), BF16),
        pltpu.VMEM((frames, 2, 2, span, width), BF16),
        pltpu.VMEM((frames, 2, 2, span, width), BF16),
        pltpu.VMEM((frames, 2, span, width), BF16),
        pltpu.VMEM((frames, 2, span, width), BF16),
        pltpu.VMEM((1, width), F32),
        pltpu.VMEM((choose.shape[1], width), F32),
        pltpu.VMEM((bits + 3, small_rows, width), F32),
        pltpu.VMEM((bits + 2, small_rows, width), F32),
        pltpu.VMEM((2, FIRST, half, block, local), BF16),
        pltpu.VMEM((2, FIRST, half, block, local), BF16),
        pltpu.VMEM((2, FIRST, half, block, local), BF16),
        pltpu.VMEM((FIRST, half, block, local), BF16),
        pltpu.VMEM((last,) + block_shape, BF16),
        pltpu.VMEM((last,) + block_shape, BF16),
        pltpu.VMEM((last,) + block_shape, BF16),
        pltpu.VMEM((last, half, block, local), BF16),
        pltpu.VMEM((2, frames, span, width), BF16),
        pltpu.SemaphoreType.DMA((frames + 6,)),
        pltpu.SemaphoreType.DMA((2, 5 * frames)),
        pltpu.SemaphoreType.DMA((2, 10)),
        pltpu.SemaphoreType.DMA((2, bits + 2)),
        pltpu.SemaphoreType.DMA((2, sum(levels))),
    ]
    for engine in engines:
        scratch += engine.scratch()
    return comm_call(
        kernel,
        2,
        (sum_end,),
        [
            pl.BlockSpec((3, 1, places, local), lambda s: (0, frame(s), 0, 0)),
            pl.BlockSpec((1, places, local), lambda s: (frame(s), 0, 0)),
            whole(project.shape),
            pl.BlockSpec((frames * places, tile), lambda s: (0, piece(s))),
            pl.BlockSpec((1, places, width), lambda s: (late(s), 0, 0)),
            pl.BlockSpec((1, 1, width), lambda s: (late(s), 0, 0)),
            whole((1, width)),
            pl.BlockSpec((1, 2, span, width), lambda s: (late(s), 0, 0, 0)),
            pl.BlockSpec((1, choose.shape[1], 1), lambda s: (late(s), 0, 0)),
            whole((2, width)),
            whole(feed_keep.shape),
            whole(feed_taken.shape),
            ANY,
            ANY,
            ANY,
        ],
        [
            whole((3, block, local)),
            whole((slots, block, local)),
            whole((2, block, units)),
            whole((small_rows, width)),
            ANY,
            ANY,
        ],
        [
            shape_of((3, block, local), F32),
            shape_of((slots, block, local), F32),
            shape_of((2, block, units), F32),
            shape_of((small_rows, width), F32),
            shape_of((frames, 2, 2, 2, span, width)),
            shape_of((frames, 2, 2, 2, span, width)),
        ],
        scratch,
        2 * frames * places * width * local * 8,
    )(
        heads,
        grad_mixed,
        project,
        normed.reshape(frames * places, width),
        tokens,
        extra[:, None, :],
        gain,
        carried,
        choose,
        gains_grad,
        feed_keep,
        feed_taken,
        result_near,
        result_far,
        temporal_grad.reshape((2, slots) + block_shape),
    )


def swap(value, axis, bit):
    size = lax.axis_size(axis)
    return lax.ppermute(value, axis, [(i, i ^ bit) for i in range(size)])


def after(value, *earlier):
    return lax.optimization_barrier((value,) + earlier)[0]


def body(
    tokens,
    frame_counts,
    actions,
    action_table,
    norm_gains,
    spatial_project,
    spatial_merge,
    temporal_project,
    temporal_merge,
    expand_weight,
    reduce_weight,
    grad_out,
):
    frames_dev, tokens_frame, width = tokens.shape
    wide_me, narrow_me = lax.axis_index("wide"), lax.axis_index("narrow")
    x_me = wide_me % 2
    span = tokens_frame // 8
    rows = 2 * frames_dev * span
    spatial_project = spatial_project.transpose(1, 0, 2)
    temporal_project = temporal_project.transpose(1, 0, 2)

    def keep_of(wide_place):
        frame_ids = wide_place * frames_dev + jnp.arange(frames_dev, dtype=jnp.int32)
        clip_places = jnp.arange(frame_counts.shape[0], dtype=jnp.int32)
        clip_count = jnp.sum(
            jnp.where((frame_ids // FRAMES)[:, None] == clip_places[None, :], frame_counts[None, :], 0),
            axis=1,
        )
        return (frame_ids % FRAMES < clip_count).astype(F32)

    keep_place = jnp.concatenate([keep_of(wide_me), keep_of(wide_me + 1 - 2 * x_me)])
    keep_place = jnp.broadcast_to(keep_place[:, None], (2 * frames_dev, span)).reshape(rows, 1)
    choose = (
        actions[:, None] == jnp.arange(action_table.shape[0], dtype=jnp.int32)[None, :]
    ).astype(BF16)
    extra = jnp.dot(choose, action_table, preferred_element_type=F32)

    (
        normed1,
        heads1,
        mixed1,
        tokens_place,
        extra_place,
        grad_place,
        expand_pair,
        reduce_pair,
        merge1_all,
        project_all,
        merge2_all,
    ) = spatial_forward(
        tokens,
        extra,
        norm_gains[0:1],
        spatial_project,
        spatial_merge,
        temporal_project,
        temporal_merge,
        expand_weight,
        reduce_weight,
        grad_out,
    )
    mixed1 = mixed1.reshape(4, rows, mixed1.shape[-1])
    hidden1, normed2, heads2, mixed2, hidden2, normed3 = temporal_forward(
        tokens_place.reshape(2 * frames_dev, span, width),
        extra_place.reshape(2 * frames_dev, 1, width),
        keep_place,
        norm_gains,
        mixed1,
        merge1_all,
        project_all,
        merge2_all,
    )

    grad_result = grad_place[0].reshape(rows, width)
    grad_result_far = grad_place[1].reshape(rows, width)
    normed3_far = swap(normed3, "narrow", 2)
    near = feed_forward(normed3, grad_result, keep_place, expand_pair, reduce_pair)
    far = feed_forward(
        after(normed3_far, near[0]), grad_result_far, keep_place, expand_pair, reduce_pair
    )
    grad_normed3_far = swap(far[4], "narrow", 2)
    feed_keep, feed_send = feed_outer(
        (normed3, normed3_far), (near[1], far[1]), (near[2], far[2]), (near[0], far[0])
    )

    branch2_grad, grad_heads2, branch1_grad, grad_mixed1, carried, gain_three, gain_two = temporal_backward(
        near[4],
        after(grad_normed3_far, feed_keep),
        hidden2,
        hidden1,
        grad_result,
        keep_place,
        norm_gains,
        heads2,
        merge2_all,
        project_all,
        merge1_all,
    )
    branch3_far = swap(after(far[3], grad_normed3_far), "narrow", 2)
    feed_taken = swap(after(feed_send, grad_normed3_far), "wide", 1)
    branch3 = near[3].astype(F32) + branch3_far.astype(F32)
    result = (hidden2 + keep_place * branch3).astype(BF16).reshape(2, frames_dev, span, width)
    temporal_grad, grad_mixed1, carried, result_far = temporal_outer(
        grad_mixed1, carried, result, mixed1, branch1_grad, mixed2, branch2_grad, normed2, grad_heads2
    )

    project1_grad, temporal_grad, feed_grad, small, output, grad_tokens = spatial_backward(
        heads1,
        grad_mixed1,
        spatial_project,
        normed1,
        tokens,
        extra,
        norm_gains[0:1],
        carried,
        choose.astype(F32)[:, :, None],
        jnp.concatenate([gain_two, gain_three]),
        result,
        result_far,
        temporal_grad,
        feed_keep,
        feed_taken,
    )
    block = width // lax.axis_size("wide")
    small = lax.dynamic_slice_in_dim(small, wide_me * block, block, axis=1)
    return (
        output.reshape(tokens.shape),
        grad_tokens.reshape(tokens.shape).astype(F32),
        small[:3],
        small[3 : 3 + action_table.shape[0]],
        project1_grad.transpose(1, 0, 2),
        temporal_grad[0].T,
        temporal_grad[2:].transpose(1, 0, 2),
        temporal_grad[1].T,
        feed_grad[0],
        feed_grad[1].T,
    )


def solution(mesh):
    return jax.shard_map(
        body,
        mesh=mesh,
        in_specs=(
            P("wide", None, None),
            P(),
            P("wide"),
            P(),
            P(),
            P(None, None, "narrow"),
            P("narrow", None),
            P(None, None, "narrow"),
            P("narrow", None),
            P(None, "narrow"),
            P("narrow", None),
            P("wide", None, None),
        ),
        out_specs=(
            P("wide", None, None),
            P("wide", None, None),
            P(None, "wide"),
            P(None, "wide"),
            P("wide", None, "narrow"),
            P("narrow", "wide"),
            P("wide", None, "narrow"),
            P("narrow", "wide"),
            P("wide", "narrow"),
            P("narrow", "wide"),
        ),
        check_vma=False,
    )
```

```python
import jax
import jax.numpy as jnp
from jax import lax
from jax.experimental import pallas as pl
from jax.experimental.pallas import tpu as pltpu
from jax.sharding import PartitionSpec as P

HD = 64
FRAMES = 16
GROUP = 16
PAIR = 2 * HD

EPSILON = 1e-06
NEGATIVE = -1e30
F32 = jnp.float32
BF16 = jnp.bfloat16
VMEM_LIMIT = 56 * 1024 * 1024
NN = (((1,), (0,)), ((), ()))
NT = (((1,), (1,)), ((), ()))
TN = (((0,), (0,)), ((), ()))


def mm(left, right, form=NN):
    return lax.dot_general(left, right, form, preferred_element_type=F32)


def root(value):
    return lax.rsqrt(jnp.mean(value * value, axis=-1, keepdims=True) + EPSILON)


def norm_back(value, gain, incoming):
    scale = root(value)
    scaled = gain * incoming
    inner = jnp.mean(scaled * value, axis=-1, keepdims=True)
    back = scale * scaled - (scale * scale * scale) * inner * value
    return back, jnp.sum(incoming * value * scale, axis=0, keepdims=True)


def sides():
    lane = lax.broadcasted_iota(jnp.int32, (1, PAIR), 1)
    low = (lane < HD).astype(F32)
    return lane < HD, low.astype(BF16), (1.0 - low).astype(BF16)


def attend_pair(queries, key_rows, value_rows, allowed):
    is_low, low, high = sides()
    mixed = []
    for side in (low, high):
        scores = mm(queries * (side * HD ** (-0.5)), key_rows, NT)
        if allowed is not None:
            scores = jnp.where(allowed, scores, NEGATIVE)
        shares = jnp.exp(scores - jnp.max(scores, axis=-1, keepdims=True))
        shares = shares * (1.0 / jnp.sum(shares, axis=-1, keepdims=True))
        mixed.append(mm(shares.astype(BF16), value_rows))
    return jnp.where(is_low, mixed[0], mixed[1]).astype(BF16)


def attend_back_pair(queries, key_rows, value_rows, grad_mixed, allowed):
    factor = HD ** (-0.5)
    is_low, low, high = sides()
    parts = []
    for side in (low, high):
        scores = mm(key_rows, queries * (side * factor), NT)
        if allowed is not None:
            scores = jnp.where(allowed, scores, NEGATIVE)
        chances = jnp.exp(scores - jnp.max(scores, axis=0, keepdims=True))
        chances = chances * (1.0 / jnp.sum(chances, axis=0, keepdims=True))
        grad_chances = mm(value_rows, grad_mixed * side, NT)
        shift = jnp.sum(grad_chances * chances, axis=0, keepdims=True)
        grad_scores = (chances * (grad_chances - shift)).astype(BF16)
        parts.append(
            (
                mm(grad_scores, key_rows, TN) * factor,
                mm(grad_scores, queries) * factor,
                mm(chances.astype(BF16), grad_mixed),
            )
        )
    return [jnp.where(is_low, a, b).astype(BF16) for a, b in zip(parts[0], parts[1])]


def whole(shape):
    return pl.BlockSpec(shape, lambda *_: (0,) * len(shape))


def call(kernel, grid, in_specs, out_specs, out_shape, scratch=(), flops=0, moved=0):
    return pl.pallas_call(
        kernel,
        grid=grid,
        in_specs=in_specs,
        out_specs=out_specs,
        out_shape=out_shape,
        scratch_shapes=list(scratch),
        compiler_params=pltpu.CompilerParams(vmem_limit_bytes=VMEM_LIMIT),
        cost_estimate=pl.CostEstimate(flops=flops, bytes_accessed=moved, transcendentals=0),
    )


def shape_of(shape, kind=BF16):
    return jax.ShapeDtypeStruct(shape, kind)


def place_masks(x_me, frames_all, transposed):
    rows = frames_all * GROUP
    shape = (rows, rows)
    query = lax.broadcasted_iota(jnp.int32, shape, 1 if transposed else 0)
    key = lax.broadcasted_iota(jnp.int32, shape, 0 if transposed else 1)
    query_frame = (query // GROUP + x_me * (frames_all // 2)) % frames_all
    key_frame = (key // GROUP + x_me * (frames_all // 2)) % frames_all
    return (query % GROUP == key % GROUP) & (key_frame <= query_frame)


def temporal_forward(tokens, extra, keep, gains, mixed1, merge1, project, merge2):
    _, span, width = tokens.shape
    rows = FRAMES * span
    local = mixed1.shape[-1]
    group_rows = FRAMES * GROUP

    def kernel(
        tokens_ref,
        extra_ref,
        keep_ref,
        gains_ref,
        mixed1_ref,
        merge1_ref,
        project_ref,
        merge2_ref,
        hidden1_ref,
        normed2_ref,
        heads_ref,
        mixed2_ref,
        hidden2_ref,
        normed3_ref,
    ):
        step = pl.program_id(0)
        keep_rows = keep_ref[...]

        @pl.when(step == 0)
        def _():
            branch = mm(mixed1_ref[0], merge1_ref[0])
            for n in range(1, 4):
                branch += mm(mixed1_ref[n], merge1_ref[n])
            begin = tokens_ref[...].astype(F32) + extra_ref[...]
            hidden1 = begin.reshape(rows, width) + keep_rows * branch
            hidden1_ref[...] = hidden1
            hidden2_ref[...] = hidden1
            normed2_ref[...] = (hidden1 * root(hidden1) * gains_ref[1:2]).astype(BF16)

        for c in range(3):
            head = mm(normed2_ref[...], project_ref[0, c]).astype(BF16)
            heads_ref[0, c] = head.reshape(FRAMES, span, local)
        allowed = place_masks(lax.axis_index("wide") % 2, FRAMES, False)
        for g in range(span // GROUP):
            band = pl.ds(g * GROUP, GROUP)
            for at in range(0, local, PAIR):
                part = pl.ds(at, PAIR)
                terms = [heads_ref[0, c, :, band, part].reshape(group_rows, PAIR) for c in range(3)]
                mixed = attend_pair(*terms, allowed)
                mixed2_ref[0, :, band, part] = mixed.reshape(FRAMES, GROUP, PAIR)
        hidden2_ref[...] += keep_rows * mm(mixed2_ref[0].reshape(rows, local), merge2_ref[0])

        @pl.when(step == 3)
        def _():
            hidden2 = hidden2_ref[...]
            normed3_ref[...] = (hidden2 * root(hidden2) * gains_ref[2:3]).astype(BF16)

    return call(
        kernel,
        (4,),
        [
            whole((FRAMES, span, width)),
            whole((FRAMES, 1, width)),
            whole((rows, 1)),
            whole((3, width)),
            whole((4, rows, local)),
            whole((4, local, width)),
            pl.BlockSpec((1, 3, width, local), lambda n: (n, 0, 0, 0)),
            pl.BlockSpec((1, local, width), lambda n: (n, 0, 0)),
        ],
        [
            whole((rows, width)),
            whole((rows, width)),
            pl.BlockSpec((1, 3, FRAMES, span, local), lambda n: (n, 0, 0, 0, 0)),
            pl.BlockSpec((1, FRAMES, span, local), lambda n: (n, 0, 0, 0)),
            whole((rows, width)),
            whole((rows, width)),
        ],
        [
            shape_of((rows, width), F32),
            shape_of((rows, width)),
            shape_of((4, 3, FRAMES, span, local)),
            shape_of((4, FRAMES, span, local)),
            shape_of((rows, width), F32),
            shape_of((rows, width)),
        ],
        flops=2 * rows * width * width * 6,
        moved=24 * 2**20,
    )(tokens, extra, keep, gains, mixed1, merge1, project, merge2)


RATE = 0.7978845608028654
CUBIC = 0.044715


def feed_forward(normed, grad, keep, expand, reduce):
    rows, width = normed.shape
    cores, _, units = expand.shape
    block = 512
    per = units // block

    def kernel(
        normed_ref,
        grad_ref,
        keep_ref,
        expand_ref,
        reduce_ref,
        active_ref,
        inner_ref,
        grad_branch_ref,
        branch_ref,
        grad_normed_ref,
        branch_sum,
        grad_sum,
    ):
        step = pl.program_id(0)

        @pl.when(step == 0)
        def _():
            grad_branch_ref[...] = (keep_ref[...] * grad_ref[...].astype(F32)).astype(BF16)
            branch_sum[...] = jnp.zeros_like(branch_sum)
            grad_sum[...] = jnp.zeros_like(grad_sum)

        inner = mm(normed_ref[...], expand_ref[0])
        grad_active = mm(grad_branch_ref[...], reduce_ref[0], NT)
        square = inner * inner
        bend = jnp.tanh(RATE * inner * (1.0 + CUBIC * square))
        half = 0.5 * (1.0 + bend)
        active = (inner * half).astype(BF16)
        slope = half + (0.5 * RATE) * inner * (1.0 - bend * bend) * (1.0 + (3.0 * CUBIC) * square)
        grad_inner = (grad_active * slope).astype(BF16)
        active_ref[...] = active
        inner_ref[...] = grad_inner
        branch_sum[...] += mm(active, reduce_ref[0])
        grad_sum[...] += mm(grad_inner, expand_ref[0], NT)

        @pl.when(step == cores * per - 1)
        def _():
            branch_ref[...] = branch_sum[...].astype(BF16)
            grad_normed_ref[...] = grad_sum[...].astype(BF16)

    full = whole((rows, width))
    return call(
        kernel,
        (cores * per,),
        [
            full,
            full,
            whole((rows, 1)),
            pl.BlockSpec((1, width, block), lambda j: (j // per, 0, j % per)),
            pl.BlockSpec((1, block, width), lambda j: (j // per, j % per, 0)),
        ],
        [
            pl.BlockSpec((rows, block), lambda j: (0, j)),
            pl.BlockSpec((rows, block), lambda j: (0, j)),
            full,
            full,
            full,
        ],
        [
            shape_of((rows, cores * units)),
            shape_of((rows, cores * units)),
            shape_of((rows, width)),
            shape_of((rows, width)),
            shape_of((rows, width)),
        ],
        scratch=[pltpu.VMEM((rows, width), F32), pltpu.VMEM((rows, width), F32)],
        flops=8 * rows * width * cores * units,
        moved=18 * 2**20,
    )(normed, grad, keep, expand, reduce)


def temporal_backward(
    grad_near, grad_far, hidden2, hidden1, grad_result, keep, gains, heads, merge2, project, merge1
):
    rows, width = hidden1.shape
    local = merge1.shape[1]
    span = rows // FRAMES
    group_rows = FRAMES * GROUP

    def kernel(
        near_ref,
        far_ref,
        hidden2_ref,
        hidden1_ref,
        result_ref,
        keep_ref,
        gains_ref,
        heads_ref,
        merge2_ref,
        project_ref,
        merge1_ref,
        branch2_ref,
        grad_heads_ref,
        branch1_ref,
        mixed1_ref,
        carried_ref,
        gain3_ref,
        gain2_ref,
        grad_hidden,
        grad_normed,
        grad_mixed,
    ):
        step = pl.program_id(0)

        @pl.when(step == 0)
        def _():
            incoming = near_ref[...].astype(F32) + far_ref[...].astype(F32)
            back, gain3_ref[...] = norm_back(hidden2_ref[...], gains_ref[2:3], incoming)
            total = result_ref[...].astype(F32) + back
            grad_hidden[...] = total
            branch2_ref[...] = (keep_ref[...] * total).astype(BF16)
            grad_normed[...] = jnp.zeros_like(grad_normed)

        back_mixed = mm(branch2_ref[...], merge2_ref[0], NT).astype(BF16)
        grad_mixed[...] = back_mixed.reshape(FRAMES, span, local)
        allowed = place_masks(lax.axis_index("wide") % 2, FRAMES, True)
        for g in range(span // GROUP):
            band = pl.ds(g * GROUP, GROUP)
            for at in range(0, local, PAIR):
                part = pl.ds(at, PAIR)
                terms = [heads_ref[0, c, :, band, part].reshape(group_rows, PAIR) for c in range(3)]
                grad = grad_mixed[:, band, part].reshape(group_rows, PAIR)
                grads = attend_back_pair(*terms, grad, allowed)
                for c in range(3):
                    grad_heads_ref[0, c, :, band, part] = grads[c].reshape(FRAMES, GROUP, PAIR)
        total = mm(grad_heads_ref[0, 0].reshape(rows, local), project_ref[0, 0], NT)
        for c in range(1, 3):
            total += mm(grad_heads_ref[0, c].reshape(rows, local), project_ref[0, c], NT)
        grad_normed[...] += total

        @pl.when(step == 3)
        def _():
            back, gain2_ref[...] = norm_back(hidden1_ref[...], gains_ref[1:2], grad_normed[...])
            total = grad_hidden[...] + back
            carried_ref[...] = total.astype(BF16)
            branch1_ref[...] = (keep_ref[...] * total).astype(BF16)
            for n in range(4):
                mixed1_ref[n] = mm(branch1_ref[...], merge1_ref[n], NT).astype(BF16)

    full = whole((rows, width))
    row = whole((1, width))
    return call(
        kernel,
        (4,),
        [
            full,
            full,
            full,
            full,
            full,
            whole((rows, 1)),
            whole((3, width)),
            pl.BlockSpec((1, 3, FRAMES, span, local), lambda n: (n, 0, 0, 0, 0)),
            pl.BlockSpec((1, local, width), lambda n: (n, 0, 0)),
            pl.BlockSpec((1, 3, width, local), lambda n: (n, 0, 0, 0)),
            whole((4, local, width)),
        ],
        [
            full,
            pl.BlockSpec((1, 3, FRAMES, span, local), lambda n: (n, 0, 0, 0, 0)),
            full,
            whole((4, rows, local)),
            full,
            row,
            row,
        ],
        [
            shape_of((rows, width)),
            shape_of((4, 3, FRAMES, span, local)),
            shape_of((rows, width)),
            shape_of((4, rows, local)),
            shape_of((rows, width)),
            shape_of((1, width), F32),
            shape_of((1, width), F32),
        ],
        scratch=[
            pltpu.VMEM((rows, width), F32),
            pltpu.VMEM((rows, width), F32),
            pltpu.VMEM((FRAMES, span, local), BF16),
        ],
        flops=2 * rows * width * width * 8,
        moved=30 * 2**20,
    )(grad_near, grad_far, hidden2, hidden1, grad_result, keep, gains, heads, merge2, project, merge1)


def here():
    wide, narrow = lax.axis_index("wide"), lax.axis_index("narrow")
    return wide, narrow, wide % 2, narrow // 2, narrow % 2


def other(wide, narrow, x, y, core):
    if x:
        wide = wide + 1 - 2 * (wide % 2)
    if y:
        narrow = (narrow + 2) % 4
    if core:
        narrow = narrow + 1 - 2 * (narrow % 2)
    return wide, narrow


def beyond(wide, narrow):
    return wide + 2 - 4 * ((wide // 2) % 2), narrow


def place_of(wide, narrow, span):
    return pl.multiple_of(((wide % 2) * 4 + narrow) * span, span)


def remote(src, dst, sems, i, device):
    return pltpu.make_async_remote_copy(
        src_ref=src,
        dst_ref=dst,
        send_sem=sems.at[0, i],
        recv_sem=sems.at[1, i],
        device_id=device,
        device_id_type=pl.DeviceIdType.MESH,
    )


def greet(devices):
    barrier = pltpu.get_barrier_semaphore()
    for device in devices:
        pl.semaphore_signal(
            barrier, inc=1, device_id=device, device_id_type=pl.DeviceIdType.MESH
        )
    pl.semaphore_wait(barrier, len(devices))


OTHERS = [(x, y, c) for x in range(2) for y in range(2) for c in range(2) if x + y + c > 0]
ANY = pl.BlockSpec(memory_space=pl.ANY)


def comm_call(kernel, number, grid, in_specs, out_specs, out_shape, scratch, flops):
    return pl.pallas_call(
        kernel,
        grid=grid,
        in_specs=in_specs,
        out_specs=out_specs,
        out_shape=out_shape,
        scratch_shapes=scratch,
        compiler_params=pltpu.CompilerParams(
            vmem_limit_bytes=VMEM_LIMIT, collective_id=number, has_side_effects=True
        ),
        cost_estimate=pl.CostEstimate(flops=flops, bytes_accessed=30 * 2**20, transcendentals=0),
    )


def spatial_forward(
    tokens, extra, gain, project, merge1, project2, merge2, expand, reduce, grad_out
):
    frames, places, width = tokens.shape
    local = project.shape[-1]
    span = places // 8
    half = frames // 2
    shards = (merge1, project2[0], project2[1], project2[2], merge2)
    count = len(shards)

    def kernel(
        tokens_ref,
        extra_ref,
        gain_ref,
        project_ref,
        all_tokens,
        all_extra,
        grad_ref,
        expand_ref,
        reduce_ref,
        merge1_ref,
        project2_ref,
        merge2_ref,
        normed_ref,
        heads_ref,
        mixed_all,
        tokens_place,
        extra_place,
        grad_near,
        grad_far,
        expand_pair,
        reduce_pair,
        merge1_all,
        project2_all,
        merge2_all,
        mixed_ref,
        local_sems,
        move_sems,
        shard_sems,
        mixed_sems,
        *stage,
    ):
        step = pl.program_id(0)
        wide, narrow, x_me, _, _ = here()
        half_me = (wide // 2) % 2
        x_other = other(wide, narrow, 1, 0, 0)
        y_other = other(wide, narrow, 0, 1, 0)
        core_other = other(wide, narrow, 0, 0, 1)
        z_other = beyond(wide, narrow)
        mine = pl.ds(place_of(wide, narrow, span), span)
        near_y = pl.ds(place_of(*y_other, span), span)
        shard = [merge1_ref] + [project2_ref.at[c] for c in range(3)] + [merge2_ref]
        full = [merge1_all] + [project2_all.at[:, c] for c in range(3)] + [merge2_all]

        own = [
            (expand_ref, expand_pair.at[0]),
            (reduce_ref, reduce_pair.at[0]),
            (all_tokens.at[:, mine], tokens_place.at[0]),
            (all_extra, extra_place.at[0]),
            (grad_ref.at[:, mine], grad_near.at[0]),
            (grad_ref.at[:, near_y], grad_far.at[0]),
        ] + [(shard[k], full[k].at[0]) for k in range(count)]
        into = [pltpu.make_async_copy(a, v, local_sems.at[0, i]) for i, ((a, _), v) in enumerate(zip(own, stage))]
        back = [pltpu.make_async_copy(v, b, local_sems.at[1, i]) for i, ((_, b), v) in enumerate(zip(own, stage))]
        far = pl.ds(place_of(*x_other, span), span)
        far_y = pl.ds(place_of(*other(wide, narrow, 1, 1, 0), span), span)
        first = [
            remote(all_tokens.at[:, far], tokens_place.at[1], move_sems, 0, x_other),
            remote(all_extra, extra_place.at[1], move_sems, 1, x_other),
            remote(expand_ref, expand_pair.at[1], move_sems, 2, core_other),
            remote(reduce_ref, reduce_pair.at[1], move_sems, 3, core_other),
        ]
        last = [
            remote(grad_ref.at[:, far], grad_near.at[1], move_sems, 4, x_other),
            remote(grad_ref.at[:, far_y], grad_far.at[1], move_sems, 5, x_other),
        ]

        def part(k, which):
            rows = shards[k].shape[0] // 2
            return pl.ds(pl.multiple_of(which * rows, rows), rows)

        def over_core(k):
            return remote(shard[k], full[k].at[1], shard_sems, 5 * k, core_other)

        def over_y(k):
            rows = part(k, half_me)
            return remote(shard[k].at[rows], full[k].at[2, rows], shard_sems, 5 * k + 1, y_other)

        def onward(k, which, i, device, slot):
            rows = part(k, which)
            return remote(full[k].at[2, rows], full[k].at[slot, rows], shard_sems, 5 * k + i, device)

        def over_z(k):
            return onward(k, half_me, 2, z_other, 2)

        def near_half(k):
            return onward(k, half_me, 3, core_other, 3)

        def far_half(k):
            return onward(k, 1 - half_me, 4, core_other, 3)

        def mixed_copies(chunk):
            copies = []
            some = pl.ds(chunk * half, half)
            for i, (x, y, c) in enumerate(OTHERS):
                device = other(wide, narrow, x, y, c)
                copies.append(
                    remote(
                        mixed_ref.at[some, pl.ds(place_of(*device, span), span)],
                        mixed_all.at[2 * y + c, x, some],
                        mixed_sems,
                        7 * chunk + i,
                        device,
                    )
                )
            here_copy = pltpu.make_async_copy(
                mixed_ref.at[some, mine], mixed_all.at[0, 0, some], local_sems.at[chunk, len(own)]
            )
            return copies, here_copy

        @pl.when(step == 0)
        def _():
            greet([other(wide, narrow, *o) for o in OTHERS] + [z_other])
            for k in range(count):
                over_y(k).start()
            for copy in first:
                copy.start()
            for k in range(count):
                over_core(k).start()
            for copy in into:
                copy.start()

        @pl.when(step == 2)
        def _():
            for copy in into:
                copy.wait()
            for copy in back:
                copy.start()

        start = tokens_ref[0].astype(F32) + extra_ref[0]
        normed = (start * root(start) * gain_ref[...]).astype(BF16)
        normed_ref[0] = normed
        for c in range(3):
            heads_ref[c, 0] = mm(normed, project_ref[c]).astype(BF16)
        for at in range(0, local, PAIR):
            lanes = pl.ds(at, PAIR)
            mixed_ref[step, :, lanes] = attend_pair(
                heads_ref[0, 0, :, lanes], heads_ref[1, 0, :, lanes], heads_ref[2, 0, :, lanes], None
            )

        def forward(k):
            over_y(k).wait_recv()
            over_z(k).start()
            near_half(k).start()

        def spread(chunk):
            copies, here_copy = mixed_copies(chunk)
            for copy in copies:
                copy.start()
            here_copy.start()
            last[chunk].start()

        @pl.when(step == half - 1)
        def _():
            spread(0)
            forward(0)

        @pl.when(step == half + 1)
        def _():
            forward(1)

        @pl.when(step == frames - 1)
        def _():
            spread(1)
            for k in range(2, count):
                forward(k)
            for k in range(count):
                over_z(k).wait_recv()
                far_half(k).start()
            for chunk in range(2):
                copies, here_copy = mixed_copies(chunk)
                for copy in copies:
                    copy.wait()
                here_copy.wait()
            for copy in first + last:
                copy.wait()
            for copy in back:
                copy.wait()
            for k in range(count):
                over_core(k).wait()
                over_y(k).wait_send()
                over_z(k).wait_send()
                near_half(k).wait()
                far_half(k).wait()

    out = comm_call(
        kernel,
        0,
        (frames,),
        [
            pl.BlockSpec((1, places, width), lambda f: (f, 0, 0)),
            pl.BlockSpec((1, 1, width), lambda f: (f, 0, 0)),
            whole((1, width)),
            whole(project.shape),
        ]
        + [ANY] * 8,
        [
            pl.BlockSpec((1, places, width), lambda f: (f, 0, 0)),
            pl.BlockSpec((3, 1, places, local), lambda f: (0, f, 0, 0)),
        ]
        + [ANY] * 10,
        [
            shape_of((frames, places, width)),
            shape_of((3, frames, places, local)),
            shape_of((4, 2, frames, span, local)),
            shape_of((2, frames, span, width)),
            shape_of((2, frames, 1, width), F32),
            shape_of((2, frames, span, width)),
            shape_of((2, frames, span, width)),
            shape_of((2,) + expand.shape),
            shape_of((2,) + reduce.shape),
            shape_of((4,) + merge1.shape),
            shape_of((4,) + project2.shape),
            shape_of((4,) + merge2.shape),
        ],
        [
            pltpu.VMEM((frames, places, local), BF16),
            pltpu.SemaphoreType.DMA((2, 7 + count)),
            pltpu.SemaphoreType.DMA((2, 6)),
            pltpu.SemaphoreType.DMA((2, 5 * count)),
            pltpu.SemaphoreType.DMA((2, 14)),
            pltpu.VMEM(expand.shape, BF16),
            pltpu.VMEM(reduce.shape, BF16),
            pltpu.VMEM((frames, span, width), BF16),
            pltpu.VMEM((frames, 1, width), F32),
            pltpu.VMEM((frames, span, width), BF16),
            pltpu.VMEM((frames, span, width), BF16),
        ]
        + [pltpu.VMEM(shard.shape, BF16) for shard in shards],
        2 * frames * places * width * local * 4,
    )(
        tokens,
        extra[:, None, :],
        gain,
        project,
        tokens,
        extra[:, None, :],
        grad_out,
        expand,
        reduce,
        merge1,
        project2,
        merge2,
    )
    return out


def feed_outer(normed, grad_inner, grad_branch, active):
    rows, width = normed[0].shape
    units = active[0].shape[1] // 2
    block = 512
    per = units // block
    wide = lax.axis_size("wide")
    split = (2, wide // 2, 2, width // wide, block)

    def kernel(
        normed0,
        normed1,
        branch0,
        branch1,
        inner0,
        inner1,
        active0,
        active1,
        keep_ref,
        send_ref,
        left,
        right,
        total,
        given,
        taken,
        sems,
    ):
        step = pl.program_id(0)
        wide, narrow, x_me, _, _ = here()
        core_other = other(wide, narrow, 0, 0, 1)

        def over(j):
            return remote(given.at[j], taken.at[j], sems, j, core_other)

        @pl.when(step == 0)
        def _():
            left[:, :rows] = normed0[...].T
            left[:, rows:] = normed1[...].T
            right[:, :rows] = branch0[...].T
            right[:, rows:] = branch1[...].T

        expand = mm(left[:, :rows], inner0[...]) + mm(left[:, rows:], inner1[...])
        reduce = mm(right[:, :rows], active0[...]) + mm(right[:, rows:], active1[...])

        @pl.when(step == 0)
        def _():
            greet([core_other])

        @pl.when(step < per)
        def _():
            given[step, 0] = expand.astype(BF16)
            given[step, 1] = reduce.astype(BF16)
            over(step).start()

        @pl.when(step >= per)
        def _():
            j = step - per
            over(j).wait_recv()
            half = split[1:]
            total[0] = (expand + taken[j, 0].astype(F32)).astype(BF16).reshape(half)
            total[1] = (reduce + taken[j, 1].astype(F32)).astype(BF16).reshape(half)
            out = keep_ref.shape
            keep_ref[...] = total[:, :, pl.ds(x_me, 1)].reshape(out)
            send_ref[...] = total[:, :, pl.ds(1 - x_me, 1)].reshape(out)

        @pl.when(step == 2 * per - 1)
        def _():
            for j in range(per):
                over(j).wait_send()

    full = whole((rows, width))
    part = pl.BlockSpec((rows, block), lambda j: (0, (j + per) % (2 * per)))
    out = pl.BlockSpec((2, width // 2, block), lambda j: (0, 0, jnp.maximum(j - per, 0)))
    return comm_call(
        kernel,
        3,
        (2 * per,),
        [full] * 4 + [part] * 4,
        [out, out],
        [shape_of((2, width // 2, units))] * 2,
        [
            pltpu.VMEM((width, 2 * rows), BF16),
            pltpu.VMEM((width, 2 * rows), BF16),
            pltpu.VMEM(split, BF16),
            pltpu.VMEM((per, 2, width, block), BF16),
            pltpu.VMEM((per, 2, width, block), BF16),
            pltpu.SemaphoreType.DMA((2, per)),
        ],
        16 * rows * width * units,
    )(*normed, *grad_branch, *grad_inner, *active)


def temporal_outer(
    grad_mixed1, carried, result, mixed1, branch1, mixed2, branch2, normed2, grad_heads
):
    rows, width = branch1.shape
    local = mixed1.shape[-1]
    span = rows // FRAMES
    frames = FRAMES // 2

    def kernel(
        grad_ref,
        carried_ref,
        result_ref,
        mixed1_ref,
        branch1_ref,
        mixed2_ref,
        branch2_ref,
        normed2_ref,
        heads_ref,
        out_ref,
        grad_own,
        carried_own,
        result_far,
        left,
        given,
        taken,
        grad_stage,
        carried_stage,
        local_sems,
        sems,
    ):
        step = pl.program_id(0)
        wide, narrow, x_me, _, _ = here()
        x_other = other(wide, narrow, 1, 0, 0)
        mine = pl.ds(place_of(wide, narrow, span), span)
        copies = [
            remote(
                grad_ref.at[2 * y + c, x],
                grad_own.at[:, mine],
                sems,
                i,
                other(wide, narrow, x, y, c),
            )
            for i, (x, y, c) in enumerate(OTHERS)
        ]
        copies.append(remote(carried_ref.at[1], carried_own.at[:, x_me], sems, 7, x_other))
        copies.append(remote(result_ref, result_far, sems, 8, other(wide, narrow, 0, 1, 0)))

        def over(y):
            return remote(given.at[y], taken.at[y], sems, 9 + y, other(wide, narrow, 0, 0, 1))

        into = [
            pltpu.make_async_copy(grad_ref.at[0, 0], grad_stage, local_sems.at[0]),
            pltpu.make_async_copy(carried_ref.at[0], carried_stage, local_sems.at[1]),
        ]
        back = [
            pltpu.make_async_copy(grad_stage, grad_own.at[:, mine], local_sems.at[2]),
            pltpu.make_async_copy(carried_stage, carried_own.at[:, x_me], local_sems.at[3]),
        ]

        @pl.when(step == 0)
        def _():
            greet([other(wide, narrow, *o) for o in OTHERS])
            for copy in copies + into:
                copy.start()
            left[0] = branch1_ref[...].T
            left[1] = branch2_ref[...].T
            left[2] = normed2_ref[...].T

        terms = [(0, mixed1_ref[0]), (1, mixed2_ref[0])] + [(2, heads_ref[0, c]) for c in range(3)]
        for k, (which, term) in enumerate(terms):
            total = mm(left[which], term)

            @pl.when(step < 2)
            def _():
                given[step, k] = total.astype(BF16)

            @pl.when(step >= 2)
            def _():
                out_ref[0, k] = total.astype(BF16)

        @pl.when(step < 2)
        def _():
            over(step).start()

        @pl.when(step >= 2)
        def _():
            over(step - 2).wait_recv()
            out_ref[0] = (out_ref[0].astype(F32) + taken[step - 2].astype(F32)).astype(BF16)

        @pl.when(step == 1)
        def _():
            for copy in into:
                copy.wait()
            for copy in back:
                copy.start()

        @pl.when(step == 3)
        def _():
            for copy in copies + back:
                copy.wait()
            for y in range(2):
                over(y).wait_send()

    full = whole((rows, width))

    def turn(j):
        return 2 * (j % 2) + 1 - j // 2

    part = pl.BlockSpec((1, rows, local), lambda j: (turn(j), 0, 0))
    return comm_call(
        kernel,
        1,
        (4,),
        [ANY] * 3
        + [part, full, part, full, full]
        + [pl.BlockSpec((1, 3, rows, local), lambda j: (turn(j), 0, 0, 0))],
        [pl.BlockSpec((1, 5, width, local), lambda j: (jnp.maximum(j - 2, 0), 0, 0, 0))] + [ANY] * 3,
        [
            shape_of((2, 5, width, local)),
            shape_of((frames, 8 * span, local)),
            shape_of((frames, 2, span, width)),
            shape_of(result.shape),
        ],
        [
            pltpu.VMEM((3, width, rows), BF16),
            pltpu.VMEM((2, 5, width, local), BF16),
            pltpu.VMEM((2, 5, width, local), BF16),
            pltpu.VMEM((frames, span, local), BF16),
            pltpu.VMEM((frames, span, width), BF16),
            pltpu.SemaphoreType.DMA((4,)),
            pltpu.SemaphoreType.DMA((2, 11)),
        ],
        10 * rows * width * width,
    )(
        grad_mixed1.reshape(4, 2, frames, span, local),
        carried.reshape(2, frames, span, width),
        result,
        mixed1,
        branch1,
        mixed2.reshape(4, rows, local),
        branch2,
        normed2,
        grad_heads.reshape(4, 3, rows, local),
    )


class Halving:
    def __init__(self, slots, rows, columns, blocks, first):
        self.slots, self.rows, self.columns, self.first = slots, rows, columns, first
        self.blocks = []
        while blocks > 1:
            blocks //= 2
            self.blocks.append(blocks)

    def scratch(self):
        out = []
        for blocks in self.blocks:
            out.append(pltpu.VMEM((self.slots, blocks, 2, self.rows, self.columns), BF16))
            out.append(pltpu.VMEM((self.slots, blocks, self.rows, self.columns), BF16))
        return out

    def bind(self, refs, sems, base, wide, narrow):
        self.held, self.taken = refs[0::2], refs[1::2]
        self.sems, self.base, self.wide, self.narrow = sems, base, wide, narrow

    def bit(self, level):
        step = 2 ** (self.first + level)
        return step, (self.wide // step) % 2

    def copy(self, level):
        step, bit = self.bit(level)
        device = (self.wide + step - 2 * step * bit, self.narrow)
        return remote(
            self.held[level].at[:, :, 1 - bit],
            self.taken[level],
            self.sems,
            self.base + level,
            device,
        )

    def fill(self, level, value, slot=0):
        count = value.shape[0]
        self.held[level][slot : slot + count] = value.astype(BF16).reshape(
            (count,) + self.held[level].shape[1:]
        )

    def result(self, level):
        _, bit = self.bit(level)
        shape = self.taken[level].shape
        own = self.held[level][:, :, pl.ds(bit, 1)].reshape(shape)
        return own.astype(F32) + self.taken[level][...].astype(F32)

    def advance(self, level):
        self.copy(level).wait_recv()
        total = self.result(level)
        if level + 1 < len(self.blocks):
            self.fill(level + 1, total)
            self.copy(level + 1).start()
            return None
        return total.reshape(self.slots, self.rows, self.columns)

    def close(self):
        for level in range(len(self.blocks)):
            self.copy(level).wait_send()


FIRST = 2


def spatial_backward(
    heads,
    grad_mixed,
    project,
    normed,
    tokens,
    extra,
    gain,
    carried,
    choose,
    gains_grad,
    result_near,
    result_far,
    temporal_grad,
    feed_keep,
    feed_taken,
):
    _, frames, places, local = heads.shape
    width = project.shape[1]
    span = places // 8
    tile = width // 4
    wide_size = lax.axis_size("wide")
    half = wide_size // 2
    block = width // wide_size
    bits = wide_size.bit_length() - 1
    slots = temporal_grad.shape[1]
    units = feed_keep.shape[-1]
    last = slots - FIRST
    feed = Halving(2, block, units, half, 1)
    own = Halving(3, block, local, wide_size, 0)
    timed = Halving(slots, block, local, half, 1)
    engines = (feed, own, timed)
    levels = [len(engine.blocks) for engine in engines]
    attend_end = frames
    outer_end = attend_end + 4
    sum_end = outer_end + frames

    def kernel(
        heads_ref,
        mixed_ref,
        project_ref,
        normed_ref,
        tokens_ref,
        extra_ref,
        gain_ref,
        carried_ref,
        choose_ref,
        gains_ref,
        feed_keep_ref,
        feed_taken_ref,
        near_ref,
        far_ref,
        temporal_ref,
        own_out,
        timed_out,
        feed_out,
        small_out,
        output_ref,
        out_ref,
        grad_heads,
        partial,
        from_core,
        halved,
        from_y,
        done,
        gain_grad,
        table,
        small,
        small_taken,
        first_own,
        first_taken,
        first_sum,
        first_y,
        last_own,
        last_taken,
        last_sum,
        last_x,
        result_stage,
        local_sems,
        sems,
        move_sems,
        small_sems,
        halving_sems,
        *held,
    ):
        step = pl.program_id(0)
        wide, narrow, x_me, y_me, c_me = here()
        x_other = other(wide, narrow, 1, 0, 0)
        y_other = other(wide, narrow, 0, 1, 0)
        core_other = other(wide, narrow, 0, 0, 1)
        beyond_x = [
            (wide + 2**k - 2 ** (k + 1) * ((wide // 2**k) % 2), narrow) for k in range(1, bits)
        ]
        partners = [core_other, x_other] + beyond_x + [y_other]
        at = base = 0
        for engine, count in zip(engines, levels):
            engine.bind(held[at : at + 2 * count], halving_sems, base, wide, narrow)
            at, base = at + 2 * count, base + count

        def core_sum(f):
            return remote(partial.at[f, :, :, 1 - c_me], from_core.at[f], sems, f, core_other)

        def y_sum(f):
            return remote(halved.at[f, :, 1 - y_me], from_y.at[f], sems, frames + f, y_other)

        def y_back(f):
            return remote(done.at[f], out_ref.at[f, :, y_me, c_me], sems, 2 * frames + f, y_other)

        def core_back(f):
            return remote(done.at[f], out_ref.at[f, :, y_me, c_me], sems, 3 * frames + f, core_other)

        def core_onward(f):
            there = out_ref.at[f, :, 1 - y_me, c_me]
            return remote(there, there, sems, 4 * frames + f, core_other)

        def keep_own(f):
            return pltpu.make_async_copy(done.at[f], out_ref.at[f, :, y_me, c_me], local_sems.at[f])

        result = (near_ref, far_ref)

        def place(y):
            return y_me if y == 0 else 1 - y_me

        def result_x(y):
            there = output_ref.at[:, x_me, place(y), c_me]
            return remote(result[y].at[1], there, move_sems, y, x_other)

        def result_core(y):
            there = output_ref.at[:, x_me, place(y), c_me]
            return remote(result[y].at[0], there, move_sems, 2 + y, core_other)

        def result_onward(y):
            there = output_ref.at[:, 1 - x_me, place(y), c_me]
            return remote(there, there, move_sems, 4 + y, core_other)

        def result_in(y):
            return pltpu.make_async_copy(
                result[y].at[0], result_stage.at[y], local_sems.at[frames + y]
            )

        def result_own(y):
            there = output_ref.at[:, x_me, place(y), c_me]
            return pltpu.make_async_copy(result_stage.at[y], there, local_sems.at[frames + 2 + y])

        early, late_slots = pl.ds(0, FIRST), pl.ds(FIRST, last)
        first_in = pltpu.make_async_copy(
            temporal_ref.at[:, early, :, x_me], first_own, local_sems.at[frames + 4]
        )
        last_in = pltpu.make_async_copy(
            temporal_ref.at[0, late_slots], last_own, local_sems.at[frames + 5]
        )
        first_over_x = remote(
            temporal_ref.at[:, early, :, 1 - x_me], first_taken, move_sems, 6, x_other
        )
        first_over_y = remote(first_sum.at[1], first_y, move_sems, 7, y_other)
        last_over_y = remote(temporal_ref.at[1, late_slots], last_taken, move_sems, 8, y_other)
        last_over_x = remote(last_sum.at[:, :, 1 - x_me], last_x, move_sems, 9, x_other)

        def small_copy(k):
            return remote(small.at[k], small_taken.at[k], small_sems, k, partners[k])

        @pl.when(step == 0)
        def _():
            greet(partners)
            last_over_y.start()
            first_over_x.start()
            feed.fill(0, feed_keep_ref[...].astype(F32) + feed_taken_ref[...].astype(F32))
            feed.copy(0).start()
            result_x(0).start()
            first_in.start()
            last_in.start()
            for y in range(2):
                result_core(y).start()
                result_in(y).start()
            gain_grad[...] = jnp.zeros_like(gain_grad)
            table[...] = jnp.zeros_like(table)

        @pl.when(step < attend_end)
        def _():
            rows = pl.ds(pl.multiple_of(step * places, places), places)
            for at in range(0, local, PAIR):
                lanes = pl.ds(at, PAIR)
                grads = attend_back_pair(
                    heads_ref[0, 0, :, lanes],
                    heads_ref[1, 0, :, lanes],
                    heads_ref[2, 0, :, lanes],
                    mixed_ref[0, :, lanes],
                    None,
                )
                for c in range(3):
                    grad_heads[c, rows, lanes] = grads[c]
            total = mm(grad_heads[0, rows], project_ref[0], NT)
            for c in range(1, 3):
                total += mm(grad_heads[c, rows], project_ref[c], NT)
            partial[step] = total.astype(BF16).reshape(2, 2, 2, span, width)
            core_sum(step).start()

        @pl.when((step >= 1) & (step < attend_end + 1))
        def _():
            f = step - 1
            core_sum(f).wait_recv()
            mine = partial[f, :, :, pl.ds(c_me, 1)].reshape(2, 2, span, width)
            halved[f] = (mine.astype(F32) + from_core[f].astype(F32)).astype(BF16)

        @pl.when(step == 1)
        def _():
            for y in range(2):
                result_in(y).wait()
                result_own(y).start()

        @pl.when(step == attend_end)
        def _():
            first_in.wait()
            first_over_x.wait_recv()
            first_sum[...] = (first_own[...].astype(F32) + first_taken[...].astype(F32)).astype(BF16)
            first_over_y.start()
            for f in range(frames):
                y_sum(f).start()
            feed.advance(0)

        @pl.when((step >= attend_end) & (step < outer_end))
        def _():
            pairs = tile // (2 * block)
            j = (step - attend_end) * pairs
            for c in range(3):
                grad = mm(normed_ref[...], grad_heads[c], TN).astype(BF16)
                own.held[0][c, pl.ds(j, pairs)] = grad.reshape(pairs, 2, block, local)

        @pl.when(step == attend_end + 2)
        def _():
            last_in.wait()
            last_over_y.wait_recv()
            last_sum[...] = (last_own[...].astype(F32) + last_taken[...].astype(F32)).astype(BF16)
            last_over_x.start()

        @pl.when(step == outer_end)
        def _():
            own.copy(0).start()
            result_x(1).start()
            total = feed.advance(1)
            if total is not None:
                feed_out[...] = total

        @pl.when(step >= outer_end)
        def _():
            f = step - outer_end
            y_sum(f).wait_recv()
            mine = halved[f, :, pl.ds(y_me, 1)].reshape(2 * span, width)
            incoming = mine.astype(F32) + from_y[f].reshape(2 * span, width).astype(F32)
            start = pl.multiple_of(narrow * span, span)
            begin = jnp.concatenate(
                [tokens_ref[0, pl.ds(start, span)], tokens_ref[0, pl.ds(4 * span + start, span)]]
            )
            begin = begin.astype(F32) + extra_ref[0]
            back, gain_part = norm_back(begin, gain_ref[...], incoming)
            gain_grad[...] += gain_part
            grad = carried_ref[0].reshape(2 * span, width).astype(F32) + back
            table[...] += choose_ref[0] * jnp.sum(grad, axis=0, keepdims=True)
            done[f] = grad.astype(BF16).reshape(2, span, width)
            y_back(f).start()
            core_back(f).start()
            keep_own(f).start()

        @pl.when(step == outer_end + 1)
        def _():
            first_over_y.wait_recv()
            timed.fill(0, first_sum[0].astype(F32) + first_y[...].astype(F32))
            last_over_x.wait_recv()
            mine = last_sum[:, :, pl.ds(x_me, 1)].reshape(last_x.shape)
            timed.fill(0, mine.astype(F32) + last_x[...].astype(F32), FIRST)
            timed.copy(0).start()

        @pl.when(step == sum_end - 2)
        def _():
            timed.advance(0)

        @pl.when(step == sum_end - 1)
        def _():
            small[0, 0:1] = gain_grad[...]
            small[0, 1:3] = gains_ref[...]
            small[0, 3:11] = table[...]
            small[0, 11:] = jnp.zeros_like(small[0, 11:])
            small_copy(0).start()

            def small_sum(k):
                small_copy(k).wait_recv()
                small[k + 1] = small[k] + small_taken[k]
                if k + 1 < len(partners):
                    small_copy(k + 1).start()

            def back(f):
                y_back(f).wait_recv()
                core_onward(f).start()

            def result_back(y):
                result_x(y).wait_recv()
                result_onward(y).start()

            def finish(engine, out, level):
                if level < len(engine.blocks):
                    total = engine.advance(level)
                    if total is not None:
                        out[...] = total

            own.advance(0)
            small_sum(0)
            result_back(0)
            back(0)
            back(1)
            finish(own, own_out, 1)
            finish(timed, timed_out, 1)
            back(2)
            result_back(1)
            small_sum(1)
            back(3)
            for level in range(2, max(levels)):
                finish(feed, feed_out, level)
                finish(timed, timed_out, level)
                finish(own, own_out, level)
            for k in range(2, len(partners)):
                small_sum(k)
            small_out[...] = small[len(partners)]
            for f in range(4, frames):
                back(f)
            for engine in engines:
                engine.close()
            for k in range(len(partners)):
                small_copy(k).wait_send()
            for f in range(frames):
                core_sum(f).wait_send()
                y_sum(f).wait_send()
                y_back(f).wait_send()
                core_back(f).wait()
                core_onward(f).wait()
                keep_own(f).wait()
            for y in range(2):
                result_x(y).wait_send()
                result_core(y).wait()
                result_onward(y).wait()
                result_own(y).wait()
            for copy in (first_over_x, first_over_y, last_over_y, last_over_x):
                copy.wait_send()

    def frame(step):
        return jnp.minimum(step, frames - 1)

    def late(step):
        return jnp.clip(step - outer_end, 0, frames - 1)

    def piece(step):
        return jnp.clip(step - attend_end, 0, 3)

    block_shape = (half, 2, block, local)
    small_rows = 16
    scratch = [
        pltpu.VMEM((3, frames * places, local), BF16),
        pltpu.VMEM((frames, 2, 2, 2, span, width), BF16),
        pltpu.VMEM((frames, 2, 2, span, width), BF16),
        pltpu.VMEM((frames, 2, 2, span, width), BF16),
        pltpu.VMEM((frames, 2, span, width), BF16),
        pltpu.VMEM((frames, 2, span, width), BF16),
        pltpu.VMEM((1, width), F32),
        pltpu.VMEM((choose.shape[1], width), F32),
        pltpu.VMEM((bits + 3, small_rows, width), F32),
        pltpu.VMEM((bits + 2, small_rows, width), F32),
        pltpu.VMEM((2, FIRST, half, block, local), BF16),
        pltpu.VMEM((2, FIRST, half, block, local), BF16),
        pltpu.VMEM((2, FIRST, half, block, local), BF16),
        pltpu.VMEM((FIRST, half, block, local), BF16),
        pltpu.VMEM((last,) + block_shape, BF16),
        pltpu.VMEM((last,) + block_shape, BF16),
        pltpu.VMEM((last,) + block_shape, BF16),
        pltpu.VMEM((last, half, block, local), BF16),
        pltpu.VMEM((2, frames, span, width), BF16),
        pltpu.SemaphoreType.DMA((frames + 6,)),
        pltpu.SemaphoreType.DMA((2, 5 * frames)),
        pltpu.SemaphoreType.DMA((2, 10)),
        pltpu.SemaphoreType.DMA((2, bits + 2)),
        pltpu.SemaphoreType.DMA((2, sum(levels))),
    ]
    for engine in engines:
        scratch += engine.scratch()
    return comm_call(
        kernel,
        2,
        (sum_end,),
        [
            pl.BlockSpec((3, 1, places, local), lambda s: (0, frame(s), 0, 0)),
            pl.BlockSpec((1, places, local), lambda s: (frame(s), 0, 0)),
            whole(project.shape),
            pl.BlockSpec((frames * places, tile), lambda s: (0, piece(s))),
            pl.BlockSpec((1, places, width), lambda s: (late(s), 0, 0)),
            pl.BlockSpec((1, 1, width), lambda s: (late(s), 0, 0)),
            whole((1, width)),
            pl.BlockSpec((1, 2, span, width), lambda s: (late(s), 0, 0, 0)),
            pl.BlockSpec((1, choose.shape[1], 1), lambda s: (late(s), 0, 0)),
            whole((2, width)),
            whole(feed_keep.shape),
            whole(feed_taken.shape),
            ANY,
            ANY,
            ANY,
        ],
        [
            whole((3, block, local)),
            whole((slots, block, local)),
            whole((2, block, units)),
            whole((small_rows, width)),
            ANY,
            ANY,
        ],
        [
            shape_of((3, block, local), F32),
            shape_of((slots, block, local), F32),
            shape_of((2, block, units), F32),
            shape_of((small_rows, width), F32),
            shape_of((frames, 2, 2, 2, span, width)),
            shape_of((frames, 2, 2, 2, span, width)),
        ],
        scratch,
        2 * frames * places * width * local * 8,
    )(
        heads,
        grad_mixed,
        project,
        normed.reshape(frames * places, width),
        tokens,
        extra[:, None, :],
        gain,
        carried,
        choose,
        gains_grad,
        feed_keep,
        feed_taken,
        result_near,
        result_far,
        temporal_grad.reshape((2, slots) + block_shape),
    )


def swap(value, axis, bit):
    size = lax.axis_size(axis)
    return lax.ppermute(value, axis, [(i, i ^ bit) for i in range(size)])


def after(value, *earlier):
    return lax.optimization_barrier((value,) + earlier)[0]


def body(
    tokens,
    frame_counts,
    actions,
    action_table,
    norm_gains,
    spatial_project,
    spatial_merge,
    temporal_project,
    temporal_merge,
    expand_weight,
    reduce_weight,
    grad_out,
):
    frames_dev, tokens_frame, width = tokens.shape
    wide_me, narrow_me = lax.axis_index("wide"), lax.axis_index("narrow")
    x_me = wide_me % 2
    span = tokens_frame // 8
    rows = 2 * frames_dev * span
    spatial_project = spatial_project.transpose(1, 0, 2)
    temporal_project = temporal_project.transpose(1, 0, 2)

    def keep_of(wide_place):
        frame_ids = wide_place * frames_dev + jnp.arange(frames_dev, dtype=jnp.int32)
        clip_places = jnp.arange(frame_counts.shape[0], dtype=jnp.int32)
        clip_count = jnp.sum(
            jnp.where((frame_ids // FRAMES)[:, None] == clip_places[None, :], frame_counts[None, :], 0),
            axis=1,
        )
        return (frame_ids % FRAMES < clip_count).astype(F32)

    keep_place = jnp.concatenate([keep_of(wide_me), keep_of(wide_me + 1 - 2 * x_me)])
    keep_place = jnp.broadcast_to(keep_place[:, None], (2 * frames_dev, span)).reshape(rows, 1)
    choose = (
        actions[:, None] == jnp.arange(action_table.shape[0], dtype=jnp.int32)[None, :]
    ).astype(BF16)
    extra = jnp.dot(choose, action_table, preferred_element_type=F32)

    (
        normed1,
        heads1,
        mixed1,
        tokens_place,
        extra_place,
        grad_result,
        grad_result_far,
        expand_pair,
        reduce_pair,
        merge1_all,
        project_all,
        merge2_all,
    ) = spatial_forward(
        tokens,
        extra,
        norm_gains[0:1],
        spatial_project,
        spatial_merge,
        temporal_project,
        temporal_merge,
        expand_weight,
        reduce_weight,
        grad_out,
    )
    mixed1 = mixed1.reshape(4, rows, mixed1.shape[-1])
    hidden1, normed2, heads2, mixed2, hidden2, normed3 = temporal_forward(
        tokens_place.reshape(2 * frames_dev, span, width),
        extra_place.reshape(2 * frames_dev, 1, width),
        keep_place,
        norm_gains,
        mixed1,
        merge1_all,
        project_all,
        merge2_all,
    )

    grad_result = grad_result.reshape(rows, width)
    grad_result_far = grad_result_far.reshape(rows, width)
    normed3_far = swap(normed3, "narrow", 2)
    near = feed_forward(normed3, grad_result, keep_place, expand_pair, reduce_pair)
    far = feed_forward(
        after(normed3_far, near[0]), grad_result_far, keep_place, expand_pair, reduce_pair
    )
    grad_normed3_far = swap(far[4], "narrow", 2)
    feed_keep, feed_send = feed_outer(
        (normed3, normed3_far), (near[1], far[1]), (near[2], far[2]), (near[0], far[0])
    )

    branch2_grad, grad_heads2, branch1_grad, grad_mixed1, carried, gain_three, gain_two = temporal_backward(
        near[4],
        after(grad_normed3_far, feed_keep),
        hidden2,
        hidden1,
        grad_result,
        keep_place,
        norm_gains,
        heads2,
        merge2_all,
        project_all,
        merge1_all,
    )
    branch3_far = swap(after(far[3], grad_normed3_far), "narrow", 2)
    feed_taken = swap(after(feed_send, grad_normed3_far), "wide", 1)
    branch3 = near[3].astype(F32) + branch3_far.astype(F32)
    result = (hidden2 + keep_place * branch3).astype(BF16).reshape(2, frames_dev, span, width)
    temporal_grad, grad_mixed1, carried, result_far = temporal_outer(
        grad_mixed1, carried, result, mixed1, branch1_grad, mixed2, branch2_grad, normed2, grad_heads2
    )

    project1_grad, temporal_grad, feed_grad, small, output, grad_tokens = spatial_backward(
        heads1,
        grad_mixed1,
        spatial_project,
        normed1,
        tokens,
        extra,
        norm_gains[0:1],
        carried,
        choose.astype(F32)[:, :, None],
        jnp.concatenate([gain_two, gain_three]),
        result,
        result_far,
        temporal_grad,
        feed_keep,
        feed_taken,
    )
    block = width // lax.axis_size("wide")
    small = lax.dynamic_slice_in_dim(small, wide_me * block, block, axis=1)
    return (
        output.reshape(tokens.shape),
        grad_tokens.reshape(tokens.shape).astype(F32),
        small[:3],
        small[3 : 3 + action_table.shape[0]],
        project1_grad.transpose(1, 0, 2),
        temporal_grad[0].T,
        temporal_grad[2:].transpose(1, 0, 2),
        temporal_grad[1].T,
        feed_grad[0],
        feed_grad[1].T,
    )


def solution(mesh):
    return jax.shard_map(
        body,
        mesh=mesh,
        in_specs=(
            P("wide", None, None),
            P(),
            P("wide"),
            P(),
            P(),
            P(None, None, "narrow"),
            P("narrow", None),
            P(None, None, "narrow"),
            P("narrow", None),
            P(None, "narrow"),
            P("narrow", None),
            P("wide", None, None),
        ),
        out_specs=(
            P("wide", None, None),
            P("wide", None, None),
            P(None, "wide"),
            P(None, "wide"),
            P("wide", None, "narrow"),
            P("narrow", "wide"),
            P("wide", None, "narrow"),
            P("narrow", "wide"),
            P("wide", "narrow"),
            P("narrow", "wide"),
        ),
        check_vma=False,
    )
```

```python
import jax
import jax.numpy as jnp
from jax import lax
from jax.experimental import pallas as pl
from jax.experimental.pallas import tpu as pltpu
from jax.sharding import PartitionSpec as P

HD = 64
FRAMES = 16
GROUP = 16
PAIR = 2 * HD

EPSILON = 1e-06
NEGATIVE = -1e30
F32 = jnp.float32
BF16 = jnp.bfloat16
VMEM_LIMIT = 56 * 1024 * 1024
NN = (((1,), (0,)), ((), ()))
NT = (((1,), (1,)), ((), ()))
TN = (((0,), (0,)), ((), ()))


def mm(left, right, form=NN):
    return lax.dot_general(left, right, form, preferred_element_type=F32)


def root(value):
    return lax.rsqrt(jnp.mean(value * value, axis=-1, keepdims=True) + EPSILON)


def norm_back(value, gain, incoming):
    scale = root(value)
    scaled = gain * incoming
    inner = jnp.mean(scaled * value, axis=-1, keepdims=True)
    back = scale * scaled - (scale * scale * scale) * inner * value
    return back, jnp.sum(incoming * value * scale, axis=0, keepdims=True)


def sides():
    lane = lax.broadcasted_iota(jnp.int32, (1, PAIR), 1)
    low = (lane < HD).astype(F32)
    return lane < HD, low.astype(BF16), (1.0 - low).astype(BF16)


def attend_pair(queries, key_rows, value_rows, allowed):
    is_low, low, high = sides()
    mixed = []
    for side in (low, high):
        scores = mm(queries * (side * HD ** (-0.5)), key_rows, NT)
        if allowed is not None:
            scores = jnp.where(allowed, scores, NEGATIVE)
        shares = jnp.exp(scores - jnp.max(scores, axis=-1, keepdims=True))
        shares = shares * (1.0 / jnp.sum(shares, axis=-1, keepdims=True))
        mixed.append(mm(shares.astype(BF16), value_rows))
    return jnp.where(is_low, mixed[0], mixed[1]).astype(BF16)


def attend_back_pair(queries, key_rows, value_rows, grad_mixed, allowed):
    factor = HD ** (-0.5)
    is_low, low, high = sides()
    parts = []
    for side in (low, high):
        scores = mm(key_rows, queries * (side * factor), NT)
        if allowed is not None:
            scores = jnp.where(allowed, scores, NEGATIVE)
        chances = jnp.exp(scores - jnp.max(scores, axis=0, keepdims=True))
        chances = chances * (1.0 / jnp.sum(chances, axis=0, keepdims=True))
        grad_chances = mm(value_rows, grad_mixed * side, NT)
        shift = jnp.sum(grad_chances * chances, axis=0, keepdims=True)
        grad_scores = (chances * (grad_chances - shift)).astype(BF16)
        parts.append(
            (
                mm(grad_scores, key_rows, TN) * factor,
                mm(grad_scores, queries) * factor,
                mm(chances.astype(BF16), grad_mixed),
            )
        )
    return [jnp.where(is_low, a, b).astype(BF16) for a, b in zip(parts[0], parts[1])]


def whole(shape):
    return pl.BlockSpec(shape, lambda *_: (0,) * len(shape))


def call(kernel, grid, in_specs, out_specs, out_shape, scratch=(), flops=0, moved=0):
    return pl.pallas_call(
        kernel,
        grid=grid,
        in_specs=in_specs,
        out_specs=out_specs,
        out_shape=out_shape,
        scratch_shapes=list(scratch),
        compiler_params=pltpu.CompilerParams(vmem_limit_bytes=VMEM_LIMIT),
        cost_estimate=pl.CostEstimate(flops=flops, bytes_accessed=moved, transcendentals=0),
    )


def shape_of(shape, kind=BF16):
    return jax.ShapeDtypeStruct(shape, kind)


def place_masks(x_me, frames_all, transposed):
    rows = frames_all * GROUP
    shape = (rows, rows)
    query = lax.broadcasted_iota(jnp.int32, shape, 1 if transposed else 0)
    key = lax.broadcasted_iota(jnp.int32, shape, 0 if transposed else 1)
    query_frame = (query // GROUP + x_me * (frames_all // 2)) % frames_all
    key_frame = (key // GROUP + x_me * (frames_all // 2)) % frames_all
    return (query % GROUP == key % GROUP) & (key_frame <= query_frame)


RATE = 0.7978845608028654
CUBIC = 0.044715


def feed_forward(normed, grad, keep, expand, reduce, which=0):
    rows, width = normed.shape
    cores, _, units = expand.shape
    block = 512
    per = units // block

    def kernel(
        normed_ref,
        grad_ref,
        keep_ref,
        expand_ref,
        reduce_ref,
        active_ref,
        inner_ref,
        grad_branch_ref,
        branch_ref,
        grad_normed_ref,
        branch_sum,
        grad_sum,
    ):
        step = pl.program_id(0)

        @pl.when(step == 0)
        def _():
            grad_branch_ref[...] = (keep_ref[...] * grad_ref[...].astype(F32)).astype(BF16)
            branch_sum[...] = jnp.zeros_like(branch_sum)
            grad_sum[...] = jnp.zeros_like(grad_sum)

        inner = mm(normed_ref[...], expand_ref[0])
        grad_active = mm(grad_branch_ref[...], reduce_ref[0], NT)
        square = inner * inner
        bend = jnp.tanh(RATE * inner * (1.0 + CUBIC * square))
        half = 0.5 * (1.0 + bend)
        active = (inner * half).astype(BF16)
        slope = half + (0.5 * RATE) * inner * (1.0 - bend * bend) * (1.0 + (3.0 * CUBIC) * square)
        grad_inner = (grad_active * slope).astype(BF16)
        active_ref[...] = active
        inner_ref[...] = grad_inner
        branch_sum[...] += mm(active, reduce_ref[0])
        grad_sum[...] += mm(grad_inner, expand_ref[0], NT)

        @pl.when(step == cores * per - 1)
        def _():
            branch_ref[...] = branch_sum[...].astype(BF16)
            grad_normed_ref[...] = grad_sum[...].astype(BF16)

    full = whole((rows, width))
    return call(
        kernel,
        (cores * per,),
        [
            full,
            pl.BlockSpec((rows, width), lambda j: (which, 0)),
            pl.BlockSpec((rows, 1), lambda j: (which, 0)),
            pl.BlockSpec((1, width, block), lambda j: (j // per, 0, j % per)),
            pl.BlockSpec((1, block, width), lambda j: (j // per, j % per, 0)),
        ],
        [
            pl.BlockSpec((rows, block), lambda j: (0, j)),
            pl.BlockSpec((rows, block), lambda j: (0, j)),
            full,
            full,
            full,
        ],
        [
            shape_of((rows, cores * units)),
            shape_of((rows, cores * units)),
            shape_of((rows, width)),
            shape_of((rows, width)),
            shape_of((rows, width)),
        ],
        scratch=[pltpu.VMEM((rows, width), F32), pltpu.VMEM((rows, width), F32)],
        flops=8 * rows * width * cores * units,
        moved=18 * 2**20,
    )(normed, grad, keep, expand, reduce)


def temporal_backward(
    grad_near, grad_first, grad_second, hidden2, hidden1, grad_result, keep, gains, heads, merge2, project, merge1
):
    rows, width = hidden1.shape
    local = merge1.shape[1]
    span = rows // FRAMES
    group_rows = FRAMES * GROUP

    def kernel(
        near_ref,
        first_ref,
        second_ref,
        hidden2_ref,
        hidden1_ref,
        result_ref,
        keep_ref,
        gains_ref,
        heads_ref,
        merge2_ref,
        project_ref,
        merge1_ref,
        branch2_ref,
        grad_heads_ref,
        branch1_ref,
        mixed1_ref,
        carried_ref,
        gain3_ref,
        gain2_ref,
        grad_hidden,
        grad_normed,
        grad_mixed,
    ):
        step = pl.program_id(0)

        @pl.when(step == 0)
        def _():
            far = jnp.concatenate([first_ref[...], second_ref[...]])
            incoming = near_ref[...].astype(F32) + far.astype(F32)
            back, gain3_ref[...] = norm_back(hidden2_ref[...], gains_ref[2:3], incoming)
            total = result_ref[...].astype(F32) + back
            grad_hidden[...] = total
            branch2_ref[...] = (keep_ref[...] * total).astype(BF16)
            grad_normed[...] = jnp.zeros_like(grad_normed)

        back_mixed = mm(branch2_ref[...], merge2_ref[0], NT).astype(BF16)
        grad_mixed[...] = back_mixed.reshape(FRAMES, span, local)
        allowed = place_masks(lax.axis_index("wide") % 2, FRAMES, True)
        for g in range(span // GROUP):
            band = pl.ds(g * GROUP, GROUP)
            for at in range(0, local, PAIR):
                part = pl.ds(at, PAIR)
                terms = [heads_ref[0, c, :, band, part].reshape(group_rows, PAIR) for c in range(3)]
                grad = grad_mixed[:, band, part].reshape(group_rows, PAIR)
                grads = attend_back_pair(*terms, grad, allowed)
                for c in range(3):
                    grad_heads_ref[0, c, :, band, part] = grads[c].reshape(FRAMES, GROUP, PAIR)
        total = mm(grad_heads_ref[0, 0].reshape(rows, local), project_ref[0, 0], NT)
        for c in range(1, 3):
            total += mm(grad_heads_ref[0, c].reshape(rows, local), project_ref[0, c], NT)
        grad_normed[...] += total

        @pl.when(step == 3)
        def _():
            back, gain2_ref[...] = norm_back(hidden1_ref[...], gains_ref[1:2], grad_normed[...])
            total = grad_hidden[...] + back
            carried_ref[...] = total.astype(BF16)
            branch1_ref[...] = (keep_ref[...] * total).astype(BF16)
            for n in range(4):
                mixed1_ref[n] = mm(branch1_ref[...], merge1_ref[n], NT).astype(BF16)

    full = whole((rows, width))
    row = whole((1, width))
    return call(
        kernel,
        (4,),
        [
            full,
            whole((rows // 2, width)),
            whole((rows // 2, width)),
            full,
            full,
            full,
            whole((rows, 1)),
            whole((3, width)),
            pl.BlockSpec((1, 3, FRAMES, span, local), lambda n: (n, 0, 0, 0, 0)),
            pl.BlockSpec((1, local, width), lambda n: (n, 0, 0)),
            pl.BlockSpec((1, 3, width, local), lambda n: (n, 0, 0, 0)),
            whole((4, local, width)),
        ],
        [
            full,
            pl.BlockSpec((1, 3, FRAMES, span, local), lambda n: (n, 0, 0, 0, 0)),
            full,
            whole((4, rows, local)),
            full,
            row,
            row,
        ],
        [
            shape_of((rows, width)),
            shape_of((4, 3, FRAMES, span, local)),
            shape_of((rows, width)),
            shape_of((4, rows, local)),
            shape_of((rows, width)),
            shape_of((1, width), F32),
            shape_of((1, width), F32),
        ],
        scratch=[
            pltpu.VMEM((rows, width), F32),
            pltpu.VMEM((rows, width), F32),
            pltpu.VMEM((FRAMES, span, local), BF16),
        ],
        flops=2 * rows * width * width * 8,
        moved=30 * 2**20,
    )(grad_near, grad_first, grad_second, hidden2, hidden1, grad_result, keep, gains, heads, merge2, project, merge1)


def here():
    wide, narrow = lax.axis_index("wide"), lax.axis_index("narrow")
    return wide, narrow, wide % 2, narrow // 2, narrow % 2


def other(wide, narrow, x, y, core):
    if x:
        wide = wide + 1 - 2 * (wide % 2)
    if y:
        narrow = (narrow + 2) % 4
    if core:
        narrow = narrow + 1 - 2 * (narrow % 2)
    return wide, narrow


def beyond(wide, narrow):
    return wide + 2 - 4 * ((wide // 2) % 2), narrow


def place_of(wide, narrow, span):
    return pl.multiple_of(((wide % 2) * 4 + narrow) * span, span)


def remote(src, dst, sems, i, device):
    return pltpu.make_async_remote_copy(
        src_ref=src,
        dst_ref=dst,
        send_sem=sems.at[0, i],
        recv_sem=sems.at[1, i],
        device_id=device,
        device_id_type=pl.DeviceIdType.MESH,
    )


def greet(devices):
    barrier = pltpu.get_barrier_semaphore()
    for device in devices:
        pl.semaphore_signal(
            barrier, inc=1, device_id=device, device_id_type=pl.DeviceIdType.MESH
        )
    pl.semaphore_wait(barrier, len(devices))


OTHERS = [(x, y, c) for x in range(2) for y in range(2) for c in range(2) if x + y + c > 0]
ANY = pl.BlockSpec(memory_space=pl.ANY)


def comm_call(kernel, number, grid, in_specs, out_specs, out_shape, scratch, flops):
    return pl.pallas_call(
        kernel,
        grid=grid,
        in_specs=in_specs,
        out_specs=out_specs,
        out_shape=out_shape,
        scratch_shapes=scratch,
        compiler_params=pltpu.CompilerParams(
            vmem_limit_bytes=VMEM_LIMIT, collective_id=number, has_side_effects=True
        ),
        cost_estimate=pl.CostEstimate(flops=flops, bytes_accessed=30 * 2**20, transcendentals=0),
    )


def attention_forward(
    tokens,
    extra,
    gains,
    project,
    merge1,
    project2,
    merge2,
    expand,
    reduce,
    grad_out,
    keep,
):
    frames, places, width = tokens.shape
    local = project.shape[-1]
    span = places // 8
    rows = FRAMES * span
    group_rows = FRAMES * GROUP
    half = frames // 2
    shards = (merge1, project2[0], project2[1], project2[2], merge2)
    count = len(shards)

    def kernel(
        tokens_ref,
        extra_ref,
        gains_ref,
        project_ref,
        keep_ref,
        all_tokens,
        all_extra,
        grad_ref,
        expand_ref,
        reduce_ref,
        merge1_ref,
        project2_ref,
        merge2_ref,
        normed_ref,
        heads_ref,
        hidden1_ref,
        normed2_ref,
        heads2_ref,
        mixed2_ref,
        hidden2_ref,
        normed3_ref,
        first_ref,
        second_ref,
        mixed_out,
        grad_near,
        grad_far,
        expand_pair,
        reduce_pair,
        merge1_out,
        project2_out,
        merge2_out,
        mixed_ref,
        mixed_all,
        tokens_place,
        extra_place,
        merge1_all,
        project2_all,
        merge2_all,
        local_sems,
        move_sems,
        shard_sems,
        mixed_sems,
        *stage,
    ):
        step = pl.program_id(0)
        wide, narrow, x_me, _, _ = here()
        half_me = (wide // 2) % 2
        x_other = other(wide, narrow, 1, 0, 0)
        y_other = other(wide, narrow, 0, 1, 0)
        core_other = other(wide, narrow, 0, 0, 1)
        z_other = beyond(wide, narrow)
        mine = pl.ds(place_of(wide, narrow, span), span)
        near_y = pl.ds(place_of(*y_other, span), span)
        shard = [merge1_ref] + [project2_ref.at[c] for c in range(3)] + [merge2_ref]
        full = [merge1_all] + [project2_all.at[:, c] for c in range(3)] + [merge2_all]

        own = [
            (expand_ref, expand_pair.at[0]),
            (reduce_ref, reduce_pair.at[0]),
            (grad_ref.at[:, mine], grad_near.at[0]),
            (grad_ref.at[:, near_y], grad_far.at[0]),
        ]
        into = [
            pltpu.make_async_copy(a, v, local_sems.at[0, i])
            for i, ((a, _), v) in enumerate(zip(own, stage))
        ]
        back = [
            pltpu.make_async_copy(v, b, local_sems.at[1, i])
            for i, ((_, b), v) in enumerate(zip(own, stage))
        ]
        inside = [
            (all_tokens.at[:, mine], tokens_place.at[0]),
            (all_extra, extra_place.at[0]),
        ] + [(shard[k], full[k].at[0]) for k in range(count)]
        inside = [
            pltpu.make_async_copy(a, b, local_sems.at[0, 4 + i]) for i, (a, b) in enumerate(inside)
        ]
        leaving = [
            (mixed_all, mixed_out),
            (merge1_all, merge1_out),
            (project2_all, project2_out),
            (merge2_all, merge2_out),
        ]
        leaving = [
            pltpu.make_async_copy(a, b, local_sems.at[1, 4 + i]) for i, (a, b) in enumerate(leaving)
        ]
        far = pl.ds(place_of(*x_other, span), span)
        far_y = pl.ds(place_of(*other(wide, narrow, 1, 1, 0), span), span)
        first = [
            remote(all_tokens.at[:, far], tokens_place.at[1], move_sems, 0, x_other),
            remote(all_extra, extra_place.at[1], move_sems, 1, x_other),
            remote(expand_ref, expand_pair.at[1], move_sems, 2, core_other),
            remote(reduce_ref, reduce_pair.at[1], move_sems, 3, core_other),
        ]
        last = [
            remote(grad_ref.at[:, far], grad_near.at[1], move_sems, 4, x_other),
            remote(grad_ref.at[:, far_y], grad_far.at[1], move_sems, 5, x_other),
        ]

        def part(k, which):
            count = shards[k].shape[0] // 2
            return pl.ds(pl.multiple_of(which * count, count), count)

        def over_core(k):
            return remote(shard[k], full[k].at[1], shard_sems, 5 * k, core_other)

        def over_y(k):
            some = part(k, half_me)
            return remote(shard[k].at[some], full[k].at[2, some], shard_sems, 5 * k + 1, y_other)

        def onward(k, which, i, device, slot):
            some = part(k, which)
            return remote(full[k].at[2, some], full[k].at[slot, some], shard_sems, 5 * k + i, device)

        def over_z(k):
            return onward(k, half_me, 2, z_other, 2)

        def near_half(k):
            return onward(k, half_me, 3, core_other, 3)

        def far_half(k):
            return onward(k, 1 - half_me, 4, core_other, 3)

        def forward(k):
            over_y(k).wait_recv()
            over_z(k).start()
            near_half(k).start()

        def complete(k):
            over_z(k).wait_recv()
            far_half(k).start()

        def mixed_copies(chunk):
            copies = []
            some = pl.ds(chunk * half, half)
            for i, (x, y, c) in enumerate(OTHERS):
                device = other(wide, narrow, x, y, c)
                copies.append(
                    remote(
                        mixed_ref.at[some, pl.ds(place_of(*device, span), span)],
                        mixed_all.at[2 * y + c, x, some],
                        mixed_sems,
                        7 * chunk + i,
                        device,
                    )
                )
            here_copy = pltpu.make_async_copy(
                mixed_ref.at[some, mine], mixed_all.at[0, 0, some], local_sems.at[chunk, 11]
            )
            return copies + [here_copy]

        @pl.when(step == 0)
        def _():
            greet([other(wide, narrow, *o) for o in OTHERS] + [z_other])
            for k in range(3):
                over_y(k).start()
            for copy in first:
                copy.start()
            for k in range(count):
                over_core(k).start()
            for copy in into + inside:
                copy.start()

        @pl.when(step == 2)
        def _():
            for copy in into:
                copy.wait()
            for copy in back:
                copy.start()

        @pl.when(step < frames)
        def _():
            start = tokens_ref[0].astype(F32) + extra_ref[0]
            normed = (start * root(start) * gains_ref[0:1]).astype(BF16)
            normed_ref[0] = normed
            for c in range(3):
                heads_ref[c, 0] = mm(normed, project_ref[c]).astype(BF16)
            for at in range(0, local, PAIR):
                lanes = pl.ds(at, PAIR)
                mixed_ref[step, :, lanes] = attend_pair(
                    heads_ref[0, 0, :, lanes],
                    heads_ref[1, 0, :, lanes],
                    heads_ref[2, 0, :, lanes],
                    None,
                )

        @pl.when(step == 2)
        def _():
            forward(0)

        @pl.when(step == half - 1)
        def _():
            for copy in mixed_copies(0):
                copy.start()

        @pl.when(step == half)
        def _():
            forward(1)

        @pl.when(step == half + 1)
        def _():
            complete(0)

        @pl.when(step == half + 2)
        def _():
            forward(2)

        @pl.when(step == frames - 1)
        def _():
            for copy in mixed_copies(1):
                copy.start()
            over_y(3).start()
            over_y(4).start()
            for copy in last:
                copy.start()
            complete(1)

        @pl.when(step == frames)
        def _():
            for copy in inside:
                copy.wait()
            over_core(0).wait_recv()
            near_half(0).wait_recv()
            far_half(0).wait_recv()
            first[0].wait_recv()
            first[1].wait_recv()
            for copy in mixed_copies(0) + mixed_copies(1):
                copy.wait()
            leaving[0].start()
            leaving[1].start()
            branch = mm(mixed_all[0].reshape(rows, local), merge1_all[0])
            for n in range(1, 4):
                branch += mm(mixed_all[n].reshape(rows, local), merge1_all[n])
            begin = tokens_place[...].astype(F32) + extra_place[...]
            hidden1 = begin.reshape(rows, width) + keep_ref[...] * branch
            hidden1_ref[...] = hidden1
            hidden2_ref[...] = hidden1
            normed2_ref[...] = (hidden1 * root(hidden1) * gains_ref[1:2]).astype(BF16)

        @pl.when(step == frames + 1)
        def _():
            complete(2)
            forward(3)
            for k in range(1, count):
                over_core(k).wait_recv()

        @pl.when(step == frames + 2)
        def _():
            forward(4)
            complete(3)
            over_z(4).wait_recv()
            far_half(4).start()

        @pl.when(step == frames + 3)
        def _():
            for k in range(1, count):
                near_half(k).wait_recv()
                far_half(k).wait_recv()
            leaving[2].start()
            leaving[3].start()

        @pl.when(step >= frames)
        def _():
            n = step - frames
            for c in range(3):
                head = mm(normed2_ref[...], project2_all[n, c]).astype(BF16)
                heads2_ref[0, c] = head.reshape(FRAMES, span, local)
            allowed = place_masks(x_me, FRAMES, False)
            for g in range(span // GROUP):
                band = pl.ds(g * GROUP, GROUP)
                for at in range(0, local, PAIR):
                    lanes = pl.ds(at, PAIR)
                    terms = [
                        heads2_ref[0, c, :, band, lanes].reshape(group_rows, PAIR) for c in range(3)
                    ]
                    mixed = attend_pair(*terms, allowed)
                    mixed2_ref[0, :, band, lanes] = mixed.reshape(FRAMES, GROUP, PAIR)
            merged = mm(mixed2_ref[0].reshape(rows, local), merge2_all[n])
            hidden2_ref[...] += keep_ref[...] * merged

        @pl.when(step == frames + 3)
        def _():
            hidden2 = hidden2_ref[...]
            normed3 = (hidden2 * root(hidden2) * gains_ref[2:3]).astype(BF16)
            normed3_ref[...] = normed3
            first_ref[...] = normed3[: rows // 2]
            second_ref[...] = normed3[rows // 2 :]
            for copy in first[2:] + last:
                copy.wait()
            for copy in first[:2]:
                copy.wait_send()
            for copy in back + leaving:
                copy.wait()
            for k in range(count):
                for copy in (over_core(k), over_y(k), over_z(k), near_half(k), far_half(k)):
                    copy.wait_send()

    def frame(step):
        return jnp.minimum(step, frames - 1)

    def turn(step):
        return jnp.maximum(step - frames, 0)

    full = whole((rows, width))
    return comm_call(
        kernel,
        0,
        (frames + 4,),
        [
            pl.BlockSpec((1, places, width), lambda s: (frame(s), 0, 0)),
            pl.BlockSpec((1, 1, width), lambda s: (frame(s), 0, 0)),
            whole((3, width)),
            whole(project.shape),
            whole((rows, 1)),
        ]
        + [ANY] * 8,
        [
            pl.BlockSpec((1, places, width), lambda s: (frame(s), 0, 0)),
            pl.BlockSpec((3, 1, places, local), lambda s: (0, frame(s), 0, 0)),
            full,
            full,
            pl.BlockSpec((1, 3, FRAMES, span, local), lambda s: (turn(s), 0, 0, 0, 0)),
            pl.BlockSpec((1, FRAMES, span, local), lambda s: (turn(s), 0, 0, 0)),
            full,
            full,
            whole((rows // 2, width)),
            whole((rows // 2, width)),
        ]
        + [ANY] * 8,
        [
            shape_of((frames, places, width)),
            shape_of((3, frames, places, local)),
            shape_of((rows, width), F32),
            shape_of((rows, width)),
            shape_of((4, 3, FRAMES, span, local)),
            shape_of((4, FRAMES, span, local)),
            shape_of((rows, width), F32),
            shape_of((rows, width)),
            shape_of((rows // 2, width)),
            shape_of((rows // 2, width)),
            shape_of((4, 2, frames, span, local)),
            shape_of((2, frames, span, width)),
            shape_of((2, frames, span, width)),
            shape_of((2,) + expand.shape),
            shape_of((2,) + reduce.shape),
            shape_of((4,) + merge1.shape),
            shape_of((4,) + project2.shape),
            shape_of((4,) + merge2.shape),
        ],
        [
            pltpu.VMEM((frames, places, local), BF16),
            pltpu.VMEM((4, 2, frames, span, local), BF16),
            pltpu.VMEM((2, frames, span, width), BF16),
            pltpu.VMEM((2, frames, 1, width), F32),
            pltpu.VMEM((4,) + merge1.shape, BF16),
            pltpu.VMEM((4,) + project2.shape, BF16),
            pltpu.VMEM((4,) + merge2.shape, BF16),
            pltpu.SemaphoreType.DMA((2, 12)),
            pltpu.SemaphoreType.DMA((2, 6)),
            pltpu.SemaphoreType.DMA((2, 5 * count)),
            pltpu.SemaphoreType.DMA((2, 14)),
            pltpu.VMEM(expand.shape, BF16),
            pltpu.VMEM(reduce.shape, BF16),
            pltpu.VMEM((frames, span, width), BF16),
            pltpu.VMEM((frames, span, width), BF16),
        ],
        2 * frames * places * width * local * 4 + 2 * rows * width * width * 6,
    )(
        tokens,
        extra[:, None, :],
        gains,
        project,
        keep,
        tokens,
        extra[:, None, :],
        grad_out,
        expand,
        reduce,
        merge1,
        project2,
        merge2,
    )


def feed_outer(normed, grad_inner, grad_branch, active):
    width = normed[0].shape[1]
    units = active[0].shape[1] // 2
    ends = [0]
    for part in normed:
        ends.append(ends[-1] + part.shape[0])
    rows, count = ends[-1], len(normed)
    block = 512
    per = units // block
    wide = lax.axis_size("wide")
    split = (2, wide // 2, 2, width // wide, block)

    def kernel(*refs):
        normed_refs, branch_refs = refs[:count], refs[count : 2 * count]
        inner_refs, active_refs = refs[2 * count : 3 * count], refs[3 * count : 4 * count]
        keep_ref, send_ref, left, right, total, given, taken, sems = refs[4 * count :]
        step = pl.program_id(0)
        wide, narrow, x_me, _, _ = here()
        core_other = other(wide, narrow, 0, 0, 1)

        def over(j):
            return remote(given.at[j], taken.at[j], sems, j, core_other)

        @pl.when(step == 0)
        def _():
            for k in range(count):
                left[:, ends[k] : ends[k + 1]] = normed_refs[k][...].T
                right[:, ends[k] : ends[k + 1]] = branch_refs[k][...].T

        def product(side, parts):
            out = mm(side[:, : ends[1]], parts[0][...])
            for k in range(1, count):
                out += mm(side[:, ends[k] : ends[k + 1]], parts[k][...])
            return out

        expand = product(left, inner_refs)
        reduce = product(right, active_refs)

        @pl.when(step == 0)
        def _():
            greet([core_other])

        @pl.when(step < per)
        def _():
            given[step, 0] = expand.astype(BF16)
            given[step, 1] = reduce.astype(BF16)
            over(step).start()

        @pl.when(step >= per)
        def _():
            j = step - per
            over(j).wait_recv()
            half = split[1:]
            total[0] = (expand + taken[j, 0].astype(F32)).astype(BF16).reshape(half)
            total[1] = (reduce + taken[j, 1].astype(F32)).astype(BF16).reshape(half)
            out = keep_ref.shape
            keep_ref[...] = total[:, :, pl.ds(x_me, 1)].reshape(out)
            send_ref[...] = total[:, :, pl.ds(1 - x_me, 1)].reshape(out)

        @pl.when(step == 2 * per - 1)
        def _():
            for j in range(per):
                over(j).wait_send()

    def columns(part):
        return pl.BlockSpec((part.shape[0], block), lambda j: (0, (j + per) % (2 * per)))

    out = pl.BlockSpec((2, width // 2, block), lambda j: (0, 0, jnp.maximum(j - per, 0)))
    return comm_call(
        kernel,
        3,
        (2 * per,),
        [whole(part.shape) for part in normed + grad_branch]
        + [columns(part) for part in grad_inner + active],
        [out, out],
        [shape_of((2, width // 2, units))] * 2,
        [
            pltpu.VMEM((width, rows), BF16),
            pltpu.VMEM((width, rows), BF16),
            pltpu.VMEM(split, BF16),
            pltpu.VMEM((per, 2, width, block), BF16),
            pltpu.VMEM((per, 2, width, block), BF16),
            pltpu.SemaphoreType.DMA((2, per)),
        ],
        8 * rows * width * units,
    )(*normed, *grad_branch, *grad_inner, *active)


def temporal_outer(
    grad_mixed1, carried, result, mixed1, branch1, mixed2, branch2, normed2, grad_heads
):
    rows, width = branch1.shape
    local = mixed1.shape[-1]
    span = rows // FRAMES
    frames = FRAMES // 2

    def kernel(
        grad_ref,
        carried_ref,
        result_ref,
        mixed1_ref,
        branch1_ref,
        mixed2_ref,
        branch2_ref,
        normed2_ref,
        heads_ref,
        out_ref,
        grad_own,
        carried_own,
        result_far,
        left,
        given,
        taken,
        grad_stage,
        carried_stage,
        local_sems,
        sems,
    ):
        step = pl.program_id(0)
        wide, narrow, x_me, _, _ = here()
        x_other = other(wide, narrow, 1, 0, 0)
        mine = pl.ds(place_of(wide, narrow, span), span)
        copies = [
            remote(
                grad_ref.at[2 * y + c, x],
                grad_own.at[:, mine],
                sems,
                i,
                other(wide, narrow, x, y, c),
            )
            for i, (x, y, c) in enumerate(OTHERS)
        ]
        copies.append(remote(carried_ref.at[1], carried_own.at[:, x_me], sems, 7, x_other))
        copies.append(remote(result_ref, result_far, sems, 8, other(wide, narrow, 0, 1, 0)))

        def over(y):
            return remote(given.at[y], taken.at[y], sems, 9 + y, other(wide, narrow, 0, 0, 1))

        into = [
            pltpu.make_async_copy(grad_ref.at[0, 0], grad_stage, local_sems.at[0]),
            pltpu.make_async_copy(carried_ref.at[0], carried_stage, local_sems.at[1]),
        ]
        back = [
            pltpu.make_async_copy(grad_stage, grad_own.at[:, mine], local_sems.at[2]),
            pltpu.make_async_copy(carried_stage, carried_own.at[:, x_me], local_sems.at[3]),
        ]

        @pl.when(step == 0)
        def _():
            greet([other(wide, narrow, *o) for o in OTHERS])
            for copy in copies + into:
                copy.start()
            left[0] = branch1_ref[...].T
            left[1] = branch2_ref[...].T
            left[2] = normed2_ref[...].T

        terms = [(0, mixed1_ref[0]), (1, mixed2_ref[0])] + [(2, heads_ref[0, c]) for c in range(3)]
        for k, (which, term) in enumerate(terms):
            total = mm(left[which], term)

            @pl.when(step < 2)
            def _():
                given[step, k] = total.astype(BF16)

            @pl.when(step >= 2)
            def _():
                out_ref[0, k] = total.astype(BF16)

        @pl.when(step < 2)
        def _():
            over(step).start()

        @pl.when(step >= 2)
        def _():
            over(step - 2).wait_recv()
            out_ref[0] = (out_ref[0].astype(F32) + taken[step - 2].astype(F32)).astype(BF16)

        @pl.when(step == 1)
        def _():
            for copy in into:
                copy.wait()
            for copy in back:
                copy.start()

        @pl.when(step == 3)
        def _():
            for copy in copies + back:
                copy.wait()
            for y in range(2):
                over(y).wait_send()

    full = whole((rows, width))

    def turn(j):
        return 2 * (j % 2) + 1 - j // 2

    part = pl.BlockSpec((1, rows, local), lambda j: (turn(j), 0, 0))
    return comm_call(
        kernel,
        1,
        (4,),
        [ANY] * 3
        + [part, full, part, full, full]
        + [pl.BlockSpec((1, 3, rows, local), lambda j: (turn(j), 0, 0, 0))],
        [pl.BlockSpec((1, 5, width, local), lambda j: (jnp.maximum(j - 2, 0), 0, 0, 0))] + [ANY] * 3,
        [
            shape_of((2, 5, width, local)),
            shape_of((frames, 8 * span, local)),
            shape_of((frames, 2, span, width)),
            shape_of(result.shape),
        ],
        [
            pltpu.VMEM((3, width, rows), BF16),
            pltpu.VMEM((2, 5, width, local), BF16),
            pltpu.VMEM((2, 5, width, local), BF16),
            pltpu.VMEM((frames, span, local), BF16),
            pltpu.VMEM((frames, span, width), BF16),
            pltpu.SemaphoreType.DMA((4,)),
            pltpu.SemaphoreType.DMA((2, 11)),
        ],
        10 * rows * width * width,
    )(
        grad_mixed1.reshape(4, 2, frames, span, local),
        carried.reshape(2, frames, span, width),
        result,
        mixed1,
        branch1,
        mixed2.reshape(4, rows, local),
        branch2,
        normed2,
        grad_heads.reshape(4, 3, rows, local),
    )


class Halving:
    def __init__(self, slots, rows, columns, blocks, first):
        self.slots, self.rows, self.columns, self.first = slots, rows, columns, first
        self.blocks = []
        while blocks > 1:
            blocks //= 2
            self.blocks.append(blocks)

    def scratch(self):
        out = []
        for blocks in self.blocks:
            out.append(pltpu.VMEM((self.slots, blocks, 2, self.rows, self.columns), BF16))
            out.append(pltpu.VMEM((self.slots, blocks, self.rows, self.columns), BF16))
        return out

    def bind(self, refs, sems, base, wide, narrow):
        self.held, self.taken = refs[0::2], refs[1::2]
        self.sems, self.base, self.wide, self.narrow = sems, base, wide, narrow

    def bit(self, level):
        step = 2 ** (self.first + level)
        return step, (self.wide // step) % 2

    def copy(self, level):
        step, bit = self.bit(level)
        device = (self.wide + step - 2 * step * bit, self.narrow)
        return remote(
            self.held[level].at[:, :, 1 - bit],
            self.taken[level],
            self.sems,
            self.base + level,
            device,
        )

    def fill(self, level, value, slot=0):
        count = value.shape[0]
        self.held[level][slot : slot + count] = value.astype(BF16).reshape(
            (count,) + self.held[level].shape[1:]
        )

    def result(self, level):
        _, bit = self.bit(level)
        shape = self.taken[level].shape
        own = self.held[level][:, :, pl.ds(bit, 1)].reshape(shape)
        return own.astype(F32) + self.taken[level][...].astype(F32)

    def advance(self, level):
        self.copy(level).wait_recv()
        total = self.result(level)
        if level + 1 < len(self.blocks):
            self.fill(level + 1, total)
            self.copy(level + 1).start()
            return None
        return total.reshape(self.slots, self.rows, self.columns)

    def close(self):
        for level in range(len(self.blocks)):
            self.copy(level).wait_send()


FIRST = 2


def spatial_backward(
    heads,
    grad_mixed,
    project,
    normed,
    tokens,
    extra,
    gain,
    carried,
    choose,
    gains_grad,
    result_near,
    result_far,
    temporal_grad,
    feed_keep,
    feed_taken,
):
    _, frames, places, local = heads.shape
    width = project.shape[1]
    span = places // 8
    tile = width // 4
    wide_size = lax.axis_size("wide")
    half = wide_size // 2
    block = width // wide_size
    bits = wide_size.bit_length() - 1
    slots = temporal_grad.shape[1]
    units = feed_keep.shape[-1]
    last = slots - FIRST
    feed = Halving(2, block, units, half, 1)
    own = Halving(3, block, local, wide_size, 0)
    timed = Halving(slots, block, local, half, 1)
    engines = (feed, own, timed)
    levels = [len(engine.blocks) for engine in engines]
    attend_end = frames
    outer_end = attend_end + 4
    sum_end = outer_end + frames

    def kernel(
        heads_ref,
        mixed_ref,
        project_ref,
        normed_ref,
        tokens_ref,
        extra_ref,
        gain_ref,
        carried_ref,
        choose_ref,
        gains_ref,
        feed_keep_ref,
        feed_taken_ref,
        near_ref,
        far_ref,
        temporal_ref,
        own_out,
        timed_out,
        feed_out,
        small_out,
        output_ref,
        out_ref,
        grad_heads,
        partial,
        from_core,
        halved,
        from_y,
        done,
        gain_grad,
        table,
        small,
        small_taken,
        first_own,
        first_taken,
        first_sum,
        first_y,
        last_own,
        last_taken,
        last_sum,
        last_x,
        result_stage,
        local_sems,
        sems,
        move_sems,
        small_sems,
        halving_sems,
        *held,
    ):
        step = pl.program_id(0)
        wide, narrow, x_me, y_me, c_me = here()
        x_other = other(wide, narrow, 1, 0, 0)
        y_other = other(wide, narrow, 0, 1, 0)
        core_other = other(wide, narrow, 0, 0, 1)
        beyond_x = [
            (wide + 2**k - 2 ** (k + 1) * ((wide // 2**k) % 2), narrow) for k in range(1, bits)
        ]
        partners = [core_other, x_other] + beyond_x + [y_other]
        at = base = 0
        for engine, count in zip(engines, levels):
            engine.bind(held[at : at + 2 * count], halving_sems, base, wide, narrow)
            at, base = at + 2 * count, base + count

        def core_sum(f):
            return remote(partial.at[f, :, :, 1 - c_me], from_core.at[f], sems, f, core_other)

        def y_sum(f):
            return remote(halved.at[f, :, 1 - y_me], from_y.at[f], sems, frames + f, y_other)

        def y_back(f):
            return remote(done.at[f], out_ref.at[f, :, y_me, c_me], sems, 2 * frames + f, y_other)

        def core_back(f):
            return remote(done.at[f], out_ref.at[f, :, y_me, c_me], sems, 3 * frames + f, core_other)

        def core_onward(f):
            there = out_ref.at[f, :, 1 - y_me, c_me]
            return remote(there, there, sems, 4 * frames + f, core_other)

        def keep_own(f):
            return pltpu.make_async_copy(done.at[f], out_ref.at[f, :, y_me, c_me], local_sems.at[f])

        result = (near_ref, far_ref)

        def place(y):
            return y_me if y == 0 else 1 - y_me

        def result_x(y):
            there = output_ref.at[:, x_me, place(y), c_me]
            return remote(result[y].at[1], there, move_sems, y, x_other)

        def result_core(y):
            there = output_ref.at[:, x_me, place(y), c_me]
            return remote(result[y].at[0], there, move_sems, 2 + y, core_other)

        def result_onward(y):
            there = output_ref.at[:, 1 - x_me, place(y), c_me]
            return remote(there, there, move_sems, 4 + y, core_other)

        def result_in(y):
            return pltpu.make_async_copy(
                result[y].at[0], result_stage.at[y], local_sems.at[frames + y]
            )

        def result_own(y):
            there = output_ref.at[:, x_me, place(y), c_me]
            return pltpu.make_async_copy(result_stage.at[y], there, local_sems.at[frames + 2 + y])

        early, late_slots = pl.ds(0, FIRST), pl.ds(FIRST, last)
        first_in = pltpu.make_async_copy(
            temporal_ref.at[:, early, :, x_me], first_own, local_sems.at[frames + 4]
        )
        last_in = pltpu.make_async_copy(
            temporal_ref.at[0, late_slots], last_own, local_sems.at[frames + 5]
        )
        first_over_x = remote(
            temporal_ref.at[:, early, :, 1 - x_me], first_taken, move_sems, 6, x_other
        )
        first_over_y = remote(first_sum.at[1], first_y, move_sems, 7, y_other)
        last_over_y = remote(temporal_ref.at[1, late_slots], last_taken, move_sems, 8, y_other)
        last_over_x = remote(last_sum.at[:, :, 1 - x_me], last_x, move_sems, 9, x_other)

        def small_copy(k):
            return remote(small.at[k], small_taken.at[k], small_sems, k, partners[k])

        @pl.when(step == 0)
        def _():
            greet(partners)
            last_over_y.start()
            first_over_x.start()
            feed.fill(0, feed_keep_ref[...].astype(F32) + feed_taken_ref[...].astype(F32))
            feed.copy(0).start()
            result_x(0).start()
            first_in.start()
            last_in.start()
            for y in range(2):
                result_core(y).start()
                result_in(y).start()
            gain_grad[...] = jnp.zeros_like(gain_grad)
            table[...] = jnp.zeros_like(table)

        @pl.when(step < attend_end)
        def _():
            rows = pl.ds(pl.multiple_of(step * places, places), places)
            for at in range(0, local, PAIR):
                lanes = pl.ds(at, PAIR)
                grads = attend_back_pair(
                    heads_ref[0, 0, :, lanes],
                    heads_ref[1, 0, :, lanes],
                    heads_ref[2, 0, :, lanes],
                    mixed_ref[0, :, lanes],
                    None,
                )
                for c in range(3):
                    grad_heads[c, rows, lanes] = grads[c]
            total = mm(grad_heads[0, rows], project_ref[0], NT)
            for c in range(1, 3):
                total += mm(grad_heads[c, rows], project_ref[c], NT)
            partial[step] = total.astype(BF16).reshape(2, 2, 2, span, width)
            core_sum(step).start()

        @pl.when((step >= 1) & (step < attend_end + 1))
        def _():
            f = step - 1
            core_sum(f).wait_recv()
            mine = partial[f, :, :, pl.ds(c_me, 1)].reshape(2, 2, span, width)
            halved[f] = (mine.astype(F32) + from_core[f].astype(F32)).astype(BF16)

        @pl.when(step == 1)
        def _():
            for y in range(2):
                result_in(y).wait()
                result_own(y).start()

        @pl.when(step == attend_end)
        def _():
            first_in.wait()
            first_over_x.wait_recv()
            first_sum[...] = (first_own[...].astype(F32) + first_taken[...].astype(F32)).astype(BF16)
            first_over_y.start()
            for f in range(frames):
                y_sum(f).start()
            feed.advance(0)

        @pl.when((step >= attend_end) & (step < outer_end))
        def _():
            pairs = tile // (2 * block)
            j = (step - attend_end) * pairs
            for c in range(3):
                grad = mm(normed_ref[...], grad_heads[c], TN).astype(BF16)
                own.held[0][c, pl.ds(j, pairs)] = grad.reshape(pairs, 2, block, local)

        @pl.when(step == attend_end + 2)
        def _():
            last_in.wait()
            last_over_y.wait_recv()
            last_sum[...] = (last_own[...].astype(F32) + last_taken[...].astype(F32)).astype(BF16)
            last_over_x.start()

        @pl.when(step == outer_end)
        def _():
            own.copy(0).start()
            result_x(1).start()
            total = feed.advance(1)
            if total is not None:
                feed_out[...] = total

        @pl.when(step >= outer_end)
        def _():
            f = step - outer_end
            y_sum(f).wait_recv()
            mine = halved[f, :, pl.ds(y_me, 1)].reshape(2 * span, width)
            incoming = mine.astype(F32) + from_y[f].reshape(2 * span, width).astype(F32)
            start = pl.multiple_of(narrow * span, span)
            begin = jnp.concatenate(
                [tokens_ref[0, pl.ds(start, span)], tokens_ref[0, pl.ds(4 * span + start, span)]]
            )
            begin = begin.astype(F32) + extra_ref[0]
            back, gain_part = norm_back(begin, gain_ref[...], incoming)
            gain_grad[...] += gain_part
            grad = carried_ref[0].reshape(2 * span, width).astype(F32) + back
            table[...] += choose_ref[0] * jnp.sum(grad, axis=0, keepdims=True)
            done[f] = grad.astype(BF16).reshape(2, span, width)
            y_back(f).start()
            core_back(f).start()
            keep_own(f).start()

        @pl.when(step == outer_end + 1)
        def _():
            first_over_y.wait_recv()
            timed.fill(0, first_sum[0].astype(F32) + first_y[...].astype(F32))
            last_over_x.wait_recv()
            mine = last_sum[:, :, pl.ds(x_me, 1)].reshape(last_x.shape)
            timed.fill(0, mine.astype(F32) + last_x[...].astype(F32), FIRST)
            timed.copy(0).start()

        @pl.when(step == sum_end - 2)
        def _():
            timed.advance(0)

        @pl.when(step == sum_end - 1)
        def _():
            small[0, 0:1] = gain_grad[...]
            small[0, 1:3] = gains_ref[...]
            small[0, 3:11] = table[...]
            small[0, 11:] = jnp.zeros_like(small[0, 11:])
            small_copy(0).start()

            def small_sum(k):
                small_copy(k).wait_recv()
                small[k + 1] = small[k] + small_taken[k]
                if k + 1 < len(partners):
                    small_copy(k + 1).start()

            def back(f):
                y_back(f).wait_recv()
                core_onward(f).start()

            def result_back(y):
                result_x(y).wait_recv()
                result_onward(y).start()

            def finish(engine, out, level):
                if level < len(engine.blocks):
                    total = engine.advance(level)
                    if total is not None:
                        out[...] = total

            own.advance(0)
            small_sum(0)
            result_back(0)
            back(0)
            back(1)
            finish(own, own_out, 1)
            finish(timed, timed_out, 1)
            back(2)
            result_back(1)
            small_sum(1)
            back(3)
            for level in range(2, max(levels)):
                finish(feed, feed_out, level)
                finish(timed, timed_out, level)
                finish(own, own_out, level)
            for k in range(2, len(partners)):
                small_sum(k)
            small_out[...] = small[len(partners)]
            for f in range(4, frames):
                back(f)
            for engine in engines:
                engine.close()
            for k in range(len(partners)):
                small_copy(k).wait_send()
            for f in range(frames):
                core_sum(f).wait_send()
                y_sum(f).wait_send()
                y_back(f).wait_send()
                core_back(f).wait()
                core_onward(f).wait()
                keep_own(f).wait()
            for y in range(2):
                result_x(y).wait_send()
                result_core(y).wait()
                result_onward(y).wait()
                result_own(y).wait()
            for copy in (first_over_x, first_over_y, last_over_y, last_over_x):
                copy.wait_send()

    def frame(step):
        return jnp.minimum(step, frames - 1)

    def late(step):
        return jnp.clip(step - outer_end, 0, frames - 1)

    def piece(step):
        return jnp.clip(step - attend_end, 0, 3)

    block_shape = (half, 2, block, local)
    small_rows = 16
    scratch = [
        pltpu.VMEM((3, frames * places, local), BF16),
        pltpu.VMEM((frames, 2, 2, 2, span, width), BF16),
        pltpu.VMEM((frames, 2, 2, span, width), BF16),
        pltpu.VMEM((frames, 2, 2, span, width), BF16),
        pltpu.VMEM((frames, 2, span, width), BF16),
        pltpu.VMEM((frames, 2, span, width), BF16),
        pltpu.VMEM((1, width), F32),
        pltpu.VMEM((choose.shape[1], width), F32),
        pltpu.VMEM((bits + 3, small_rows, width), F32),
        pltpu.VMEM((bits + 2, small_rows, width), F32),
        pltpu.VMEM((2, FIRST, half, block, local), BF16),
        pltpu.VMEM((2, FIRST, half, block, local), BF16),
        pltpu.VMEM((2, FIRST, half, block, local), BF16),
        pltpu.VMEM((FIRST, half, block, local), BF16),
        pltpu.VMEM((last,) + block_shape, BF16),
        pltpu.VMEM((last,) + block_shape, BF16),
        pltpu.VMEM((last,) + block_shape, BF16),
        pltpu.VMEM((last, half, block, local), BF16),
        pltpu.VMEM((2, frames, span, width), BF16),
        pltpu.SemaphoreType.DMA((frames + 6,)),
        pltpu.SemaphoreType.DMA((2, 5 * frames)),
        pltpu.SemaphoreType.DMA((2, 10)),
        pltpu.SemaphoreType.DMA((2, bits + 2)),
        pltpu.SemaphoreType.DMA((2, sum(levels))),
    ]
    for engine in engines:
        scratch += engine.scratch()
    return comm_call(
        kernel,
        2,
        (sum_end,),
        [
            pl.BlockSpec((3, 1, places, local), lambda s: (0, frame(s), 0, 0)),
            pl.BlockSpec((1, places, local), lambda s: (frame(s), 0, 0)),
            whole(project.shape),
            pl.BlockSpec((frames * places, tile), lambda s: (0, piece(s))),
            pl.BlockSpec((1, places, width), lambda s: (late(s), 0, 0)),
            pl.BlockSpec((1, 1, width), lambda s: (late(s), 0, 0)),
            whole((1, width)),
            pl.BlockSpec((1, 2, span, width), lambda s: (late(s), 0, 0, 0)),
            pl.BlockSpec((1, choose.shape[1], 1), lambda s: (late(s), 0, 0)),
            whole((2, width)),
            whole(feed_keep.shape),
            whole(feed_taken.shape),
            ANY,
            ANY,
            ANY,
        ],
        [
            whole((3, block, local)),
            whole((slots, block, local)),
            whole((2, block, units)),
            whole((small_rows, width)),
            ANY,
            ANY,
        ],
        [
            shape_of((3, block, local), F32),
            shape_of((slots, block, local), F32),
            shape_of((2, block, units), F32),
            shape_of((small_rows, width), F32),
            shape_of((frames, 2, 2, 2, span, width)),
            shape_of((frames, 2, 2, 2, span, width)),
        ],
        scratch,
        2 * frames * places * width * local * 8,
    )(
        heads,
        grad_mixed,
        project,
        normed.reshape(frames * places, width),
        tokens,
        extra[:, None, :],
        gain,
        carried,
        choose,
        gains_grad,
        feed_keep,
        feed_taken,
        result_near,
        result_far,
        temporal_grad.reshape((2, slots) + block_shape),
    )


def finish(output, grad_tokens, own, timed, feed, small, table_rows):
    frames, places, width = output.shape
    block = width // lax.axis_size("wide")
    local = own.shape[-1]
    units = feed.shape[-1]

    def kernel(
        output_ref,
        grad_ref,
        own_ref,
        timed_ref,
        feed_ref,
        small_ref,
        output_out,
        grad_out,
        gains_out,
        table_out,
        project1_out,
        merge1_out,
        project2_out,
        merge2_out,
        expand_out,
        reduce_out,
    ):
        output_out[...] = output_ref[...]
        grad_out[...] = grad_ref[...].astype(F32)

        @pl.when(pl.program_id(0) == 0)
        def _():
            project1_out[...] = own_ref[...]
            merge1_out[...] = timed_ref[0].T
            merge2_out[...] = timed_ref[1].T
            project2_out[...] = timed_ref[2:]
            expand_out[...] = feed_ref[0]
            reduce_out[...] = feed_ref[1].T
            me = lax.axis_index("wide")
            total = jnp.zeros((small_ref.shape[0], block), F32)
            for w in range(width // block):
                total += jnp.where(me == w, small_ref[:, w * block : (w + 1) * block], 0.0)
            gains_out[...] = total[:3]
            table_out[...] = total[3 : 3 + table_rows]

    frame = pl.BlockSpec((1, places, width), lambda f: (f, 0, 0))
    shapes = [
        (3, block),
        (table_rows, block),
        own.shape,
        (local, block),
        (3, block, local),
        (local, block),
        (block, units),
        (units, block),
    ]
    return call(
        kernel,
        (frames,),
        [frame, frame] + [whole(part.shape) for part in (own, timed, feed, small)],
        [frame, frame] + [whole(shape) for shape in shapes],
        [shape_of(output.shape), shape_of(output.shape, F32)]
        + [shape_of(shape, F32) for shape in shapes],
        moved=30 * 2**20,
    )(output, grad_tokens, own, timed, feed, small)


def swap(value, axis, bit):
    size = lax.axis_size(axis)
    return lax.ppermute(value, axis, [(i, i ^ bit) for i in range(size)])


def after(value, *earlier):
    return lax.optimization_barrier((value,) + earlier)[0]


def body(
    tokens,
    frame_counts,
    actions,
    action_table,
    norm_gains,
    spatial_project,
    spatial_merge,
    temporal_project,
    temporal_merge,
    expand_weight,
    reduce_weight,
    grad_out,
):
    frames_dev, tokens_frame, width = tokens.shape
    wide_me, narrow_me = lax.axis_index("wide"), lax.axis_index("narrow")
    x_me = wide_me % 2
    span = tokens_frame // 8
    rows = 2 * frames_dev * span
    spatial_project = spatial_project.transpose(1, 0, 2)
    temporal_project = temporal_project.transpose(1, 0, 2)

    def keep_of(wide_place):
        frame_ids = wide_place * frames_dev + jnp.arange(frames_dev, dtype=jnp.int32)
        clip_places = jnp.arange(frame_counts.shape[0], dtype=jnp.int32)
        clip_count = jnp.sum(
            jnp.where((frame_ids // FRAMES)[:, None] == clip_places[None, :], frame_counts[None, :], 0),
            axis=1,
        )
        return (frame_ids % FRAMES < clip_count).astype(F32)

    keep_place = jnp.concatenate([keep_of(wide_me), keep_of(wide_me + 1 - 2 * x_me)])
    keep_place = jnp.broadcast_to(keep_place[:, None], (2 * frames_dev, span)).reshape(rows, 1)
    choose = (
        actions[:, None] == jnp.arange(action_table.shape[0], dtype=jnp.int32)[None, :]
    ).astype(BF16)
    extra = jnp.dot(choose, action_table, preferred_element_type=F32)

    (
        normed1,
        heads1,
        hidden1,
        normed2,
        heads2,
        mixed2,
        hidden2,
        normed3,
        normed3_first,
        normed3_second,
        mixed1,
        grad_result,
        grad_result_far,
        expand_pair,
        reduce_pair,
        merge1_all,
        project_all,
        merge2_all,
    ) = attention_forward(
        tokens,
        extra,
        norm_gains,
        spatial_project,
        spatial_merge,
        temporal_project,
        temporal_merge,
        expand_weight,
        reduce_weight,
        grad_out,
        keep_place,
    )
    mixed1 = mixed1.reshape(4, rows, mixed1.shape[-1])

    grad_result = grad_result.reshape(rows, width)
    grad_result_far = grad_result_far.reshape(rows, width)
    first_far = swap(normed3_first, "narrow", 2)
    second_far = swap(normed3_second, "narrow", 2)
    near = feed_forward(normed3, grad_result, keep_place, expand_pair, reduce_pair)
    first_far = after(first_far, near[0])
    first = feed_forward(first_far, grad_result_far, keep_place, expand_pair, reduce_pair, 0)
    second_far = after(second_far, first[0])
    second = feed_forward(second_far, grad_result_far, keep_place, expand_pair, reduce_pair, 1)
    grad_first = swap(first[4], "narrow", 2)
    grad_second = swap(second[4], "narrow", 2)
    feed_keep, feed_send = feed_outer(
        [normed3, first_far, second_far],
        [near[1], first[1], second[1]],
        [near[2], first[2], second[2]],
        [near[0], first[0], second[0]],
    )

    branch2_grad, grad_heads2, branch1_grad, grad_mixed1, carried, gain_three, gain_two = temporal_backward(
        near[4],
        after(grad_first, feed_keep),
        grad_second,
        hidden2,
        hidden1,
        grad_result,
        keep_place,
        norm_gains,
        heads2,
        merge2_all,
        project_all,
        merge1_all,
    )
    branch3_far = jnp.concatenate(
        [
            swap(after(first[3], grad_second), "narrow", 2),
            swap(after(second[3], grad_second), "narrow", 2),
        ]
    )
    feed_taken = swap(after(feed_send, grad_second), "wide", 1)
    branch3 = near[3].astype(F32) + branch3_far.astype(F32)
    result = (hidden2 + keep_place * branch3).astype(BF16).reshape(2, frames_dev, span, width)
    temporal_grad, grad_mixed1, carried, result_far = temporal_outer(
        grad_mixed1, carried, result, mixed1, branch1_grad, mixed2, branch2_grad, normed2, grad_heads2
    )

    project1_grad, temporal_grad, feed_grad, small, output, grad_tokens = spatial_backward(
        heads1,
        grad_mixed1,
        spatial_project,
        normed1,
        tokens,
        extra,
        norm_gains[0:1],
        carried,
        choose.astype(F32)[:, :, None],
        jnp.concatenate([gain_two, gain_three]),
        result,
        result_far,
        temporal_grad,
        feed_keep,
        feed_taken,
    )
    (
        output,
        grad_tokens,
        gains_grad,
        table_grad,
        project1_grad,
        merge1_grad,
        project2_grad,
        merge2_grad,
        expand_grad,
        reduce_grad,
    ) = finish(
        output.reshape(tokens.shape),
        grad_tokens.reshape(tokens.shape),
        project1_grad,
        temporal_grad,
        feed_grad,
        small,
        action_table.shape[0],
    )
    return (
        output,
        grad_tokens,
        gains_grad,
        table_grad,
        project1_grad.transpose(1, 0, 2),
        merge1_grad,
        project2_grad.transpose(1, 0, 2),
        merge2_grad,
        expand_grad,
        reduce_grad,
    )


def solution(mesh):
    return jax.shard_map(
        body,
        mesh=mesh,
        in_specs=(
            P("wide", None, None),
            P(),
            P("wide"),
            P(),
            P(),
            P(None, None, "narrow"),
            P("narrow", None),
            P(None, None, "narrow"),
            P("narrow", None),
            P(None, "narrow"),
            P("narrow", None),
            P("wide", None, None),
        ),
        out_specs=(
            P("wide", None, None),
            P("wide", None, None),
            P(None, "wide"),
            P(None, "wide"),
            P("wide", None, "narrow"),
            P("narrow", "wide"),
            P("wide", None, "narrow"),
            P("narrow", "wide"),
            P("wide", "narrow"),
            P("narrow", "wide"),
        ),
        check_vma=False,
    )
```

```python
import jax
import jax.numpy as jnp
from jax import lax
from jax.experimental import pallas as pl
from jax.experimental.pallas import tpu as pltpu
from jax.sharding import PartitionSpec as P

HD = 64
FRAMES = 16
GROUP = 16
PAIR = 2 * HD

EPSILON = 1e-06
NEGATIVE = -1e30
F32 = jnp.float32
BF16 = jnp.bfloat16
VMEM_LIMIT = 56 * 1024 * 1024
NN = (((1,), (0,)), ((), ()))
NT = (((1,), (1,)), ((), ()))
TN = (((0,), (0,)), ((), ()))


def mm(left, right, form=NN):
    return lax.dot_general(left, right, form, preferred_element_type=F32)


def root(value):
    return lax.rsqrt(jnp.mean(value * value, axis=-1, keepdims=True) + EPSILON)


def norm_back(value, gain, incoming):
    scale = root(value)
    scaled = gain * incoming
    inner = jnp.mean(scaled * value, axis=-1, keepdims=True)
    back = scale * scaled - (scale * scale * scale) * inner * value
    return back, jnp.sum(incoming * value * scale, axis=0, keepdims=True)


def sides():
    lane = lax.broadcasted_iota(jnp.int32, (1, PAIR), 1)
    low = (lane < HD).astype(F32)
    return lane < HD, low.astype(BF16), (1.0 - low).astype(BF16)


def attend_pair(queries, key_rows, value_rows, allowed):
    is_low, low, high = sides()
    mixed = []
    for side in (low, high):
        scores = mm(queries * (side * HD ** (-0.5)), key_rows, NT)
        if allowed is not None:
            scores = jnp.where(allowed, scores, NEGATIVE)
        shares = jnp.exp(scores - jnp.max(scores, axis=-1, keepdims=True))
        shares = shares * (1.0 / jnp.sum(shares, axis=-1, keepdims=True))
        mixed.append(mm(shares.astype(BF16), value_rows))
    return jnp.where(is_low, mixed[0], mixed[1]).astype(BF16)


def attend_back_pair(queries, key_rows, value_rows, grad_mixed, allowed):
    factor = HD ** (-0.5)
    is_low, low, high = sides()
    parts = []
    for side in (low, high):
        scores = mm(key_rows, queries * (side * factor), NT)
        if allowed is not None:
            scores = jnp.where(allowed, scores, NEGATIVE)
        chances = jnp.exp(scores - jnp.max(scores, axis=0, keepdims=True))
        chances = chances * (1.0 / jnp.sum(chances, axis=0, keepdims=True))
        grad_chances = mm(value_rows, grad_mixed * side, NT)
        shift = jnp.sum(grad_chances * chances, axis=0, keepdims=True)
        grad_scores = (chances * (grad_chances - shift)).astype(BF16)
        parts.append(
            (
                mm(grad_scores, key_rows, TN) * factor,
                mm(grad_scores, queries) * factor,
                mm(chances.astype(BF16), grad_mixed),
            )
        )
    return [jnp.where(is_low, a, b).astype(BF16) for a, b in zip(parts[0], parts[1])]


def whole(shape):
    return pl.BlockSpec(shape, lambda *_: (0,) * len(shape))


def call(kernel, grid, in_specs, out_specs, out_shape, scratch=(), flops=0, moved=0):
    return pl.pallas_call(
        kernel,
        grid=grid,
        in_specs=in_specs,
        out_specs=out_specs,
        out_shape=out_shape,
        scratch_shapes=list(scratch),
        compiler_params=pltpu.CompilerParams(vmem_limit_bytes=VMEM_LIMIT),
        cost_estimate=pl.CostEstimate(flops=flops, bytes_accessed=moved, transcendentals=0),
    )


def shape_of(shape, kind=BF16):
    return jax.ShapeDtypeStruct(shape, kind)


def place_masks(x_me, frames_all, transposed):
    rows = frames_all * GROUP
    shape = (rows, rows)
    query = lax.broadcasted_iota(jnp.int32, shape, 1 if transposed else 0)
    key = lax.broadcasted_iota(jnp.int32, shape, 0 if transposed else 1)
    query_frame = (query // GROUP + x_me * (frames_all // 2)) % frames_all
    key_frame = (key // GROUP + x_me * (frames_all // 2)) % frames_all
    return (query % GROUP == key % GROUP) & (key_frame <= query_frame)


RATE = 0.7978845608028654
CUBIC = 0.044715


def feed_forward(normed, grad, keep, expand, reduce, which=0):
    rows, width = normed.shape
    cores, _, units = expand.shape
    block = 512
    per = units // block

    def kernel(
        normed_ref,
        grad_ref,
        keep_ref,
        expand_ref,
        reduce_ref,
        active_ref,
        inner_ref,
        grad_branch_ref,
        branch_ref,
        grad_normed_ref,
        branch_sum,
        grad_sum,
    ):
        step = pl.program_id(0)

        @pl.when(step == 0)
        def _():
            grad_branch_ref[...] = (keep_ref[...] * grad_ref[...].astype(F32)).astype(BF16)
            branch_sum[...] = jnp.zeros_like(branch_sum)
            grad_sum[...] = jnp.zeros_like(grad_sum)

        inner = mm(normed_ref[...], expand_ref[0])
        grad_active = mm(grad_branch_ref[...], reduce_ref[0], NT)
        square = inner * inner
        bend = jnp.tanh(RATE * inner * (1.0 + CUBIC * square))
        half = 0.5 * (1.0 + bend)
        active = (inner * half).astype(BF16)
        slope = half + (0.5 * RATE) * inner * (1.0 - bend * bend) * (1.0 + (3.0 * CUBIC) * square)
        grad_inner = (grad_active * slope).astype(BF16)
        active_ref[...] = active
        inner_ref[...] = grad_inner
        branch_sum[...] += mm(active, reduce_ref[0])
        grad_sum[...] += mm(grad_inner, expand_ref[0], NT)

        @pl.when(step == cores * per - 1)
        def _():
            branch_ref[...] = branch_sum[...].astype(BF16)
            grad_normed_ref[...] = grad_sum[...].astype(BF16)

    full = whole((rows, width))
    return call(
        kernel,
        (cores * per,),
        [
            full,
            pl.BlockSpec((rows, width), lambda j: (which, 0)),
            pl.BlockSpec((rows, 1), lambda j: (which, 0)),
            pl.BlockSpec((1, width, block), lambda j: (j // per, 0, j % per)),
            pl.BlockSpec((1, block, width), lambda j: (j // per, j % per, 0)),
        ],
        [
            pl.BlockSpec((rows, block), lambda j: (0, j)),
            pl.BlockSpec((rows, block), lambda j: (0, j)),
            full,
            full,
            full,
        ],
        [
            shape_of((rows, cores * units)),
            shape_of((rows, cores * units)),
            shape_of((rows, width)),
            shape_of((rows, width)),
            shape_of((rows, width)),
        ],
        scratch=[pltpu.VMEM((rows, width), F32), pltpu.VMEM((rows, width), F32)],
        flops=8 * rows * width * cores * units,
        moved=18 * 2**20,
    )(normed, grad, keep, expand, reduce)


def temporal_backward(
    grad_near, grad_first, grad_second, hidden2, hidden1, grad_result, keep, gains, heads, merge2, project, merge1
):
    rows, width = hidden1.shape
    local = merge1.shape[1]
    span = rows // FRAMES
    group_rows = FRAMES * GROUP

    def kernel(
        near_ref,
        first_ref,
        second_ref,
        hidden2_ref,
        hidden1_ref,
        result_ref,
        keep_ref,
        gains_ref,
        heads_ref,
        merge2_ref,
        project_ref,
        merge1_ref,
        branch2_ref,
        grad_heads_ref,
        branch1_ref,
        mixed1_ref,
        carried_ref,
        gain3_ref,
        gain2_ref,
        grad_hidden,
        grad_normed,
        grad_mixed,
    ):
        step = pl.program_id(0)

        @pl.when(step == 0)
        def _():
            far = jnp.concatenate([first_ref[...], second_ref[...]])
            incoming = near_ref[...].astype(F32) + far.astype(F32)
            back, gain3_ref[...] = norm_back(hidden2_ref[...], gains_ref[2:3], incoming)
            total = result_ref[...].astype(F32) + back
            grad_hidden[...] = total
            branch2_ref[...] = (keep_ref[...] * total).astype(BF16)
            grad_normed[...] = jnp.zeros_like(grad_normed)

        back_mixed = mm(branch2_ref[...], merge2_ref[0], NT).astype(BF16)
        grad_mixed[...] = back_mixed.reshape(FRAMES, span, local)
        allowed = place_masks(lax.axis_index("wide") % 2, FRAMES, True)
        for g in range(span // GROUP):
            band = pl.ds(g * GROUP, GROUP)
            for at in range(0, local, PAIR):
                part = pl.ds(at, PAIR)
                terms = [heads_ref[0, c, :, band, part].reshape(group_rows, PAIR) for c in range(3)]
                grad = grad_mixed[:, band, part].reshape(group_rows, PAIR)
                grads = attend_back_pair(*terms, grad, allowed)
                for c in range(3):
                    grad_heads_ref[0, c, :, band, part] = grads[c].reshape(FRAMES, GROUP, PAIR)
        total = mm(grad_heads_ref[0, 0].reshape(rows, local), project_ref[0, 0], NT)
        for c in range(1, 3):
            total += mm(grad_heads_ref[0, c].reshape(rows, local), project_ref[0, c], NT)
        grad_normed[...] += total

        @pl.when(step == 3)
        def _():
            back, gain2_ref[...] = norm_back(hidden1_ref[...], gains_ref[1:2], grad_normed[...])
            total = grad_hidden[...] + back
            carried_ref[...] = total.astype(BF16)
            branch1_ref[...] = (keep_ref[...] * total).astype(BF16)
            for n in range(4):
                mixed1_ref[n] = mm(branch1_ref[...], merge1_ref[n], NT).astype(BF16)

    full = whole((rows, width))
    row = whole((1, width))
    return call(
        kernel,
        (4,),
        [
            full,
            whole((rows // 2, width)),
            whole((rows // 2, width)),
            full,
            full,
            full,
            whole((rows, 1)),
            whole((3, width)),
            pl.BlockSpec((1, 3, FRAMES, span, local), lambda n: (n, 0, 0, 0, 0)),
            pl.BlockSpec((1, local, width), lambda n: (n, 0, 0)),
            pl.BlockSpec((1, 3, width, local), lambda n: (n, 0, 0, 0)),
            whole((4, local, width)),
        ],
        [
            full,
            pl.BlockSpec((1, 3, FRAMES, span, local), lambda n: (n, 0, 0, 0, 0)),
            full,
            whole((4, rows, local)),
            full,
            row,
            row,
        ],
        [
            shape_of((rows, width)),
            shape_of((4, 3, FRAMES, span, local)),
            shape_of((rows, width)),
            shape_of((4, rows, local)),
            shape_of((rows, width)),
            shape_of((1, width), F32),
            shape_of((1, width), F32),
        ],
        scratch=[
            pltpu.VMEM((rows, width), F32),
            pltpu.VMEM((rows, width), F32),
            pltpu.VMEM((FRAMES, span, local), BF16),
        ],
        flops=2 * rows * width * width * 8,
        moved=30 * 2**20,
    )(grad_near, grad_first, grad_second, hidden2, hidden1, grad_result, keep, gains, heads, merge2, project, merge1)


def here():
    wide, narrow = lax.axis_index("wide"), lax.axis_index("narrow")
    return wide, narrow, wide % 2, narrow // 2, narrow % 2


def other(wide, narrow, x, y, core):
    if x:
        wide = wide + 1 - 2 * (wide % 2)
    if y:
        narrow = (narrow + 2) % 4
    if core:
        narrow = narrow + 1 - 2 * (narrow % 2)
    return wide, narrow


def beyond(wide, narrow):
    return wide + 2 - 4 * ((wide // 2) % 2), narrow


def place_of(wide, narrow, span):
    return pl.multiple_of(((wide % 2) * 4 + narrow) * span, span)


def remote(src, dst, sems, i, device):
    return pltpu.make_async_remote_copy(
        src_ref=src,
        dst_ref=dst,
        send_sem=sems.at[0, i],
        recv_sem=sems.at[1, i],
        device_id=device,
        device_id_type=pl.DeviceIdType.MESH,
    )


def greet(devices):
    barrier = pltpu.get_barrier_semaphore()
    for device in devices:
        pl.semaphore_signal(
            barrier, inc=1, device_id=device, device_id_type=pl.DeviceIdType.MESH
        )
    pl.semaphore_wait(barrier, len(devices))


OTHERS = [(x, y, c) for x in range(2) for y in range(2) for c in range(2) if x + y + c > 0]
ANY = pl.BlockSpec(memory_space=pl.ANY)


def comm_call(kernel, number, grid, in_specs, out_specs, out_shape, scratch, flops, moved=30 * 2**20):
    return pl.pallas_call(
        kernel,
        grid=grid,
        in_specs=in_specs,
        out_specs=out_specs,
        out_shape=out_shape,
        scratch_shapes=scratch,
        compiler_params=pltpu.CompilerParams(
            vmem_limit_bytes=VMEM_LIMIT, collective_id=number, has_side_effects=True
        ),
        cost_estimate=pl.CostEstimate(flops=flops, bytes_accessed=moved, transcendentals=0),
    )


def attention_forward(
    tokens,
    extra,
    gains,
    project,
    merge1,
    project2,
    merge2,
    expand,
    reduce,
    grad_out,
    keep,
):
    frames, places, width = tokens.shape
    local = project.shape[-1]
    span = places // 8
    rows = FRAMES * span
    group_rows = FRAMES * GROUP
    half = frames // 2
    shards = (merge1, project2[0], project2[1], project2[2], merge2)
    count = len(shards)

    def kernel(
        tokens_ref,
        extra_ref,
        gains_ref,
        project_ref,
        keep_ref,
        all_tokens,
        all_extra,
        grad_ref,
        expand_ref,
        reduce_ref,
        merge1_ref,
        project2_ref,
        merge2_ref,
        normed_ref,
        heads_ref,
        hidden1_ref,
        normed2_ref,
        heads2_ref,
        mixed2_ref,
        hidden2_ref,
        normed3_ref,
        first_ref,
        second_ref,
        mixed_out,
        grad_near,
        grad_far,
        expand_pair,
        reduce_pair,
        merge1_out,
        project2_out,
        merge2_out,
        mixed_ref,
        mixed_all,
        tokens_place,
        extra_place,
        merge1_all,
        project2_all,
        merge2_all,
        local_sems,
        move_sems,
        shard_sems,
        mixed_sems,
        *stage,
    ):
        step = pl.program_id(0)
        wide, narrow, x_me, _, _ = here()
        half_me = (wide // 2) % 2
        x_other = other(wide, narrow, 1, 0, 0)
        y_other = other(wide, narrow, 0, 1, 0)
        core_other = other(wide, narrow, 0, 0, 1)
        z_other = beyond(wide, narrow)
        mine = pl.ds(place_of(wide, narrow, span), span)
        near_y = pl.ds(place_of(*y_other, span), span)
        shard = [merge1_ref] + [project2_ref.at[c] for c in range(3)] + [merge2_ref]
        full = [merge1_all] + [project2_all.at[:, c] for c in range(3)] + [merge2_all]

        own = [
            (expand_ref, expand_pair.at[0]),
            (reduce_ref, reduce_pair.at[0]),
            (grad_ref.at[:, mine], grad_near.at[0]),
            (grad_ref.at[:, near_y], grad_far.at[0]),
        ]
        into = [
            pltpu.make_async_copy(a, v, local_sems.at[0, i])
            for i, ((a, _), v) in enumerate(zip(own, stage))
        ]
        back = [
            pltpu.make_async_copy(v, b, local_sems.at[1, i])
            for i, ((_, b), v) in enumerate(zip(own, stage))
        ]
        inside = [
            (all_tokens.at[:, mine], tokens_place.at[0]),
            (all_extra, extra_place.at[0]),
        ] + [(shard[k], full[k].at[0]) for k in range(count)]
        inside = [
            pltpu.make_async_copy(a, b, local_sems.at[0, 4 + i]) for i, (a, b) in enumerate(inside)
        ]
        leaving = [
            (mixed_all, mixed_out),
            (merge1_all, merge1_out),
            (project2_all, project2_out),
            (merge2_all, merge2_out),
        ]
        leaving = [
            pltpu.make_async_copy(a, b, local_sems.at[1, 4 + i]) for i, (a, b) in enumerate(leaving)
        ]
        far = pl.ds(place_of(*x_other, span), span)
        far_y = pl.ds(place_of(*other(wide, narrow, 1, 1, 0), span), span)
        first = [
            remote(all_tokens.at[:, far], tokens_place.at[1], move_sems, 0, x_other),
            remote(all_extra, extra_place.at[1], move_sems, 1, x_other),
            remote(expand_ref, expand_pair.at[1], move_sems, 2, core_other),
            remote(reduce_ref, reduce_pair.at[1], move_sems, 3, core_other),
        ]
        last = [
            remote(grad_ref.at[:, far], grad_near.at[1], move_sems, 4, x_other),
            remote(grad_ref.at[:, far_y], grad_far.at[1], move_sems, 5, x_other),
        ]

        def part(k, which):
            count = shards[k].shape[0] // 2
            return pl.ds(pl.multiple_of(which * count, count), count)

        def over_core(k):
            return remote(shard[k], full[k].at[1], shard_sems, 5 * k, core_other)

        def over_y(k):
            some = part(k, half_me)
            return remote(shard[k].at[some], full[k].at[2, some], shard_sems, 5 * k + 1, y_other)

        def onward(k, which, i, device, slot):
            some = part(k, which)
            return remote(full[k].at[2, some], full[k].at[slot, some], shard_sems, 5 * k + i, device)

        def over_z(k):
            return onward(k, half_me, 2, z_other, 2)

        def near_half(k):
            return onward(k, half_me, 3, core_other, 3)

        def far_half(k):
            return onward(k, 1 - half_me, 4, core_other, 3)

        def forward(k):
            over_y(k).wait_recv()
            over_z(k).start()
            near_half(k).start()

        def complete(k):
            over_z(k).wait_recv()
            far_half(k).start()

        def mixed_copies(chunk):
            copies = []
            some = pl.ds(chunk * half, half)
            for i, (x, y, c) in enumerate(OTHERS):
                device = other(wide, narrow, x, y, c)
                copies.append(
                    remote(
                        mixed_ref.at[some, pl.ds(place_of(*device, span), span)],
                        mixed_all.at[2 * y + c, x, some],
                        mixed_sems,
                        7 * chunk + i,
                        device,
                    )
                )
            here_copy = pltpu.make_async_copy(
                mixed_ref.at[some, mine], mixed_all.at[0, 0, some], local_sems.at[chunk, 11]
            )
            return copies + [here_copy]

        @pl.when(step == 0)
        def _():
            greet([other(wide, narrow, *o) for o in OTHERS] + [z_other])
            for k in range(3):
                over_y(k).start()
            for copy in first:
                copy.start()
            for k in range(count):
                over_core(k).start()
            for copy in into + inside:
                copy.start()

        @pl.when(step == 2)
        def _():
            for copy in into:
                copy.wait()
            for copy in back:
                copy.start()

        @pl.when(step < frames)
        def _():
            start = tokens_ref[0].astype(F32) + extra_ref[0]
            normed = (start * root(start) * gains_ref[0:1]).astype(BF16)
            normed_ref[0] = normed
            for c in range(3):
                heads_ref[c, 0] = mm(normed, project_ref[c]).astype(BF16)
            for at in range(0, local, PAIR):
                lanes = pl.ds(at, PAIR)
                mixed_ref[step, :, lanes] = attend_pair(
                    heads_ref[0, 0, :, lanes],
                    heads_ref[1, 0, :, lanes],
                    heads_ref[2, 0, :, lanes],
                    None,
                )

        @pl.when(step == 2)
        def _():
            forward(0)

        @pl.when(step == half - 1)
        def _():
            for copy in mixed_copies(0):
                copy.start()

        @pl.when(step == half)
        def _():
            forward(1)

        @pl.when(step == half + 1)
        def _():
            complete(0)

        @pl.when(step == half + 2)
        def _():
            forward(2)

        @pl.when(step == frames - 1)
        def _():
            for copy in mixed_copies(1):
                copy.start()
            over_y(3).start()
            over_y(4).start()
            for copy in last:
                copy.start()
            complete(1)

        @pl.when(step == frames)
        def _():
            for copy in inside:
                copy.wait()
            over_core(0).wait_recv()
            near_half(0).wait_recv()
            far_half(0).wait_recv()
            first[0].wait_recv()
            first[1].wait_recv()
            for copy in mixed_copies(0) + mixed_copies(1):
                copy.wait()
            leaving[0].start()
            leaving[1].start()
            branch = mm(mixed_all[0].reshape(rows, local), merge1_all[0])
            for n in range(1, 4):
                branch += mm(mixed_all[n].reshape(rows, local), merge1_all[n])
            begin = tokens_place[...].astype(F32) + extra_place[...]
            hidden1 = begin.reshape(rows, width) + keep_ref[...] * branch
            hidden1_ref[...] = hidden1
            hidden2_ref[...] = hidden1
            normed2_ref[...] = (hidden1 * root(hidden1) * gains_ref[1:2]).astype(BF16)

        @pl.when(step == frames + 1)
        def _():
            complete(2)
            forward(3)
            for k in range(1, count):
                over_core(k).wait_recv()

        @pl.when(step == frames + 2)
        def _():
            forward(4)
            complete(3)
            over_z(4).wait_recv()
            far_half(4).start()

        @pl.when(step == frames + 3)
        def _():
            for k in range(1, count):
                near_half(k).wait_recv()
                far_half(k).wait_recv()
            leaving[2].start()
            leaving[3].start()

        @pl.when(step >= frames)
        def _():
            n = step - frames
            for c in range(3):
                head = mm(normed2_ref[...], project2_all[n, c]).astype(BF16)
                heads2_ref[0, c] = head.reshape(FRAMES, span, local)
            allowed = place_masks(x_me, FRAMES, False)
            for g in range(span // GROUP):
                band = pl.ds(g * GROUP, GROUP)
                for at in range(0, local, PAIR):
                    lanes = pl.ds(at, PAIR)
                    terms = [
                        heads2_ref[0, c, :, band, lanes].reshape(group_rows, PAIR) for c in range(3)
                    ]
                    mixed = attend_pair(*terms, allowed)
                    mixed2_ref[0, :, band, lanes] = mixed.reshape(FRAMES, GROUP, PAIR)
            merged = mm(mixed2_ref[0].reshape(rows, local), merge2_all[n])
            hidden2_ref[...] += keep_ref[...] * merged

        @pl.when(step == frames + 3)
        def _():
            hidden2 = hidden2_ref[...]
            normed3 = (hidden2 * root(hidden2) * gains_ref[2:3]).astype(BF16)
            normed3_ref[...] = normed3
            first_ref[...] = normed3[: rows // 2]
            second_ref[...] = normed3[rows // 2 :]
            for copy in first[2:] + last:
                copy.wait()
            for copy in first[:2]:
                copy.wait_send()
            for copy in back + leaving:
                copy.wait()
            for k in range(count):
                for copy in (over_core(k), over_y(k), over_z(k), near_half(k), far_half(k)):
                    copy.wait_send()

    def frame(step):
        return jnp.minimum(step, frames - 1)

    def turn(step):
        return jnp.maximum(step - frames, 0)

    full = whole((rows, width))
    return comm_call(
        kernel,
        0,
        (frames + 4,),
        [
            pl.BlockSpec((1, places, width), lambda s: (frame(s), 0, 0)),
            pl.BlockSpec((1, 1, width), lambda s: (frame(s), 0, 0)),
            whole((3, width)),
            whole(project.shape),
            whole((rows, 1)),
        ]
        + [ANY] * 8,
        [
            pl.BlockSpec((1, places, width), lambda s: (frame(s), 0, 0)),
            pl.BlockSpec((3, 1, places, local), lambda s: (0, frame(s), 0, 0)),
            full,
            full,
            pl.BlockSpec((1, 3, FRAMES, span, local), lambda s: (turn(s), 0, 0, 0, 0)),
            pl.BlockSpec((1, FRAMES, span, local), lambda s: (turn(s), 0, 0, 0)),
            full,
            full,
            whole((rows // 2, width)),
            whole((rows // 2, width)),
        ]
        + [ANY] * 8,
        [
            shape_of((frames, places, width)),
            shape_of((3, frames, places, local)),
            shape_of((rows, width), F32),
            shape_of((rows, width)),
            shape_of((4, 3, FRAMES, span, local)),
            shape_of((4, FRAMES, span, local)),
            shape_of((rows, width), F32),
            shape_of((rows, width)),
            shape_of((rows // 2, width)),
            shape_of((rows // 2, width)),
            shape_of((4, 2, frames, span, local)),
            shape_of((2, frames, span, width)),
            shape_of((2, frames, span, width)),
            shape_of((2,) + expand.shape),
            shape_of((2,) + reduce.shape),
            shape_of((4,) + merge1.shape),
            shape_of((4,) + project2.shape),
            shape_of((4,) + merge2.shape),
        ],
        [
            pltpu.VMEM((frames, places, local), BF16),
            pltpu.VMEM((4, 2, frames, span, local), BF16),
            pltpu.VMEM((2, frames, span, width), BF16),
            pltpu.VMEM((2, frames, 1, width), F32),
            pltpu.VMEM((4,) + merge1.shape, BF16),
            pltpu.VMEM((4,) + project2.shape, BF16),
            pltpu.VMEM((4,) + merge2.shape, BF16),
            pltpu.SemaphoreType.DMA((2, 12)),
            pltpu.SemaphoreType.DMA((2, 6)),
            pltpu.SemaphoreType.DMA((2, 5 * count)),
            pltpu.SemaphoreType.DMA((2, 14)),
            pltpu.VMEM(expand.shape, BF16),
            pltpu.VMEM(reduce.shape, BF16),
            pltpu.VMEM((frames, span, width), BF16),
            pltpu.VMEM((frames, span, width), BF16),
        ],
        2 * frames * places * width * local * 4 + 2 * rows * width * width * 6,
    )(
        tokens,
        extra[:, None, :],
        gains,
        project,
        keep,
        tokens,
        extra[:, None, :],
        grad_out,
        expand,
        reduce,
        merge1,
        project2,
        merge2,
    )


def feed_outer(normed, grad_inner, grad_branch, active):
    width = normed[0].shape[1]
    units = active[0].shape[1] // 2
    ends = [0]
    for part in normed:
        ends.append(ends[-1] + part.shape[0])
    rows, count = ends[-1], len(normed)
    block = 512
    per = units // block
    wide = lax.axis_size("wide")
    split = (2, wide // 2, 2, width // wide, block)

    def kernel(*refs):
        normed_refs, branch_refs = refs[:count], refs[count : 2 * count]
        inner_refs, active_refs = refs[2 * count : 3 * count], refs[3 * count : 4 * count]
        keep_ref, send_ref, left, right, total, given, taken, sems = refs[4 * count :]
        step = pl.program_id(0)
        wide, narrow, x_me, _, _ = here()
        core_other = other(wide, narrow, 0, 0, 1)

        def over(j):
            return remote(given.at[j], taken.at[j], sems, j, core_other)

        @pl.when(step == 0)
        def _():
            for k in range(count):
                left[:, ends[k] : ends[k + 1]] = normed_refs[k][...].T
                right[:, ends[k] : ends[k + 1]] = branch_refs[k][...].T

        def product(side, parts):
            out = mm(side[:, : ends[1]], parts[0][...])
            for k in range(1, count):
                out += mm(side[:, ends[k] : ends[k + 1]], parts[k][...])
            return out

        expand = product(left, inner_refs)
        reduce = product(right, active_refs)

        @pl.when(step == 0)
        def _():
            greet([core_other])

        @pl.when(step < per)
        def _():
            given[step, 0] = expand.astype(BF16)
            given[step, 1] = reduce.astype(BF16)
            over(step).start()

        @pl.when(step >= per)
        def _():
            j = step - per
            over(j).wait_recv()
            half = split[1:]
            total[0] = (expand + taken[j, 0].astype(F32)).astype(BF16).reshape(half)
            total[1] = (reduce + taken[j, 1].astype(F32)).astype(BF16).reshape(half)
            out = keep_ref.shape
            keep_ref[...] = total[:, :, pl.ds(x_me, 1)].reshape(out)
            send_ref[...] = total[:, :, pl.ds(1 - x_me, 1)].reshape(out)

        @pl.when(step == 2 * per - 1)
        def _():
            for j in range(per):
                over(j).wait_send()

    def columns(part):
        return pl.BlockSpec((part.shape[0], block), lambda j: (0, (j + per) % (2 * per)))

    out = pl.BlockSpec((2, width // 2, block), lambda j: (0, 0, jnp.maximum(j - per, 0)))
    return comm_call(
        kernel,
        3,
        (2 * per,),
        [whole(part.shape) for part in normed + grad_branch]
        + [columns(part) for part in grad_inner + active],
        [out, out],
        [shape_of((2, width // 2, units))] * 2,
        [
            pltpu.VMEM((width, rows), BF16),
            pltpu.VMEM((width, rows), BF16),
            pltpu.VMEM(split, BF16),
            pltpu.VMEM((per, 2, width, block), BF16),
            pltpu.VMEM((per, 2, width, block), BF16),
            pltpu.SemaphoreType.DMA((2, per)),
        ],
        2**20,
        2**20,
    )(*normed, *grad_branch, *grad_inner, *active)


def temporal_outer(
    grad_mixed1, carried, result, mixed1, branch1, mixed2, branch2, normed2, grad_heads
):
    rows, width = branch1.shape
    local = mixed1.shape[-1]
    span = rows // FRAMES
    frames = FRAMES // 2

    def kernel(
        grad_ref,
        carried_ref,
        result_ref,
        mixed1_ref,
        branch1_ref,
        mixed2_ref,
        branch2_ref,
        normed2_ref,
        heads_ref,
        out_ref,
        grad_own,
        carried_own,
        result_far,
        left,
        given,
        taken,
        grad_stage,
        carried_stage,
        local_sems,
        sems,
    ):
        step = pl.program_id(0)
        wide, narrow, x_me, _, _ = here()
        x_other = other(wide, narrow, 1, 0, 0)
        mine = pl.ds(place_of(wide, narrow, span), span)
        copies = [
            remote(
                grad_ref.at[2 * y + c, x],
                grad_own.at[:, mine],
                sems,
                i,
                other(wide, narrow, x, y, c),
            )
            for i, (x, y, c) in enumerate(OTHERS)
        ]
        copies.append(remote(carried_ref.at[1], carried_own.at[:, x_me], sems, 7, x_other))
        copies.append(remote(result_ref.at[0], result_far, sems, 8, other(wide, narrow, 0, 1, 0)))

        def over(y):
            return remote(given.at[y], taken.at[y], sems, 9 + y, other(wide, narrow, 0, 0, 1))

        into = [
            pltpu.make_async_copy(grad_ref.at[0, 0], grad_stage, local_sems.at[0]),
            pltpu.make_async_copy(carried_ref.at[0], carried_stage, local_sems.at[1]),
        ]
        back = [
            pltpu.make_async_copy(grad_stage, grad_own.at[:, mine], local_sems.at[2]),
            pltpu.make_async_copy(carried_stage, carried_own.at[:, x_me], local_sems.at[3]),
        ]

        @pl.when(step == 0)
        def _():
            greet([other(wide, narrow, *o) for o in OTHERS])
            for copy in copies + into:
                copy.start()
            left[0] = branch1_ref[...].T
            left[1] = branch2_ref[...].T
            left[2] = normed2_ref[...].T

        terms = [(0, mixed1_ref[0]), (1, mixed2_ref[0])] + [(2, heads_ref[0, c]) for c in range(3)]
        for k, (which, term) in enumerate(terms):
            total = mm(left[which], term)

            @pl.when(step < 2)
            def _():
                given[step, k] = total.astype(BF16)

            @pl.when(step >= 2)
            def _():
                out_ref[0, k] = total.astype(BF16)

        @pl.when(step < 2)
        def _():
            over(step).start()

        @pl.when(step >= 2)
        def _():
            over(step - 2).wait_recv()
            out_ref[0] = (out_ref[0].astype(F32) + taken[step - 2].astype(F32)).astype(BF16)

        @pl.when(step == 1)
        def _():
            for copy in into:
                copy.wait()
            for copy in back:
                copy.start()

        @pl.when(step == 3)
        def _():
            for copy in copies + back:
                copy.wait()
            for y in range(2):
                over(y).wait_send()

    full = whole((rows, width))

    def turn(j):
        return 2 * (j % 2) + 1 - j // 2

    part = pl.BlockSpec((1, rows, local), lambda j: (turn(j), 0, 0))
    return comm_call(
        kernel,
        1,
        (4,),
        [ANY] * 3
        + [part, full, part, full, full]
        + [pl.BlockSpec((1, 3, rows, local), lambda j: (turn(j), 0, 0, 0))],
        [pl.BlockSpec((1, 5, width, local), lambda j: (jnp.maximum(j - 2, 0), 0, 0, 0))] + [ANY] * 3,
        [
            shape_of((2, 5, width, local)),
            shape_of((frames, 8 * span, local)),
            shape_of((frames, 2, span, width)),
            shape_of(result.shape[1:]),
        ],
        [
            pltpu.VMEM((3, width, rows), BF16),
            pltpu.VMEM((2, 5, width, local), BF16),
            pltpu.VMEM((2, 5, width, local), BF16),
            pltpu.VMEM((frames, span, local), BF16),
            pltpu.VMEM((frames, span, width), BF16),
            pltpu.SemaphoreType.DMA((4,)),
            pltpu.SemaphoreType.DMA((2, 11)),
        ],
        10 * rows * width * width,
    )(
        grad_mixed1.reshape(4, 2, frames, span, local),
        carried.reshape(2, frames, span, width),
        result,
        mixed1,
        branch1,
        mixed2.reshape(4, rows, local),
        branch2,
        normed2,
        grad_heads.reshape(4, 3, rows, local),
    )


class Halving:
    def __init__(self, slots, rows, columns, blocks, first):
        self.slots, self.rows, self.columns, self.first = slots, rows, columns, first
        self.blocks = []
        while blocks > 1:
            blocks //= 2
            self.blocks.append(blocks)

    def scratch(self):
        out = []
        for blocks in self.blocks:
            out.append(pltpu.VMEM((self.slots, blocks, 2, self.rows, self.columns), BF16))
            out.append(pltpu.VMEM((self.slots, blocks, self.rows, self.columns), BF16))
        return out

    def bind(self, refs, sems, base, wide, narrow):
        self.held, self.taken = refs[0::2], refs[1::2]
        self.sems, self.base, self.wide, self.narrow = sems, base, wide, narrow

    def bit(self, level):
        step = 2 ** (self.first + level)
        return step, (self.wide // step) % 2

    def copy(self, level):
        step, bit = self.bit(level)
        device = (self.wide + step - 2 * step * bit, self.narrow)
        return remote(
            self.held[level].at[:, :, 1 - bit],
            self.taken[level],
            self.sems,
            self.base + level,
            device,
        )

    def fill(self, level, value, slot=0):
        count = value.shape[0]
        self.held[level][slot : slot + count] = value.astype(BF16).reshape(
            (count,) + self.held[level].shape[1:]
        )

    def result(self, level):
        _, bit = self.bit(level)
        shape = self.taken[level].shape
        own = self.held[level][:, :, pl.ds(bit, 1)].reshape(shape)
        return own.astype(F32) + self.taken[level][...].astype(F32)

    def advance(self, level):
        self.copy(level).wait_recv()
        total = self.result(level)
        if level + 1 < len(self.blocks):
            self.fill(level + 1, total)
            self.copy(level + 1).start()
            return None
        return total.reshape(self.slots, self.rows, self.columns)

    def close(self):
        for level in range(len(self.blocks)):
            self.copy(level).wait_send()


FIRST = 2


def spatial_backward(
    heads,
    grad_mixed,
    project,
    normed,
    tokens,
    extra,
    gain,
    carried,
    choose,
    gains_grad,
    result_near,
    result_far,
    temporal_grad,
    feed_keep,
    feed_taken,
):
    _, frames, places, local = heads.shape
    width = project.shape[1]
    span = places // 8
    tile = width // 4
    wide_size = lax.axis_size("wide")
    half = wide_size // 2
    block = width // wide_size
    bits = wide_size.bit_length() - 1
    slots = temporal_grad.shape[1]
    units = feed_keep.shape[-1]
    last = slots - FIRST
    feed = Halving(2, block, units, half, 1)
    own = Halving(3, block, local, wide_size, 0)
    timed = Halving(slots, block, local, half, 1)
    engines = (feed, own, timed)
    levels = [len(engine.blocks) for engine in engines]
    attend_end = frames
    outer_end = attend_end + 4
    sum_end = outer_end + frames

    def kernel(
        heads_ref,
        mixed_ref,
        project_ref,
        normed_ref,
        tokens_ref,
        extra_ref,
        gain_ref,
        carried_ref,
        choose_ref,
        gains_ref,
        feed_keep_ref,
        feed_taken_ref,
        near_ref,
        far_ref,
        temporal_ref,
        own_out,
        timed_out,
        feed_out,
        small_out,
        output_ref,
        out_ref,
        grad_heads,
        partial,
        from_core,
        halved,
        from_y,
        done,
        gain_grad,
        table,
        small,
        small_taken,
        first_own,
        first_taken,
        first_sum,
        first_y,
        last_own,
        last_taken,
        last_sum,
        last_x,
        result_stage,
        local_sems,
        sems,
        move_sems,
        small_sems,
        halving_sems,
        *held,
    ):
        step = pl.program_id(0)
        wide, narrow, x_me, y_me, c_me = here()
        x_other = other(wide, narrow, 1, 0, 0)
        y_other = other(wide, narrow, 0, 1, 0)
        core_other = other(wide, narrow, 0, 0, 1)
        beyond_x = [
            (wide + 2**k - 2 ** (k + 1) * ((wide // 2**k) % 2), narrow) for k in range(1, bits)
        ]
        partners = [core_other, x_other] + beyond_x + [y_other]
        at = base = 0
        for engine, count in zip(engines, levels):
            engine.bind(held[at : at + 2 * count], halving_sems, base, wide, narrow)
            at, base = at + 2 * count, base + count

        def core_sum(f):
            return remote(partial.at[f, :, :, 1 - c_me], from_core.at[f], sems, f, core_other)

        def y_sum(f):
            return remote(halved.at[f, :, 1 - y_me], from_y.at[f], sems, frames + f, y_other)

        def y_back(f):
            return remote(done.at[f], out_ref.at[f, :, y_me, c_me], sems, 2 * frames + f, y_other)

        def core_back(f):
            return remote(done.at[f], out_ref.at[f, :, y_me, c_me], sems, 3 * frames + f, core_other)

        def core_onward(f):
            there = out_ref.at[f, :, 1 - y_me, c_me]
            return remote(there, there, sems, 4 * frames + f, core_other)

        def keep_own(f):
            return pltpu.make_async_copy(done.at[f], out_ref.at[f, :, y_me, c_me], local_sems.at[f])

        result = (near_ref.at[0], far_ref)

        def place(y):
            return y_me if y == 0 else 1 - y_me

        def result_x():
            there = output_ref.at[:, x_me, y_me, c_me]
            return remote(near_ref.at[1], there, move_sems, 0, x_other)

        def result_y():
            there = output_ref.at[:, 1 - x_me, y_me, c_me]
            return remote(there, there, move_sems, 1, y_other)

        def result_core(y):
            there = output_ref.at[:, x_me, place(y), c_me]
            return remote(result[y], there, move_sems, 2 + y, core_other)

        def result_onward(y):
            there = output_ref.at[:, 1 - x_me, place(y), c_me]
            return remote(there, there, move_sems, 4 + y, core_other)

        def result_in(y):
            return pltpu.make_async_copy(result[y], result_stage.at[y], local_sems.at[frames + y])

        def result_own(y):
            there = output_ref.at[:, x_me, place(y), c_me]
            return pltpu.make_async_copy(result_stage.at[y], there, local_sems.at[frames + 2 + y])

        early, late_slots = pl.ds(0, FIRST), pl.ds(FIRST, last)
        first_in = pltpu.make_async_copy(
            temporal_ref.at[:, early, :, x_me], first_own, local_sems.at[frames + 4]
        )
        last_in = pltpu.make_async_copy(
            temporal_ref.at[0, late_slots], last_own, local_sems.at[frames + 5]
        )
        first_over_x = remote(
            temporal_ref.at[:, early, :, 1 - x_me], first_taken, move_sems, 6, x_other
        )
        first_over_y = remote(first_sum.at[1], first_y, move_sems, 7, y_other)
        last_over_y = remote(temporal_ref.at[1, late_slots], last_taken, move_sems, 8, y_other)
        last_over_x = remote(last_sum.at[:, :, 1 - x_me], last_x, move_sems, 9, x_other)

        def small_copy(k):
            return remote(small.at[k], small_taken.at[k], small_sems, k, partners[k])

        @pl.when(step == 0)
        def _():
            greet(partners)
            last_over_y.start()
            first_over_x.start()
            feed.fill(0, feed_keep_ref[...].astype(F32) + feed_taken_ref[...].astype(F32))
            feed.copy(0).start()
            result_x().start()
            first_in.start()
            last_in.start()
            for y in range(2):
                result_core(y).start()
                result_in(y).start()
            gain_grad[...] = jnp.zeros_like(gain_grad)
            table[...] = jnp.zeros_like(table)

        @pl.when(step < attend_end)
        def _():
            rows = pl.ds(pl.multiple_of(step * places, places), places)
            for at in range(0, local, PAIR):
                lanes = pl.ds(at, PAIR)
                grads = attend_back_pair(
                    heads_ref[0, 0, :, lanes],
                    heads_ref[1, 0, :, lanes],
                    heads_ref[2, 0, :, lanes],
                    mixed_ref[0, :, lanes],
                    None,
                )
                for c in range(3):
                    grad_heads[c, rows, lanes] = grads[c]
            total = mm(grad_heads[0, rows], project_ref[0], NT)
            for c in range(1, 3):
                total += mm(grad_heads[c, rows], project_ref[c], NT)
            partial[step] = total.astype(BF16).reshape(2, 2, 2, span, width)
            core_sum(step).start()

        @pl.when((step >= 1) & (step < attend_end + 1))
        def _():
            f = step - 1
            core_sum(f).wait_recv()
            mine = partial[f, :, :, pl.ds(c_me, 1)].reshape(2, 2, span, width)
            halved[f] = (mine.astype(F32) + from_core[f].astype(F32)).astype(BF16)

        @pl.when(step == 1)
        def _():
            for y in range(2):
                result_in(y).wait()
                result_own(y).start()

        @pl.when(step == attend_end)
        def _():
            for f in range(frames // 2):
                y_sum(f).start()
            first_in.wait()
            first_over_x.wait_recv()
            first_sum[...] = (first_own[...].astype(F32) + first_taken[...].astype(F32)).astype(BF16)
            first_over_y.start()
            for f in range(frames // 2, frames):
                y_sum(f).start()
            feed.advance(0)

        @pl.when((step >= attend_end) & (step < outer_end))
        def _():
            pairs = tile // (2 * block)
            j = (step - attend_end) * pairs
            for c in range(3):
                grad = mm(normed_ref[...], grad_heads[c], TN).astype(BF16)
                own.held[0][c, pl.ds(j, pairs)] = grad.reshape(pairs, 2, block, local)

        @pl.when(step == attend_end + 2)
        def _():
            last_in.wait()
            last_over_y.wait_recv()
            last_sum[...] = (last_own[...].astype(F32) + last_taken[...].astype(F32)).astype(BF16)
            last_over_x.start()

        @pl.when(step == outer_end)
        def _():
            own.copy(0).start()
            result_x().wait_recv()
            result_y().start()
            result_onward(0).start()
            total = feed.advance(1)
            if total is not None:
                feed_out[...] = total

        @pl.when(step >= outer_end)
        def _():
            f = step - outer_end
            y_sum(f).wait_recv()
            mine = halved[f, :, pl.ds(y_me, 1)].reshape(2 * span, width)
            incoming = mine.astype(F32) + from_y[f].reshape(2 * span, width).astype(F32)
            start = pl.multiple_of(narrow * span, span)
            begin = jnp.concatenate(
                [tokens_ref[0, pl.ds(start, span)], tokens_ref[0, pl.ds(4 * span + start, span)]]
            )
            begin = begin.astype(F32) + extra_ref[0]
            back, gain_part = norm_back(begin, gain_ref[...], incoming)
            gain_grad[...] += gain_part
            grad = carried_ref[0].reshape(2 * span, width).astype(F32) + back
            table[...] += choose_ref[0] * jnp.sum(grad, axis=0, keepdims=True)
            done[f] = grad.astype(BF16).reshape(2, span, width)
            y_back(f).start()
            core_back(f).start()
            keep_own(f).start()

        @pl.when(step == outer_end + 1)
        def _():
            first_over_y.wait_recv()
            timed.fill(0, first_sum[0].astype(F32) + first_y[...].astype(F32))
            last_over_x.wait_recv()
            mine = last_sum[:, :, pl.ds(x_me, 1)].reshape(last_x.shape)
            timed.fill(0, mine.astype(F32) + last_x[...].astype(F32), FIRST)
            timed.copy(0).start()

        @pl.when(step == sum_end - 2)
        def _():
            timed.advance(0)

        @pl.when(step == sum_end - 1)
        def _():
            small[0, 0:1] = gain_grad[...]
            small[0, 1:3] = gains_ref[...]
            small[0, 3:11] = table[...]
            small[0, 11:] = jnp.zeros_like(small[0, 11:])
            small_copy(0).start()

            def small_sum(k):
                small_copy(k).wait_recv()
                small[k + 1] = small[k] + small_taken[k]
                if k + 1 < len(partners):
                    small_copy(k + 1).start()

            def back(f):
                y_back(f).wait_recv()
                core_onward(f).start()

            def finish(engine, out, level):
                if level < len(engine.blocks):
                    total = engine.advance(level)
                    if total is not None:
                        out[...] = total

            own.advance(0)
            small_sum(0)
            back(0)
            back(1)
            finish(own, own_out, 1)
            finish(timed, timed_out, 1)
            back(2)
            result_y().wait_recv()
            result_onward(1).start()
            small_sum(1)
            back(3)
            for level in range(2, max(levels)):
                finish(feed, feed_out, level)
                finish(timed, timed_out, level)
                finish(own, own_out, level)
            for k in range(2, len(partners)):
                small_sum(k)
            small_out[...] = small[len(partners)]
            for f in range(4, frames):
                back(f)
            for engine in engines:
                engine.close()
            for k in range(len(partners)):
                small_copy(k).wait_send()
            for f in range(frames):
                core_sum(f).wait_send()
                y_sum(f).wait_send()
                y_back(f).wait_send()
                core_back(f).wait()
                core_onward(f).wait()
                keep_own(f).wait()
            result_x().wait_send()
            result_y().wait_send()
            for y in range(2):
                result_core(y).wait()
                result_onward(y).wait()
                result_own(y).wait()
            for copy in (first_over_x, first_over_y, last_over_y, last_over_x):
                copy.wait_send()

    def frame(step):
        return jnp.minimum(step, frames - 1)

    def late(step):
        return jnp.clip(step - outer_end, 0, frames - 1)

    def piece(step):
        return jnp.clip(step - attend_end, 0, 3)

    block_shape = (half, 2, block, local)
    small_rows = 16
    scratch = [
        pltpu.VMEM((3, frames * places, local), BF16),
        pltpu.VMEM((frames, 2, 2, 2, span, width), BF16),
        pltpu.VMEM((frames, 2, 2, span, width), BF16),
        pltpu.VMEM((frames, 2, 2, span, width), BF16),
        pltpu.VMEM((frames, 2, span, width), BF16),
        pltpu.VMEM((frames, 2, span, width), BF16),
        pltpu.VMEM((1, width), F32),
        pltpu.VMEM((choose.shape[1], width), F32),
        pltpu.VMEM((bits + 3, small_rows, width), F32),
        pltpu.VMEM((bits + 2, small_rows, width), F32),
        pltpu.VMEM((2, FIRST, half, block, local), BF16),
        pltpu.VMEM((2, FIRST, half, block, local), BF16),
        pltpu.VMEM((2, FIRST, half, block, local), BF16),
        pltpu.VMEM((FIRST, half, block, local), BF16),
        pltpu.VMEM((last,) + block_shape, BF16),
        pltpu.VMEM((last,) + block_shape, BF16),
        pltpu.VMEM((last,) + block_shape, BF16),
        pltpu.VMEM((last, half, block, local), BF16),
        pltpu.VMEM((2, frames, span, width), BF16),
        pltpu.SemaphoreType.DMA((frames + 6,)),
        pltpu.SemaphoreType.DMA((2, 5 * frames)),
        pltpu.SemaphoreType.DMA((2, 10)),
        pltpu.SemaphoreType.DMA((2, bits + 2)),
        pltpu.SemaphoreType.DMA((2, sum(levels))),
    ]
    for engine in engines:
        scratch += engine.scratch()
    return comm_call(
        kernel,
        2,
        (sum_end,),
        [
            pl.BlockSpec((3, 1, places, local), lambda s: (0, frame(s), 0, 0)),
            pl.BlockSpec((1, places, local), lambda s: (frame(s), 0, 0)),
            whole(project.shape),
            pl.BlockSpec((frames * places, tile), lambda s: (0, piece(s))),
            pl.BlockSpec((1, places, width), lambda s: (late(s), 0, 0)),
            pl.BlockSpec((1, 1, width), lambda s: (late(s), 0, 0)),
            whole((1, width)),
            pl.BlockSpec((1, 2, span, width), lambda s: (late(s), 0, 0, 0)),
            pl.BlockSpec((1, choose.shape[1], 1), lambda s: (late(s), 0, 0)),
            whole((2, width)),
            whole(feed_keep.shape),
            whole(feed_taken.shape),
            ANY,
            ANY,
            ANY,
        ],
        [
            whole((3, block, local)),
            whole((slots, block, local)),
            whole((2, block, units)),
            whole((small_rows, width)),
            ANY,
            ANY,
        ],
        [
            shape_of((3, block, local), F32),
            shape_of((slots, block, local), F32),
            shape_of((2, block, units), F32),
            shape_of((small_rows, width), F32),
            shape_of((frames, 2, 2, 2, span, width)),
            shape_of((frames, 2, 2, 2, span, width)),
        ],
        scratch,
        2 * frames * places * width * local * 8,
    )(
        heads,
        grad_mixed,
        project,
        normed.reshape(frames * places, width),
        tokens,
        extra[:, None, :],
        gain,
        carried,
        choose,
        gains_grad,
        feed_keep,
        feed_taken,
        result_near,
        result_far,
        temporal_grad.reshape((2, slots) + block_shape),
    )


def finish(output, grad_tokens, own, timed, feed, small, table_rows):
    frames, places, width = output.shape
    block = width // lax.axis_size("wide")
    local = own.shape[-1]
    units = feed.shape[-1]

    def kernel(
        output_ref,
        grad_ref,
        own_ref,
        timed_ref,
        feed_ref,
        small_ref,
        output_out,
        grad_out,
        gains_out,
        table_out,
        project1_out,
        merge1_out,
        project2_out,
        merge2_out,
        expand_out,
        reduce_out,
    ):
        output_out[...] = output_ref[...]
        grad_out[...] = grad_ref[...].astype(F32)

        @pl.when(pl.program_id(0) == 0)
        def _():
            project1_out[...] = own_ref[...]
            merge1_out[...] = timed_ref[0].T
            merge2_out[...] = timed_ref[1].T
            project2_out[...] = timed_ref[2:]
            expand_out[...] = feed_ref[0]
            reduce_out[...] = feed_ref[1].T
            me = lax.axis_index("wide")
            total = jnp.zeros((small_ref.shape[0], block), F32)
            for w in range(width // block):
                total += jnp.where(me == w, small_ref[:, w * block : (w + 1) * block], 0.0)
            gains_out[...] = total[:3]
            table_out[...] = total[3 : 3 + table_rows]

    frame = pl.BlockSpec((2, places, width), lambda f: (f, 0, 0))
    shapes = [
        (3, block),
        (table_rows, block),
        own.shape,
        (local, block),
        (3, block, local),
        (local, block),
        (block, units),
        (units, block),
    ]
    return call(
        kernel,
        (frames // 2,),
        [frame, frame] + [whole(part.shape) for part in (own, timed, feed, small)],
        [frame, frame] + [whole(shape) for shape in shapes],
        [shape_of(output.shape), shape_of(output.shape, F32)]
        + [shape_of(shape, F32) for shape in shapes],
        moved=30 * 2**20,
    )(output, grad_tokens, own, timed, feed, small)


def swap(value, axis, bit):
    size = lax.axis_size(axis)
    return lax.ppermute(value, axis, [(i, i ^ bit) for i in range(size)])


def after(value, *earlier):
    return lax.optimization_barrier((value,) + earlier)[0]


def body(
    tokens,
    frame_counts,
    actions,
    action_table,
    norm_gains,
    spatial_project,
    spatial_merge,
    temporal_project,
    temporal_merge,
    expand_weight,
    reduce_weight,
    grad_out,
):
    frames_dev, tokens_frame, width = tokens.shape
    wide_me, narrow_me = lax.axis_index("wide"), lax.axis_index("narrow")
    x_me = wide_me % 2
    span = tokens_frame // 8
    rows = 2 * frames_dev * span
    spatial_project = spatial_project.transpose(1, 0, 2)
    temporal_project = temporal_project.transpose(1, 0, 2)

    def keep_of(wide_place):
        frame_ids = wide_place * frames_dev + jnp.arange(frames_dev, dtype=jnp.int32)
        clip_places = jnp.arange(frame_counts.shape[0], dtype=jnp.int32)
        clip_count = jnp.sum(
            jnp.where((frame_ids // FRAMES)[:, None] == clip_places[None, :], frame_counts[None, :], 0),
            axis=1,
        )
        return (frame_ids % FRAMES < clip_count).astype(F32)

    keep_place = jnp.concatenate([keep_of(wide_me), keep_of(wide_me + 1 - 2 * x_me)])
    keep_place = jnp.broadcast_to(keep_place[:, None], (2 * frames_dev, span)).reshape(rows, 1)
    choose = (
        actions[:, None] == jnp.arange(action_table.shape[0], dtype=jnp.int32)[None, :]
    ).astype(BF16)
    extra = jnp.dot(choose, action_table, preferred_element_type=F32)

    (
        normed1,
        heads1,
        hidden1,
        normed2,
        heads2,
        mixed2,
        hidden2,
        normed3,
        normed3_first,
        normed3_second,
        mixed1,
        grad_result,
        grad_result_far,
        expand_pair,
        reduce_pair,
        merge1_all,
        project_all,
        merge2_all,
    ) = attention_forward(
        tokens,
        extra,
        norm_gains,
        spatial_project,
        spatial_merge,
        temporal_project,
        temporal_merge,
        expand_weight,
        reduce_weight,
        grad_out,
        keep_place,
    )
    mixed1 = mixed1.reshape(4, rows, mixed1.shape[-1])

    grad_result = grad_result.reshape(rows, width)
    grad_result_far = grad_result_far.reshape(rows, width)
    first_far = swap(normed3_first, "narrow", 2)
    second_far = swap(normed3_second, "narrow", 2)
    near = feed_forward(normed3, grad_result, keep_place, expand_pair, reduce_pair)
    first_far = after(first_far, near[0])
    first = feed_forward(first_far, grad_result_far, keep_place, expand_pair, reduce_pair, 0)
    second_far = after(second_far, first[0])
    second = feed_forward(second_far, grad_result_far, keep_place, expand_pair, reduce_pair, 1)
    grad_first = swap(first[4], "narrow", 2)
    grad_second = swap(second[4], "narrow", 2)
    feed_keep, feed_send = feed_outer(
        [normed3, first_far, second_far],
        [near[1], first[1], second[1]],
        [near[2], first[2], second[2]],
        [near[0], first[0], second[0]],
    )

    branch2_grad, grad_heads2, branch1_grad, grad_mixed1, carried, gain_three, gain_two = temporal_backward(
        near[4],
        after(grad_first, feed_keep),
        grad_second,
        hidden2,
        hidden1,
        grad_result,
        keep_place,
        norm_gains,
        heads2,
        merge2_all,
        project_all,
        merge1_all,
    )
    branch3_far = jnp.concatenate(
        [
            swap(after(first[3], grad_second), "narrow", 2),
            swap(after(second[3], grad_second), "narrow", 2),
        ]
    )
    feed_taken = swap(after(feed_send, grad_second), "wide", 1)
    branch3 = near[3].astype(F32) + branch3_far.astype(F32)
    result = (hidden2 + keep_place * branch3).astype(BF16).reshape(2, frames_dev, span, width)
    temporal_grad, grad_mixed1, carried, result_far = temporal_outer(
        grad_mixed1, carried, result, mixed1, branch1_grad, mixed2, branch2_grad, normed2, grad_heads2
    )

    project1_grad, temporal_grad, feed_grad, small, output, grad_tokens = spatial_backward(
        heads1,
        grad_mixed1,
        spatial_project,
        normed1,
        tokens,
        extra,
        norm_gains[0:1],
        carried,
        choose.astype(F32)[:, :, None],
        jnp.concatenate([gain_two, gain_three]),
        result,
        result_far,
        temporal_grad,
        feed_keep,
        feed_taken,
    )
    (
        output,
        grad_tokens,
        gains_grad,
        table_grad,
        project1_grad,
        merge1_grad,
        project2_grad,
        merge2_grad,
        expand_grad,
        reduce_grad,
    ) = finish(
        output.reshape(tokens.shape),
        grad_tokens.reshape(tokens.shape),
        project1_grad,
        temporal_grad,
        feed_grad,
        small,
        action_table.shape[0],
    )
    return (
        output,
        grad_tokens,
        gains_grad,
        table_grad,
        project1_grad.transpose(1, 0, 2),
        merge1_grad,
        project2_grad.transpose(1, 0, 2),
        merge2_grad,
        expand_grad,
        reduce_grad,
    )


def solution(mesh):
    return jax.shard_map(
        body,
        mesh=mesh,
        in_specs=(
            P("wide", None, None),
            P(),
            P("wide"),
            P(),
            P(),
            P(None, None, "narrow"),
            P("narrow", None),
            P(None, None, "narrow"),
            P("narrow", None),
            P(None, "narrow"),
            P("narrow", None),
            P("wide", None, None),
        ),
        out_specs=(
            P("wide", None, None),
            P("wide", None, None),
            P(None, "wide"),
            P(None, "wide"),
            P("wide", None, "narrow"),
            P("narrow", "wide"),
            P("wide", None, "narrow"),
            P("narrow", "wide"),
            P("wide", "narrow"),
            P("narrow", "wide"),
        ),
        check_vma=False,
    )
```

```python
import jax
import jax.numpy as jnp
from jax import lax
from jax.experimental import pallas as pl
from jax.experimental.pallas import tpu as pltpu
from jax.sharding import PartitionSpec as P

HD = 64
FRAMES = 16
GROUP = 16
PAIR = 2 * HD

EPSILON = 1e-06
NEGATIVE = -1e30
F32 = jnp.float32
BF16 = jnp.bfloat16
VMEM_LIMIT = 56 * 1024 * 1024
NN = (((1,), (0,)), ((), ()))
NT = (((1,), (1,)), ((), ()))
TN = (((0,), (0,)), ((), ()))


def mm(left, right, form=NN):
    return lax.dot_general(left, right, form, preferred_element_type=F32)


def root(value):
    return lax.rsqrt(jnp.mean(value * value, axis=-1, keepdims=True) + EPSILON)


def norm_back(value, gain, incoming):
    scale = root(value)
    scaled = gain * incoming
    inner = jnp.mean(scaled * value, axis=-1, keepdims=True)
    back = scale * scaled - (scale * scale * scale) * inner * value
    return back, jnp.sum(incoming * value * scale, axis=0, keepdims=True)


def sides():
    lane = lax.broadcasted_iota(jnp.int32, (1, PAIR), 1)
    low = (lane < HD).astype(F32)
    return lane < HD, low.astype(BF16), (1.0 - low).astype(BF16)


def attend_pair(queries, key_rows, value_rows, allowed):
    is_low, low, high = sides()
    mixed = []
    for side in (low, high):
        scores = mm(queries * (side * HD ** (-0.5)), key_rows, NT)
        if allowed is not None:
            scores = jnp.where(allowed, scores, NEGATIVE)
        shares = jnp.exp(scores - jnp.max(scores, axis=-1, keepdims=True))
        shares = shares * (1.0 / jnp.sum(shares, axis=-1, keepdims=True))
        mixed.append(mm(shares.astype(BF16), value_rows))
    return jnp.where(is_low, mixed[0], mixed[1]).astype(BF16)


def attend_back_pair(queries, key_rows, value_rows, grad_mixed, allowed):
    factor = HD ** (-0.5)
    is_low, low, high = sides()
    parts = []
    for side in (low, high):
        scores = mm(key_rows, queries * (side * factor), NT)
        if allowed is not None:
            scores = jnp.where(allowed, scores, NEGATIVE)
        chances = jnp.exp(scores - jnp.max(scores, axis=0, keepdims=True))
        chances = chances * (1.0 / jnp.sum(chances, axis=0, keepdims=True))
        grad_chances = mm(value_rows, grad_mixed * side, NT)
        shift = jnp.sum(grad_chances * chances, axis=0, keepdims=True)
        grad_scores = (chances * (grad_chances - shift)).astype(BF16)
        parts.append(
            (
                mm(grad_scores, key_rows, TN) * factor,
                mm(grad_scores, queries) * factor,
                mm(chances.astype(BF16), grad_mixed),
            )
        )
    return [jnp.where(is_low, a, b).astype(BF16) for a, b in zip(parts[0], parts[1])]


def whole(shape):
    return pl.BlockSpec(shape, lambda *_: (0,) * len(shape))


def call(kernel, grid, in_specs, out_specs, out_shape, scratch=(), flops=0, moved=0):
    return pl.pallas_call(
        kernel,
        grid=grid,
        in_specs=in_specs,
        out_specs=out_specs,
        out_shape=out_shape,
        scratch_shapes=list(scratch),
        compiler_params=pltpu.CompilerParams(vmem_limit_bytes=VMEM_LIMIT),
        cost_estimate=pl.CostEstimate(flops=flops, bytes_accessed=moved, transcendentals=0),
    )


def shape_of(shape, kind=BF16):
    return jax.ShapeDtypeStruct(shape, kind)


def place_masks(x_me, frames_all, transposed):
    rows = frames_all * GROUP
    shape = (rows, rows)
    query = lax.broadcasted_iota(jnp.int32, shape, 1 if transposed else 0)
    key = lax.broadcasted_iota(jnp.int32, shape, 0 if transposed else 1)
    query_frame = (query // GROUP + x_me * (frames_all // 2)) % frames_all
    key_frame = (key // GROUP + x_me * (frames_all // 2)) % frames_all
    return (query % GROUP == key % GROUP) & (key_frame <= query_frame)


RATE = 0.7978845608028654
CUBIC = 0.044715


def feed_forward(normed, grad, keep, expand, reduce, which=0):
    rows, width = normed.shape
    cores, _, units = expand.shape
    block = 512
    per = units // block

    def kernel(
        normed_ref,
        grad_ref,
        keep_ref,
        expand_ref,
        reduce_ref,
        active_ref,
        inner_ref,
        grad_branch_ref,
        branch_ref,
        grad_normed_ref,
        branch_sum,
        grad_sum,
    ):
        step = pl.program_id(0)

        @pl.when(step == 0)
        def _():
            grad_branch_ref[...] = (keep_ref[...] * grad_ref[...].astype(F32)).astype(BF16)
            branch_sum[...] = jnp.zeros_like(branch_sum)
            grad_sum[...] = jnp.zeros_like(grad_sum)

        inner = mm(normed_ref[...], expand_ref[0])
        grad_active = mm(grad_branch_ref[...], reduce_ref[0], NT)
        square = inner * inner
        bend = jnp.tanh(RATE * inner * (1.0 + CUBIC * square))
        half = 0.5 * (1.0 + bend)
        active = (inner * half).astype(BF16)
        slope = half + (0.5 * RATE) * inner * (1.0 - bend * bend) * (1.0 + (3.0 * CUBIC) * square)
        grad_inner = (grad_active * slope).astype(BF16)
        active_ref[...] = active
        inner_ref[...] = grad_inner
        branch_sum[...] += mm(active, reduce_ref[0])
        grad_sum[...] += mm(grad_inner, expand_ref[0], NT)

        @pl.when(step == cores * per - 1)
        def _():
            branch_ref[...] = branch_sum[...].astype(BF16)
            grad_normed_ref[...] = grad_sum[...].astype(BF16)

    full = whole((rows, width))
    return call(
        kernel,
        (cores * per,),
        [
            full,
            pl.BlockSpec((rows, width), lambda j: (which, 0)),
            pl.BlockSpec((rows, 1), lambda j: (which, 0)),
            pl.BlockSpec((1, width, block), lambda j: (j // per, 0, j % per)),
            pl.BlockSpec((1, block, width), lambda j: (j // per, j % per, 0)),
        ],
        [
            pl.BlockSpec((rows, block), lambda j: (0, j)),
            pl.BlockSpec((rows, block), lambda j: (0, j)),
            full,
            full,
            full,
        ],
        [
            shape_of((rows, cores * units)),
            shape_of((rows, cores * units)),
            shape_of((rows, width)),
            shape_of((rows, width)),
            shape_of((rows, width)),
        ],
        scratch=[pltpu.VMEM((rows, width), F32), pltpu.VMEM((rows, width), F32)],
        flops=8 * rows * width * cores * units,
        moved=18 * 2**20,
    )(normed, grad, keep, expand, reduce)


def temporal_backward(
    grad_near, grad_first, grad_second, hidden2, hidden1, grad_result, keep, gains, heads, merge2, project, merge1
):
    rows, width = hidden1.shape
    local = merge1.shape[1]
    span = rows // FRAMES
    group_rows = FRAMES * GROUP

    def kernel(
        near_ref,
        first_ref,
        second_ref,
        hidden2_ref,
        hidden1_ref,
        result_ref,
        keep_ref,
        gains_ref,
        heads_ref,
        merge2_ref,
        project_ref,
        merge1_ref,
        branch2_ref,
        grad_heads_ref,
        branch1_ref,
        mixed1_ref,
        carried_ref,
        gain3_ref,
        gain2_ref,
        grad_hidden,
        grad_normed,
        grad_mixed,
    ):
        step = pl.program_id(0)

        @pl.when(step == 0)
        def _():
            far = jnp.concatenate([first_ref[...], second_ref[...]])
            incoming = near_ref[...].astype(F32) + far.astype(F32)
            back, gain3_ref[...] = norm_back(hidden2_ref[...], gains_ref[2:3], incoming)
            total = result_ref[...].astype(F32) + back
            grad_hidden[...] = total
            branch2_ref[...] = (keep_ref[...] * total).astype(BF16)
            grad_normed[...] = jnp.zeros_like(grad_normed)

        back_mixed = mm(branch2_ref[...], merge2_ref[0], NT).astype(BF16)
        grad_mixed[...] = back_mixed.reshape(FRAMES, span, local)
        allowed = place_masks(lax.axis_index("wide") % 2, FRAMES, True)
        for g in range(span // GROUP):
            band = pl.ds(g * GROUP, GROUP)
            for at in range(0, local, PAIR):
                part = pl.ds(at, PAIR)
                terms = [heads_ref[0, c, :, band, part].reshape(group_rows, PAIR) for c in range(3)]
                grad = grad_mixed[:, band, part].reshape(group_rows, PAIR)
                grads = attend_back_pair(*terms, grad, allowed)
                for c in range(3):
                    grad_heads_ref[0, c, :, band, part] = grads[c].reshape(FRAMES, GROUP, PAIR)
        total = mm(grad_heads_ref[0, 0].reshape(rows, local), project_ref[0, 0], NT)
        for c in range(1, 3):
            total += mm(grad_heads_ref[0, c].reshape(rows, local), project_ref[0, c], NT)
        grad_normed[...] += total

        @pl.when(step == 3)
        def _():
            back, gain2_ref[...] = norm_back(hidden1_ref[...], gains_ref[1:2], grad_normed[...])
            total = grad_hidden[...] + back
            carried_ref[...] = total.astype(BF16)
            branch1_ref[...] = (keep_ref[...] * total).astype(BF16)
            for n in range(4):
                mixed1_ref[n] = mm(branch1_ref[...], merge1_ref[n], NT).astype(BF16)

    full = whole((rows, width))
    row = whole((1, width))
    return call(
        kernel,
        (4,),
        [
            full,
            whole((rows // 2, width)),
            whole((rows // 2, width)),
            full,
            full,
            full,
            whole((rows, 1)),
            whole((3, width)),
            pl.BlockSpec((1, 3, FRAMES, span, local), lambda n: (n, 0, 0, 0, 0)),
            pl.BlockSpec((1, local, width), lambda n: (n, 0, 0)),
            pl.BlockSpec((1, 3, width, local), lambda n: (n, 0, 0, 0)),
            whole((4, local, width)),
        ],
        [
            full,
            pl.BlockSpec((1, 3, FRAMES, span, local), lambda n: (n, 0, 0, 0, 0)),
            full,
            whole((4, rows, local)),
            full,
            row,
            row,
        ],
        [
            shape_of((rows, width)),
            shape_of((4, 3, FRAMES, span, local)),
            shape_of((rows, width)),
            shape_of((4, rows, local)),
            shape_of((rows, width)),
            shape_of((1, width), F32),
            shape_of((1, width), F32),
        ],
        scratch=[
            pltpu.VMEM((rows, width), F32),
            pltpu.VMEM((rows, width), F32),
            pltpu.VMEM((FRAMES, span, local), BF16),
        ],
        flops=2 * rows * width * width * 8,
        moved=30 * 2**20,
    )(grad_near, grad_first, grad_second, hidden2, hidden1, grad_result, keep, gains, heads, merge2, project, merge1)


def here():
    wide, narrow = lax.axis_index("wide"), lax.axis_index("narrow")
    return wide, narrow, wide % 2, narrow // 2, narrow % 2


def other(wide, narrow, x, y, core):
    if x:
        wide = wide + 1 - 2 * (wide % 2)
    if y:
        narrow = (narrow + 2) % 4
    if core:
        narrow = narrow + 1 - 2 * (narrow % 2)
    return wide, narrow


def beyond(wide, narrow):
    return wide + 2 - 4 * ((wide // 2) % 2), narrow


def place_of(wide, narrow, span):
    return pl.multiple_of(((wide % 2) * 4 + narrow) * span, span)


def remote(src, dst, sems, i, device):
    return pltpu.make_async_remote_copy(
        src_ref=src,
        dst_ref=dst,
        send_sem=sems.at[0, i],
        recv_sem=sems.at[1, i],
        device_id=device,
        device_id_type=pl.DeviceIdType.MESH,
    )


def greet(devices):
    barrier = pltpu.get_barrier_semaphore()
    for device in devices:
        pl.semaphore_signal(
            barrier, inc=1, device_id=device, device_id_type=pl.DeviceIdType.MESH
        )
    pl.semaphore_wait(barrier, len(devices))


OTHERS = [(x, y, c) for x in range(2) for y in range(2) for c in range(2) if x + y + c > 0]
ANY = pl.BlockSpec(memory_space=pl.ANY)


def comm_call(kernel, number, grid, in_specs, out_specs, out_shape, scratch, flops, moved=30 * 2**20):
    return pl.pallas_call(
        kernel,
        grid=grid,
        in_specs=in_specs,
        out_specs=out_specs,
        out_shape=out_shape,
        scratch_shapes=scratch,
        compiler_params=pltpu.CompilerParams(
            vmem_limit_bytes=VMEM_LIMIT, collective_id=number, has_side_effects=True
        ),
        cost_estimate=pl.CostEstimate(flops=flops, bytes_accessed=moved, transcendentals=0),
    )


def attention_forward(
    tokens,
    extra,
    gains,
    project,
    merge1,
    project2,
    merge2,
    expand,
    reduce,
    grad_out,
    keep,
):
    frames, places, width = tokens.shape
    local = project.shape[-1]
    span = places // 8
    rows = FRAMES * span
    group_rows = FRAMES * GROUP
    half = frames // 2
    shards = (merge1, project2[0], project2[1], project2[2], merge2)
    count = len(shards)

    def kernel(
        tokens_ref,
        extra_ref,
        gains_ref,
        project_ref,
        keep_ref,
        all_tokens,
        all_extra,
        grad_ref,
        expand_ref,
        reduce_ref,
        merge1_ref,
        project2_ref,
        merge2_ref,
        normed_ref,
        heads_ref,
        hidden1_ref,
        normed2_ref,
        heads2_ref,
        mixed2_ref,
        hidden2_ref,
        normed3_ref,
        first_ref,
        second_ref,
        mixed_out,
        grad_near,
        grad_far,
        expand_pair,
        reduce_pair,
        merge1_out,
        project2_out,
        merge2_out,
        mixed_ref,
        mixed_all,
        tokens_place,
        extra_place,
        merge1_all,
        project2_all,
        merge2_all,
        local_sems,
        move_sems,
        shard_sems,
        mixed_sems,
        *stage,
    ):
        step = pl.program_id(0)
        wide, narrow, x_me, _, _ = here()
        half_me = (wide // 2) % 2
        x_other = other(wide, narrow, 1, 0, 0)
        y_other = other(wide, narrow, 0, 1, 0)
        core_other = other(wide, narrow, 0, 0, 1)
        z_other = beyond(wide, narrow)
        mine = pl.ds(place_of(wide, narrow, span), span)
        near_y = pl.ds(place_of(*y_other, span), span)
        shard = [merge1_ref] + [project2_ref.at[c] for c in range(3)] + [merge2_ref]
        full = [merge1_all] + [project2_all.at[:, c] for c in range(3)] + [merge2_all]

        own = [
            (expand_ref, expand_pair.at[0]),
            (reduce_ref, reduce_pair.at[0]),
            (grad_ref.at[:, mine], grad_near.at[0]),
            (grad_ref.at[:, near_y], grad_far.at[0]),
        ]
        into = [
            pltpu.make_async_copy(a, v, local_sems.at[0, i])
            for i, ((a, _), v) in enumerate(zip(own, stage))
        ]
        back = [
            pltpu.make_async_copy(v, b, local_sems.at[1, i])
            for i, ((_, b), v) in enumerate(zip(own, stage))
        ]
        inside = [
            (all_tokens.at[:, mine], tokens_place.at[0]),
            (all_extra, extra_place.at[0]),
        ] + [(shard[k], full[k].at[0]) for k in range(count)]
        inside = [
            pltpu.make_async_copy(a, b, local_sems.at[0, 4 + i]) for i, (a, b) in enumerate(inside)
        ]
        leaving = [
            (mixed_all, mixed_out),
            (merge1_all, merge1_out),
            (project2_all, project2_out),
            (merge2_all, merge2_out),
        ]
        leaving = [
            pltpu.make_async_copy(a, b, local_sems.at[1, 4 + i]) for i, (a, b) in enumerate(leaving)
        ]
        far = pl.ds(place_of(*x_other, span), span)
        far_y = pl.ds(place_of(*other(wide, narrow, 1, 1, 0), span), span)
        first = [
            remote(all_tokens.at[:, far], tokens_place.at[1], move_sems, 0, x_other),
            remote(all_extra, extra_place.at[1], move_sems, 1, x_other),
            remote(expand_ref, expand_pair.at[1], move_sems, 2, core_other),
            remote(reduce_ref, reduce_pair.at[1], move_sems, 3, core_other),
        ]
        last = [
            remote(grad_ref.at[:, far], grad_near.at[1], move_sems, 4, x_other),
            remote(grad_ref.at[:, far_y], grad_far.at[1], move_sems, 5, x_other),
        ]

        def part(k, which):
            count = shards[k].shape[0] // 2
            return pl.ds(pl.multiple_of(which * count, count), count)

        def over_core(k):
            return remote(shard[k], full[k].at[1], shard_sems, 5 * k, core_other)

        def over_y(k):
            some = part(k, half_me)
            return remote(shard[k].at[some], full[k].at[2, some], shard_sems, 5 * k + 1, y_other)

        def onward(k, which, i, device, slot):
            some = part(k, which)
            return remote(full[k].at[2, some], full[k].at[slot, some], shard_sems, 5 * k + i, device)

        def over_z(k):
            return onward(k, half_me, 2, z_other, 2)

        def near_half(k):
            return onward(k, half_me, 3, core_other, 3)

        def far_half(k):
            return onward(k, 1 - half_me, 4, core_other, 3)

        def forward(k):
            over_y(k).wait_recv()
            over_z(k).start()
            near_half(k).start()

        def complete(k):
            over_z(k).wait_recv()
            far_half(k).start()

        def mixed_copies(chunk):
            copies = []
            some = pl.ds(chunk * half, half)
            for i, (x, y, c) in enumerate(OTHERS):
                device = other(wide, narrow, x, y, c)
                copies.append(
                    remote(
                        mixed_ref.at[some, pl.ds(place_of(*device, span), span)],
                        mixed_all.at[2 * y + c, x, some],
                        mixed_sems,
                        7 * chunk + i,
                        device,
                    )
                )
            here_copy = pltpu.make_async_copy(
                mixed_ref.at[some, mine], mixed_all.at[0, 0, some], local_sems.at[chunk, 11]
            )
            return copies + [here_copy]

        @pl.when(step == 0)
        def _():
            greet([other(wide, narrow, *o) for o in OTHERS] + [z_other])
            for k in range(3):
                over_y(k).start()
            for copy in first:
                copy.start()
            for k in range(count):
                over_core(k).start()
            for copy in into + inside:
                copy.start()

        @pl.when(step == 2)
        def _():
            for copy in into:
                copy.wait()
            for copy in back:
                copy.start()

        @pl.when(step < frames)
        def _():
            start = tokens_ref[0].astype(F32) + extra_ref[0]
            normed = (start * root(start) * gains_ref[0:1]).astype(BF16)
            normed_ref[0] = normed
            for c in range(3):
                heads_ref[c, 0] = mm(normed, project_ref[c]).astype(BF16)
            for at in range(0, local, PAIR):
                lanes = pl.ds(at, PAIR)
                mixed_ref[step, :, lanes] = attend_pair(
                    heads_ref[0, 0, :, lanes],
                    heads_ref[1, 0, :, lanes],
                    heads_ref[2, 0, :, lanes],
                    None,
                )

        @pl.when(step == 2)
        def _():
            forward(0)

        @pl.when(step == half - 1)
        def _():
            for copy in mixed_copies(0):
                copy.start()

        @pl.when(step == half)
        def _():
            forward(1)

        @pl.when(step == half + 1)
        def _():
            complete(0)

        @pl.when(step == half + 2)
        def _():
            forward(2)

        @pl.when(step == frames - 1)
        def _():
            for copy in mixed_copies(1):
                copy.start()
            over_y(3).start()
            over_y(4).start()
            for copy in last:
                copy.start()
            complete(1)

        @pl.when(step == frames)
        def _():
            for copy in inside:
                copy.wait()
            over_core(0).wait_recv()
            near_half(0).wait_recv()
            far_half(0).wait_recv()
            first[0].wait_recv()
            first[1].wait_recv()
            for copy in mixed_copies(0) + mixed_copies(1):
                copy.wait()
            leaving[0].start()
            leaving[1].start()
            branch = mm(mixed_all[0].reshape(rows, local), merge1_all[0])
            for n in range(1, 4):
                branch += mm(mixed_all[n].reshape(rows, local), merge1_all[n])
            begin = tokens_place[...].astype(F32) + extra_place[...]
            hidden1 = begin.reshape(rows, width) + keep_ref[...] * branch
            hidden1_ref[...] = hidden1
            hidden2_ref[...] = hidden1
            normed2_ref[...] = (hidden1 * root(hidden1) * gains_ref[1:2]).astype(BF16)

        @pl.when(step == frames + 1)
        def _():
            complete(2)
            forward(3)
            for k in range(1, count):
                over_core(k).wait_recv()

        @pl.when(step == frames + 2)
        def _():
            forward(4)
            complete(3)

        @pl.when(step == frames + 3)
        def _():
            for k in range(1, 4):
                near_half(k).wait_recv()
                far_half(k).wait_recv()
            leaving[2].start()

        @pl.when(step >= frames)
        def _():
            n = step - frames
            for c in range(3):
                head = mm(normed2_ref[...], project2_all[n, c]).astype(BF16)
                heads2_ref[0, c] = head.reshape(FRAMES, span, local)
            allowed = place_masks(x_me, FRAMES, False)
            for g in range(span // GROUP):
                band = pl.ds(g * GROUP, GROUP)
                for at in range(0, local, PAIR):
                    lanes = pl.ds(at, PAIR)
                    terms = [
                        heads2_ref[0, c, :, band, lanes].reshape(group_rows, PAIR) for c in range(3)
                    ]
                    mixed = attend_pair(*terms, allowed)
                    mixed2_ref[0, :, band, lanes] = mixed.reshape(FRAMES, GROUP, PAIR)

        @pl.when(step == frames + 2)
        def _():
            complete(4)

        @pl.when(step == frames + 3)
        def _():
            near_half(4).wait_recv()
            far_half(4).wait_recv()
            leaving[3].start()

        @pl.when(step >= frames)
        def _():
            merged = mm(mixed2_ref[0].reshape(rows, local), merge2_all[step - frames])
            hidden2_ref[...] += keep_ref[...] * merged

        @pl.when(step == frames + 3)
        def _():
            hidden2 = hidden2_ref[...]
            normed3 = (hidden2 * root(hidden2) * gains_ref[2:3]).astype(BF16)
            normed3_ref[...] = normed3
            first_ref[...] = normed3[: rows // 2]
            second_ref[...] = normed3[rows // 2 :]
            for copy in first[2:] + last:
                copy.wait()
            for copy in first[:2]:
                copy.wait_send()
            for copy in back + leaving:
                copy.wait()
            for k in range(count):
                for copy in (over_core(k), over_y(k), over_z(k), near_half(k), far_half(k)):
                    copy.wait_send()

    def frame(step):
        return jnp.minimum(step, frames - 1)

    def turn(step):
        return jnp.maximum(step - frames, 0)

    full = whole((rows, width))
    return comm_call(
        kernel,
        0,
        (frames + 4,),
        [
            pl.BlockSpec((1, places, width), lambda s: (frame(s), 0, 0)),
            pl.BlockSpec((1, 1, width), lambda s: (frame(s), 0, 0)),
            whole((3, width)),
            whole(project.shape),
            whole((rows, 1)),
        ]
        + [ANY] * 8,
        [
            pl.BlockSpec((1, places, width), lambda s: (frame(s), 0, 0)),
            pl.BlockSpec((3, 1, places, local), lambda s: (0, frame(s), 0, 0)),
            full,
            full,
            pl.BlockSpec((1, 3, FRAMES, span, local), lambda s: (turn(s), 0, 0, 0, 0)),
            pl.BlockSpec((1, FRAMES, span, local), lambda s: (turn(s), 0, 0, 0)),
            full,
            full,
            whole((rows // 2, width)),
            whole((rows // 2, width)),
        ]
        + [ANY] * 8,
        [
            shape_of((frames, places, width)),
            shape_of((3, frames, places, local)),
            shape_of((rows, width), F32),
            shape_of((rows, width)),
            shape_of((4, 3, FRAMES, span, local)),
            shape_of((4, FRAMES, span, local)),
            shape_of((rows, width), F32),
            shape_of((rows, width)),
            shape_of((rows // 2, width)),
            shape_of((rows // 2, width)),
            shape_of((4, 2, frames, span, local)),
            shape_of((2, frames, span, width)),
            shape_of((2, frames, span, width)),
            shape_of((2,) + expand.shape),
            shape_of((2,) + reduce.shape),
            shape_of((4,) + merge1.shape),
            shape_of((4,) + project2.shape),
            shape_of((4,) + merge2.shape),
        ],
        [
            pltpu.VMEM((frames, places, local), BF16),
            pltpu.VMEM((4, 2, frames, span, local), BF16),
            pltpu.VMEM((2, frames, span, width), BF16),
            pltpu.VMEM((2, frames, 1, width), F32),
            pltpu.VMEM((4,) + merge1.shape, BF16),
            pltpu.VMEM((4,) + project2.shape, BF16),
            pltpu.VMEM((4,) + merge2.shape, BF16),
            pltpu.SemaphoreType.DMA((2, 12)),
            pltpu.SemaphoreType.DMA((2, 6)),
            pltpu.SemaphoreType.DMA((2, 5 * count)),
            pltpu.SemaphoreType.DMA((2, 14)),
            pltpu.VMEM(expand.shape, BF16),
            pltpu.VMEM(reduce.shape, BF16),
            pltpu.VMEM((frames, span, width), BF16),
            pltpu.VMEM((frames, span, width), BF16),
        ],
        2 * frames * places * width * local * 4 + 2 * rows * width * width * 6,
    )(
        tokens,
        extra[:, None, :],
        gains,
        project,
        keep,
        tokens,
        extra[:, None, :],
        grad_out,
        expand,
        reduce,
        merge1,
        project2,
        merge2,
    )


def feed_outer(normed, grad_inner, grad_branch, active):
    width = normed[0].shape[1]
    units = active[0].shape[1] // 2
    ends = [0]
    for part in normed:
        ends.append(ends[-1] + part.shape[0])
    rows, count = ends[-1], len(normed)
    block = 512
    per = units // block
    wide = lax.axis_size("wide")
    split = (2, wide // 2, 2, width // wide, block)

    def kernel(*refs):
        normed_refs, branch_refs = refs[:count], refs[count : 2 * count]
        inner_refs, active_refs = refs[2 * count : 3 * count], refs[3 * count : 4 * count]
        keep_ref, send_ref, left, right, total, given, taken, sems = refs[4 * count :]
        step = pl.program_id(0)
        wide, narrow, x_me, _, _ = here()
        core_other = other(wide, narrow, 0, 0, 1)

        def over(j):
            return remote(given.at[j], taken.at[j], sems, j, core_other)

        @pl.when(step == 0)
        def _():
            for k in range(count):
                left[:, ends[k] : ends[k + 1]] = normed_refs[k][...].T
                right[:, ends[k] : ends[k + 1]] = branch_refs[k][...].T

        def product(side, parts):
            out = mm(side[:, : ends[1]], parts[0][...])
            for k in range(1, count):
                out += mm(side[:, ends[k] : ends[k + 1]], parts[k][...])
            return out

        expand = product(left, inner_refs)
        reduce = product(right, active_refs)

        @pl.when(step == 0)
        def _():
            greet([core_other])

        @pl.when(step < per)
        def _():
            given[step, 0] = expand.astype(BF16)
            given[step, 1] = reduce.astype(BF16)
            over(step).start()

        @pl.when(step >= per)
        def _():
            j = step - per
            over(j).wait_recv()
            half = split[1:]
            total[0] = (expand + taken[j, 0].astype(F32)).astype(BF16).reshape(half)
            total[1] = (reduce + taken[j, 1].astype(F32)).astype(BF16).reshape(half)
            out = keep_ref.shape
            keep_ref[...] = total[:, :, pl.ds(x_me, 1)].reshape(out)
            send_ref[...] = total[:, :, pl.ds(1 - x_me, 1)].reshape(out)

        @pl.when(step == 2 * per - 1)
        def _():
            for j in range(per):
                over(j).wait_send()

    def columns(part):
        return pl.BlockSpec((part.shape[0], block), lambda j: (0, (j + per) % (2 * per)))

    out = pl.BlockSpec((2, width // 2, block), lambda j: (0, 0, jnp.maximum(j - per, 0)))
    return comm_call(
        kernel,
        3,
        (2 * per,),
        [whole(part.shape) for part in normed + grad_branch]
        + [columns(part) for part in grad_inner + active],
        [out, out],
        [shape_of((2, width // 2, units))] * 2,
        [
            pltpu.VMEM((width, rows), BF16),
            pltpu.VMEM((width, rows), BF16),
            pltpu.VMEM(split, BF16),
            pltpu.VMEM((per, 2, width, block), BF16),
            pltpu.VMEM((per, 2, width, block), BF16),
            pltpu.SemaphoreType.DMA((2, per)),
        ],
        2**20,
        2**20,
    )(*normed, *grad_branch, *grad_inner, *active)


def temporal_outer(
    grad_mixed1, carried, result, mixed1, branch1, mixed2, branch2, normed2, grad_heads
):
    rows, width = branch1.shape
    local = mixed1.shape[-1]
    span = rows // FRAMES
    frames = FRAMES // 2

    def kernel(
        grad_ref,
        carried_ref,
        result_ref,
        mixed1_ref,
        branch1_ref,
        mixed2_ref,
        branch2_ref,
        normed2_ref,
        heads_ref,
        out_ref,
        grad_own,
        carried_own,
        result_far,
        left,
        given,
        taken,
        grad_stage,
        carried_stage,
        local_sems,
        sems,
    ):
        step = pl.program_id(0)
        wide, narrow, x_me, _, _ = here()
        x_other = other(wide, narrow, 1, 0, 0)
        mine = pl.ds(place_of(wide, narrow, span), span)
        copies = [
            remote(
                grad_ref.at[2 * y + c, x],
                grad_own.at[:, mine],
                sems,
                i,
                other(wide, narrow, x, y, c),
            )
            for i, (x, y, c) in enumerate(OTHERS)
        ]
        copies.append(remote(carried_ref.at[1], carried_own.at[:, x_me], sems, 7, x_other))
        copies.append(remote(result_ref.at[0], result_far, sems, 8, other(wide, narrow, 0, 1, 0)))

        def over(y):
            return remote(given.at[y], taken.at[y], sems, 9 + y, other(wide, narrow, 0, 0, 1))

        into = [
            pltpu.make_async_copy(grad_ref.at[0, 0], grad_stage, local_sems.at[0]),
            pltpu.make_async_copy(carried_ref.at[0], carried_stage, local_sems.at[1]),
        ]
        back = [
            pltpu.make_async_copy(grad_stage, grad_own.at[:, mine], local_sems.at[2]),
            pltpu.make_async_copy(carried_stage, carried_own.at[:, x_me], local_sems.at[3]),
        ]

        @pl.when(step == 0)
        def _():
            greet([other(wide, narrow, *o) for o in OTHERS])
            for copy in copies + into:
                copy.start()
            left[0] = branch1_ref[...].T
            left[1] = branch2_ref[...].T
            left[2] = normed2_ref[...].T

        terms = [(0, mixed1_ref[0]), (1, mixed2_ref[0])] + [(2, heads_ref[0, c]) for c in range(3)]
        for k, (which, term) in enumerate(terms):
            total = mm(left[which], term)

            @pl.when(step < 2)
            def _():
                given[step, k] = total.astype(BF16)

            @pl.when(step >= 2)
            def _():
                out_ref[0, k] = total.astype(BF16)

        @pl.when(step < 2)
        def _():
            over(step).start()

        @pl.when(step >= 2)
        def _():
            over(step - 2).wait_recv()
            out_ref[0] = (out_ref[0].astype(F32) + taken[step - 2].astype(F32)).astype(BF16)

        @pl.when(step == 1)
        def _():
            for copy in into:
                copy.wait()
            for copy in back:
                copy.start()

        @pl.when(step == 3)
        def _():
            for copy in copies + back:
                copy.wait()
            for y in range(2):
                over(y).wait_send()

    full = whole((rows, width))

    def turn(j):
        return 2 * (j % 2) + 1 - j // 2

    part = pl.BlockSpec((1, rows, local), lambda j: (turn(j), 0, 0))
    return comm_call(
        kernel,
        1,
        (4,),
        [ANY] * 3
        + [part, full, part, full, full]
        + [pl.BlockSpec((1, 3, rows, local), lambda j: (turn(j), 0, 0, 0))],
        [pl.BlockSpec((1, 5, width, local), lambda j: (jnp.maximum(j - 2, 0), 0, 0, 0))] + [ANY] * 3,
        [
            shape_of((2, 5, width, local)),
            shape_of((frames, 8 * span, local)),
            shape_of((frames, 2, span, width)),
            shape_of(result.shape[1:]),
        ],
        [
            pltpu.VMEM((3, width, rows), BF16),
            pltpu.VMEM((2, 5, width, local), BF16),
            pltpu.VMEM((2, 5, width, local), BF16),
            pltpu.VMEM((frames, span, local), BF16),
            pltpu.VMEM((frames, span, width), BF16),
            pltpu.SemaphoreType.DMA((4,)),
            pltpu.SemaphoreType.DMA((2, 11)),
        ],
        10 * rows * width * width,
    )(
        grad_mixed1.reshape(4, 2, frames, span, local),
        carried.reshape(2, frames, span, width),
        result,
        mixed1,
        branch1,
        mixed2.reshape(4, rows, local),
        branch2,
        normed2,
        grad_heads.reshape(4, 3, rows, local),
    )


class Halving:
    def __init__(self, slots, rows, columns, blocks, first):
        self.slots, self.rows, self.columns, self.first = slots, rows, columns, first
        self.blocks = []
        while blocks > 1:
            blocks //= 2
            self.blocks.append(blocks)

    def scratch(self):
        out = []
        for blocks in self.blocks:
            out.append(pltpu.VMEM((self.slots, blocks, 2, self.rows, self.columns), BF16))
            out.append(pltpu.VMEM((self.slots, blocks, self.rows, self.columns), BF16))
        return out

    def bind(self, refs, sems, base, wide, narrow):
        self.held, self.taken = refs[0::2], refs[1::2]
        self.sems, self.base, self.wide, self.narrow = sems, base, wide, narrow

    def bit(self, level):
        step = 2 ** (self.first + level)
        return step, (self.wide // step) % 2

    def copy(self, level):
        step, bit = self.bit(level)
        device = (self.wide + step - 2 * step * bit, self.narrow)
        return remote(
            self.held[level].at[:, :, 1 - bit],
            self.taken[level],
            self.sems,
            self.base + level,
            device,
        )

    def fill(self, level, value, slot=0):
        count = value.shape[0]
        self.held[level][slot : slot + count] = value.astype(BF16).reshape(
            (count,) + self.held[level].shape[1:]
        )

    def result(self, level):
        _, bit = self.bit(level)
        shape = self.taken[level].shape
        own = self.held[level][:, :, pl.ds(bit, 1)].reshape(shape)
        return own.astype(F32) + self.taken[level][...].astype(F32)

    def advance(self, level):
        self.copy(level).wait_recv()
        total = self.result(level)
        if level + 1 < len(self.blocks):
            self.fill(level + 1, total)
            self.copy(level + 1).start()
            return None
        return total.reshape(self.slots, self.rows, self.columns)

    def close(self):
        for level in range(len(self.blocks)):
            self.copy(level).wait_send()


FIRST = 2


def spatial_backward(
    heads,
    grad_mixed,
    project,
    normed,
    tokens,
    extra,
    gain,
    carried,
    choose,
    gain_two,
    gain_three,
    result_near,
    result_far,
    temporal_grad,
    feed_keep,
    feed_taken,
):
    _, frames, places, local = heads.shape
    width = project.shape[1]
    span = places // 8
    tile = width // 4
    wide_size = lax.axis_size("wide")
    half = wide_size // 2
    block = width // wide_size
    bits = wide_size.bit_length() - 1
    slots = temporal_grad.shape[1]
    units = feed_keep.shape[-1]
    last = slots - FIRST
    feed = Halving(2, block, units, half, 1)
    own = Halving(3, block, local, wide_size, 0)
    timed = Halving(slots, block, local, half, 1)
    engines = (feed, own, timed)
    levels = [len(engine.blocks) for engine in engines]
    attend_end = frames
    outer_end = attend_end + 4
    sum_end = outer_end + frames

    def kernel(
        heads_ref,
        mixed_ref,
        project_ref,
        normed_ref,
        tokens_ref,
        extra_ref,
        gain_ref,
        carried_ref,
        choose_ref,
        gain_two_ref,
        gain_three_ref,
        feed_keep_ref,
        feed_taken_ref,
        near_ref,
        far_ref,
        temporal_ref,
        own_out,
        timed_out,
        feed_out,
        small_out,
        output_ref,
        out_ref,
        grad_heads,
        partial,
        from_core,
        halved,
        from_y,
        done,
        gain_grad,
        table,
        small,
        small_taken,
        first_own,
        first_taken,
        first_sum,
        first_y,
        last_own,
        last_taken,
        last_sum,
        last_x,
        result_stage,
        local_sems,
        sems,
        move_sems,
        small_sems,
        halving_sems,
        *held,
    ):
        step = pl.program_id(0)
        wide, narrow, x_me, y_me, c_me = here()
        x_other = other(wide, narrow, 1, 0, 0)
        y_other = other(wide, narrow, 0, 1, 0)
        core_other = other(wide, narrow, 0, 0, 1)
        beyond_x = [
            (wide + 2**k - 2 ** (k + 1) * ((wide // 2**k) % 2), narrow) for k in range(1, bits)
        ]
        partners = [core_other, x_other] + beyond_x + [y_other]
        at = base = 0
        for engine, count in zip(engines, levels):
            engine.bind(held[at : at + 2 * count], halving_sems, base, wide, narrow)
            at, base = at + 2 * count, base + count

        def core_sum(f):
            return remote(partial.at[f, :, :, 1 - c_me], from_core.at[f], sems, f, core_other)

        def y_sum(f):
            return remote(halved.at[f, :, 1 - y_me], from_y.at[f], sems, frames + f, y_other)

        def y_back(f):
            return remote(done.at[f], out_ref.at[f, :, y_me, c_me], sems, 2 * frames + f, y_other)

        def core_back(f):
            return remote(done.at[f], out_ref.at[f, :, y_me, c_me], sems, 3 * frames + f, core_other)

        def core_onward(f):
            there = out_ref.at[f, :, 1 - y_me, c_me]
            return remote(there, there, sems, 4 * frames + f, core_other)

        def keep_own(f):
            return pltpu.make_async_copy(done.at[f], out_ref.at[f, :, y_me, c_me], local_sems.at[f])

        result = (near_ref.at[0], far_ref)

        def place(y):
            return y_me if y == 0 else 1 - y_me

        def result_x():
            there = output_ref.at[:, x_me, y_me, c_me]
            return remote(near_ref.at[1], there, move_sems, 0, x_other)

        def result_y():
            there = output_ref.at[:, 1 - x_me, y_me, c_me]
            return remote(there, there, move_sems, 1, y_other)

        def result_core(y):
            there = output_ref.at[:, x_me, place(y), c_me]
            return remote(result[y], there, move_sems, 2 + y, core_other)

        def result_onward(y):
            there = output_ref.at[:, 1 - x_me, place(y), c_me]
            return remote(there, there, move_sems, 4 + y, core_other)

        def result_in(y):
            return pltpu.make_async_copy(result[y], result_stage.at[y], local_sems.at[frames + y])

        def result_own(y):
            there = output_ref.at[:, x_me, place(y), c_me]
            return pltpu.make_async_copy(result_stage.at[y], there, local_sems.at[frames + 2 + y])

        early, late_slots = pl.ds(0, FIRST), pl.ds(FIRST, last)
        first_in = pltpu.make_async_copy(
            temporal_ref.at[:, early, :, x_me], first_own, local_sems.at[frames + 4]
        )
        last_in = pltpu.make_async_copy(
            temporal_ref.at[0, late_slots], last_own, local_sems.at[frames + 5]
        )
        first_over_x = remote(
            temporal_ref.at[:, early, :, 1 - x_me], first_taken, move_sems, 6, x_other
        )
        first_over_y = remote(first_sum.at[1], first_y, move_sems, 7, y_other)
        last_over_y = remote(temporal_ref.at[1, late_slots], last_taken, move_sems, 8, y_other)
        last_over_x = remote(last_sum.at[:, :, 1 - x_me], last_x, move_sems, 9, x_other)

        def small_copy(k):
            return remote(small.at[k], small_taken.at[k], small_sems, k, partners[k])

        @pl.when(step == 0)
        def _():
            greet(partners)
            last_over_y.start()
            first_over_x.start()
            feed.fill(0, feed_keep_ref[...].astype(F32) + feed_taken_ref[...].astype(F32))
            feed.copy(0).start()
            result_x().start()
            first_in.start()
            last_in.start()
            for y in range(2):
                result_core(y).start()
                result_in(y).start()
            gain_grad[...] = jnp.zeros_like(gain_grad)
            table[...] = jnp.zeros_like(table)

        @pl.when(step < attend_end)
        def _():
            rows = pl.ds(pl.multiple_of(step * places, places), places)
            for at in range(0, local, PAIR):
                lanes = pl.ds(at, PAIR)
                grads = attend_back_pair(
                    heads_ref[0, 0, :, lanes],
                    heads_ref[1, 0, :, lanes],
                    heads_ref[2, 0, :, lanes],
                    mixed_ref[0, :, lanes],
                    None,
                )
                for c in range(3):
                    grad_heads[c, rows, lanes] = grads[c]
            total = mm(grad_heads[0, rows], project_ref[0], NT)
            for c in range(1, 3):
                total += mm(grad_heads[c, rows], project_ref[c], NT)
            partial[step] = total.astype(BF16).reshape(2, 2, 2, span, width)
            core_sum(step).start()

        @pl.when((step >= 1) & (step < attend_end + 1))
        def _():
            f = step - 1
            core_sum(f).wait_recv()
            mine = partial[f, :, :, pl.ds(c_me, 1)].reshape(2, 2, span, width)
            halved[f] = (mine.astype(F32) + from_core[f].astype(F32)).astype(BF16)

        @pl.when(step == 1)
        def _():
            for y in range(2):
                result_in(y).wait()
                result_own(y).start()

        @pl.when(step == attend_end)
        def _():
            for f in range(frames // 2):
                y_sum(f).start()
            first_in.wait()
            first_over_x.wait_recv()
            first_sum[...] = (first_own[...].astype(F32) + first_taken[...].astype(F32)).astype(BF16)
            first_over_y.start()
            for f in range(frames // 2, frames):
                y_sum(f).start()
            feed.advance(0)

        @pl.when((step >= attend_end) & (step < outer_end))
        def _():
            pairs = tile // (2 * block)
            j = (step - attend_end) * pairs
            for c in range(3):
                grad = mm(normed_ref[...], grad_heads[c], TN).astype(BF16)
                own.held[0][c, pl.ds(j, pairs)] = grad.reshape(pairs, 2, block, local)

        @pl.when(step == attend_end + 2)
        def _():
            last_in.wait()
            last_over_y.wait_recv()
            last_sum[...] = (last_own[...].astype(F32) + last_taken[...].astype(F32)).astype(BF16)
            last_over_x.start()

        @pl.when(step == outer_end)
        def _():
            own.copy(0).start()
            result_x().wait_recv()
            result_y().start()
            result_onward(0).start()
            total = feed.advance(1)
            if total is not None:
                feed_out[...] = total

        @pl.when(step >= outer_end)
        def _():
            f = step - outer_end
            y_sum(f).wait_recv()
            mine = halved[f, :, pl.ds(y_me, 1)].reshape(2 * span, width)
            incoming = mine.astype(F32) + from_y[f].reshape(2 * span, width).astype(F32)
            start = pl.multiple_of(narrow * span, span)
            begin = jnp.concatenate(
                [tokens_ref[0, pl.ds(start, span)], tokens_ref[0, pl.ds(4 * span + start, span)]]
            )
            begin = begin.astype(F32) + extra_ref[0]
            back, gain_part = norm_back(begin, gain_ref[0:1], incoming)
            gain_grad[...] += gain_part
            grad = carried_ref[0].reshape(2 * span, width).astype(F32) + back
            table[...] += choose_ref[0] * jnp.sum(grad, axis=0, keepdims=True)
            done[f] = grad.astype(BF16).reshape(2, span, width)
            y_back(f).start()
            core_back(f).start()
            keep_own(f).start()

        @pl.when(step == outer_end + 1)
        def _():
            first_over_y.wait_recv()
            timed.fill(0, first_sum[0].astype(F32) + first_y[...].astype(F32))
            last_over_x.wait_recv()
            mine = last_sum[:, :, pl.ds(x_me, 1)].reshape(last_x.shape)
            timed.fill(0, mine.astype(F32) + last_x[...].astype(F32), FIRST)
            timed.copy(0).start()

        @pl.when(step == sum_end - 2)
        def _():
            timed.advance(0)

        @pl.when(step == sum_end - 1)
        def _():
            small[0, 0:1] = gain_grad[...]
            small[0, 1:2] = gain_two_ref[...]
            small[0, 2:3] = gain_three_ref[...]
            small[0, 3:11] = table[...]
            small[0, 11:] = jnp.zeros_like(small[0, 11:])
            small_copy(0).start()

            def small_sum(k):
                small_copy(k).wait_recv()
                small[k + 1] = small[k] + small_taken[k]
                if k + 1 < len(partners):
                    small_copy(k + 1).start()

            def back(f):
                y_back(f).wait_recv()
                core_onward(f).start()

            def finish(engine, out, level):
                if level < len(engine.blocks):
                    total = engine.advance(level)
                    if total is not None:
                        out[...] = total

            own.advance(0)
            small_sum(0)
            back(0)
            back(1)
            finish(own, own_out, 1)
            finish(timed, timed_out, 1)
            back(2)
            result_y().wait_recv()
            result_onward(1).start()
            small_sum(1)
            back(3)
            for level in range(2, max(levels)):
                finish(feed, feed_out, level)
                finish(timed, timed_out, level)
                finish(own, own_out, level)
            for k in range(2, len(partners)):
                small_sum(k)
            small_out[...] = small[len(partners)]
            for f in range(4, frames):
                back(f)
            for engine in engines:
                engine.close()
            for k in range(len(partners)):
                small_copy(k).wait_send()
            for f in range(frames):
                core_sum(f).wait_send()
                y_sum(f).wait_send()
                y_back(f).wait_send()
                core_back(f).wait()
                core_onward(f).wait()
                keep_own(f).wait()
            result_x().wait_send()
            result_y().wait_send()
            for y in range(2):
                result_core(y).wait()
                result_onward(y).wait()
                result_own(y).wait()
            for copy in (first_over_x, first_over_y, last_over_y, last_over_x):
                copy.wait_send()

    def frame(step):
        return jnp.minimum(step, frames - 1)

    def late(step):
        return jnp.clip(step - outer_end, 0, frames - 1)

    def piece(step):
        return jnp.clip(step - attend_end, 0, 3)

    block_shape = (half, 2, block, local)
    small_rows = 16
    scratch = [
        pltpu.VMEM((3, frames * places, local), BF16),
        pltpu.VMEM((frames, 2, 2, 2, span, width), BF16),
        pltpu.VMEM((frames, 2, 2, span, width), BF16),
        pltpu.VMEM((frames, 2, 2, span, width), BF16),
        pltpu.VMEM((frames, 2, span, width), BF16),
        pltpu.VMEM((frames, 2, span, width), BF16),
        pltpu.VMEM((1, width), F32),
        pltpu.VMEM((choose.shape[1], width), F32),
        pltpu.VMEM((bits + 3, small_rows, width), F32),
        pltpu.VMEM((bits + 2, small_rows, width), F32),
        pltpu.VMEM((2, FIRST, half, block, local), BF16),
        pltpu.VMEM((2, FIRST, half, block, local), BF16),
        pltpu.VMEM((2, FIRST, half, block, local), BF16),
        pltpu.VMEM((FIRST, half, block, local), BF16),
        pltpu.VMEM((last,) + block_shape, BF16),
        pltpu.VMEM((last,) + block_shape, BF16),
        pltpu.VMEM((last,) + block_shape, BF16),
        pltpu.VMEM((last, half, block, local), BF16),
        pltpu.VMEM((2, frames, span, width), BF16),
        pltpu.SemaphoreType.DMA((frames + 6,)),
        pltpu.SemaphoreType.DMA((2, 5 * frames)),
        pltpu.SemaphoreType.DMA((2, 10)),
        pltpu.SemaphoreType.DMA((2, bits + 2)),
        pltpu.SemaphoreType.DMA((2, sum(levels))),
    ]
    for engine in engines:
        scratch += engine.scratch()
    return comm_call(
        kernel,
        2,
        (sum_end,),
        [
            pl.BlockSpec((3, 1, places, local), lambda s: (0, frame(s), 0, 0)),
            pl.BlockSpec((1, places, local), lambda s: (frame(s), 0, 0)),
            whole(project.shape),
            pl.BlockSpec((frames * places, tile), lambda s: (0, piece(s))),
            pl.BlockSpec((1, places, width), lambda s: (late(s), 0, 0)),
            pl.BlockSpec((1, 1, width), lambda s: (late(s), 0, 0)),
            whole(gain.shape),
            pl.BlockSpec((1, 2, span, width), lambda s: (late(s), 0, 0, 0)),
            pl.BlockSpec((1, choose.shape[1], 1), lambda s: (late(s), 0, 0)),
            whole((1, width)),
            whole((1, width)),
            whole(feed_keep.shape),
            whole(feed_taken.shape),
            ANY,
            ANY,
            ANY,
        ],
        [
            whole((3, block, local)),
            whole((slots, block, local)),
            whole((2, block, units)),
            whole((small_rows, width)),
            ANY,
            ANY,
        ],
        [
            shape_of((3, block, local), F32),
            shape_of((slots, block, local), F32),
            shape_of((2, block, units), F32),
            shape_of((small_rows, width), F32),
            shape_of((frames, 2, 2, 2, span, width)),
            shape_of((frames, 2, 2, 2, span, width)),
        ],
        scratch,
        2 * frames * places * width * local * 8,
    )(
        heads,
        grad_mixed,
        project,
        normed.reshape(frames * places, width),
        tokens,
        extra[:, None, :],
        gain,
        carried,
        choose,
        gain_two,
        gain_three,
        feed_keep,
        feed_taken,
        result_near,
        result_far,
        temporal_grad.reshape((2, slots) + block_shape),
    )


def finish(output, grad_tokens, own, timed, feed, small, table_rows):
    frames, places, width = output.shape
    block = width // lax.axis_size("wide")
    local = own.shape[-1]
    units = feed.shape[-1]

    def kernel(
        output_ref,
        grad_ref,
        own_ref,
        timed_ref,
        feed_ref,
        small_ref,
        output_out,
        grad_out,
        gains_out,
        table_out,
        project1_out,
        merge1_out,
        project2_out,
        merge2_out,
        expand_out,
        reduce_out,
    ):
        output_out[...] = output_ref[...]
        grad_out[...] = grad_ref[...].astype(F32)

        @pl.when(pl.program_id(0) == 0)
        def _():
            project1_out[...] = own_ref[...]
            merge1_out[...] = timed_ref[0].T
            merge2_out[...] = timed_ref[1].T
            project2_out[...] = timed_ref[2:]
            expand_out[...] = feed_ref[0]
            reduce_out[...] = feed_ref[1].T
            me = lax.axis_index("wide")
            total = jnp.zeros((small_ref.shape[0], block), F32)
            for w in range(width // block):
                total += jnp.where(me == w, small_ref[:, w * block : (w + 1) * block], 0.0)
            gains_out[...] = total[:3]
            table_out[...] = total[3 : 3 + table_rows]

    frame = pl.BlockSpec((2, places, width), lambda f: (f, 0, 0))
    shapes = [
        (3, block),
        (table_rows, block),
        own.shape,
        (local, block),
        (3, block, local),
        (local, block),
        (block, units),
        (units, block),
    ]
    return call(
        kernel,
        (frames // 2,),
        [frame, frame] + [whole(part.shape) for part in (own, timed, feed, small)],
        [frame, frame] + [whole(shape) for shape in shapes],
        [shape_of(output.shape), shape_of(output.shape, F32)]
        + [shape_of(shape, F32) for shape in shapes],
        moved=30 * 2**20,
    )(output, grad_tokens, own, timed, feed, small)


def swap(value, axis, bit):
    size = lax.axis_size(axis)
    return lax.ppermute(value, axis, [(i, i ^ bit) for i in range(size)])


def after(value, *earlier):
    return lax.optimization_barrier((value,) + earlier)[0]


def body(
    tokens,
    frame_counts,
    actions,
    action_table,
    norm_gains,
    spatial_project,
    spatial_merge,
    temporal_project,
    temporal_merge,
    expand_weight,
    reduce_weight,
    grad_out,
):
    frames_dev, tokens_frame, width = tokens.shape
    wide_me, narrow_me = lax.axis_index("wide"), lax.axis_index("narrow")
    x_me = wide_me % 2
    span = tokens_frame // 8
    rows = 2 * frames_dev * span
    spatial_project = spatial_project.transpose(1, 0, 2)
    temporal_project = temporal_project.transpose(1, 0, 2)

    def keep_of(wide_place):
        frame_ids = wide_place * frames_dev + jnp.arange(frames_dev, dtype=jnp.int32)
        clip_places = jnp.arange(frame_counts.shape[0], dtype=jnp.int32)
        clip_count = jnp.sum(
            jnp.where((frame_ids // FRAMES)[:, None] == clip_places[None, :], frame_counts[None, :], 0),
            axis=1,
        )
        return (frame_ids % FRAMES < clip_count).astype(F32)

    keep_place = jnp.concatenate([keep_of(wide_me), keep_of(wide_me + 1 - 2 * x_me)])
    keep_place = jnp.broadcast_to(keep_place[:, None], (2 * frames_dev, span)).reshape(rows, 1)
    choose = (
        actions[:, None] == jnp.arange(action_table.shape[0], dtype=jnp.int32)[None, :]
    ).astype(BF16)
    extra = jnp.dot(choose, action_table, preferred_element_type=F32)

    (
        normed1,
        heads1,
        hidden1,
        normed2,
        heads2,
        mixed2,
        hidden2,
        normed3,
        normed3_first,
        normed3_second,
        mixed1,
        grad_result,
        grad_result_far,
        expand_pair,
        reduce_pair,
        merge1_all,
        project_all,
        merge2_all,
    ) = attention_forward(
        tokens,
        extra,
        norm_gains,
        spatial_project,
        spatial_merge,
        temporal_project,
        temporal_merge,
        expand_weight,
        reduce_weight,
        grad_out,
        keep_place,
    )
    mixed1 = mixed1.reshape(4, rows, mixed1.shape[-1])

    grad_result = grad_result.reshape(rows, width)
    grad_result_far = grad_result_far.reshape(rows, width)
    first_far = swap(normed3_first, "narrow", 2)
    second_far = swap(normed3_second, "narrow", 2)
    near = feed_forward(normed3, grad_result, keep_place, expand_pair, reduce_pair)
    first_far = after(first_far, near[0])
    first = feed_forward(first_far, grad_result_far, keep_place, expand_pair, reduce_pair, 0)
    second_far = after(second_far, first[0])
    second = feed_forward(second_far, grad_result_far, keep_place, expand_pair, reduce_pair, 1)
    grad_first = swap(first[4], "narrow", 2)
    grad_second = swap(second[4], "narrow", 2)
    feed_keep, feed_send = feed_outer(
        [normed3, first_far, second_far],
        [near[1], first[1], second[1]],
        [near[2], first[2], second[2]],
        [near[0], first[0], second[0]],
    )

    branch2_grad, grad_heads2, branch1_grad, grad_mixed1, carried, gain_three, gain_two = temporal_backward(
        near[4],
        after(grad_first, feed_keep),
        grad_second,
        hidden2,
        hidden1,
        grad_result,
        keep_place,
        norm_gains,
        heads2,
        merge2_all,
        project_all,
        merge1_all,
    )
    branch3_far = jnp.concatenate(
        [
            swap(after(first[3], grad_second), "narrow", 2),
            swap(after(second[3], grad_second), "narrow", 2),
        ]
    )
    feed_taken = swap(after(feed_send, grad_second), "wide", 1)
    branch3 = near[3].astype(F32) + branch3_far.astype(F32)
    result = (hidden2 + keep_place * branch3).astype(BF16).reshape(2, frames_dev, span, width)
    temporal_grad, grad_mixed1, carried, result_far = temporal_outer(
        grad_mixed1, carried, result, mixed1, branch1_grad, mixed2, branch2_grad, normed2, grad_heads2
    )

    project1_grad, temporal_grad, feed_grad, small, output, grad_tokens = spatial_backward(
        heads1,
        grad_mixed1,
        spatial_project,
        normed1,
        tokens,
        extra,
        norm_gains,
        carried,
        choose.astype(F32)[:, :, None],
        gain_two,
        gain_three,
        result,
        result_far,
        temporal_grad,
        feed_keep,
        feed_taken,
    )
    (
        output,
        grad_tokens,
        gains_grad,
        table_grad,
        project1_grad,
        merge1_grad,
        project2_grad,
        merge2_grad,
        expand_grad,
        reduce_grad,
    ) = finish(
        output.reshape(tokens.shape),
        grad_tokens.reshape(tokens.shape),
        project1_grad,
        temporal_grad,
        feed_grad,
        small,
        action_table.shape[0],
    )
    return (
        output,
        grad_tokens,
        gains_grad,
        table_grad,
        project1_grad.transpose(1, 0, 2),
        merge1_grad,
        project2_grad.transpose(1, 0, 2),
        merge2_grad,
        expand_grad,
        reduce_grad,
    )


def solution(mesh):
    return jax.shard_map(
        body,
        mesh=mesh,
        in_specs=(
            P("wide", None, None),
            P(),
            P("wide"),
            P(),
            P(),
            P(None, None, "narrow"),
            P("narrow", None),
            P(None, None, "narrow"),
            P("narrow", None),
            P(None, "narrow"),
            P("narrow", None),
            P("wide", None, None),
        ),
        out_specs=(
            P("wide", None, None),
            P("wide", None, None),
            P(None, "wide"),
            P(None, "wide"),
            P("wide", None, "narrow"),
            P("narrow", "wide"),
            P("wide", None, "narrow"),
            P("narrow", "wide"),
            P("wide", "narrow"),
            P("narrow", "wide"),
        ),
        check_vma=False,
    )
```

```python
import jax
import jax.numpy as jnp
from jax import lax
from jax.experimental import pallas as pl
from jax.experimental.pallas import tpu as pltpu
from jax.sharding import PartitionSpec as P

HD = 64
FRAMES = 16
GROUP = 16
PAIR = 2 * HD

EPSILON = 1e-06
NEGATIVE = -1e30
F32 = jnp.float32
BF16 = jnp.bfloat16
VMEM_LIMIT = 56 * 1024 * 1024
NN = (((1,), (0,)), ((), ()))
NT = (((1,), (1,)), ((), ()))
TN = (((0,), (0,)), ((), ()))


def mm(left, right, form=NN):
    return lax.dot_general(left, right, form, preferred_element_type=F32)


def root(value):
    return lax.rsqrt(jnp.mean(value * value, axis=-1, keepdims=True) + EPSILON)


def norm_back(value, gain, incoming):
    scale = root(value)
    scaled = gain * incoming
    inner = jnp.mean(scaled * value, axis=-1, keepdims=True)
    back = scale * scaled - (scale * scale * scale) * inner * value
    return back, jnp.sum(incoming * value * scale, axis=0, keepdims=True)


def sides():
    lane = lax.broadcasted_iota(jnp.int32, (1, PAIR), 1)
    low = (lane < HD).astype(F32)
    return lane < HD, low.astype(BF16), (1.0 - low).astype(BF16)


def attend_pair(queries, key_rows, value_rows, allowed):
    is_low, low, high = sides()
    mixed = []
    for side in (low, high):
        scores = mm(queries * (side * HD ** (-0.5)), key_rows, NT)
        if allowed is not None:
            scores = jnp.where(allowed, scores, NEGATIVE)
        shares = jnp.exp(scores - jnp.max(scores, axis=-1, keepdims=True))
        shares = shares * (1.0 / jnp.sum(shares, axis=-1, keepdims=True))
        mixed.append(mm(shares.astype(BF16), value_rows))
    return jnp.where(is_low, mixed[0], mixed[1]).astype(BF16)


def attend_back_pair(queries, key_rows, value_rows, grad_mixed, allowed):
    factor = HD ** (-0.5)
    is_low, low, high = sides()
    parts = []
    for side in (low, high):
        scores = mm(key_rows, queries * (side * factor), NT)
        if allowed is not None:
            scores = jnp.where(allowed, scores, NEGATIVE)
        chances = jnp.exp(scores - jnp.max(scores, axis=0, keepdims=True))
        chances = chances * (1.0 / jnp.sum(chances, axis=0, keepdims=True))
        grad_chances = mm(value_rows, grad_mixed * side, NT)
        shift = jnp.sum(grad_chances * chances, axis=0, keepdims=True)
        grad_scores = (chances * (grad_chances - shift)).astype(BF16)
        parts.append(
            (
                mm(grad_scores, key_rows, TN) * factor,
                mm(grad_scores, queries) * factor,
                mm(chances.astype(BF16), grad_mixed),
            )
        )
    return [jnp.where(is_low, a, b).astype(BF16) for a, b in zip(parts[0], parts[1])]


def whole(shape):
    return pl.BlockSpec(shape, lambda *_: (0,) * len(shape))


def call(kernel, grid, in_specs, out_specs, out_shape, scratch=(), flops=0, moved=0):
    return pl.pallas_call(
        kernel,
        grid=grid,
        in_specs=in_specs,
        out_specs=out_specs,
        out_shape=out_shape,
        scratch_shapes=list(scratch),
        compiler_params=pltpu.CompilerParams(vmem_limit_bytes=VMEM_LIMIT),
        cost_estimate=pl.CostEstimate(flops=flops, bytes_accessed=moved, transcendentals=0),
    )


def shape_of(shape, kind=BF16):
    return jax.ShapeDtypeStruct(shape, kind)


def place_masks(x_me, frames_all, transposed):
    rows = frames_all * GROUP
    shape = (rows, rows)
    query = lax.broadcasted_iota(jnp.int32, shape, 1 if transposed else 0)
    key = lax.broadcasted_iota(jnp.int32, shape, 0 if transposed else 1)
    query_frame = (query // GROUP + x_me * (frames_all // 2)) % frames_all
    key_frame = (key // GROUP + x_me * (frames_all // 2)) % frames_all
    return (query % GROUP == key % GROUP) & (key_frame <= query_frame)


RATE = 0.7978845608028654
CUBIC = 0.044715


def feed_forward(normed, grad, keep, expand, reduce, which=0):
    rows, width = normed.shape
    cores, _, units = expand.shape
    block = 512
    per = units // block

    def kernel(
        normed_ref,
        grad_ref,
        keep_ref,
        expand_ref,
        reduce_ref,
        active_ref,
        inner_ref,
        grad_branch_ref,
        branch_ref,
        grad_normed_ref,
        branch_sum,
        grad_sum,
    ):
        step = pl.program_id(0)

        @pl.when(step == 0)
        def _():
            grad_branch_ref[...] = (keep_ref[...] * grad_ref[...].astype(F32)).astype(BF16)
            branch_sum[...] = jnp.zeros_like(branch_sum)
            grad_sum[...] = jnp.zeros_like(grad_sum)

        inner = mm(normed_ref[...], expand_ref[0])
        grad_active = mm(grad_branch_ref[...], reduce_ref[0], NT)
        square = inner * inner
        bend = jnp.tanh(RATE * inner * (1.0 + CUBIC * square))
        half = 0.5 * (1.0 + bend)
        active = (inner * half).astype(BF16)
        slope = half + (0.5 * RATE) * inner * (1.0 - bend * bend) * (1.0 + (3.0 * CUBIC) * square)
        grad_inner = (grad_active * slope).astype(BF16)
        active_ref[...] = active
        inner_ref[...] = grad_inner
        branch_sum[...] += mm(active, reduce_ref[0])
        grad_sum[...] += mm(grad_inner, expand_ref[0], NT)

        @pl.when(step == cores * per - 1)
        def _():
            branch_ref[...] = branch_sum[...].astype(BF16)
            grad_normed_ref[...] = grad_sum[...].astype(BF16)

    full = whole((rows, width))
    return call(
        kernel,
        (cores * per,),
        [
            full,
            pl.BlockSpec((rows, width), lambda j: (which, 0)),
            pl.BlockSpec((rows, 1), lambda j: (which, 0)),
            pl.BlockSpec((1, width, block), lambda j: (j // per, 0, j % per)),
            pl.BlockSpec((1, block, width), lambda j: (j // per, j % per, 0)),
        ],
        [
            pl.BlockSpec((rows, block), lambda j: (0, j)),
            pl.BlockSpec((rows, block), lambda j: (0, j)),
            full,
            full,
            full,
        ],
        [
            shape_of((rows, cores * units)),
            shape_of((rows, cores * units)),
            shape_of((rows, width)),
            shape_of((rows, width)),
            shape_of((rows, width)),
        ],
        scratch=[pltpu.VMEM((rows, width), F32), pltpu.VMEM((rows, width), F32)],
        flops=8 * rows * width * cores * units,
        moved=18 * 2**20,
    )(normed, grad, keep, expand, reduce)


def temporal_backward(
    grad_near, grad_first, grad_second, hidden2, hidden1, grad_result, keep, gains, heads, merge2, project, merge1
):
    rows, width = hidden1.shape
    local = merge1.shape[1]
    span = rows // FRAMES
    group_rows = FRAMES * GROUP

    def kernel(
        near_ref,
        first_ref,
        second_ref,
        hidden2_ref,
        hidden1_ref,
        result_ref,
        keep_ref,
        gains_ref,
        heads_ref,
        merge2_ref,
        project_ref,
        merge1_ref,
        branch2_ref,
        grad_heads_ref,
        branch1_ref,
        mixed1_ref,
        carried_ref,
        gain3_ref,
        gain2_ref,
        grad_hidden,
        grad_normed,
        grad_mixed,
    ):
        step = pl.program_id(0)

        @pl.when(step == 0)
        def _():
            far = jnp.concatenate([first_ref[...], second_ref[...]])
            incoming = near_ref[...].astype(F32) + far.astype(F32)
            back, gain3_ref[...] = norm_back(hidden2_ref[...], gains_ref[2:3], incoming)
            total = result_ref[...].astype(F32) + back
            grad_hidden[...] = total
            branch2_ref[...] = (keep_ref[...] * total).astype(BF16)
            grad_normed[...] = jnp.zeros_like(grad_normed)

        back_mixed = mm(branch2_ref[...], merge2_ref[0], NT).astype(BF16)
        grad_mixed[...] = back_mixed.reshape(FRAMES, span, local)
        allowed = place_masks(lax.axis_index("wide") % 2, FRAMES, True)
        for g in range(span // GROUP):
            band = pl.ds(g * GROUP, GROUP)
            for at in range(0, local, PAIR):
                part = pl.ds(at, PAIR)
                terms = [heads_ref[0, c, :, band, part].reshape(group_rows, PAIR) for c in range(3)]
                grad = grad_mixed[:, band, part].reshape(group_rows, PAIR)
                grads = attend_back_pair(*terms, grad, allowed)
                for c in range(3):
                    grad_heads_ref[0, c, :, band, part] = grads[c].reshape(FRAMES, GROUP, PAIR)
        total = mm(grad_heads_ref[0, 0].reshape(rows, local), project_ref[0, 0], NT)
        for c in range(1, 3):
            total += mm(grad_heads_ref[0, c].reshape(rows, local), project_ref[0, c], NT)
        grad_normed[...] += total

        @pl.when(step == 3)
        def _():
            back, gain2_ref[...] = norm_back(hidden1_ref[...], gains_ref[1:2], grad_normed[...])
            total = grad_hidden[...] + back
            carried_ref[...] = total.astype(BF16)
            branch1_ref[...] = (keep_ref[...] * total).astype(BF16)
            for n in range(4):
                mixed1_ref[n] = mm(branch1_ref[...], merge1_ref[n], NT).astype(BF16)

    full = whole((rows, width))
    row = whole((1, width))
    return call(
        kernel,
        (4,),
        [
            full,
            whole((rows // 2, width)),
            whole((rows // 2, width)),
            full,
            full,
            full,
            whole((rows, 1)),
            whole((3, width)),
            pl.BlockSpec((1, 3, FRAMES, span, local), lambda n: (n, 0, 0, 0, 0)),
            pl.BlockSpec((1, local, width), lambda n: (n, 0, 0)),
            pl.BlockSpec((1, 3, width, local), lambda n: (n, 0, 0, 0)),
            whole((4, local, width)),
        ],
        [
            full,
            pl.BlockSpec((1, 3, FRAMES, span, local), lambda n: (n, 0, 0, 0, 0)),
            full,
            whole((4, rows, local)),
            full,
            row,
            row,
        ],
        [
            shape_of((rows, width)),
            shape_of((4, 3, FRAMES, span, local)),
            shape_of((rows, width)),
            shape_of((4, rows, local)),
            shape_of((rows, width)),
            shape_of((1, width), F32),
            shape_of((1, width), F32),
        ],
        scratch=[
            pltpu.VMEM((rows, width), F32),
            pltpu.VMEM((rows, width), F32),
            pltpu.VMEM((FRAMES, span, local), BF16),
        ],
        flops=2 * rows * width * width * 8,
        moved=30 * 2**20,
    )(grad_near, grad_first, grad_second, hidden2, hidden1, grad_result, keep, gains, heads, merge2, project, merge1)


def here():
    wide, narrow = lax.axis_index("wide"), lax.axis_index("narrow")
    return wide, narrow, wide % 2, narrow // 2, narrow % 2


def other(wide, narrow, x, y, core):
    if x:
        wide = wide + 1 - 2 * (wide % 2)
    if y:
        narrow = (narrow + 2) % 4
    if core:
        narrow = narrow + 1 - 2 * (narrow % 2)
    return wide, narrow


def beyond(wide, narrow):
    return wide + 2 - 4 * ((wide // 2) % 2), narrow


def place_of(wide, narrow, span):
    return pl.multiple_of(((wide % 2) * 4 + narrow) * span, span)


def remote(src, dst, sems, i, device):
    return pltpu.make_async_remote_copy(
        src_ref=src,
        dst_ref=dst,
        send_sem=sems.at[0, i],
        recv_sem=sems.at[1, i],
        device_id=device,
        device_id_type=pl.DeviceIdType.MESH,
    )


def greet(devices):
    barrier = pltpu.get_barrier_semaphore()
    for device in devices:
        pl.semaphore_signal(
            barrier, inc=1, device_id=device, device_id_type=pl.DeviceIdType.MESH
        )
    pl.semaphore_wait(barrier, len(devices))


OTHERS = [(x, y, c) for x in range(2) for y in range(2) for c in range(2) if x + y + c > 0]
ANY = pl.BlockSpec(memory_space=pl.ANY)


def comm_call(kernel, number, grid, in_specs, out_specs, out_shape, scratch, flops, moved=30 * 2**20):
    return pl.pallas_call(
        kernel,
        grid=grid,
        in_specs=in_specs,
        out_specs=out_specs,
        out_shape=out_shape,
        scratch_shapes=scratch,
        compiler_params=pltpu.CompilerParams(
            vmem_limit_bytes=VMEM_LIMIT, collective_id=number, has_side_effects=True
        ),
        cost_estimate=pl.CostEstimate(flops=flops, bytes_accessed=moved, transcendentals=0),
    )


def attention_forward(
    tokens,
    extra,
    gains,
    project,
    merge1,
    project2,
    merge2,
    expand,
    reduce,
    grad_out,
    keep,
):
    frames, places, width = tokens.shape
    local = project.shape[-1]
    span = places // 8
    rows = FRAMES * span
    group_rows = FRAMES * GROUP
    half = frames // 2
    shards = (merge1, project2[0], project2[1], project2[2], merge2)
    count = len(shards)

    def kernel(
        tokens_ref,
        extra_ref,
        gains_ref,
        project_ref,
        keep_ref,
        all_tokens,
        all_extra,
        grad_ref,
        expand_ref,
        reduce_ref,
        merge1_ref,
        project2_ref,
        merge2_ref,
        normed_ref,
        heads_ref,
        hidden1_ref,
        normed2_ref,
        heads2_ref,
        mixed2_ref,
        hidden2_ref,
        normed3_ref,
        first_ref,
        second_ref,
        mixed_out,
        grad_near,
        grad_far,
        expand_pair,
        reduce_pair,
        merge1_out,
        project2_out,
        merge2_out,
        mixed_ref,
        mixed_all,
        tokens_place,
        extra_place,
        merge1_all,
        project2_all,
        merge2_all,
        local_sems,
        move_sems,
        shard_sems,
        mixed_sems,
        *stage,
    ):
        step = pl.program_id(0)
        wide, narrow, x_me, _, _ = here()
        half_me = (wide // 2) % 2
        x_other = other(wide, narrow, 1, 0, 0)
        y_other = other(wide, narrow, 0, 1, 0)
        core_other = other(wide, narrow, 0, 0, 1)
        z_other = beyond(wide, narrow)
        mine = pl.ds(place_of(wide, narrow, span), span)
        near_y = pl.ds(place_of(*y_other, span), span)
        shard = [merge1_ref] + [project2_ref.at[c] for c in range(3)] + [merge2_ref]
        full = [merge1_all] + [project2_all.at[:, c] for c in range(3)] + [merge2_all]

        own = [
            (expand_ref, expand_pair.at[0]),
            (reduce_ref, reduce_pair.at[0]),
            (grad_ref.at[:, mine], grad_near.at[0]),
            (grad_ref.at[:, near_y], grad_far.at[0]),
        ]
        into = [
            pltpu.make_async_copy(a, v, local_sems.at[0, i])
            for i, ((a, _), v) in enumerate(zip(own, stage))
        ]
        back = [
            pltpu.make_async_copy(v, b, local_sems.at[1, i])
            for i, ((_, b), v) in enumerate(zip(own, stage))
        ]
        inside = [
            (all_tokens.at[:, mine], tokens_place.at[0]),
            (all_extra, extra_place.at[0]),
        ] + [(shard[k], full[k].at[0]) for k in range(count)]
        inside = [
            pltpu.make_async_copy(a, b, local_sems.at[0, 4 + i]) for i, (a, b) in enumerate(inside)
        ]
        leaving = [
            (mixed_all, mixed_out),
            (merge1_all, merge1_out),
            (project2_all, project2_out),
            (merge2_all, merge2_out),
        ]
        leaving = [
            pltpu.make_async_copy(a, b, local_sems.at[1, 4 + i]) for i, (a, b) in enumerate(leaving)
        ]
        far = pl.ds(place_of(*x_other, span), span)
        far_y = pl.ds(place_of(*other(wide, narrow, 1, 1, 0), span), span)
        first = [
            remote(all_tokens.at[:, far], tokens_place.at[1], move_sems, 0, x_other),
            remote(all_extra, extra_place.at[1], move_sems, 1, x_other),
            remote(expand_ref, expand_pair.at[1], move_sems, 2, core_other),
            remote(reduce_ref, reduce_pair.at[1], move_sems, 3, core_other),
        ]
        last = [
            remote(grad_ref.at[:, far], grad_near.at[1], move_sems, 4, x_other),
            remote(grad_ref.at[:, far_y], grad_far.at[1], move_sems, 5, x_other),
        ]

        def part(k, which):
            count = shards[k].shape[0] // 2
            return pl.ds(pl.multiple_of(which * count, count), count)

        def over_core(k):
            return remote(shard[k], full[k].at[1], shard_sems, 5 * k, core_other)

        def over_y(k):
            some = part(k, half_me)
            return remote(shard[k].at[some], full[k].at[2, some], shard_sems, 5 * k + 1, y_other)

        def onward(k, which, i, device, slot):
            some = part(k, which)
            return remote(full[k].at[2, some], full[k].at[slot, some], shard_sems, 5 * k + i, device)

        def over_z(k):
            return onward(k, half_me, 2, z_other, 2)

        def near_half(k):
            return onward(k, half_me, 3, core_other, 3)

        def far_half(k):
            return onward(k, 1 - half_me, 4, core_other, 3)

        def forward(k):
            over_y(k).wait_recv()
            over_z(k).start()
            near_half(k).start()

        def complete(k):
            over_z(k).wait_recv()
            far_half(k).start()

        def mixed_copies(chunk):
            copies = []
            some = pl.ds(chunk * (half // 2), half // 2)
            for i, (x, y, c) in enumerate(OTHERS):
                device = other(wide, narrow, x, y, c)
                copies.append(
                    remote(
                        mixed_ref.at[some, pl.ds(place_of(*device, span), span)],
                        mixed_all.at[2 * y + c, x, some],
                        mixed_sems,
                        7 * chunk + i,
                        device,
                    )
                )
            here_copy = pltpu.make_async_copy(
                mixed_ref.at[some, mine], mixed_all.at[0, 0, some], local_sems.at[chunk % 2, 11 + chunk // 2]
            )
            return copies + [here_copy]

        @pl.when(step == 0)
        def _():
            greet([other(wide, narrow, *o) for o in OTHERS] + [z_other])
            for k in range(3):
                over_y(k).start()
            for copy in first:
                copy.start()
            for k in range(count):
                over_core(k).start()
            for copy in into + inside:
                copy.start()

        @pl.when(step == 2)
        def _():
            for copy in into:
                copy.wait()
            for copy in back:
                copy.start()

        @pl.when(step < frames)
        def _():
            start = tokens_ref[0].astype(F32) + extra_ref[0]
            normed = (start * root(start) * gains_ref[0:1]).astype(BF16)
            normed_ref[0] = normed
            for c in range(3):
                heads_ref[c, 0] = mm(normed, project_ref[c]).astype(BF16)
            for at in range(0, local, PAIR):
                lanes = pl.ds(at, PAIR)
                mixed_ref[step, :, lanes] = attend_pair(
                    heads_ref[0, 0, :, lanes],
                    heads_ref[1, 0, :, lanes],
                    heads_ref[2, 0, :, lanes],
                    None,
                )

        @pl.when(step == 2)
        def _():
            forward(0)

        for chunk in range(3):

            @pl.when(step == 2 * chunk + 1)
            def _():
                for copy in mixed_copies(chunk):
                    copy.start()

        @pl.when(step == half)
        def _():
            forward(1)

        @pl.when(step == half + 1)
        def _():
            complete(0)

        @pl.when(step == half + 2)
        def _():
            forward(2)

        @pl.when(step == frames - 1)
        def _():
            for copy in mixed_copies(3):
                copy.start()
            over_y(3).start()
            over_y(4).start()
            for copy in last:
                copy.start()
            complete(1)

        @pl.when(step == frames)
        def _():
            for copy in inside:
                copy.wait()
            over_core(0).wait_recv()
            near_half(0).wait_recv()
            far_half(0).wait_recv()
            first[0].wait_recv()
            first[1].wait_recv()
            for chunk in range(4):
                for copy in mixed_copies(chunk):
                    copy.wait()
            leaving[0].start()
            leaving[1].start()
            branch = mm(mixed_all[0].reshape(rows, local), merge1_all[0])
            for n in range(1, 4):
                branch += mm(mixed_all[n].reshape(rows, local), merge1_all[n])
            begin = tokens_place[...].astype(F32) + extra_place[...]
            hidden1 = begin.reshape(rows, width) + keep_ref[...] * branch
            hidden1_ref[...] = hidden1
            hidden2_ref[...] = hidden1
            normed2_ref[...] = (hidden1 * root(hidden1) * gains_ref[1:2]).astype(BF16)

        @pl.when(step == frames + 1)
        def _():
            complete(2)
            forward(3)
            for k in range(1, count):
                over_core(k).wait_recv()

        @pl.when(step == frames + 2)
        def _():
            complete(3)

        @pl.when(step == frames + 3)
        def _():
            for k in range(1, 4):
                near_half(k).wait_recv()
                far_half(k).wait_recv()
            leaving[2].start()

        @pl.when(step >= frames)
        def _():
            n = step - frames
            for c in range(3):
                head = mm(normed2_ref[...], project2_all[n, c]).astype(BF16)
                heads2_ref[0, c] = head.reshape(FRAMES, span, local)
            allowed = place_masks(x_me, FRAMES, False)
            for g in range(span // GROUP):
                band = pl.ds(g * GROUP, GROUP)
                for at in range(0, local, PAIR):
                    lanes = pl.ds(at, PAIR)
                    terms = [
                        heads2_ref[0, c, :, band, lanes].reshape(group_rows, PAIR) for c in range(3)
                    ]
                    mixed = attend_pair(*terms, allowed)
                    mixed2_ref[0, :, band, lanes] = mixed.reshape(FRAMES, GROUP, PAIR)

        @pl.when(step == frames + 1)
        def _():
            forward(4)

        @pl.when(step == frames + 2)
        def _():
            complete(4)

        @pl.when(step == frames + 3)
        def _():
            near_half(4).wait_recv()
            far_half(4).wait_recv()
            leaving[3].start()

        @pl.when(step >= frames)
        def _():
            merged = mm(mixed2_ref[0].reshape(rows, local), merge2_all[step - frames])
            hidden2_ref[...] += keep_ref[...] * merged

        @pl.when(step == frames + 3)
        def _():
            hidden2 = hidden2_ref[...]
            normed3 = (hidden2 * root(hidden2) * gains_ref[2:3]).astype(BF16)
            normed3_ref[...] = normed3
            first_ref[...] = normed3[: rows // 2]
            second_ref[...] = normed3[rows // 2 :]
            for copy in first[2:] + last:
                copy.wait()
            for copy in first[:2]:
                copy.wait_send()
            for copy in back + leaving:
                copy.wait()
            for k in range(count):
                for copy in (over_core(k), over_y(k), over_z(k), near_half(k), far_half(k)):
                    copy.wait_send()

    def frame(step):
        return jnp.minimum(step, frames - 1)

    def turn(step):
        return jnp.maximum(step - frames, 0)

    full = whole((rows, width))
    return comm_call(
        kernel,
        0,
        (frames + 4,),
        [
            pl.BlockSpec((1, places, width), lambda s: (frame(s), 0, 0)),
            pl.BlockSpec((1, 1, width), lambda s: (frame(s), 0, 0)),
            whole((3, width)),
            whole(project.shape),
            whole((rows, 1)),
        ]
        + [ANY] * 8,
        [
            pl.BlockSpec((1, places, width), lambda s: (frame(s), 0, 0)),
            pl.BlockSpec((3, 1, places, local), lambda s: (0, frame(s), 0, 0)),
            full,
            full,
            pl.BlockSpec((1, 3, FRAMES, span, local), lambda s: (turn(s), 0, 0, 0, 0)),
            pl.BlockSpec((1, FRAMES, span, local), lambda s: (turn(s), 0, 0, 0)),
            full,
            full,
            whole((rows // 2, width)),
            whole((rows // 2, width)),
        ]
        + [ANY] * 8,
        [
            shape_of((frames, places, width)),
            shape_of((3, frames, places, local)),
            shape_of((rows, width), F32),
            shape_of((rows, width)),
            shape_of((4, 3, FRAMES, span, local)),
            shape_of((4, FRAMES, span, local)),
            shape_of((rows, width), F32),
            shape_of((rows, width)),
            shape_of((rows // 2, width)),
            shape_of((rows // 2, width)),
            shape_of((4, 2, frames, span, local)),
            shape_of((2, frames, span, width)),
            shape_of((2, frames, span, width)),
            shape_of((2,) + expand.shape),
            shape_of((2,) + reduce.shape),
            shape_of((4,) + merge1.shape),
            shape_of((4,) + project2.shape),
            shape_of((4,) + merge2.shape),
        ],
        [
            pltpu.VMEM((frames, places, local), BF16),
            pltpu.VMEM((4, 2, frames, span, local), BF16),
            pltpu.VMEM((2, frames, span, width), BF16),
            pltpu.VMEM((2, frames, 1, width), F32),
            pltpu.VMEM((4,) + merge1.shape, BF16),
            pltpu.VMEM((4,) + project2.shape, BF16),
            pltpu.VMEM((4,) + merge2.shape, BF16),
            pltpu.SemaphoreType.DMA((2, 13)),
            pltpu.SemaphoreType.DMA((2, 6)),
            pltpu.SemaphoreType.DMA((2, 5 * count)),
            pltpu.SemaphoreType.DMA((2, 28)),
            pltpu.VMEM(expand.shape, BF16),
            pltpu.VMEM(reduce.shape, BF16),
            pltpu.VMEM((frames, span, width), BF16),
            pltpu.VMEM((frames, span, width), BF16),
        ],
        2 * frames * places * width * local * 4 + 2 * rows * width * width * 6,
    )(
        tokens,
        extra[:, None, :],
        gains,
        project,
        keep,
        tokens,
        extra[:, None, :],
        grad_out,
        expand,
        reduce,
        merge1,
        project2,
        merge2,
    )


def feed_outer(normed, grad_inner, grad_branch, active):
    width = normed[0].shape[1]
    units = active[0].shape[1] // 2
    ends = [0]
    for part in normed:
        ends.append(ends[-1] + part.shape[0])
    rows, count = ends[-1], len(normed)
    block = 512
    per = units // block
    wide = lax.axis_size("wide")
    split = (2, wide // 2, 2, width // wide, block)

    def kernel(*refs):
        normed_refs, branch_refs = refs[:count], refs[count : 2 * count]
        inner_refs, active_refs = refs[2 * count : 3 * count], refs[3 * count : 4 * count]
        keep_ref, send_ref, left, right, total, given, taken, sems = refs[4 * count :]
        step = pl.program_id(0)
        wide, narrow, x_me, _, _ = here()
        core_other = other(wide, narrow, 0, 0, 1)

        def over(j):
            return remote(given.at[j], taken.at[j], sems, j, core_other)

        @pl.when(step == 0)
        def _():
            for k in range(count):
                left[:, ends[k] : ends[k + 1]] = normed_refs[k][...].T
                right[:, ends[k] : ends[k + 1]] = branch_refs[k][...].T

        def product(side, parts):
            out = mm(side[:, : ends[1]], parts[0][...])
            for k in range(1, count):
                out += mm(side[:, ends[k] : ends[k + 1]], parts[k][...])
            return out

        expand = product(left, inner_refs)
        reduce = product(right, active_refs)

        @pl.when(step == 0)
        def _():
            greet([core_other])

        @pl.when(step < per)
        def _():
            given[step, 0] = expand.astype(BF16)
            given[step, 1] = reduce.astype(BF16)
            over(step).start()

        @pl.when(step >= per)
        def _():
            j = step - per
            over(j).wait_recv()
            half = split[1:]
            total[0] = (expand + taken[j, 0].astype(F32)).astype(BF16).reshape(half)
            total[1] = (reduce + taken[j, 1].astype(F32)).astype(BF16).reshape(half)
            out = keep_ref.shape
            keep_ref[...] = total[:, :, pl.ds(x_me, 1)].reshape(out)
            send_ref[...] = total[:, :, pl.ds(1 - x_me, 1)].reshape(out)

        @pl.when(step == 2 * per - 1)
        def _():
            for j in range(per):
                over(j).wait_send()

    def columns(part):
        return pl.BlockSpec((part.shape[0], block), lambda j: (0, (j + per) % (2 * per)))

    out = pl.BlockSpec((2, width // 2, block), lambda j: (0, 0, jnp.maximum(j - per, 0)))
    return comm_call(
        kernel,
        3,
        (2 * per,),
        [whole(part.shape) for part in normed + grad_branch]
        + [columns(part) for part in grad_inner + active],
        [out, out],
        [shape_of((2, width // 2, units))] * 2,
        [
            pltpu.VMEM((width, rows), BF16),
            pltpu.VMEM((width, rows), BF16),
            pltpu.VMEM(split, BF16),
            pltpu.VMEM((per, 2, width, block), BF16),
            pltpu.VMEM((per, 2, width, block), BF16),
            pltpu.SemaphoreType.DMA((2, per)),
        ],
        2**20,
        2**20,
    )(*normed, *grad_branch, *grad_inner, *active)


def temporal_outer(
    grad_mixed1, carried, result, mixed1, branch1, mixed2, branch2, normed2, grad_heads
):
    rows, width = branch1.shape
    local = mixed1.shape[-1]
    span = rows // FRAMES
    frames = FRAMES // 2

    def kernel(
        grad_ref,
        carried_ref,
        result_ref,
        mixed1_ref,
        branch1_ref,
        mixed2_ref,
        branch2_ref,
        normed2_ref,
        heads_ref,
        out_ref,
        grad_own,
        carried_own,
        result_far,
        left,
        given,
        taken,
        grad_stage,
        carried_stage,
        local_sems,
        sems,
    ):
        step = pl.program_id(0)
        wide, narrow, x_me, _, _ = here()
        x_other = other(wide, narrow, 1, 0, 0)
        mine = pl.ds(place_of(wide, narrow, span), span)
        copies = [
            remote(
                grad_ref.at[2 * y + c, x],
                grad_own.at[:, mine],
                sems,
                i,
                other(wide, narrow, x, y, c),
            )
            for i, (x, y, c) in enumerate(OTHERS)
        ]
        copies.append(remote(carried_ref.at[1], carried_own.at[:, x_me], sems, 7, x_other))
        copies.append(remote(result_ref.at[0], result_far, sems, 8, other(wide, narrow, 0, 1, 0)))

        def over(y):
            return remote(given.at[y], taken.at[y], sems, 9 + y, other(wide, narrow, 0, 0, 1))

        into = [
            pltpu.make_async_copy(grad_ref.at[0, 0], grad_stage, local_sems.at[0]),
            pltpu.make_async_copy(carried_ref.at[0], carried_stage, local_sems.at[1]),
        ]
        back = [
            pltpu.make_async_copy(grad_stage, grad_own.at[:, mine], local_sems.at[2]),
            pltpu.make_async_copy(carried_stage, carried_own.at[:, x_me], local_sems.at[3]),
        ]

        @pl.when(step == 0)
        def _():
            greet([other(wide, narrow, *o) for o in OTHERS])
            for copy in copies + into:
                copy.start()
            left[0] = branch1_ref[...].T
            left[1] = branch2_ref[...].T
            left[2] = normed2_ref[...].T

        terms = [(0, mixed1_ref[0]), (1, mixed2_ref[0])] + [(2, heads_ref[0, c]) for c in range(3)]
        for k, (which, term) in enumerate(terms):
            total = mm(left[which], term)

            @pl.when(step < 2)
            def _():
                given[step, k] = total.astype(BF16)

            @pl.when(step >= 2)
            def _():
                out_ref[0, k] = total.astype(BF16)

        @pl.when(step < 2)
        def _():
            over(step).start()

        @pl.when(step >= 2)
        def _():
            over(step - 2).wait_recv()
            out_ref[0] = (out_ref[0].astype(F32) + taken[step - 2].astype(F32)).astype(BF16)

        @pl.when(step == 1)
        def _():
            for copy in into:
                copy.wait()
            for copy in back:
                copy.start()

        @pl.when(step == 3)
        def _():
            for copy in copies + back:
                copy.wait()
            for y in range(2):
                over(y).wait_send()

    full = whole((rows, width))

    def turn(j):
        return 2 * (j % 2) + 1 - j // 2

    part = pl.BlockSpec((1, rows, local), lambda j: (turn(j), 0, 0))
    return comm_call(
        kernel,
        1,
        (4,),
        [ANY] * 3
        + [part, full, part, full, full]
        + [pl.BlockSpec((1, 3, rows, local), lambda j: (turn(j), 0, 0, 0))],
        [pl.BlockSpec((1, 5, width, local), lambda j: (jnp.maximum(j - 2, 0), 0, 0, 0))] + [ANY] * 3,
        [
            shape_of((2, 5, width, local)),
            shape_of((frames, 8 * span, local)),
            shape_of((frames, 2, span, width)),
            shape_of(result.shape[1:]),
        ],
        [
            pltpu.VMEM((3, width, rows), BF16),
            pltpu.VMEM((2, 5, width, local), BF16),
            pltpu.VMEM((2, 5, width, local), BF16),
            pltpu.VMEM((frames, span, local), BF16),
            pltpu.VMEM((frames, span, width), BF16),
            pltpu.SemaphoreType.DMA((4,)),
            pltpu.SemaphoreType.DMA((2, 11)),
        ],
        10 * rows * width * width,
    )(
        grad_mixed1.reshape(4, 2, frames, span, local),
        carried.reshape(2, frames, span, width),
        result,
        mixed1,
        branch1,
        mixed2.reshape(4, rows, local),
        branch2,
        normed2,
        grad_heads.reshape(4, 3, rows, local),
    )


class Halving:
    def __init__(self, slots, rows, columns, blocks, first):
        self.slots, self.rows, self.columns, self.first = slots, rows, columns, first
        self.blocks = []
        while blocks > 1:
            blocks //= 2
            self.blocks.append(blocks)

    def scratch(self):
        out = []
        for blocks in self.blocks:
            out.append(pltpu.VMEM((self.slots, blocks, 2, self.rows, self.columns), BF16))
            out.append(pltpu.VMEM((self.slots, blocks, self.rows, self.columns), BF16))
        return out

    def bind(self, refs, sems, base, wide, narrow):
        self.held, self.taken = refs[0::2], refs[1::2]
        self.sems, self.base, self.wide, self.narrow = sems, base, wide, narrow

    def bit(self, level):
        step = 2 ** (self.first + level)
        return step, (self.wide // step) % 2

    def copy(self, level):
        step, bit = self.bit(level)
        device = (self.wide + step - 2 * step * bit, self.narrow)
        return remote(
            self.held[level].at[:, :, 1 - bit],
            self.taken[level],
            self.sems,
            self.base + level,
            device,
        )

    def fill(self, level, value, slot=0):
        count = value.shape[0]
        self.held[level][slot : slot + count] = value.astype(BF16).reshape(
            (count,) + self.held[level].shape[1:]
        )

    def result(self, level):
        _, bit = self.bit(level)
        shape = self.taken[level].shape
        own = self.held[level][:, :, pl.ds(bit, 1)].reshape(shape)
        return own.astype(F32) + self.taken[level][...].astype(F32)

    def advance(self, level):
        self.copy(level).wait_recv()
        total = self.result(level)
        if level + 1 < len(self.blocks):
            self.fill(level + 1, total)
            self.copy(level + 1).start()
            return None
        return total.reshape(self.slots, self.rows, self.columns)

    def close(self):
        for level in range(len(self.blocks)):
            self.copy(level).wait_send()


FIRST = 2


def spatial_backward(
    heads,
    grad_mixed,
    project,
    normed,
    tokens,
    extra,
    gain,
    carried,
    choose,
    gain_two,
    gain_three,
    result_near,
    result_far,
    temporal_grad,
    feed_keep,
    feed_taken,
):
    _, frames, places, local = heads.shape
    width = project.shape[1]
    span = places // 8
    tile = width // 4
    wide_size = lax.axis_size("wide")
    half = wide_size // 2
    block = width // wide_size
    bits = wide_size.bit_length() - 1
    slots = temporal_grad.shape[1]
    units = feed_keep.shape[-1]
    last = slots - FIRST
    feed = Halving(2, block, units, half, 1)
    own = Halving(3, block, local, wide_size, 0)
    timed = Halving(slots, block, local, half, 1)
    engines = (feed, own, timed)
    levels = [len(engine.blocks) for engine in engines]
    attend_end = frames
    outer_end = attend_end + 4
    sum_end = outer_end + frames

    def kernel(
        heads_ref,
        mixed_ref,
        project_ref,
        normed_ref,
        tokens_ref,
        extra_ref,
        gain_ref,
        carried_ref,
        choose_ref,
        gain_two_ref,
        gain_three_ref,
        feed_keep_ref,
        feed_taken_ref,
        near_ref,
        far_ref,
        temporal_ref,
        own_out,
        timed_out,
        feed_out,
        small_out,
        output_ref,
        out_ref,
        grad_heads,
        partial,
        from_core,
        halved,
        from_y,
        done,
        gain_grad,
        table,
        small,
        small_taken,
        first_own,
        first_taken,
        first_sum,
        first_y,
        last_own,
        last_taken,
        last_sum,
        last_x,
        result_stage,
        local_sems,
        sems,
        move_sems,
        small_sems,
        halving_sems,
        *held,
    ):
        step = pl.program_id(0)
        wide, narrow, x_me, y_me, c_me = here()
        x_other = other(wide, narrow, 1, 0, 0)
        y_other = other(wide, narrow, 0, 1, 0)
        core_other = other(wide, narrow, 0, 0, 1)
        beyond_x = [
            (wide + 2**k - 2 ** (k + 1) * ((wide // 2**k) % 2), narrow) for k in range(1, bits)
        ]
        partners = [core_other, x_other] + beyond_x + [y_other]
        at = base = 0
        for engine, count in zip(engines, levels):
            engine.bind(held[at : at + 2 * count], halving_sems, base, wide, narrow)
            at, base = at + 2 * count, base + count

        def core_sum(f):
            return remote(partial.at[f, :, :, 1 - c_me], from_core.at[f], sems, f, core_other)

        def y_sum(f):
            return remote(halved.at[f, :, 1 - y_me], from_y.at[f], sems, frames + f, y_other)

        def y_back(f):
            return remote(done.at[f], out_ref.at[f, :, y_me, c_me], sems, 2 * frames + f, y_other)

        def core_back(f):
            return remote(done.at[f], out_ref.at[f, :, y_me, c_me], sems, 3 * frames + f, core_other)

        def core_onward(f):
            there = out_ref.at[f, :, 1 - y_me, c_me]
            return remote(there, there, sems, 4 * frames + f, core_other)

        def keep_own(f):
            return pltpu.make_async_copy(done.at[f], out_ref.at[f, :, y_me, c_me], local_sems.at[f])

        result = (near_ref.at[0], far_ref)

        def place(y):
            return y_me if y == 0 else 1 - y_me

        def result_x():
            there = output_ref.at[:, x_me, y_me, c_me]
            return remote(near_ref.at[1], there, move_sems, 0, x_other)

        def result_y():
            there = output_ref.at[:, 1 - x_me, y_me, c_me]
            return remote(there, there, move_sems, 1, y_other)

        def result_core(y):
            there = output_ref.at[:, x_me, place(y), c_me]
            return remote(result[y], there, move_sems, 2 + y, core_other)

        def result_onward(y):
            there = output_ref.at[:, 1 - x_me, place(y), c_me]
            return remote(there, there, move_sems, 4 + y, core_other)

        def result_in(y):
            return pltpu.make_async_copy(result[y], result_stage.at[y], local_sems.at[frames + y])

        def result_own(y):
            there = output_ref.at[:, x_me, place(y), c_me]
            return pltpu.make_async_copy(result_stage.at[y], there, local_sems.at[frames + 2 + y])

        early, late_slots = pl.ds(0, FIRST), pl.ds(FIRST, last)
        first_in = pltpu.make_async_copy(
            temporal_ref.at[:, early, :, x_me], first_own, local_sems.at[frames + 4]
        )
        last_in = pltpu.make_async_copy(
            temporal_ref.at[0, late_slots], last_own, local_sems.at[frames + 5]
        )
        first_over_x = remote(
            temporal_ref.at[:, early, :, 1 - x_me], first_taken, move_sems, 6, x_other
        )
        first_over_y = remote(first_sum.at[1], first_y, move_sems, 7, y_other)
        last_over_y = remote(temporal_ref.at[1, late_slots], last_taken, move_sems, 8, y_other)
        last_over_x = remote(last_sum.at[:, :, 1 - x_me], last_x, move_sems, 9, x_other)

        def small_copy(k):
            return remote(small.at[k], small_taken.at[k], small_sems, k, partners[k])

        @pl.when(step == 0)
        def _():
            greet(partners)
            last_over_y.start()
            first_over_x.start()
            feed.fill(0, feed_keep_ref[...].astype(F32) + feed_taken_ref[...].astype(F32))
            feed.copy(0).start()
            result_x().start()
            first_in.start()
            last_in.start()
            for y in range(2):
                result_core(y).start()
                result_in(y).start()
            gain_grad[...] = jnp.zeros_like(gain_grad)
            table[...] = jnp.zeros_like(table)

        @pl.when(step < attend_end)
        def _():
            rows = pl.ds(pl.multiple_of(step * places, places), places)
            for at in range(0, local, PAIR):
                lanes = pl.ds(at, PAIR)
                grads = attend_back_pair(
                    heads_ref[0, 0, :, lanes],
                    heads_ref[1, 0, :, lanes],
                    heads_ref[2, 0, :, lanes],
                    mixed_ref[0, :, lanes],
                    None,
                )
                for c in range(3):
                    grad_heads[c, rows, lanes] = grads[c]
            total = mm(grad_heads[0, rows], project_ref[0], NT)
            for c in range(1, 3):
                total += mm(grad_heads[c, rows], project_ref[c], NT)
            partial[step] = total.astype(BF16).reshape(2, 2, 2, span, width)
            core_sum(step).start()

        @pl.when((step >= 1) & (step < attend_end + 1))
        def _():
            f = step - 1
            core_sum(f).wait_recv()
            mine = partial[f, :, :, pl.ds(c_me, 1)].reshape(2, 2, span, width)
            halved[f] = (mine.astype(F32) + from_core[f].astype(F32)).astype(BF16)

        @pl.when(step == 1)
        def _():
            for y in range(2):
                result_in(y).wait()
                result_own(y).start()

        @pl.when(step == attend_end)
        def _():
            for f in range(frames // 2):
                y_sum(f).start()
            first_in.wait()
            first_over_x.wait_recv()
            first_sum[...] = (first_own[...].astype(F32) + first_taken[...].astype(F32)).astype(BF16)
            first_over_y.start()
            for f in range(frames // 2, frames):
                y_sum(f).start()
            feed.advance(0)

        @pl.when((step >= attend_end) & (step < outer_end))
        def _():
            pairs = tile // (2 * block)
            j = (step - attend_end) * pairs
            for c in range(3):
                grad = mm(normed_ref[...], grad_heads[c], TN).astype(BF16)
                own.held[0][c, pl.ds(j, pairs)] = grad.reshape(pairs, 2, block, local)

        @pl.when(step == attend_end + 2)
        def _():
            last_in.wait()
            last_over_y.wait_recv()
            last_sum[...] = (last_own[...].astype(F32) + last_taken[...].astype(F32)).astype(BF16)
            last_over_x.start()

        @pl.when(step == outer_end)
        def _():
            own.copy(0).start()
            result_x().wait_recv()
            result_y().start()
            result_onward(0).start()
            total = feed.advance(1)
            if total is not None:
                feed_out[...] = total

        @pl.when(step >= outer_end)
        def _():
            f = step - outer_end
            y_sum(f).wait_recv()
            mine = halved[f, :, pl.ds(y_me, 1)].reshape(2 * span, width)
            incoming = mine.astype(F32) + from_y[f].reshape(2 * span, width).astype(F32)
            start = pl.multiple_of(narrow * span, span)
            begin = jnp.concatenate(
                [tokens_ref[0, pl.ds(start, span)], tokens_ref[0, pl.ds(4 * span + start, span)]]
            )
            begin = begin.astype(F32) + extra_ref[0]
            back, gain_part = norm_back(begin, gain_ref[0:1], incoming)
            gain_grad[...] += gain_part
            grad = carried_ref[0].reshape(2 * span, width).astype(F32) + back
            table[...] += choose_ref[0] * jnp.sum(grad, axis=0, keepdims=True)
            done[f] = grad.astype(BF16).reshape(2, span, width)
            y_back(f).start()
            core_back(f).start()
            keep_own(f).start()

        @pl.when(step == outer_end + 1)
        def _():
            first_over_y.wait_recv()
            timed.fill(0, first_sum[0].astype(F32) + first_y[...].astype(F32))
            last_over_x.wait_recv()
            mine = last_sum[:, :, pl.ds(x_me, 1)].reshape(last_x.shape)
            timed.fill(0, mine.astype(F32) + last_x[...].astype(F32), FIRST)
            timed.copy(0).start()

        @pl.when(step == sum_end - 2)
        def _():
            timed.advance(0)

        @pl.when(step == sum_end - 1)
        def _():
            small[0, 0:1] = gain_grad[...]
            small[0, 1:2] = gain_two_ref[...]
            small[0, 2:3] = gain_three_ref[...]
            small[0, 3:11] = table[...]
            small[0, 11:] = jnp.zeros_like(small[0, 11:])
            small_copy(0).start()

            def small_sum(k):
                small_copy(k).wait_recv()
                small[k + 1] = small[k] + small_taken[k]
                if k + 1 < len(partners):
                    small_copy(k + 1).start()

            def back(f):
                y_back(f).wait_recv()
                core_onward(f).start()

            def finish(engine, out, level):
                if level < len(engine.blocks):
                    total = engine.advance(level)
                    if total is not None:
                        out[...] = total

            own.advance(0)
            small_sum(0)
            back(0)
            back(1)
            finish(own, own_out, 1)
            finish(timed, timed_out, 1)
            back(2)
            result_y().wait_recv()
            result_onward(1).start()
            small_sum(1)
            back(3)
            for level in range(2, max(levels)):
                finish(feed, feed_out, level)
                finish(timed, timed_out, level)
                finish(own, own_out, level)
            for k in range(2, len(partners)):
                small_sum(k)
            small_out[...] = small[len(partners)]
            for f in range(4, frames):
                back(f)
            for engine in engines:
                engine.close()
            for k in range(len(partners)):
                small_copy(k).wait_send()
            for f in range(frames):
                core_sum(f).wait_send()
                y_sum(f).wait_send()
                y_back(f).wait_send()
                core_back(f).wait()
                core_onward(f).wait()
                keep_own(f).wait()
            result_x().wait_send()
            result_y().wait_send()
            for y in range(2):
                result_core(y).wait()
                result_onward(y).wait()
                result_own(y).wait()
            for copy in (first_over_x, first_over_y, last_over_y, last_over_x):
                copy.wait_send()

    def frame(step):
        return jnp.minimum(step, frames - 1)

    def late(step):
        return jnp.clip(step - outer_end, 0, frames - 1)

    def piece(step):
        return jnp.clip(step - attend_end, 0, 3)

    block_shape = (half, 2, block, local)
    small_rows = 16
    scratch = [
        pltpu.VMEM((3, frames * places, local), BF16),
        pltpu.VMEM((frames, 2, 2, 2, span, width), BF16),
        pltpu.VMEM((frames, 2, 2, span, width), BF16),
        pltpu.VMEM((frames, 2, 2, span, width), BF16),
        pltpu.VMEM((frames, 2, span, width), BF16),
        pltpu.VMEM((frames, 2, span, width), BF16),
        pltpu.VMEM((1, width), F32),
        pltpu.VMEM((choose.shape[1], width), F32),
        pltpu.VMEM((bits + 3, small_rows, width), F32),
        pltpu.VMEM((bits + 2, small_rows, width), F32),
        pltpu.VMEM((2, FIRST, half, block, local), BF16),
        pltpu.VMEM((2, FIRST, half, block, local), BF16),
        pltpu.VMEM((2, FIRST, half, block, local), BF16),
        pltpu.VMEM((FIRST, half, block, local), BF16),
        pltpu.VMEM((last,) + block_shape, BF16),
        pltpu.VMEM((last,) + block_shape, BF16),
        pltpu.VMEM((last,) + block_shape, BF16),
        pltpu.VMEM((last, half, block, local), BF16),
        pltpu.VMEM((2, frames, span, width), BF16),
        pltpu.SemaphoreType.DMA((frames + 6,)),
        pltpu.SemaphoreType.DMA((2, 5 * frames)),
        pltpu.SemaphoreType.DMA((2, 10)),
        pltpu.SemaphoreType.DMA((2, bits + 2)),
        pltpu.SemaphoreType.DMA((2, sum(levels))),
    ]
    for engine in engines:
        scratch += engine.scratch()
    return comm_call(
        kernel,
        2,
        (sum_end,),
        [
            pl.BlockSpec((3, 1, places, local), lambda s: (0, frame(s), 0, 0)),
            pl.BlockSpec((1, places, local), lambda s: (frame(s), 0, 0)),
            whole(project.shape),
            pl.BlockSpec((frames * places, tile), lambda s: (0, piece(s))),
            pl.BlockSpec((1, places, width), lambda s: (late(s), 0, 0)),
            pl.BlockSpec((1, 1, width), lambda s: (late(s), 0, 0)),
            whole(gain.shape),
            pl.BlockSpec((1, 2, span, width), lambda s: (late(s), 0, 0, 0)),
            pl.BlockSpec((1, choose.shape[1], 1), lambda s: (late(s), 0, 0)),
            whole((1, width)),
            whole((1, width)),
            whole(feed_keep.shape),
            whole(feed_taken.shape),
            ANY,
            ANY,
            ANY,
        ],
        [
            whole((3, block, local)),
            whole((slots, block, local)),
            whole((2, block, units)),
            whole((small_rows, width)),
            ANY,
            ANY,
        ],
        [
            shape_of((3, block, local), F32),
            shape_of((slots, block, local), F32),
            shape_of((2, block, units), F32),
            shape_of((small_rows, width), F32),
            shape_of((frames, 2, 2, 2, span, width)),
            shape_of((frames, 2, 2, 2, span, width)),
        ],
        scratch,
        2 * frames * places * width * local * 8,
    )(
        heads,
        grad_mixed,
        project,
        normed.reshape(frames * places, width),
        tokens,
        extra[:, None, :],
        gain,
        carried,
        choose,
        gain_two,
        gain_three,
        feed_keep,
        feed_taken,
        result_near,
        result_far,
        temporal_grad.reshape((2, slots) + block_shape),
    )


def finish(output, grad_tokens, own, timed, feed, small, table_rows):
    frames, places, width = output.shape
    block = width // lax.axis_size("wide")
    local = own.shape[-1]
    units = feed.shape[-1]

    def kernel(
        output_ref,
        grad_ref,
        own_ref,
        timed_ref,
        feed_ref,
        small_ref,
        output_out,
        grad_out,
        gains_out,
        table_out,
        project1_out,
        merge1_out,
        project2_out,
        merge2_out,
        expand_out,
        reduce_out,
    ):
        output_out[...] = output_ref[...]
        grad_out[...] = grad_ref[...].astype(F32)

        @pl.when(pl.program_id(0) == 0)
        def _():
            project1_out[...] = own_ref[...]
            merge1_out[...] = timed_ref[0].T
            merge2_out[...] = timed_ref[1].T
            project2_out[...] = timed_ref[2:]
            expand_out[...] = feed_ref[0]
            reduce_out[...] = feed_ref[1].T
            me = lax.axis_index("wide")
            total = jnp.zeros((small_ref.shape[0], block), F32)
            for w in range(width // block):
                total += jnp.where(me == w, small_ref[:, w * block : (w + 1) * block], 0.0)
            gains_out[...] = total[:3]
            table_out[...] = total[3 : 3 + table_rows]

    frame = pl.BlockSpec((2, places, width), lambda f: (f, 0, 0))
    shapes = [
        (3, block),
        (table_rows, block),
        own.shape,
        (local, block),
        (3, block, local),
        (local, block),
        (block, units),
        (units, block),
    ]
    return call(
        kernel,
        (frames // 2,),
        [frame, frame] + [whole(part.shape) for part in (own, timed, feed, small)],
        [frame, frame] + [whole(shape) for shape in shapes],
        [shape_of(output.shape), shape_of(output.shape, F32)]
        + [shape_of(shape, F32) for shape in shapes],
        moved=30 * 2**20,
    )(output, grad_tokens, own, timed, feed, small)


def swap(value, axis, bit):
    size = lax.axis_size(axis)
    return lax.ppermute(value, axis, [(i, i ^ bit) for i in range(size)])


def after(value, *earlier):
    return lax.optimization_barrier((value,) + earlier)[0]


def body(
    tokens,
    frame_counts,
    actions,
    action_table,
    norm_gains,
    spatial_project,
    spatial_merge,
    temporal_project,
    temporal_merge,
    expand_weight,
    reduce_weight,
    grad_out,
):
    frames_dev, tokens_frame, width = tokens.shape
    wide_me, narrow_me = lax.axis_index("wide"), lax.axis_index("narrow")
    x_me = wide_me % 2
    span = tokens_frame // 8
    rows = 2 * frames_dev * span
    spatial_project = spatial_project.transpose(1, 0, 2)
    temporal_project = temporal_project.transpose(1, 0, 2)

    def keep_of(wide_place):
        frame_ids = wide_place * frames_dev + jnp.arange(frames_dev, dtype=jnp.int32)
        clip_places = jnp.arange(frame_counts.shape[0], dtype=jnp.int32)
        clip_count = jnp.sum(
            jnp.where((frame_ids // FRAMES)[:, None] == clip_places[None, :], frame_counts[None, :], 0),
            axis=1,
        )
        return (frame_ids % FRAMES < clip_count).astype(F32)

    keep_place = jnp.concatenate([keep_of(wide_me), keep_of(wide_me + 1 - 2 * x_me)])
    keep_place = jnp.broadcast_to(keep_place[:, None], (2 * frames_dev, span)).reshape(rows, 1)
    choose = (
        actions[:, None] == jnp.arange(action_table.shape[0], dtype=jnp.int32)[None, :]
    ).astype(BF16)
    extra = jnp.dot(choose, action_table, preferred_element_type=F32)

    (
        normed1,
        heads1,
        hidden1,
        normed2,
        heads2,
        mixed2,
        hidden2,
        normed3,
        normed3_first,
        normed3_second,
        mixed1,
        grad_result,
        grad_result_far,
        expand_pair,
        reduce_pair,
        merge1_all,
        project_all,
        merge2_all,
    ) = attention_forward(
        tokens,
        extra,
        norm_gains,
        spatial_project,
        spatial_merge,
        temporal_project,
        temporal_merge,
        expand_weight,
        reduce_weight,
        grad_out,
        keep_place,
    )
    mixed1 = mixed1.reshape(4, rows, mixed1.shape[-1])

    grad_result = grad_result.reshape(rows, width)
    grad_result_far = grad_result_far.reshape(rows, width)
    first_far = swap(normed3_first, "narrow", 2)
    second_far = swap(normed3_second, "narrow", 2)
    near = feed_forward(normed3, grad_result, keep_place, expand_pair, reduce_pair)
    first_far = after(first_far, near[0])
    first = feed_forward(first_far, grad_result_far, keep_place, expand_pair, reduce_pair, 0)
    second_far = after(second_far, first[0])
    second = feed_forward(second_far, grad_result_far, keep_place, expand_pair, reduce_pair, 1)
    grad_first = swap(first[4], "narrow", 2)
    grad_second = swap(second[4], "narrow", 2)
    feed_keep, feed_send = feed_outer(
        [normed3, first_far, second_far],
        [near[1], first[1], second[1]],
        [near[2], first[2], second[2]],
        [near[0], first[0], second[0]],
    )

    branch2_grad, grad_heads2, branch1_grad, grad_mixed1, carried, gain_three, gain_two = temporal_backward(
        near[4],
        after(grad_first, feed_keep),
        grad_second,
        hidden2,
        hidden1,
        grad_result,
        keep_place,
        norm_gains,
        heads2,
        merge2_all,
        project_all,
        merge1_all,
    )
    branch3_far = jnp.concatenate(
        [
            swap(after(first[3], grad_second), "narrow", 2),
            swap(after(second[3], grad_second), "narrow", 2),
        ]
    )
    feed_taken = swap(after(feed_send, grad_second), "wide", 1)
    branch3 = near[3].astype(F32) + branch3_far.astype(F32)
    result = (hidden2 + keep_place * branch3).astype(BF16).reshape(2, frames_dev, span, width)
    temporal_grad, grad_mixed1, carried, result_far = temporal_outer(
        grad_mixed1, carried, result, mixed1, branch1_grad, mixed2, branch2_grad, normed2, grad_heads2
    )

    project1_grad, temporal_grad, feed_grad, small, output, grad_tokens = spatial_backward(
        heads1,
        grad_mixed1,
        spatial_project,
        normed1,
        tokens,
        extra,
        norm_gains,
        carried,
        choose.astype(F32)[:, :, None],
        gain_two,
        gain_three,
        result,
        result_far,
        temporal_grad,
        feed_keep,
        feed_taken,
    )
    (
        output,
        grad_tokens,
        gains_grad,
        table_grad,
        project1_grad,
        merge1_grad,
        project2_grad,
        merge2_grad,
        expand_grad,
        reduce_grad,
    ) = finish(
        output.reshape(tokens.shape),
        grad_tokens.reshape(tokens.shape),
        project1_grad,
        temporal_grad,
        feed_grad,
        small,
        action_table.shape[0],
    )
    return (
        output,
        grad_tokens,
        gains_grad,
        table_grad,
        project1_grad.transpose(1, 0, 2),
        merge1_grad,
        project2_grad.transpose(1, 0, 2),
        merge2_grad,
        expand_grad,
        reduce_grad,
    )


def solution(mesh):
    return jax.shard_map(
        body,
        mesh=mesh,
        in_specs=(
            P("wide", None, None),
            P(),
            P("wide"),
            P(),
            P(),
            P(None, None, "narrow"),
            P("narrow", None),
            P(None, None, "narrow"),
            P("narrow", None),
            P(None, "narrow"),
            P("narrow", None),
            P("wide", None, None),
        ),
        out_specs=(
            P("wide", None, None),
            P("wide", None, None),
            P(None, "wide"),
            P(None, "wide"),
            P("wide", None, "narrow"),
            P("narrow", "wide"),
            P("wide", None, "narrow"),
            P("narrow", "wide"),
            P("wide", "narrow"),
            P("narrow", "wide"),
        ),
        check_vma=False,
    )
```

```python
import jax
import jax.numpy as jnp
from jax import lax
from jax.experimental import pallas as pl
from jax.experimental.pallas import tpu as pltpu
from jax.sharding import PartitionSpec as P

HD = 64
FRAMES = 16
GROUP = 16
PAIR = 2 * HD

EPSILON = 1e-06
NEGATIVE = -1e30
F32 = jnp.float32
BF16 = jnp.bfloat16
VMEM_LIMIT = 56 * 1024 * 1024
NN = (((1,), (0,)), ((), ()))
NT = (((1,), (1,)), ((), ()))
TN = (((0,), (0,)), ((), ()))


def mm(left, right, form=NN):
    return lax.dot_general(left, right, form, preferred_element_type=F32)


def root(value):
    return lax.rsqrt(jnp.mean(value * value, axis=-1, keepdims=True) + EPSILON)


def norm_back(value, gain, incoming):
    scale = root(value)
    scaled = gain * incoming
    inner = jnp.mean(scaled * value, axis=-1, keepdims=True)
    back = scale * scaled - (scale * scale * scale) * inner * value
    return back, jnp.sum(incoming * value * scale, axis=0, keepdims=True)


def sides():
    lane = lax.broadcasted_iota(jnp.int32, (1, PAIR), 1)
    low = (lane < HD).astype(F32)
    return lane < HD, low.astype(BF16), (1.0 - low).astype(BF16)


def attend_pair(queries, key_rows, value_rows, allowed):
    is_low, low, high = sides()
    mixed = []
    for side in (low, high):
        scores = mm(queries * (side * HD ** (-0.5)), key_rows, NT)
        if allowed is not None:
            scores = jnp.where(allowed, scores, NEGATIVE)
        shares = jnp.exp(scores - jnp.max(scores, axis=-1, keepdims=True))
        shares = shares * (1.0 / jnp.sum(shares, axis=-1, keepdims=True))
        mixed.append(mm(shares.astype(BF16), value_rows))
    return jnp.where(is_low, mixed[0], mixed[1]).astype(BF16)


def attend_back_pair(queries, key_rows, value_rows, grad_mixed, allowed):
    factor = HD ** (-0.5)
    is_low, low, high = sides()
    parts = []
    for side in (low, high):
        scores = mm(key_rows, queries * (side * factor), NT)
        if allowed is not None:
            scores = jnp.where(allowed, scores, NEGATIVE)
        chances = jnp.exp(scores - jnp.max(scores, axis=0, keepdims=True))
        chances = chances * (1.0 / jnp.sum(chances, axis=0, keepdims=True))
        grad_chances = mm(value_rows, grad_mixed * side, NT)
        shift = jnp.sum(grad_chances * chances, axis=0, keepdims=True)
        grad_scores = (chances * (grad_chances - shift)).astype(BF16)
        parts.append(
            (
                mm(grad_scores, key_rows, TN) * factor,
                mm(grad_scores, queries) * factor,
                mm(chances.astype(BF16), grad_mixed),
            )
        )
    return [jnp.where(is_low, a, b).astype(BF16) for a, b in zip(parts[0], parts[1])]


def whole(shape):
    return pl.BlockSpec(shape, lambda *_: (0,) * len(shape))


def call(kernel, grid, in_specs, out_specs, out_shape, scratch=(), flops=0, moved=0):
    return pl.pallas_call(
        kernel,
        grid=grid,
        in_specs=in_specs,
        out_specs=out_specs,
        out_shape=out_shape,
        scratch_shapes=list(scratch),
        compiler_params=pltpu.CompilerParams(vmem_limit_bytes=VMEM_LIMIT),
        cost_estimate=pl.CostEstimate(flops=flops, bytes_accessed=moved, transcendentals=0),
    )


def shape_of(shape, kind=BF16):
    return jax.ShapeDtypeStruct(shape, kind)


def place_masks(x_me, frames_all, transposed):
    rows = frames_all * GROUP
    shape = (rows, rows)
    query = lax.broadcasted_iota(jnp.int32, shape, 1 if transposed else 0)
    key = lax.broadcasted_iota(jnp.int32, shape, 0 if transposed else 1)
    query_frame = (query // GROUP + x_me * (frames_all // 2)) % frames_all
    key_frame = (key // GROUP + x_me * (frames_all // 2)) % frames_all
    return (query % GROUP == key % GROUP) & (key_frame <= query_frame)


RATE = 0.7978845608028654
CUBIC = 0.044715


def feed_forward(normed, grad, keep, expand, reduce, which=0):
    rows, width = normed.shape
    cores, _, units = expand.shape
    block = 512
    per = units // block

    def kernel(
        normed_ref,
        grad_ref,
        keep_ref,
        expand_ref,
        reduce_ref,
        active_ref,
        inner_ref,
        grad_branch_ref,
        branch_ref,
        grad_normed_ref,
        branch_sum,
        grad_sum,
    ):
        step = pl.program_id(0)

        @pl.when(step == 0)
        def _():
            grad_branch_ref[...] = (keep_ref[...] * grad_ref[...].astype(F32)).astype(BF16)
            branch_sum[...] = jnp.zeros_like(branch_sum)
            grad_sum[...] = jnp.zeros_like(grad_sum)

        inner = mm(normed_ref[...], expand_ref[0])
        grad_active = mm(grad_branch_ref[...], reduce_ref[0], NT)
        square = inner * inner
        bend = jnp.tanh(RATE * inner * (1.0 + CUBIC * square))
        half = 0.5 * (1.0 + bend)
        active = (inner * half).astype(BF16)
        slope = half + (0.5 * RATE) * inner * (1.0 - bend * bend) * (1.0 + (3.0 * CUBIC) * square)
        grad_inner = (grad_active * slope).astype(BF16)
        active_ref[...] = active
        inner_ref[...] = grad_inner
        branch_sum[...] += mm(active, reduce_ref[0])
        grad_sum[...] += mm(grad_inner, expand_ref[0], NT)

        @pl.when(step == cores * per - 1)
        def _():
            branch_ref[...] = branch_sum[...].astype(BF16)
            grad_normed_ref[...] = grad_sum[...].astype(BF16)

    full = whole((rows, width))
    return call(
        kernel,
        (cores * per,),
        [
            full,
            pl.BlockSpec((rows, width), lambda j: (which, 0)),
            pl.BlockSpec((rows, 1), lambda j: (which, 0)),
            pl.BlockSpec((1, width, block), lambda j: (j // per, 0, j % per)),
            pl.BlockSpec((1, block, width), lambda j: (j // per, j % per, 0)),
        ],
        [
            pl.BlockSpec((rows, block), lambda j: (0, j)),
            pl.BlockSpec((rows, block), lambda j: (0, j)),
            full,
            full,
            full,
        ],
        [
            shape_of((rows, cores * units)),
            shape_of((rows, cores * units)),
            shape_of((rows, width)),
            shape_of((rows, width)),
            shape_of((rows, width)),
        ],
        scratch=[pltpu.VMEM((rows, width), F32), pltpu.VMEM((rows, width), F32)],
        flops=8 * rows * width * cores * units,
        moved=18 * 2**20,
    )(normed, grad, keep, expand, reduce)


def temporal_backward(
    grad_near, grad_first, grad_second, hidden2, hidden1, grad_result, keep, gains, heads, merge2, project, merge1
):
    rows, width = hidden1.shape
    local = merge1.shape[1]
    span = rows // FRAMES
    group_rows = FRAMES * GROUP

    def kernel(
        near_ref,
        first_ref,
        second_ref,
        hidden2_ref,
        hidden1_ref,
        result_ref,
        keep_ref,
        gains_ref,
        heads_ref,
        merge2_ref,
        project_ref,
        merge1_ref,
        branch2_ref,
        grad_heads_ref,
        branch1_ref,
        mixed1_ref,
        carried_ref,
        gain3_ref,
        gain2_ref,
        grad_hidden,
        grad_normed,
        grad_mixed,
    ):
        step = pl.program_id(0)

        @pl.when(step == 0)
        def _():
            far = jnp.concatenate([first_ref[...], second_ref[...]])
            incoming = near_ref[...].astype(F32) + far.astype(F32)
            back, gain3_ref[...] = norm_back(hidden2_ref[...], gains_ref[2:3], incoming)
            total = result_ref[...].astype(F32) + back
            grad_hidden[...] = total
            branch2_ref[...] = (keep_ref[...] * total).astype(BF16)
            grad_normed[...] = jnp.zeros_like(grad_normed)

        back_mixed = mm(branch2_ref[...], merge2_ref[0], NT).astype(BF16)
        grad_mixed[...] = back_mixed.reshape(FRAMES, span, local)
        allowed = place_masks(lax.axis_index("wide") % 2, FRAMES, True)
        for g in range(span // GROUP):
            band = pl.ds(g * GROUP, GROUP)
            for at in range(0, local, PAIR):
                part = pl.ds(at, PAIR)
                terms = [heads_ref[0, c, :, band, part].reshape(group_rows, PAIR) for c in range(3)]
                grad = grad_mixed[:, band, part].reshape(group_rows, PAIR)
                grads = attend_back_pair(*terms, grad, allowed)
                for c in range(3):
                    grad_heads_ref[0, c, :, band, part] = grads[c].reshape(FRAMES, GROUP, PAIR)
        total = mm(grad_heads_ref[0, 0].reshape(rows, local), project_ref[0, 0], NT)
        for c in range(1, 3):
            total += mm(grad_heads_ref[0, c].reshape(rows, local), project_ref[0, c], NT)
        grad_normed[...] += total

        @pl.when(step == 3)
        def _():
            back, gain2_ref[...] = norm_back(hidden1_ref[...], gains_ref[1:2], grad_normed[...])
            total = grad_hidden[...] + back
            carried_ref[...] = total.astype(BF16)
            branch1_ref[...] = (keep_ref[...] * total).astype(BF16)
            for n in range(4):
                mixed1_ref[n] = mm(branch1_ref[...], merge1_ref[n], NT).astype(BF16)

    full = whole((rows, width))
    row = whole((1, width))
    return call(
        kernel,
        (4,),
        [
            full,
            whole((rows // 2, width)),
            whole((rows // 2, width)),
            full,
            full,
            full,
            whole((rows, 1)),
            whole((3, width)),
            pl.BlockSpec((1, 3, FRAMES, span, local), lambda n: (n, 0, 0, 0, 0)),
            pl.BlockSpec((1, local, width), lambda n: (n, 0, 0)),
            pl.BlockSpec((1, 3, width, local), lambda n: (n, 0, 0, 0)),
            whole((4, local, width)),
        ],
        [
            full,
            pl.BlockSpec((1, 3, FRAMES, span, local), lambda n: (n, 0, 0, 0, 0)),
            full,
            whole((4, rows, local)),
            full,
            row,
            row,
        ],
        [
            shape_of((rows, width)),
            shape_of((4, 3, FRAMES, span, local)),
            shape_of((rows, width)),
            shape_of((4, rows, local)),
            shape_of((rows, width)),
            shape_of((1, width), F32),
            shape_of((1, width), F32),
        ],
        scratch=[
            pltpu.VMEM((rows, width), F32),
            pltpu.VMEM((rows, width), F32),
            pltpu.VMEM((FRAMES, span, local), BF16),
        ],
        flops=2 * rows * width * width * 8,
        moved=30 * 2**20,
    )(grad_near, grad_first, grad_second, hidden2, hidden1, grad_result, keep, gains, heads, merge2, project, merge1)


def here():
    wide, narrow = lax.axis_index("wide"), lax.axis_index("narrow")
    return wide, narrow, wide % 2, narrow // 2, narrow % 2


def other(wide, narrow, x, y, core):
    if x:
        wide = wide + 1 - 2 * (wide % 2)
    if y:
        narrow = (narrow + 2) % 4
    if core:
        narrow = narrow + 1 - 2 * (narrow % 2)
    return wide, narrow


def beyond(wide, narrow):
    return wide + 2 - 4 * ((wide // 2) % 2), narrow


def place_of(wide, narrow, span):
    return pl.multiple_of(((wide % 2) * 4 + narrow) * span, span)


def remote(src, dst, sems, i, device):
    return pltpu.make_async_remote_copy(
        src_ref=src,
        dst_ref=dst,
        send_sem=sems.at[0, i],
        recv_sem=sems.at[1, i],
        device_id=device,
        device_id_type=pl.DeviceIdType.MESH,
    )


def greet(devices):
    barrier = pltpu.get_barrier_semaphore()
    for device in devices:
        pl.semaphore_signal(
            barrier, inc=1, device_id=device, device_id_type=pl.DeviceIdType.MESH
        )
    pl.semaphore_wait(barrier, len(devices))


OTHERS = [(x, y, c) for x in range(2) for y in range(2) for c in range(2) if x + y + c > 0]
ANY = pl.BlockSpec(memory_space=pl.ANY)


def comm_call(kernel, number, grid, in_specs, out_specs, out_shape, scratch, flops, moved=30 * 2**20):
    return pl.pallas_call(
        kernel,
        grid=grid,
        in_specs=in_specs,
        out_specs=out_specs,
        out_shape=out_shape,
        scratch_shapes=scratch,
        compiler_params=pltpu.CompilerParams(
            vmem_limit_bytes=VMEM_LIMIT, collective_id=number, has_side_effects=True
        ),
        cost_estimate=pl.CostEstimate(flops=flops, bytes_accessed=moved, transcendentals=0),
    )


def attention_forward(
    tokens,
    extra,
    gains,
    project,
    merge1,
    project2,
    merge2,
    expand,
    reduce,
    grad_out,
    keep,
):
    frames, places, width = tokens.shape
    local = project.shape[-1]
    span = places // 8
    rows = FRAMES * span
    group_rows = FRAMES * GROUP
    half = frames // 2
    shards = (merge1, project2[0], project2[1], project2[2], merge2)
    count = len(shards)

    def kernel(
        tokens_ref,
        extra_ref,
        gains_ref,
        project_ref,
        keep_ref,
        all_tokens,
        all_extra,
        grad_ref,
        expand_ref,
        reduce_ref,
        merge1_ref,
        project2_ref,
        merge2_ref,
        normed_ref,
        heads_ref,
        hidden1_ref,
        normed2_ref,
        heads2_ref,
        mixed2_ref,
        hidden2_ref,
        normed3_ref,
        first_ref,
        second_ref,
        mixed_out,
        grad_near,
        grad_far,
        expand_pair,
        reduce_pair,
        merge1_out,
        project2_out,
        merge2_out,
        mixed_ref,
        mixed_all,
        tokens_place,
        extra_place,
        merge1_all,
        project2_all,
        merge2_all,
        local_sems,
        move_sems,
        shard_sems,
        mixed_sems,
        *stage,
    ):
        step = pl.program_id(0)
        wide, narrow, x_me, _, _ = here()
        half_me = (wide // 2) % 2
        x_other = other(wide, narrow, 1, 0, 0)
        y_other = other(wide, narrow, 0, 1, 0)
        core_other = other(wide, narrow, 0, 0, 1)
        z_other = beyond(wide, narrow)
        mine = pl.ds(place_of(wide, narrow, span), span)
        near_y = pl.ds(place_of(*y_other, span), span)
        shard = [merge1_ref] + [project2_ref.at[c] for c in range(3)] + [merge2_ref]
        full = [merge1_all] + [project2_all.at[:, c] for c in range(3)] + [merge2_all]

        own = [
            (expand_ref, expand_pair.at[0]),
            (reduce_ref, reduce_pair.at[0]),
            (grad_ref.at[:, mine], grad_near.at[0]),
            (grad_ref.at[:, near_y], grad_far.at[0]),
        ]
        into = [
            pltpu.make_async_copy(a, v, local_sems.at[0, i])
            for i, ((a, _), v) in enumerate(zip(own, stage))
        ]
        back = [
            pltpu.make_async_copy(v, b, local_sems.at[1, i])
            for i, ((_, b), v) in enumerate(zip(own, stage))
        ]
        inside = [
            (all_tokens.at[:, mine], tokens_place.at[0]),
            (all_extra, extra_place.at[0]),
        ] + [(shard[k], full[k].at[0]) for k in range(count)]
        inside = [
            pltpu.make_async_copy(a, b, local_sems.at[0, 4 + i]) for i, (a, b) in enumerate(inside)
        ]
        leaving = [
            (mixed_all, mixed_out),
            (merge1_all, merge1_out),
            (project2_all, project2_out),
            (merge2_all, merge2_out),
        ]
        leaving = [
            pltpu.make_async_copy(a, b, local_sems.at[1, 4 + i]) for i, (a, b) in enumerate(leaving)
        ]
        far = pl.ds(place_of(*x_other, span), span)
        far_y = pl.ds(place_of(*other(wide, narrow, 1, 1, 0), span), span)
        first = [
            remote(all_tokens.at[:, far], tokens_place.at[1], move_sems, 0, x_other),
            remote(all_extra, extra_place.at[1], move_sems, 1, x_other),
            remote(expand_ref, expand_pair.at[1], move_sems, 2, core_other),
            remote(reduce_ref, reduce_pair.at[1], move_sems, 3, core_other),
        ]
        last = [
            remote(grad_ref.at[:, far], grad_near.at[1], move_sems, 4, x_other),
            remote(grad_ref.at[:, far_y], grad_far.at[1], move_sems, 5, x_other),
        ]

        def part(k, which):
            count = shards[k].shape[0] // 2
            return pl.ds(pl.multiple_of(which * count, count), count)

        def over_core(k):
            return remote(shard[k], full[k].at[1], shard_sems, 5 * k, core_other)

        def over_y(k):
            some = part(k, half_me)
            return remote(shard[k].at[some], full[k].at[2, some], shard_sems, 5 * k + 1, y_other)

        def onward(k, which, i, device, slot):
            some = part(k, which)
            return remote(full[k].at[2, some], full[k].at[slot, some], shard_sems, 5 * k + i, device)

        def over_z(k):
            return onward(k, half_me, 2, z_other, 2)

        def near_half(k):
            return onward(k, half_me, 3, core_other, 3)

        def far_half(k):
            return onward(k, 1 - half_me, 4, core_other, 3)

        def forward(k):
            over_y(k).wait_recv()
            over_z(k).start()
            near_half(k).start()

        def complete(k):
            over_z(k).wait_recv()
            far_half(k).start()

        def mixed_copies(chunk):
            copies = []
            some = pl.ds(chunk * (half // 2), half // 2)
            for i, (x, y, c) in enumerate(OTHERS):
                device = other(wide, narrow, x, y, c)
                copies.append(
                    remote(
                        mixed_ref.at[some, pl.ds(place_of(*device, span), span)],
                        mixed_all.at[2 * y + c, x, some],
                        mixed_sems,
                        7 * chunk + i,
                        device,
                    )
                )
            here_copy = pltpu.make_async_copy(
                mixed_ref.at[some, mine], mixed_all.at[0, 0, some], local_sems.at[chunk % 2, 11 + chunk // 2]
            )
            return copies + [here_copy]

        @pl.when(step == 0)
        def _():
            greet([other(wide, narrow, *o) for o in OTHERS] + [z_other])
            for k in range(3):
                over_y(k).start()
            for copy in first:
                copy.start()
            for k in range(count):
                over_core(k).start()
            for copy in into + inside:
                copy.start()

        @pl.when(step == 2)
        def _():
            for copy in into:
                copy.wait()
            for copy in back:
                copy.start()

        @pl.when(step < frames)
        def _():
            start = tokens_ref[0].astype(F32) + extra_ref[0]
            normed = (start * root(start) * gains_ref[0:1]).astype(BF16)
            normed_ref[0] = normed
            for c in range(3):
                heads_ref[c, 0] = mm(normed, project_ref[c]).astype(BF16)
            for at in range(0, local, PAIR):
                lanes = pl.ds(at, PAIR)
                mixed_ref[step, :, lanes] = attend_pair(
                    heads_ref[0, 0, :, lanes],
                    heads_ref[1, 0, :, lanes],
                    heads_ref[2, 0, :, lanes],
                    None,
                )

        @pl.when(step == 2)
        def _():
            forward(0)

        for chunk in range(3):

            @pl.when(step == 2 * chunk + 1)
            def _():
                for copy in mixed_copies(chunk):
                    copy.start()

        @pl.when(step == half)
        def _():
            forward(1)

        @pl.when(step == half + 1)
        def _():
            complete(0)

        @pl.when(step == half + 2)
        def _():
            forward(2)

        @pl.when(step == frames - 1)
        def _():
            for copy in mixed_copies(3):
                copy.start()
            over_y(3).start()
            over_y(4).start()
            for copy in last:
                copy.start()
            complete(1)

        @pl.when(step == frames)
        def _():
            for copy in inside:
                copy.wait()
            over_core(0).wait_recv()
            near_half(0).wait_recv()
            far_half(0).wait_recv()
            first[0].wait_recv()
            first[1].wait_recv()
            for chunk in range(4):
                for copy in mixed_copies(chunk):
                    copy.wait()
            leaving[0].start()
            leaving[1].start()
            branch = mm(mixed_all[0].reshape(rows, local), merge1_all[0])
            for n in range(1, 4):
                branch += mm(mixed_all[n].reshape(rows, local), merge1_all[n])
            begin = tokens_place[...].astype(F32) + extra_place[...]
            hidden1 = begin.reshape(rows, width) + keep_ref[...] * branch
            hidden1_ref[...] = hidden1
            hidden2_ref[...] = hidden1
            normed2_ref[...] = (hidden1 * root(hidden1) * gains_ref[1:2]).astype(BF16)

        @pl.when(step == frames + 1)
        def _():
            complete(2)
            forward(3)
            for k in range(1, count):
                over_core(k).wait_recv()

        @pl.when(step == frames + 2)
        def _():
            complete(3)

        @pl.when(step == frames + 3)
        def _():
            for k in range(1, 4):
                near_half(k).wait_recv()
                far_half(k).wait_recv()
            leaving[2].start()

        @pl.when(step >= frames)
        def _():
            n = step - frames
            for c in range(3):
                head = mm(normed2_ref[...], project2_all[n, c]).astype(BF16)
                heads2_ref[0, c] = head.reshape(FRAMES, span, local)
            allowed = place_masks(x_me, FRAMES, False)
            for g in range(span // GROUP):
                band = pl.ds(g * GROUP, GROUP)
                for at in range(0, local, PAIR):
                    lanes = pl.ds(at, PAIR)
                    terms = [
                        heads2_ref[0, c, :, band, lanes].reshape(group_rows, PAIR) for c in range(3)
                    ]
                    mixed = attend_pair(*terms, allowed)
                    mixed2_ref[0, :, band, lanes] = mixed.reshape(FRAMES, GROUP, PAIR)

        @pl.when(step == frames + 1)
        def _():
            forward(4)

        @pl.when(step == frames + 2)
        def _():
            complete(4)

        @pl.when(step == frames + 3)
        def _():
            near_half(4).wait_recv()
            far_half(4).wait_recv()
            leaving[3].start()

        @pl.when(step >= frames)
        def _():
            merged = mm(mixed2_ref[0].reshape(rows, local), merge2_all[step - frames])
            hidden2_ref[...] += keep_ref[...] * merged

        @pl.when(step == frames + 3)
        def _():
            hidden2 = hidden2_ref[...]
            normed3 = (hidden2 * root(hidden2) * gains_ref[2:3]).astype(BF16)
            normed3_ref[...] = normed3
            first_ref[...] = normed3[: rows // 2]
            second_ref[...] = normed3[rows // 2 :]
            for copy in first[2:] + last:
                copy.wait()
            for copy in first[:2]:
                copy.wait_send()
            for copy in back + leaving:
                copy.wait()
            for k in range(count):
                for copy in (over_core(k), over_y(k), over_z(k), near_half(k), far_half(k)):
                    copy.wait_send()

    def frame(step):
        return jnp.minimum(step, frames - 1)

    def turn(step):
        return jnp.maximum(step - frames, 0)

    full = whole((rows, width))
    return comm_call(
        kernel,
        0,
        (frames + 4,),
        [
            pl.BlockSpec((1, places, width), lambda s: (frame(s), 0, 0)),
            pl.BlockSpec((1, 1, width), lambda s: (frame(s), 0, 0)),
            whole((3, width)),
            whole(project.shape),
            whole((rows, 1)),
        ]
        + [ANY] * 8,
        [
            pl.BlockSpec((1, places, width), lambda s: (frame(s), 0, 0)),
            pl.BlockSpec((3, 1, places, local), lambda s: (0, frame(s), 0, 0)),
            full,
            full,
            pl.BlockSpec((1, 3, FRAMES, span, local), lambda s: (turn(s), 0, 0, 0, 0)),
            pl.BlockSpec((1, FRAMES, span, local), lambda s: (turn(s), 0, 0, 0)),
            full,
            full,
            whole((rows // 2, width)),
            whole((rows // 2, width)),
        ]
        + [ANY] * 8,
        [
            shape_of((frames, places, width)),
            shape_of((3, frames, places, local)),
            shape_of((rows, width), F32),
            shape_of((rows, width)),
            shape_of((4, 3, FRAMES, span, local)),
            shape_of((4, FRAMES, span, local)),
            shape_of((rows, width), F32),
            shape_of((rows, width)),
            shape_of((rows // 2, width)),
            shape_of((rows // 2, width)),
            shape_of((4, 2, frames, span, local)),
            shape_of((2, frames, span, width)),
            shape_of((2, frames, span, width)),
            shape_of((2,) + expand.shape),
            shape_of((2,) + reduce.shape),
            shape_of((4,) + merge1.shape),
            shape_of((4,) + project2.shape),
            shape_of((4,) + merge2.shape),
        ],
        [
            pltpu.VMEM((frames, places, local), BF16),
            pltpu.VMEM((4, 2, frames, span, local), BF16),
            pltpu.VMEM((2, frames, span, width), BF16),
            pltpu.VMEM((2, frames, 1, width), F32),
            pltpu.VMEM((4,) + merge1.shape, BF16),
            pltpu.VMEM((4,) + project2.shape, BF16),
            pltpu.VMEM((4,) + merge2.shape, BF16),
            pltpu.SemaphoreType.DMA((2, 13)),
            pltpu.SemaphoreType.DMA((2, 6)),
            pltpu.SemaphoreType.DMA((2, 5 * count)),
            pltpu.SemaphoreType.DMA((2, 28)),
            pltpu.VMEM(expand.shape, BF16),
            pltpu.VMEM(reduce.shape, BF16),
            pltpu.VMEM((frames, span, width), BF16),
            pltpu.VMEM((frames, span, width), BF16),
        ],
        2 * frames * places * width * local * 4 + 2 * rows * width * width * 6,
    )(
        tokens,
        extra[:, None, :],
        gains,
        project,
        keep,
        tokens,
        extra[:, None, :],
        grad_out,
        expand,
        reduce,
        merge1,
        project2,
        merge2,
    )


def feed_outer(normed, grad_inner, grad_branch, active):
    width = normed[0].shape[1]
    units = active[0].shape[1] // 2
    ends = [0]
    for part in normed:
        ends.append(ends[-1] + part.shape[0])
    rows, count = ends[-1], len(normed)
    block = 512
    per = units // block
    wide = lax.axis_size("wide")
    split = (2, wide // 2, 2, width // wide, block)

    def kernel(*refs):
        normed_refs, branch_refs = refs[:count], refs[count : 2 * count]
        inner_refs, active_refs = refs[2 * count : 3 * count], refs[3 * count : 4 * count]
        keep_ref, send_ref, left, right, total, given, taken, sems = refs[4 * count :]
        step = pl.program_id(0)
        wide, narrow, x_me, _, _ = here()
        core_other = other(wide, narrow, 0, 0, 1)

        def over(j):
            return remote(given.at[j], taken.at[j], sems, j, core_other)

        @pl.when(step == 0)
        def _():
            for k in range(count):
                left[:, ends[k] : ends[k + 1]] = normed_refs[k][...].T
                right[:, ends[k] : ends[k + 1]] = branch_refs[k][...].T

        def product(side, parts):
            out = mm(side[:, : ends[1]], parts[0][...])
            for k in range(1, count):
                out += mm(side[:, ends[k] : ends[k + 1]], parts[k][...])
            return out

        expand = product(left, inner_refs)
        reduce = product(right, active_refs)

        @pl.when(step == 0)
        def _():
            greet([core_other])

        @pl.when(step < per)
        def _():
            given[step, 0] = expand.astype(BF16)
            given[step, 1] = reduce.astype(BF16)
            over(step).start()

        @pl.when(step >= per)
        def _():
            j = step - per
            over(j).wait_recv()
            half = split[1:]
            total[0] = (expand + taken[j, 0].astype(F32)).astype(BF16).reshape(half)
            total[1] = (reduce + taken[j, 1].astype(F32)).astype(BF16).reshape(half)
            out = keep_ref.shape
            keep_ref[...] = total[:, :, pl.ds(x_me, 1)].reshape(out)
            send_ref[...] = total[:, :, pl.ds(1 - x_me, 1)].reshape(out)

        @pl.when(step == 2 * per - 1)
        def _():
            for j in range(per):
                over(j).wait_send()

    def columns(part):
        return pl.BlockSpec((part.shape[0], block), lambda j: (0, (j + per) % (2 * per)))

    out = pl.BlockSpec((2, width // 2, block), lambda j: (0, 0, jnp.maximum(j - per, 0)))
    return comm_call(
        kernel,
        3,
        (2 * per,),
        [whole(part.shape) for part in normed + grad_branch]
        + [columns(part) for part in grad_inner + active],
        [out, out],
        [shape_of((2, width // 2, units))] * 2,
        [
            pltpu.VMEM((width, rows), BF16),
            pltpu.VMEM((width, rows), BF16),
            pltpu.VMEM(split, BF16),
            pltpu.VMEM((per, 2, width, block), BF16),
            pltpu.VMEM((per, 2, width, block), BF16),
            pltpu.SemaphoreType.DMA((2, per)),
        ],
        2**20,
        2**20,
    )(*normed, *grad_branch, *grad_inner, *active)


def temporal_outer(
    grad_mixed1, carried, result, mixed1, branch1, mixed2, branch2, normed2, grad_heads
):
    rows, width = branch1.shape
    local = mixed1.shape[-1]
    span = rows // FRAMES
    frames = FRAMES // 2

    def kernel(
        grad_ref,
        carried_ref,
        result_ref,
        mixed1_ref,
        branch1_ref,
        mixed2_ref,
        branch2_ref,
        normed2_ref,
        heads_ref,
        out_ref,
        grad_own,
        carried_own,
        result_far,
        left,
        given,
        taken,
        grad_stage,
        carried_stage,
        local_sems,
        sems,
    ):
        step = pl.program_id(0)
        wide, narrow, x_me, _, _ = here()
        x_other = other(wide, narrow, 1, 0, 0)
        mine = pl.ds(place_of(wide, narrow, span), span)
        copies = [
            remote(
                grad_ref.at[2 * y + c, x],
                grad_own.at[:, mine],
                sems,
                i,
                other(wide, narrow, x, y, c),
            )
            for i, (x, y, c) in enumerate(OTHERS)
        ]
        copies.append(remote(carried_ref.at[1], carried_own.at[:, x_me], sems, 7, x_other))
        copies.append(remote(result_ref.at[0], result_far, sems, 8, other(wide, narrow, 0, 1, 0)))

        def over(y):
            return remote(given.at[y], taken.at[y], sems, 9 + y, other(wide, narrow, 0, 0, 1))

        into = [
            pltpu.make_async_copy(grad_ref.at[0, 0], grad_stage, local_sems.at[0]),
            pltpu.make_async_copy(carried_ref.at[0], carried_stage, local_sems.at[1]),
        ]
        back = [
            pltpu.make_async_copy(grad_stage, grad_own.at[:, mine], local_sems.at[2]),
            pltpu.make_async_copy(carried_stage, carried_own.at[:, x_me], local_sems.at[3]),
        ]

        @pl.when(step == 0)
        def _():
            greet([other(wide, narrow, *o) for o in OTHERS])
            for copy in copies + into:
                copy.start()
            left[0] = branch1_ref[...].T
            left[1] = branch2_ref[...].T
            left[2] = normed2_ref[...].T

        terms = [(0, mixed1_ref[0]), (1, mixed2_ref[0])] + [(2, heads_ref[0, c]) for c in range(3)]
        for k, (which, term) in enumerate(terms):
            total = mm(left[which], term)

            @pl.when(step < 2)
            def _():
                given[step, k] = total.astype(BF16)

            @pl.when(step >= 2)
            def _():
                out_ref[0, k] = total.astype(BF16)

        @pl.when(step < 2)
        def _():
            over(step).start()

        @pl.when(step >= 2)
        def _():
            over(step - 2).wait_recv()
            out_ref[0] = (out_ref[0].astype(F32) + taken[step - 2].astype(F32)).astype(BF16)

        @pl.when(step == 1)
        def _():
            for copy in into:
                copy.wait()
            for copy in back:
                copy.start()

        @pl.when(step == 3)
        def _():
            for copy in copies + back:
                copy.wait()
            for y in range(2):
                over(y).wait_send()

    full = whole((rows, width))

    def turn(j):
        return 2 * (j % 2) + 1 - j // 2

    part = pl.BlockSpec((1, rows, local), lambda j: (turn(j), 0, 0))
    return comm_call(
        kernel,
        1,
        (4,),
        [ANY] * 3
        + [part, full, part, full, full]
        + [pl.BlockSpec((1, 3, rows, local), lambda j: (turn(j), 0, 0, 0))],
        [pl.BlockSpec((1, 5, width, local), lambda j: (jnp.maximum(j - 2, 0), 0, 0, 0))] + [ANY] * 3,
        [
            shape_of((2, 5, width, local)),
            shape_of((frames, 8 * span, local)),
            shape_of((frames, 2, span, width)),
            shape_of(result.shape[1:]),
        ],
        [
            pltpu.VMEM((3, width, rows), BF16),
            pltpu.VMEM((2, 5, width, local), BF16),
            pltpu.VMEM((2, 5, width, local), BF16),
            pltpu.VMEM((frames, span, local), BF16),
            pltpu.VMEM((frames, span, width), BF16),
            pltpu.SemaphoreType.DMA((4,)),
            pltpu.SemaphoreType.DMA((2, 11)),
        ],
        10 * rows * width * width,
    )(
        grad_mixed1.reshape(4, 2, frames, span, local),
        carried.reshape(2, frames, span, width),
        result,
        mixed1,
        branch1,
        mixed2.reshape(4, rows, local),
        branch2,
        normed2,
        grad_heads.reshape(4, 3, rows, local),
    )


class Halving:
    def __init__(self, slots, rows, columns, blocks, first):
        self.slots, self.rows, self.columns, self.first = slots, rows, columns, first
        self.blocks = []
        while blocks > 1:
            blocks //= 2
            self.blocks.append(blocks)

    def scratch(self):
        out = []
        for blocks in self.blocks:
            out.append(pltpu.VMEM((self.slots, blocks, 2, self.rows, self.columns), BF16))
            out.append(pltpu.VMEM((self.slots, blocks, self.rows, self.columns), BF16))
        return out

    def bind(self, refs, sems, base, wide, narrow):
        self.held, self.taken = refs[0::2], refs[1::2]
        self.sems, self.base, self.wide, self.narrow = sems, base, wide, narrow

    def bit(self, level):
        step = 2 ** (self.first + level)
        return step, (self.wide // step) % 2

    def copy(self, level):
        step, bit = self.bit(level)
        device = (self.wide + step - 2 * step * bit, self.narrow)
        return remote(
            self.held[level].at[:, :, 1 - bit],
            self.taken[level],
            self.sems,
            self.base + level,
            device,
        )

    def fill(self, level, value, slot=0):
        count = value.shape[0]
        self.held[level][slot : slot + count] = value.astype(BF16).reshape(
            (count,) + self.held[level].shape[1:]
        )

    def result(self, level):
        _, bit = self.bit(level)
        shape = self.taken[level].shape
        own = self.held[level][:, :, pl.ds(bit, 1)].reshape(shape)
        return own.astype(F32) + self.taken[level][...].astype(F32)

    def advance(self, level):
        self.copy(level).wait_recv()
        total = self.result(level)
        if level + 1 < len(self.blocks):
            self.fill(level + 1, total)
            self.copy(level + 1).start()
            return None
        return total.reshape(self.slots, self.rows, self.columns)

    def close(self):
        for level in range(len(self.blocks)):
            self.copy(level).wait_send()


FIRST = 2


def spatial_backward(
    heads,
    grad_mixed,
    project,
    normed,
    tokens,
    extra,
    gain,
    carried,
    choose,
    gain_two,
    gain_three,
    result_near,
    result_far,
    temporal_grad,
    feed_keep,
    feed_taken,
):
    _, frames, places, local = heads.shape
    width = project.shape[1]
    span = places // 8
    tile = width // 4
    wide_size = lax.axis_size("wide")
    half = wide_size // 2
    block = width // wide_size
    bits = wide_size.bit_length() - 1
    slots = temporal_grad.shape[1]
    units = feed_keep.shape[-1]
    last = slots - FIRST
    feed = Halving(2, block, units, half, 1)
    own = Halving(3, block, local, wide_size, 0)
    timed = Halving(slots, block, local, half, 1)
    engines = (feed, own, timed)
    levels = [len(engine.blocks) for engine in engines]
    attend_end = frames
    outer_end = attend_end + 4
    sum_end = outer_end + frames

    def kernel(
        heads_ref,
        mixed_ref,
        project_ref,
        normed_ref,
        tokens_ref,
        extra_ref,
        gain_ref,
        carried_ref,
        choose_ref,
        gain_two_ref,
        gain_three_ref,
        feed_keep_ref,
        feed_taken_ref,
        near_ref,
        far_ref,
        temporal_ref,
        own_out,
        timed_out,
        feed_out,
        small_out,
        output_ref,
        out_ref,
        grad_heads,
        partial,
        from_core,
        halved,
        from_y,
        done,
        gain_grad,
        table,
        small,
        small_taken,
        first_own,
        first_taken,
        first_sum,
        first_y,
        last_own,
        last_taken,
        last_sum,
        last_x,
        result_stage,
        local_sems,
        sems,
        move_sems,
        small_sems,
        halving_sems,
        *held,
    ):
        step = pl.program_id(0)
        wide, narrow, x_me, y_me, c_me = here()
        x_other = other(wide, narrow, 1, 0, 0)
        y_other = other(wide, narrow, 0, 1, 0)
        core_other = other(wide, narrow, 0, 0, 1)
        beyond_x = [
            (wide + 2**k - 2 ** (k + 1) * ((wide // 2**k) % 2), narrow) for k in range(1, bits)
        ]
        partners = [core_other, x_other] + beyond_x + [y_other]
        at = base = 0
        for engine, count in zip(engines, levels):
            engine.bind(held[at : at + 2 * count], halving_sems, base, wide, narrow)
            at, base = at + 2 * count, base + count

        def core_sum(f):
            return remote(partial.at[f, :, :, 1 - c_me], from_core.at[f], sems, f, core_other)

        def y_sum(f):
            return remote(halved.at[f, :, 1 - y_me], from_y.at[f], sems, frames + f, y_other)

        def y_back(f):
            return remote(done.at[f], out_ref.at[f, :, y_me, c_me], sems, 2 * frames + f, y_other)

        def core_back(f):
            return remote(done.at[f], out_ref.at[f, :, y_me, c_me], sems, 3 * frames + f, core_other)

        def core_onward(f):
            there = out_ref.at[f, :, 1 - y_me, c_me]
            return remote(there, there, sems, 4 * frames + f, core_other)

        def keep_own(f):
            return pltpu.make_async_copy(done.at[f], out_ref.at[f, :, y_me, c_me], local_sems.at[f])

        result = (near_ref.at[0], far_ref)

        def place(y):
            return y_me if y == 0 else 1 - y_me

        def result_x():
            there = output_ref.at[:, x_me, y_me, c_me]
            return remote(near_ref.at[1], there, move_sems, 0, x_other)

        def result_y():
            there = output_ref.at[:, 1 - x_me, y_me, c_me]
            return remote(there, there, move_sems, 1, y_other)

        def result_core(y):
            there = output_ref.at[:, x_me, place(y), c_me]
            return remote(result[y], there, move_sems, 2 + y, core_other)

        def result_onward(y):
            there = output_ref.at[:, 1 - x_me, place(y), c_me]
            return remote(there, there, move_sems, 4 + y, core_other)

        def result_in(y):
            return pltpu.make_async_copy(result[y], result_stage.at[y], local_sems.at[frames + y])

        def result_own(y):
            there = output_ref.at[:, x_me, place(y), c_me]
            return pltpu.make_async_copy(result_stage.at[y], there, local_sems.at[frames + 2 + y])

        early, late_slots = pl.ds(0, FIRST), pl.ds(FIRST, last)
        first_in = pltpu.make_async_copy(
            temporal_ref.at[:, early, :, x_me], first_own, local_sems.at[frames + 4]
        )
        last_in = pltpu.make_async_copy(
            temporal_ref.at[0, late_slots], last_own, local_sems.at[frames + 5]
        )
        first_over_x = remote(
            temporal_ref.at[:, early, :, 1 - x_me], first_taken, move_sems, 6, x_other
        )
        first_over_y = remote(first_sum.at[1], first_y, move_sems, 7, y_other)
        last_over_y = remote(temporal_ref.at[1, late_slots], last_taken, move_sems, 8, y_other)
        last_over_x = remote(last_sum.at[:, :, 1 - x_me], last_x, move_sems, 9, x_other)

        def small_copy(k):
            return remote(small.at[k], small_taken.at[k], small_sems, k, partners[k])

        @pl.when(step == 0)
        def _():
            greet(partners)
            last_over_y.start()
            first_over_x.start()
            feed.fill(0, feed_keep_ref[...].astype(F32) + feed_taken_ref[...].astype(F32))
            feed.copy(0).start()
            result_x().start()
            first_in.start()
            last_in.start()
            for y in range(2):
                result_core(y).start()
                result_in(y).start()
            gain_grad[...] = jnp.zeros_like(gain_grad)
            table[...] = jnp.zeros_like(table)

        @pl.when(step < attend_end)
        def _():
            rows = pl.ds(pl.multiple_of(step * places, places), places)
            for at in range(0, local, PAIR):
                lanes = pl.ds(at, PAIR)
                grads = attend_back_pair(
                    heads_ref[0, 0, :, lanes],
                    heads_ref[1, 0, :, lanes],
                    heads_ref[2, 0, :, lanes],
                    mixed_ref[0, :, lanes],
                    None,
                )
                for c in range(3):
                    grad_heads[c, rows, lanes] = grads[c]
            total = mm(grad_heads[0, rows], project_ref[0], NT)
            for c in range(1, 3):
                total += mm(grad_heads[c, rows], project_ref[c], NT)
            partial[step] = total.astype(BF16).reshape(2, 2, 2, span, width)
            core_sum(step).start()

        @pl.when((step >= 1) & (step < attend_end + 1))
        def _():
            f = step - 1
            core_sum(f).wait_recv()
            mine = partial[f, :, :, pl.ds(c_me, 1)].reshape(2, 2, span, width)
            halved[f] = (mine.astype(F32) + from_core[f].astype(F32)).astype(BF16)

        @pl.when(step == 1)
        def _():
            for y in range(2):
                result_in(y).wait()
                result_own(y).start()

        @pl.when(step == attend_end)
        def _():
            for f in range(frames // 2):
                y_sum(f).start()
            first_in.wait()
            first_over_x.wait_recv()
            first_sum[...] = (first_own[...].astype(F32) + first_taken[...].astype(F32)).astype(BF16)
            first_over_y.start()
            for f in range(frames // 2, frames):
                y_sum(f).start()
            feed.advance(0)

        @pl.when((step >= attend_end) & (step < outer_end))
        def _():
            pairs = tile // (2 * block)
            j = (step - attend_end) * pairs
            for c in range(3):
                grad = mm(normed_ref[...], grad_heads[c], TN).astype(BF16)
                own.held[0][c, pl.ds(j, pairs)] = grad.reshape(pairs, 2, block, local)

        @pl.when(step == attend_end + 2)
        def _():
            last_in.wait()
            last_over_y.wait_recv()
            last_sum[...] = (last_own[...].astype(F32) + last_taken[...].astype(F32)).astype(BF16)
            last_over_x.start()

        @pl.when(step == outer_end)
        def _():
            own.copy(0).start()
            result_x().wait_recv()
            result_y().start()
            result_onward(0).start()
            total = feed.advance(1)
            if total is not None:
                feed_out[...] = total

        @pl.when(step >= outer_end)
        def _():
            f = step - outer_end
            y_sum(f).wait_recv()
            mine = halved[f, :, pl.ds(y_me, 1)].reshape(2 * span, width)
            incoming = mine.astype(F32) + from_y[f].reshape(2 * span, width).astype(F32)
            start = pl.multiple_of(narrow * span, span)
            begin = jnp.concatenate(
                [tokens_ref[0, pl.ds(start, span)], tokens_ref[0, pl.ds(4 * span + start, span)]]
            )
            begin = begin.astype(F32) + extra_ref[0]
            back, gain_part = norm_back(begin, gain_ref[0:1], incoming)
            gain_grad[...] += gain_part
            grad = carried_ref[0].reshape(2 * span, width).astype(F32) + back
            table[...] += choose_ref[0] * jnp.sum(grad, axis=0, keepdims=True)
            done[f] = grad.astype(BF16).reshape(2, span, width)
            y_back(f).start()
            core_back(f).start()
            keep_own(f).start()

        @pl.when(step == outer_end + 1)
        def _():
            first_over_y.wait_recv()
            timed.fill(0, first_sum[0].astype(F32) + first_y[...].astype(F32))
            last_over_x.wait_recv()
            mine = last_sum[:, :, pl.ds(x_me, 1)].reshape(last_x.shape)
            timed.fill(0, mine.astype(F32) + last_x[...].astype(F32), FIRST)
            timed.copy(0).start()

        @pl.when(step == sum_end - 2)
        def _():
            timed.advance(0)

        @pl.when(step == sum_end - 1)
        def _():
            small[0, 0:1] = gain_grad[...]
            small[0, 1:2] = gain_two_ref[...]
            small[0, 2:3] = gain_three_ref[...]
            small[0, 3:11] = table[...]
            small[0, 11:] = jnp.zeros_like(small[0, 11:])
            small_copy(0).start()

            def small_sum(k):
                small_copy(k).wait_recv()
                small[k + 1] = small[k] + small_taken[k]
                if k + 1 < len(partners):
                    small_copy(k + 1).start()

            def back(f):
                y_back(f).wait_recv()
                core_onward(f).start()

            def finish(engine, out, level):
                if level < len(engine.blocks):
                    total = engine.advance(level)
                    if total is not None:
                        out[...] = total

            own.advance(0)
            small_sum(0)
            back(0)
            back(1)
            finish(own, own_out, 1)
            finish(timed, timed_out, 1)
            back(2)
            result_y().wait_recv()
            result_onward(1).start()
            small_sum(1)
            back(3)
            for level in range(2, max(levels)):
                finish(feed, feed_out, level)
                finish(timed, timed_out, level)
                finish(own, own_out, level)
            for k in range(2, len(partners)):
                small_sum(k)
            small_out[...] = small[len(partners)]
            for f in range(4, frames):
                back(f)
            for engine in engines:
                engine.close()
            for k in range(len(partners)):
                small_copy(k).wait_send()
            for f in range(frames):
                core_sum(f).wait_send()
                y_sum(f).wait_send()
                y_back(f).wait_send()
                core_back(f).wait()
                core_onward(f).wait()
                keep_own(f).wait()
            result_x().wait_send()
            result_y().wait_send()
            for y in range(2):
                result_core(y).wait()
                result_onward(y).wait()
                result_own(y).wait()
            for copy in (first_over_x, first_over_y, last_over_y, last_over_x):
                copy.wait_send()

    def frame(step):
        return jnp.minimum(step, frames - 1)

    def late(step):
        return jnp.clip(step - outer_end, 0, frames - 1)

    def piece(step):
        return jnp.clip(step - attend_end, 0, 3)

    block_shape = (half, 2, block, local)
    small_rows = 16
    scratch = [
        pltpu.VMEM((3, frames * places, local), BF16),
        pltpu.VMEM((frames, 2, 2, 2, span, width), BF16),
        pltpu.VMEM((frames, 2, 2, span, width), BF16),
        pltpu.VMEM((frames, 2, 2, span, width), BF16),
        pltpu.VMEM((frames, 2, span, width), BF16),
        pltpu.VMEM((frames, 2, span, width), BF16),
        pltpu.VMEM((1, width), F32),
        pltpu.VMEM((choose.shape[1], width), F32),
        pltpu.VMEM((bits + 3, small_rows, width), F32),
        pltpu.VMEM((bits + 2, small_rows, width), F32),
        pltpu.VMEM((2, FIRST, half, block, local), BF16),
        pltpu.VMEM((2, FIRST, half, block, local), BF16),
        pltpu.VMEM((2, FIRST, half, block, local), BF16),
        pltpu.VMEM((FIRST, half, block, local), BF16),
        pltpu.VMEM((last,) + block_shape, BF16),
        pltpu.VMEM((last,) + block_shape, BF16),
        pltpu.VMEM((last,) + block_shape, BF16),
        pltpu.VMEM((last, half, block, local), BF16),
        pltpu.VMEM((2, frames, span, width), BF16),
        pltpu.SemaphoreType.DMA((frames + 6,)),
        pltpu.SemaphoreType.DMA((2, 5 * frames)),
        pltpu.SemaphoreType.DMA((2, 10)),
        pltpu.SemaphoreType.DMA((2, bits + 2)),
        pltpu.SemaphoreType.DMA((2, sum(levels))),
    ]
    for engine in engines:
        scratch += engine.scratch()
    return comm_call(
        kernel,
        2,
        (sum_end,),
        [
            pl.BlockSpec((3, 1, places, local), lambda s: (0, frame(s), 0, 0)),
            pl.BlockSpec((1, places, local), lambda s: (frame(s), 0, 0)),
            whole(project.shape),
            pl.BlockSpec((frames * places, tile), lambda s: (0, piece(s))),
            pl.BlockSpec((1, places, width), lambda s: (late(s), 0, 0)),
            pl.BlockSpec((1, 1, width), lambda s: (late(s), 0, 0)),
            whole(gain.shape),
            pl.BlockSpec((1, 2, span, width), lambda s: (late(s), 0, 0, 0)),
            pl.BlockSpec((1, choose.shape[1], 1), lambda s: (late(s), 0, 0)),
            whole((1, width)),
            whole((1, width)),
            whole(feed_keep.shape),
            whole(feed_taken.shape),
            ANY,
            ANY,
            ANY,
        ],
        [
            whole((3, block, local)),
            whole((slots, block, local)),
            whole((2, block, units)),
            whole((small_rows, width)),
            ANY,
            ANY,
        ],
        [
            shape_of((3, block, local), F32),
            shape_of((slots, block, local), F32),
            shape_of((2, block, units), F32),
            shape_of((small_rows, width), F32),
            shape_of((frames, 2, 2, 2, span, width)),
            shape_of((frames, 2, 2, 2, span, width)),
        ],
        scratch,
        2 * frames * places * width * local * 8,
    )(
        heads,
        grad_mixed,
        project,
        normed.reshape(frames * places, width),
        tokens,
        extra[:, None, :],
        gain,
        carried,
        choose,
        gain_two,
        gain_three,
        feed_keep,
        feed_taken,
        result_near,
        result_far,
        temporal_grad.reshape((2, slots) + block_shape),
    )


def finish(output, grad_tokens, own, timed, feed, small, table_rows):
    frames, places, width = output.shape
    block = width // lax.axis_size("wide")
    local = own.shape[-1]
    units = feed.shape[-1]

    def kernel(
        output_ref,
        grad_ref,
        own_ref,
        timed_ref,
        feed_ref,
        small_ref,
        output_out,
        grad_out,
        gains_out,
        table_out,
        project1_out,
        merge1_out,
        project2_out,
        merge2_out,
        expand_out,
        reduce_out,
    ):
        output_out[...] = output_ref[...]
        grad_out[...] = grad_ref[...].astype(F32)

        @pl.when(pl.program_id(0) == 0)
        def _():
            project1_out[...] = own_ref[...]
            merge1_out[...] = timed_ref[0].T
            merge2_out[...] = timed_ref[1].T
            project2_out[...] = timed_ref[2:]
            expand_out[...] = feed_ref[0]
            reduce_out[...] = feed_ref[1].T
            me = lax.axis_index("wide")
            total = jnp.zeros((small_ref.shape[0], block), F32)
            for w in range(width // block):
                total += jnp.where(me == w, small_ref[:, w * block : (w + 1) * block], 0.0)
            gains_out[...] = total[:3]
            table_out[...] = total[3 : 3 + table_rows]

    frame = pl.BlockSpec((4, places, width), lambda f: (f, 0, 0))
    shapes = [
        (3, block),
        (table_rows, block),
        own.shape,
        (local, block),
        (3, block, local),
        (local, block),
        (block, units),
        (units, block),
    ]
    return call(
        kernel,
        (frames // 4,),
        [frame, frame] + [whole(part.shape) for part in (own, timed, feed, small)],
        [frame, frame] + [whole(shape) for shape in shapes],
        [shape_of(output.shape), shape_of(output.shape, F32)]
        + [shape_of(shape, F32) for shape in shapes],
        moved=30 * 2**20,
    )(output, grad_tokens, own, timed, feed, small)


def swap(value, axis, bit):
    size = lax.axis_size(axis)
    return lax.ppermute(value, axis, [(i, i ^ bit) for i in range(size)])


def after(value, *earlier):
    return lax.optimization_barrier((value,) + earlier)[0]


def body(
    tokens,
    frame_counts,
    actions,
    action_table,
    norm_gains,
    spatial_project,
    spatial_merge,
    temporal_project,
    temporal_merge,
    expand_weight,
    reduce_weight,
    grad_out,
):
    frames_dev, tokens_frame, width = tokens.shape
    wide_me, narrow_me = lax.axis_index("wide"), lax.axis_index("narrow")
    x_me = wide_me % 2
    span = tokens_frame // 8
    rows = 2 * frames_dev * span
    spatial_project = spatial_project.transpose(1, 0, 2)
    temporal_project = temporal_project.transpose(1, 0, 2)

    def keep_of(wide_place):
        frame_ids = wide_place * frames_dev + jnp.arange(frames_dev, dtype=jnp.int32)
        clip_places = jnp.arange(frame_counts.shape[0], dtype=jnp.int32)
        clip_count = jnp.sum(
            jnp.where((frame_ids // FRAMES)[:, None] == clip_places[None, :], frame_counts[None, :], 0),
            axis=1,
        )
        return (frame_ids % FRAMES < clip_count).astype(F32)

    keep_place = jnp.concatenate([keep_of(wide_me), keep_of(wide_me + 1 - 2 * x_me)])
    keep_place = jnp.broadcast_to(keep_place[:, None], (2 * frames_dev, span)).reshape(rows, 1)
    choose = (
        actions[:, None] == jnp.arange(action_table.shape[0], dtype=jnp.int32)[None, :]
    ).astype(BF16)
    extra = jnp.dot(choose, action_table, preferred_element_type=F32)

    (
        normed1,
        heads1,
        hidden1,
        normed2,
        heads2,
        mixed2,
        hidden2,
        normed3,
        normed3_first,
        normed3_second,
        mixed1,
        grad_result,
        grad_result_far,
        expand_pair,
        reduce_pair,
        merge1_all,
        project_all,
        merge2_all,
    ) = attention_forward(
        tokens,
        extra,
        norm_gains,
        spatial_project,
        spatial_merge,
        temporal_project,
        temporal_merge,
        expand_weight,
        reduce_weight,
        grad_out,
        keep_place,
    )
    mixed1 = mixed1.reshape(4, rows, mixed1.shape[-1])

    grad_result = grad_result.reshape(rows, width)
    grad_result_far = grad_result_far.reshape(rows, width)
    first_far = swap(normed3_first, "narrow", 2)
    second_far = swap(normed3_second, "narrow", 2)
    near = feed_forward(normed3, grad_result, keep_place, expand_pair, reduce_pair)
    first_far = after(first_far, near[0])
    first = feed_forward(first_far, grad_result_far, keep_place, expand_pair, reduce_pair, 0)
    second_far = after(second_far, first[0])
    second = feed_forward(second_far, grad_result_far, keep_place, expand_pair, reduce_pair, 1)
    grad_first = swap(first[4], "narrow", 2)
    grad_second = swap(second[4], "narrow", 2)
    feed_keep, feed_send = feed_outer(
        [normed3, first_far, second_far],
        [near[1], first[1], second[1]],
        [near[2], first[2], second[2]],
        [near[0], first[0], second[0]],
    )

    branch2_grad, grad_heads2, branch1_grad, grad_mixed1, carried, gain_three, gain_two = temporal_backward(
        near[4],
        after(grad_first, feed_keep),
        grad_second,
        hidden2,
        hidden1,
        grad_result,
        keep_place,
        norm_gains,
        heads2,
        merge2_all,
        project_all,
        merge1_all,
    )
    branch3_far = jnp.concatenate(
        [
            swap(after(first[3], grad_second), "narrow", 2),
            swap(after(second[3], grad_second), "narrow", 2),
        ]
    )
    feed_taken = swap(after(feed_send, grad_second), "wide", 1)
    branch3 = near[3].astype(F32) + branch3_far.astype(F32)
    result = (hidden2 + keep_place * branch3).astype(BF16).reshape(2, frames_dev, span, width)
    temporal_grad, grad_mixed1, carried, result_far = temporal_outer(
        grad_mixed1, carried, result, mixed1, branch1_grad, mixed2, branch2_grad, normed2, grad_heads2
    )

    project1_grad, temporal_grad, feed_grad, small, output, grad_tokens = spatial_backward(
        heads1,
        grad_mixed1,
        spatial_project,
        normed1,
        tokens,
        extra,
        norm_gains,
        carried,
        choose.astype(F32)[:, :, None],
        gain_two,
        gain_three,
        result,
        result_far,
        temporal_grad,
        feed_keep,
        feed_taken,
    )
    (
        output,
        grad_tokens,
        gains_grad,
        table_grad,
        project1_grad,
        merge1_grad,
        project2_grad,
        merge2_grad,
        expand_grad,
        reduce_grad,
    ) = finish(
        output.reshape(tokens.shape),
        grad_tokens.reshape(tokens.shape),
        project1_grad,
        temporal_grad,
        feed_grad,
        small,
        action_table.shape[0],
    )
    return (
        output,
        grad_tokens,
        gains_grad,
        table_grad,
        project1_grad.transpose(1, 0, 2),
        merge1_grad,
        project2_grad.transpose(1, 0, 2),
        merge2_grad,
        expand_grad,
        reduce_grad,
    )


def solution(mesh):
    return jax.shard_map(
        body,
        mesh=mesh,
        in_specs=(
            P("wide", None, None),
            P(),
            P("wide"),
            P(),
            P(),
            P(None, None, "narrow"),
            P("narrow", None),
            P(None, None, "narrow"),
            P("narrow", None),
            P(None, "narrow"),
            P("narrow", None),
            P("wide", None, None),
        ),
        out_specs=(
            P("wide", None, None),
            P("wide", None, None),
            P(None, "wide"),
            P(None, "wide"),
            P("wide", None, "narrow"),
            P("narrow", "wide"),
            P("wide", None, "narrow"),
            P("narrow", "wide"),
            P("wide", "narrow"),
            P("narrow", "wide"),
        ),
        check_vma=False,
    )
```
